256 devices in a mesh: gx: 32 (over z, x_hi, core), gy: 8 (over x_lo, y).
Axes of the slice: x: 4 (x_hi: 2, x_lo: 2; x = x_hi * 2 + x_lo), y: 4, z: 8, core: 2. Of those that a mesh axis runs over, the one named last changes fastest.
Arguments:
- charges: bfloat16 [640, 160, 128], P('gx', 'gy'), may hold values from -6 to 6
- kernels: bfloat16 [2, 21, 21, 21], replicated, may hold values from -0.0625 to 0.0625
Outputs:
- potential: float32 [640, 160, 128], P('gx', 'gy')
The draws below stay inside these ranges and needn't reach their ends.
All inputs are finite; a program needn't handle non-finite values.
Results may differ from the reference program's by a relative error of at most 0.0003.
Values may be sent and summed in bfloat16 or wider, within the bound.
No kernel may reach another device: no remote copies, remote signals or barrier semaphores. Data moves between devices by JAX's collectives and lax.ppermute only.
A program may use at most 64 MiB of HBM per device.

```python
import math
import jax
import jax.numpy as jnp
from jax import lax

NZ = 128
REACH = 10
NX = 640
NY = 160


def legendre_pair(count):
    position = 2.0 * (jnp.arange(count).astype(jnp.float32) + 0.5) / count - 1.0
    cubic = 0.5 * (5.0 * position ** 3 - 3.0 * position)
    quartic = 0.125 * (35.0 * position ** 4 - 30.0 * position ** 2 + 3.0)
    return cubic + quartic


def draw_charges(key, part):
    key = jax.random.fold_in(key, 11)
    noise = jax.random.normal(key, (NX, NY, NZ), jnp.float32)
    cells_x = jnp.arange(NX).astype(jnp.float32)
    along_x = 0.3 * jnp.cos(2.0 * math.pi * 4.0 * cells_x / NX)
    along_y = 0.15 * legendre_pair(NY)
    along_z = 0.15 * legendre_pair(NZ)
    total = noise + along_x[:, None, None] + along_y[None, :, None] + along_z[None, None, :]
    return jnp.clip(total, -6.0, 6.0).astype(jnp.bfloat16)


def scatter_about(rng, shape, deviation, most, dtype=jnp.bfloat16):
    entries = deviation * jax.random.normal(rng, shape, jnp.float32)
    return jnp.clip(entries, min=-most, max=most).astype(dtype)


def setup_inputs(seed: int = 0) -> dict:
    key_of = jax.random.split(jax.random.key(seed), 3)
    charges = draw_charges(jax.random.fold_in(key_of[2], 71), 0)
    kernels = scatter_about(key_of[1], (2, 2 * REACH + 1, 2 * REACH + 1, 2 * REACH + 1), ((2 * REACH + 1) ** 3) ** -0.5, 0.0625)
    return {"charges": charges, "kernels": kernels}


spread_norm = 1.2533141

def interp_weight(offset):
    distance = jnp.abs(offset)
    unit = jnp.ones(offset.shape, jnp.float32)
    return jnp.where(distance == 0, unit, jnp.where(distance == 1, 0.5625 * unit, jnp.where(distance == 3, -0.0625 * unit, 0.0 * unit)))

def restrict_matrix(count, width, margin):
    rows_idx = jnp.arange(count).astype(jnp.int32)
    cols_idx = jnp.arange(width).astype(jnp.int32)
    return interp_weight(cols_idx[None, :] - margin - 2 * rows_idx[:, None])

def gauss_weight(offset, spread):
    scaled = offset.astype(jnp.float32) / spread
    return jnp.exp(-scaled * scaled) / jnp.sqrt(jnp.float32(spread * spread_norm))

def top_matrix(coarse_count, spread):
    prolong = restrict_matrix(coarse_count, 2 * coarse_count, 0).T
    cells = jnp.arange(coarse_count).astype(jnp.int32)
    gauss = gauss_weight(cells[:, None] - cells[None, :], spread)
    return jnp.dot(prolong, gauss, precision=lax.Precision.HIGHEST)

def band_matrix(kernel_row, length):
    cells = jnp.arange(length).astype(jnp.int32)
    offset = cells[:, None] - cells[None, :] + 10
    inside = (offset >= 0) & (offset <= 20)
    values = jnp.take(kernel_row, jnp.clip(offset, 0, 20))
    return jnp.where(inside, values, jnp.zeros_like(values))

def direct_sum(field, kernel):
    size_x, size_y, size_z = field.shape
    padded = jnp.pad(field, ((10, 10), (10, 10), (0, 0)))

    def per_plane(shift_a, total):
        slab = lax.dynamic_slice_in_dim(padded, shift_a, size_x, 0)
        plane = lax.dynamic_index_in_dim(kernel, shift_a, 0, keepdims=False)
        for shift_b in range(21):
            band = band_matrix(plane[shift_b], size_z)
            total = total + jnp.einsum('xyz,zw->xyw', slab[:, shift_b:shift_b + size_y, :], band, precision=lax.Precision.HIGHEST)
        return total
    return lax.fori_loop(0, 21, per_plane, jnp.zeros(field.shape, jnp.float32))

def restrict_all(field):
    size_x, size_y, size_z = field.shape
    along_x = restrict_matrix(size_x // 2, size_x, 0)
    along_y = restrict_matrix(size_y // 2, size_y, 0)
    along_z = restrict_matrix(size_z // 2, size_z, 0)
    out = jnp.einsum('ip,pqz->iqz', along_x, field, precision=lax.Precision.HIGHEST)
    out = jnp.einsum('jq,iqz->ijz', along_y, out, precision=lax.Precision.HIGHEST)
    return jnp.einsum('kz,ijz->ijk', along_z, out, precision=lax.Precision.HIGHEST)

def prolong_all(field):
    size_x, size_y, size_z = field.shape
    along_x = restrict_matrix(size_x, 2 * size_x, 0)
    along_y = restrict_matrix(size_y, 2 * size_y, 0)
    along_z = restrict_matrix(size_z, 2 * size_z, 0)
    out = jnp.einsum('ip,ijk->pjk', along_x, field, precision=lax.Precision.HIGHEST)
    out = jnp.einsum('jq,pjk->pqk', along_y, out, precision=lax.Precision.HIGHEST)
    return jnp.einsum('kz,pqk->pqz', along_z, out, precision=lax.Precision.HIGHEST)

def reference(charges, kernels):
    spread = NX / 16.0
    fine_field = charges.astype(jnp.float32)
    tables = kernels.astype(jnp.float32)
    fine_part = direct_sum(fine_field, tables[0])
    middle = lax.optimization_barrier(restrict_all(fine_field).astype(jnp.bfloat16)).astype(jnp.float32)
    middle_sum = direct_sum(middle, tables[1])
    coarse = restrict_all(middle)
    matrix_x = top_matrix(NX // 4, spread)
    matrix_y = top_matrix(NY // 4, spread)
    matrix_z = top_matrix(NZ // 4, spread)
    top = jnp.einsum('ia,abc->ibc', matrix_x, coarse, precision=lax.Precision.HIGHEST)
    top = jnp.einsum('jb,ibc->ijc', matrix_y, top, precision=lax.Precision.HIGHEST)
    top = jnp.einsum('kc,ijc->ijk', matrix_z, top, precision=lax.Precision.HIGHEST)
    middle_potential = middle_sum + top
    return fine_part + prolong_all(middle_potential)
```

```python
import functools
import numpy as np
import jax
import jax.numpy as jnp
from jax import lax
from jax.experimental import pallas as pl
from jax.experimental.pallas import tpu as pltpu
from jax.sharding import PartitionSpec as P

f32 = jnp.float32
bf16 = jnp.bfloat16
spread_norm = 1.2533141
HIGHEST = lax.Precision.HIGHEST
REACH = 10
TAPS = 21


def weight_np(offset):
    d = np.abs(offset)
    return np.where(d == 0, 1.0, np.where(d == 1, 0.5625, np.where(d == 3, -0.0625, 0.0)))


def top_matrix_np(n, spread):
    prolong = weight_np(np.arange(2 * n)[:, None] - 2 * np.arange(n)[None, :])
    offset = (np.arange(n)[:, None] - np.arange(n)[None, :]) / spread
    return prolong @ (np.exp(-offset * offset) / np.sqrt(spread * spread_norm))


def lane_tiles(m):
    return m.reshape(m.shape[0], -1, 128).transpose(1, 0, 2).astype(np.float32)


def matrix_x_np(spread):
    m = top_matrix_np(160, spread).reshape(320, 32, 5)
    out = np.zeros((328, 32, 8))
    out[1:321, :, :5] = m
    return lane_tiles(out.reshape(328, 256))


def matrix_y_np(spread):
    m = top_matrix_np(40, spread).reshape(80, 8, 5)
    out = np.zeros((88, 8, 8))
    out[2:82, :, :5] = m
    return lane_tiles(np.repeat(out.reshape(88, 64), 32, axis=1))


def matrix_z_np(spread):
    m = top_matrix_np(32, spread).T
    out = np.zeros((2, 8, 32, 2, 64))
    for par in range(2):
        out[par, :, :, par, :] = m[None]
    return out.reshape(512, 128).astype(np.float32)


def spots_np():
    taps = np.arange(TAPS)[:, None]
    lanes = np.arange(128)[None, :]
    near = lanes == (REACH - taps) % 128
    far = lanes == (64 + REACH - taps) % 128
    return near, far


def weight(d):
    d = jnp.abs(d)
    return jnp.where(d == 0, 1.0, jnp.where(d == 1, 0.5625, jnp.where(d == 3, -0.0625, 0.0))).astype(f32)


def iota2(shape):
    return (lax.broadcasted_iota(jnp.int32, shape, 0), lax.broadcasted_iota(jnp.int32, shape, 1))


def vmem_call(body, out_shape, scratch, name, args, smem=0, flops=0):
    specs = [pl.BlockSpec(memory_space=pltpu.SMEM)] * smem
    specs += [pl.BlockSpec(memory_space=pltpu.VMEM)] * (len(args) - smem)
    return pl.pallas_call(
        body,
        out_shape=out_shape,
        in_specs=specs,
        out_specs=jax.tree.map(lambda _: pl.BlockSpec(memory_space=pltpu.VMEM), out_shape),
        scratch_shapes=scratch,
        compiler_params=pltpu.CompilerParams(vmem_limit_bytes=32 << 20),
        cost_estimate=pl.CostEstimate(flops=flops, bytes_accessed=1 << 16, transcendentals=0),
        name=name,
    )(*args)


def rim_kernel(blk_ref, ylo_ref, yhi_ref, xlo_ref, xhi_ref, wide):
    for out_ref, start in ((xlo_ref, 0), (xhi_ref, 10)):
        wide[:, 0:10, :] = ylo_ref[start : start + 10].astype(f32)
        wide[:, 10:30, :] = blk_ref[start : start + 10].astype(f32)
        wide[:, 30:40, :] = yhi_ref[start : start + 10].astype(f32)
        out_ref[...] = wide[...].astype(bf16)


def restrict_kernel(
    where_ref, blk_ref, ylo_ref, yhi_ref, xlo_ref, xhi_ref,
    d_ref, right_ref, left_ref, own_ref, coarse_ref,
    planes, cells, mid, row,
):
    for x in range(40):
        p, i = x % 2, x // 2
        if x < 10:
            d_ref[p, i, 0:40, :] = xlo_ref[x].astype(f32)
        elif x >= 30:
            d_ref[p, i, 0:40, :] = xhi_ref[x - 30].astype(f32)
        else:
            d_ref[p, i, 0:10, :] = ylo_ref[x - 10].astype(f32)
            d_ref[p, i, 10:30, :] = blk_ref[x - 10].astype(f32)
            d_ref[p, i, 30:40, :] = yhi_ref[x - 10].astype(f32)
        d_ref[p, i, 40:48, :] = jnp.zeros((8, 128), f32)

    def fine(x):
        return d_ref[x % 2, x // 2]

    for i in range(16):
        c = 2 * i + 4
        planes[i] = (
            fine(c) + 0.5625 * (fine(c - 1) + fine(c + 1)) - 0.0625 * (fine(c - 3) + fine(c + 3))
        )
    for i in range(16):
        def tap(o):
            return planes[i, pl.ds(4 + o, 16, stride=2), :]
        cells[16 * i : 16 * i + 16, :] = (
            tap(0) + 0.5625 * (tap(-1) + tap(1)) - 0.0625 * (tap(-3) + tap(3))
        )
    zero = jnp.zeros((16, 128), f32)
    rows = []
    for n in range(9):
        pair = []
        for y in (2 * n - 4, 2 * n - 3):
            inside = -3 <= y <= 12
            pair.append(cells[pl.ds(y + 3, 16, stride=16), :] if inside else zero)
        rows.append(jnp.concatenate(pair, axis=1))
    r, c = iota2((256, 128))
    down_z = jnp.where(r // 128 == c // 64, weight(r % 128 - 2 * (c % 64)), 0.0)
    value = jnp.dot(
        jnp.concatenate(rows, axis=0), down_z, precision=HIGHEST, preferred_element_type=f32
    )
    r, c = iota2((144, 128))
    cell_x = 10 * where_ref[0] - 3 + r % 16
    cell_y = 10 * where_ref[1] - 4 + 2 * (r // 16) + c // 64
    inside = (cell_x >= 0) & (cell_x < 320) & (cell_y >= 0) & (cell_y < 80)
    value = jnp.where(inside, value, 0.0).astype(bf16).astype(f32)
    for n in range(9):
        mid[n, 0:16, :] = value[16 * n : 16 * n + 16]
        mid[n, 16:24, :] = jnp.zeros((8, 128), f32)
    for n in range(5):
        own_ref[n] = value[16 * n + 32 : 16 * n + 48].astype(bf16)
        right_ref[n] = mid[n + 2, 2:10, :].astype(bf16)
        left_ref[n] = mid[n + 2, 6:15, :].astype(bf16)

    lane = lax.broadcasted_iota(jnp.int32, (1, 128), 1)
    odd = lane >= 64
    weight_0 = jnp.where(odd, 0.5625, 1.0)
    weight_1 = jnp.where(odd, 0.5625, 0.0)
    weight_3 = jnp.where(odd, -0.0625, 0.0)
    r, c = iota2((128, 32))
    down_z = weight(r % 64 - 2 * c)
    row[...] = jnp.zeros((8, 256), f32)
    sums = []
    for y in range(5):
        n = y + 2
        def tap(o):
            def part(k):
                return mid[k, pl.ds(3 + o, 8, stride=2), :]
            return (
                weight_0 * part(n) + weight_1 * part(n - 1) + weight_3 * (part(n - 2) + part(n + 1))
            )
        sums.append(tap(0) + 0.5625 * (tap(-1) + tap(1)) - 0.0625 * (tap(-3) + tap(3)))
    out = jnp.dot(
        jnp.concatenate(sums, axis=0), down_z, precision=HIGHEST, preferred_element_type=f32
    )
    for y in range(5):
        row[:, 32 * y : 32 * y + 32] = out[8 * y : 8 * y + 8]
    for k in range(coarse_ref.shape[0]):
        coarse_ref[k] = row[...]


def fine_kernel(lo, hi, first, d_ref, v_ref, *refs):
    if first:
        out_ref, w0, w1, e0, e1 = refs
        out_ref[...] = jnp.zeros((240, 256), f32)
    else:
        acc_ref, out_ref, w0, w1, e0, e1 = refs
        out_ref[...] = acc_ref[...]
    r, c = iota2((128, 128))
    mask = jnp.abs(r - c) <= REACH
    zero = jnp.zeros((128, 128), bf16)
    for w in (w0, w1):
        w[0:128, 128:256] = zero
        w[2688:2816, 0:128] = zero

    def build(w, b):
        for a in range(TAPS):
            line = jnp.broadcast_to(v_ref[pl.ds(a * TAPS + b, 1), :], (128, 128))
            line = pltpu.roll(line, 0, 1, stride=1, stride_axis=0)
            band = jnp.where(mask, line, 0.0).astype(bf16)
            w[a * 128 : (a + 1) * 128, 0:128] = band
            w[(a + 1) * 128 : (a + 2) * 128, 128:256] = band

    def dot(w, e, b):
        for p in range(2):
            for q in range(10):
                part = d_ref[p, 2 * q : 2 * q + 2, pl.ds(b, 24), :].reshape(48, 128)
                e[0, 48 * q : 48 * q + 48, p * 128 : (p + 1) * 128] = part.astype(bf16)
            for q in range(9):
                part = d_ref[p, 2 * q + 1 : 2 * q + 3, pl.ds(b, 24), :].reshape(48, 128)
                e[1, 48 * q : 48 * q + 48, p * 128 : (p + 1) * 128] = part.astype(bf16)
        lhs = jnp.concatenate(
            [e[k % 2, 24 * (k - k % 2) : 24 * (k - k % 2) + 240, :] for k in range(11)], axis=1
        )
        out_ref[...] += jnp.dot(lhs, w[...], preferred_element_type=f32)

    build(w0, lo)

    def step(t, _):
        b = lo + 2 * t
        build(w1, b + 1)
        dot(w0, e0, b)
        build(w0, jnp.minimum(b + 2, TAPS - 1))
        dot(w1, e1, b + 1)
        return 0

    lax.fori_loop(0, (hi - lo) // 2, step, 0)
    if (hi - lo) % 2:
        dot(w0, e0, hi - 1)


def fine_sum(lo, hi, d, v, acc=None):
    args = (d, v) if acc is None else (d, v, acc)
    return vmem_call(
        functools.partial(fine_kernel, lo, hi, acc is None),
        jax.ShapeDtypeStruct((240, 256), f32),
        [pltpu.VMEM((2816, 256), bf16)] * 2 + [pltpu.VMEM((2, 480, 256), bf16)] * 2,
        "fine_sum",
        args,
        flops=(hi - lo) * 2 * 240 * 2816 * 256,
    )


def spread_kernel(where_ref, coarse_ref, mx_ref, own_ref, lo_ref, hi_ref, out_ref, buf):
    start = 10 * where_ref[0]
    rows = jnp.concatenate([mx_ref[h, pl.ds(start, 16), :] for h in range(2)], axis=1)
    part = jnp.dot(rows, coarse_ref[...], precision=HIGHEST, preferred_element_type=f32)
    for n in range(5):
        buf[33 * n : 33 * n + 8, :] = lo_ref[n].astype(f32)
        buf[33 * n + 8 : 33 * n + 24, :] = own_ref[n].astype(f32)
        buf[33 * n + 24 : 33 * n + 33, :] = hi_ref[n].astype(f32)
    buf[165:176, :] = jnp.zeros((11, 128), f32)
    high = part.astype(bf16)
    low = (part - high.astype(f32)).astype(bf16)
    cells = buf[...].astype(bf16)
    for k in range(out_ref.shape[0]):
        out_ref[k, 0:176, :] = cells
        out_ref[k, 176:192, :] = high[:, 0:128]
        out_ref[k, 192:208, :] = high[:, 128:256]
        out_ref[k, 208:224, :] = low[:, 0:128]
        out_ref[k, 224:240, :] = low[:, 128:256]


def final_kernel(
    where_ref, recv_ref, my_ref, mz_ref, near_ref, far_ref, fine_ref, out_ref,
    cells, w0, w1, acc, moved, wide, line,
):
    index_x = where_ref[0]
    index_y = where_ref[1]
    count = recv_ref.shape[0]
    cells[:, 32:40, :] = jnp.zeros((18, 8, 128), f32)
    for step in range(-2, 3):
        source = index_y + step
        inside = (source >= 0) & (source < count)
        got = recv_ref[jnp.clip(source, 0, count - 1), 0:176, :].astype(f32)
        line[...] = jnp.where(inside, got, 0.0)
        for p in range(5):
            n = 5 * step + 6 + p
            if 0 <= n < 18:
                cells[n, 0:33, :] = line[33 * p : 33 * p + 33, :]

    r, c = iota2((128, 128))
    mask = jnp.abs(r % 64 - c % 64) <= REACH
    zero = jnp.zeros((128, 128), bf16)
    for w in (w0, w1):
        w[0:128, 128:256] = zero
        w[1408:1536, 0:128] = zero

    def build(w, a):
        base = TAPS * TAPS + a * TAPS
        for j in range(11):
            same = near_ref[pl.ds(base + 2 * j, 1), :]
            upper = same
            lower = same
            if j > 0:
                upper = same + far_ref[pl.ds(base + 2 * j - 1, 1), :]
            if j < 10:
                lower = same + far_ref[pl.ds(base + 2 * j + 1, 1), :]
            upper = pltpu.roll(jnp.broadcast_to(upper, (64, 128)), 0, 1, stride=1, stride_axis=0)
            lower = pltpu.roll(jnp.broadcast_to(lower, (64, 128)), 64, 1, stride=1, stride_axis=0)
            band = jnp.where(mask, jnp.concatenate([upper, lower], axis=0), 0.0).astype(bf16)
            w[128 * j : 128 * j + 128, 0:128] = band
            w[128 * j + 128 : 128 * j + 256, 128:256] = band

    def dot(w, a):
        part = [cells[n, pl.ds(a, 16), :].astype(bf16) for n in range(18)]
        lhs = jnp.concatenate(
            [jnp.concatenate(part[2 * g : 2 * g + 12], axis=1) for g in range(4)], axis=0
        )
        acc[...] += jnp.dot(lhs, w[...], preferred_element_type=f32)

    acc[...] = jnp.zeros((64, 256), f32)
    build(w0, 0)

    def step(t, _):
        a = 2 * t
        build(w1, a + 1)
        dot(w0, a)
        build(w0, a + 2)
        dot(w1, a + 1)
        return 0

    lax.fori_loop(0, 10, step, 0)
    dot(w0, TAPS - 1)

    start = 10 * index_y
    sums = [[None] * 16, [None] * 16]
    for k in range(count):
        high = [recv_ref[k, 176 + 16 * h : 192 + 16 * h, :].astype(f32) for h in range(2)]
        low = [recv_ref[k, 208 + 16 * h : 224 + 16 * h, :].astype(f32) for h in range(2)]
        for h in range(2):
            value = high[h] + low[h]
            rows_y = my_ref[2 * k + h, pl.ds(start, 16), :]
            for y in range(16):
                term = value * rows_y[y : y + 1, :]
                sums[h][y] = term if k == 0 else sums[h][y] + term
    rows = [
        jnp.concatenate([sums[h][2 * n + p] for p in range(2) for h in range(2)], axis=1)
        for n in range(8)
    ]
    top = jnp.dot(
        jnp.concatenate(rows, axis=0), mz_ref[...], precision=HIGHEST, preferred_element_type=f32
    )
    both = []
    for n in range(8):
        g, u = n // 2, n % 2
        both.append(acc[16 * g : 16 * g + 16, 128 * u : 128 * u + 128])
    total = jnp.concatenate(both, axis=0) + top
    r, c = iota2((128, 128))
    cell_x = 10 * index_x - 1 + r % 16
    cell_y = 10 * index_y - 2 + 2 * (r // 16) + c // 64
    inside = (cell_x >= 0) & (cell_x < 320) & (cell_y >= 0) & (cell_y < 80)
    total = jnp.where(inside, total, 0.0)
    r, c = iota2((128, 256))
    up_z = jnp.where(r // 64 == c // 128, weight(c % 128 - 2 * (r % 64)), 0.0)
    wide[...] = jnp.dot(total, up_z, precision=HIGHEST, preferred_element_type=f32)

    def middle_y(y):
        n, par = (y + 2) // 2, y % 2
        return wide[16 * n : 16 * n + 16, 128 * par : 128 * par + 128]

    for y in range(20):
        m = y // 2
        if y % 2 == 0:
            value = middle_y(m)
        else:
            value = 0.5625 * (middle_y(m) + middle_y(m + 1)) - 0.0625 * (
                middle_y(m - 1) + middle_y(m + 2)
            )
        moved[16 * y : 16 * y + 16, :] = value
    planes = [moved[pl.ds(k, 20, stride=16), :] for k in range(13)]
    for x in range(20):
        m = x // 2
        if x % 2 == 0:
            value = planes[m + 1]
        else:
            value = 0.5625 * (planes[m + 1] + planes[m + 2]) - 0.0625 * (planes[m] + planes[m + 3])
        out_ref[x] = value + fine_ref[24 * m : 24 * m + 20, 128 * (x % 2) : 128 * (x % 2) + 128]


def halo(low_edge, high_edge, axis):
    count = lax.axis_size(axis)
    forward = [(i, i + 1) for i in range(count - 1)]
    backward = [(i + 1, i) for i in range(count - 1)]
    return lax.ppermute(high_edge, axis, forward), lax.ppermute(low_edge, axis, backward)


def per_device(charges, kernels):
    count_x = lax.axis_size("gx")
    count_y = lax.axis_size("gy")
    where = jnp.stack([lax.axis_index("gx"), lax.axis_index("gy")]).astype(jnp.int32)
    spread = charges.shape[0] * count_x / 16.0
    shape = jax.ShapeDtypeStruct
    near, far = (
        jnp.dot(kernels.reshape(-1, TAPS), jnp.asarray(m, bf16), preferred_element_type=f32)
        for m in spots_np()
    )
    y_lo, y_hi = halo(charges[:, :10], charges[:, 10:], "gy")
    edge_lo, edge_hi = vmem_call(
        rim_kernel,
        [shape((10, 40, 128), bf16)] * 2,
        [pltpu.VMEM((10, 40, 128), f32)],
        "rim",
        (charges, y_lo, y_hi),
    )
    x_lo, x_hi = halo(edge_lo, edge_hi, "gx")
    d, right, left, own, coarse = vmem_call(
        restrict_kernel,
        [
            shape((2, 20, 48, 128), f32),
            shape((5, 8, 128), bf16),
            shape((5, 9, 128), bf16),
            shape((5, 16, 128), bf16),
            shape((count_x, 8, 256), f32),
        ],
        [
            pltpu.VMEM((16, 48, 128), f32),
            pltpu.VMEM((256, 128), f32),
            pltpu.VMEM((9, 24, 128), f32),
            pltpu.VMEM((8, 256), f32),
        ],
        "restrict",
        (where, charges, y_lo, y_hi, x_lo, x_hi),
        smem=1,
    )
    mid_lo, mid_hi = halo(left, right, "gx")
    coarse = lax.all_to_all(coarse, "gx", 0, 0).reshape(256, 256)
    fine = fine_sum(0, 11, d, near)
    parts = vmem_call(
        spread_kernel,
        shape((count_y, 240, 128), bf16),
        [pltpu.VMEM((176, 128), f32)],
        "spread",
        (where, coarse, jnp.asarray(matrix_x_np(spread)), own, mid_lo, mid_hi),
        smem=1,
    )
    parts = lax.all_to_all(parts, "gy", 0, 0)
    fine = fine_sum(11, 21, d, near, fine)
    return vmem_call(
        final_kernel,
        shape((20, 20, 128), f32),
        [
            pltpu.VMEM((18, 40, 128), f32),
            pltpu.VMEM((1536, 256), bf16),
            pltpu.VMEM((1536, 256), bf16),
            pltpu.VMEM((64, 256), f32),
            pltpu.VMEM((320, 128), f32),
            pltpu.VMEM((128, 256), f32),
            pltpu.VMEM((176, 128), f32),
        ],
        "final",
        (
            where,
            parts,
            jnp.asarray(matrix_y_np(spread)),
            jnp.asarray(matrix_z_np(spread)),
            near,
            far,
            fine,
        ),
        smem=1,
    )


def solution(mesh):
    return jax.shard_map(
        per_device,
        mesh=mesh,
        in_specs=(P("gx", "gy", None), P()),
        out_specs=P("gx", "gy", None),
        check_vma=False,
    )
```

```python
import functools
import numpy as np
import jax
import jax.numpy as jnp
from jax import lax
from jax.experimental import pallas as pl
from jax.experimental.pallas import tpu as pltpu
from jax.sharding import PartitionSpec as P

f32 = jnp.float32
bf16 = jnp.bfloat16
spread_norm = 1.2533141
HIGHEST = lax.Precision.HIGHEST
REACH = 10
TAPS = 21
SPLIT = 15


def weight_np(offset):
    d = np.abs(offset)
    return np.where(d == 0, 1.0, np.where(d == 1, 0.5625, np.where(d == 3, -0.0625, 0.0)))


def top_matrix_np(n, spread):
    prolong = weight_np(np.arange(2 * n)[:, None] - 2 * np.arange(n)[None, :])
    offset = (np.arange(n)[:, None] - np.arange(n)[None, :]) / spread
    return prolong @ (np.exp(-offset * offset) / np.sqrt(spread * spread_norm))


def lane_tiles(m):
    return m.reshape(m.shape[0], -1, 128).transpose(1, 0, 2).astype(np.float32)


def matrix_x_np(spread):
    m = top_matrix_np(160, spread).reshape(320, 32, 5)
    out = np.zeros((328, 32, 8))
    out[1:321, :, :5] = m
    return lane_tiles(out.reshape(328, 256))


def matrix_y_np(spread):
    m = top_matrix_np(40, spread).reshape(80, 8, 5)
    out = np.zeros((88, 8, 8))
    out[2:82, :, :5] = m
    return lane_tiles(np.repeat(out.reshape(88, 64), 32, axis=1))


def matrix_z_np(spread):
    m = top_matrix_np(32, spread).T
    out = np.zeros((2, 8, 32, 2, 64))
    for par in range(2):
        out[par, :, :, par, :] = m[None]
    return out.reshape(512, 128).astype(np.float32)


def spots_np():
    taps = np.arange(TAPS)[:, None]
    lanes = np.arange(128)[None, :]
    near = lanes == (REACH - taps) % 128
    far = lanes == (64 + REACH - taps) % 128
    return near, far


def weight(d):
    d = jnp.abs(d)
    return jnp.where(d == 0, 1.0, jnp.where(d == 1, 0.5625, jnp.where(d == 3, -0.0625, 0.0))).astype(f32)


def iota2(shape):
    return (lax.broadcasted_iota(jnp.int32, shape, 0), lax.broadcasted_iota(jnp.int32, shape, 1))


def vmem_call(body, out_shape, scratch, name, args, smem=0, flops=0):
    specs = [pl.BlockSpec(memory_space=pltpu.SMEM)] * smem
    specs += [pl.BlockSpec(memory_space=pltpu.VMEM)] * (len(args) - smem)
    return pl.pallas_call(
        body,
        out_shape=out_shape,
        in_specs=specs,
        out_specs=jax.tree.map(lambda _: pl.BlockSpec(memory_space=pltpu.VMEM), out_shape),
        scratch_shapes=scratch,
        compiler_params=pltpu.CompilerParams(vmem_limit_bytes=32 << 20),
        cost_estimate=pl.CostEstimate(flops=flops, bytes_accessed=1 << 16, transcendentals=0),
        name=name,
    )(*args)


def rim_kernel(blk_ref, ylo_ref, yhi_ref, xlo_ref, xhi_ref, wide):
    for out_ref, start in ((xlo_ref, 0), (xhi_ref, 10)):
        wide[:, 0:10, :] = ylo_ref[start : start + 10].astype(f32)
        wide[:, 10:30, :] = blk_ref[start : start + 10].astype(f32)
        wide[:, 30:40, :] = yhi_ref[start : start + 10].astype(f32)
        out_ref[...] = wide[...].astype(bf16)


def restrict_kernel(
    where_ref, blk_ref, ylo_ref, yhi_ref, xlo_ref, xhi_ref,
    d_ref, out_ref,
    planes, cells, mid, pay,
):
    for x in range(40):
        p, i = x % 2, x // 2
        if x < 10:
            d_ref[p, i, 0:40, :] = xlo_ref[x].astype(f32)
        elif x >= 30:
            d_ref[p, i, 0:40, :] = xhi_ref[x - 30].astype(f32)
        else:
            d_ref[p, i, 0:10, :] = ylo_ref[x - 10].astype(f32)
            d_ref[p, i, 10:30, :] = blk_ref[x - 10].astype(f32)
            d_ref[p, i, 30:40, :] = yhi_ref[x - 10].astype(f32)
        d_ref[p, i, 40:48, :] = jnp.zeros((8, 128), f32)

    def fine(x):
        return d_ref[x % 2, x // 2]

    for i in range(16):
        c = 2 * i + 4
        planes[i] = (
            fine(c) + 0.5625 * (fine(c - 1) + fine(c + 1)) - 0.0625 * (fine(c - 3) + fine(c + 3))
        )
    for i in range(16):
        def tap(o):
            return planes[i, pl.ds(4 + o, 16, stride=2), :]
        cells[16 * i : 16 * i + 16, :] = (
            tap(0) + 0.5625 * (tap(-1) + tap(1)) - 0.0625 * (tap(-3) + tap(3))
        )
    zero = jnp.zeros((16, 128), f32)
    rows = []
    for n in range(9):
        pair = []
        for y in (2 * n - 4, 2 * n - 3):
            inside = -3 <= y <= 12
            pair.append(cells[pl.ds(y + 3, 16, stride=16), :] if inside else zero)
        rows.append(jnp.concatenate(pair, axis=1))
    r, c = iota2((256, 128))
    down_z = jnp.where(r // 128 == c // 64, weight(r % 128 - 2 * (c % 64)), 0.0)
    value = jnp.dot(
        jnp.concatenate(rows, axis=0), down_z, precision=HIGHEST, preferred_element_type=f32
    )
    r, c = iota2((144, 128))
    cell_x = 10 * where_ref[0] - 3 + r % 16
    cell_y = 10 * where_ref[1] - 4 + 2 * (r // 16) + c // 64
    inside = (cell_x >= 0) & (cell_x < 320) & (cell_y >= 0) & (cell_y < 80)
    value = jnp.where(inside, value, 0.0).astype(bf16).astype(f32)
    for n in range(9):
        mid[n, 0:16, :] = value[16 * n : 16 * n + 16]
        mid[n, 16:24, :] = jnp.zeros((8, 128), f32)
    pay[48:56, :] = jnp.zeros((8, 128), f32)
    for n in range(5):
        pay[10 * n : 10 * n + 10, :] = mid[n + 2, 3:13, :]

    lane = lax.broadcasted_iota(jnp.int32, (1, 128), 1)
    odd = lane >= 64
    weight_0 = jnp.where(odd, 0.5625, 1.0)
    weight_1 = jnp.where(odd, 0.5625, 0.0)
    weight_3 = jnp.where(odd, -0.0625, 0.0)
    r, c = iota2((128, 32))
    down_z = weight(r % 64 - 2 * c)
    sums = []
    for y in range(5):
        n = y + 2
        def tap(o):
            def part(k):
                return mid[k, pl.ds(3 + o, 8, stride=2), :]
            return (
                weight_0 * part(n) + weight_1 * part(n - 1) + weight_3 * (part(n - 2) + part(n + 1))
            )
        sums.append(tap(0) + 0.5625 * (tap(-1) + tap(1)) - 0.0625 * (tap(-3) + tap(3)))
    out = jnp.dot(
        jnp.concatenate(sums, axis=0), down_z, precision=HIGHEST, preferred_element_type=f32
    )
    wide = jnp.concatenate([out[8 * y : 8 * y + 8] for y in range(4)], axis=1)
    last = out[32:40]
    high = wide.astype(bf16).astype(f32)
    last_high = last.astype(bf16).astype(f32)
    pay[56:64, :] = jnp.concatenate(
        [last_high, last - last_high, jnp.zeros((8, 64), f32)], axis=1
    )
    pay[64:72, :] = high
    pay[72:80, :] = wide - high
    packed = pay[...].astype(bf16)
    for k in range(out_ref.shape[0]):
        out_ref[k] = packed


def fine_kernel(lo, hi, first, d_ref, v_ref, *refs):
    if first:
        out_ref, w0, w1, e0, e1 = refs
        out_ref[...] = jnp.zeros((240, 256), f32)
    else:
        acc_ref, out_ref, w0, w1, e0, e1 = refs
        out_ref[...] = acc_ref[...]
    r, c = iota2((128, 128))
    mask = jnp.abs(r - c) <= REACH
    zero = jnp.zeros((128, 128), bf16)
    for w in (w0, w1):
        w[0:128, 128:256] = zero
        w[2688:2816, 0:128] = zero

    def build(w, b):
        for a in range(TAPS):
            line = jnp.broadcast_to(v_ref[pl.ds(a * TAPS + b, 1), :], (128, 128))
            line = pltpu.roll(line, 0, 1, stride=1, stride_axis=0)
            band = jnp.where(mask, line, 0.0).astype(bf16)
            w[a * 128 : (a + 1) * 128, 0:128] = band
            w[(a + 1) * 128 : (a + 2) * 128, 128:256] = band

    def dot(w, e, b):
        for p in range(2):
            for q in range(10):
                part = d_ref[p, 2 * q : 2 * q + 2, pl.ds(b, 24), :].reshape(48, 128)
                e[0, 48 * q : 48 * q + 48, p * 128 : (p + 1) * 128] = part.astype(bf16)
            for q in range(9):
                part = d_ref[p, 2 * q + 1 : 2 * q + 3, pl.ds(b, 24), :].reshape(48, 128)
                e[1, 48 * q : 48 * q + 48, p * 128 : (p + 1) * 128] = part.astype(bf16)
        lhs = jnp.concatenate(
            [e[k % 2, 24 * (k - k % 2) : 24 * (k - k % 2) + 240, :] for k in range(11)], axis=1
        )
        out_ref[...] += jnp.dot(lhs, w[...], preferred_element_type=f32)

    build(w0, lo)

    def step(t, _):
        b = lo + 2 * t
        build(w1, b + 1)
        dot(w0, e0, b)
        build(w0, jnp.minimum(b + 2, TAPS - 1))
        dot(w1, e1, b + 1)
        return 0

    lax.fori_loop(0, (hi - lo) // 2, step, 0)
    if (hi - lo) % 2:
        dot(w0, e0, hi - 1)


def fine_sum(lo, hi, d, v, acc=None):
    args = (d, v) if acc is None else (d, v, acc)
    return vmem_call(
        functools.partial(fine_kernel, lo, hi, acc is None),
        jax.ShapeDtypeStruct((240, 256), f32),
        [pltpu.VMEM((2816, 256), bf16)] * 2 + [pltpu.VMEM((2, 480, 256), bf16)] * 2,
        "fine_sum",
        args,
        flops=(hi - lo) * 2 * 240 * 2816 * 256,
    )


def spread_kernel(where_ref, recv_ref, mx_ref, out_ref, buf, line):
    index_x = where_ref[0]
    count = recv_ref.shape[0]
    start = 10 * index_x
    rows = jnp.concatenate([mx_ref[h, pl.ds(start, 16), :] for h in range(2)], axis=1)
    coarse = recv_ref[:, 48:80, :].astype(f32)
    last = coarse[:, 8:16, :].reshape(8 * count, 128)
    wide = (coarse[:, 16:24, :] + coarse[:, 24:32, :]).reshape(8 * count, 128)
    wide = jnp.dot(rows, wide, precision=HIGHEST, preferred_element_type=f32)
    last = jnp.dot(rows, last, precision=HIGHEST, preferred_element_type=f32)
    last = last[:, 0:32] + last[:, 32:64]
    part = jnp.concatenate([wide, last, jnp.zeros((16, 96), f32)], axis=1)
    for step, first, size, at in ((-2, 9, 1, 0), (-1, 0, 10, 1), (0, 0, 10, 11), (1, 0, 10, 21), (2, 0, 2, 31)):
        source = index_x + step
        inside = (source >= 0) & (source < count)
        got = recv_ref[jnp.clip(source, 0, count - 1), 0:64, :].astype(f32)
        line[...] = jnp.where(inside, got, 0.0)
        for n in range(5):
            buf[33 * n + at : 33 * n + at + size, :] = line[10 * n + first : 10 * n + first + size, :]
    buf[165:176, :] = jnp.zeros((11, 128), f32)
    high = part.astype(bf16)
    low = (part - high.astype(f32)).astype(bf16)
    cells = buf[...].astype(bf16)
    for k in range(out_ref.shape[0]):
        out_ref[k, 0:176, :] = cells
        out_ref[k, 176:192, :] = high[:, 0:128]
        out_ref[k, 192:208, :] = high[:, 128:256]
        out_ref[k, 208:224, :] = low[:, 0:128]
        out_ref[k, 224:240, :] = low[:, 128:256]


def final_kernel(
    where_ref, recv_ref, my_ref, mz_ref, near_ref, far_ref, fine_ref, out_ref,
    cells, w0, w1, acc, moved, wide, line,
):
    index_x = where_ref[0]
    index_y = where_ref[1]
    count = recv_ref.shape[0]
    cells[:, 32:40, :] = jnp.zeros((17, 8, 128), f32)
    for step in range(-2, 3):
        source = index_y + step
        inside = (source >= 0) & (source < count)
        got = recv_ref[jnp.clip(source, 0, count - 1), 0:176, :].astype(f32)
        line[...] = jnp.where(inside, got, 0.0)
        for p in range(5):
            n = 5 * step + 6 + p
            if 0 <= n < 17:
                cells[n, 0:33, :] = line[33 * p : 33 * p + 33, :]

    r, c = iota2((128, 128))
    mask = jnp.abs(r % 64 - c % 64) <= REACH

    def build(w, a):
        base = TAPS * TAPS + a * TAPS
        for j in range(11):
            same = near_ref[pl.ds(base + 2 * j, 1), :]
            upper = same
            lower = same
            if j > 0:
                upper = same + far_ref[pl.ds(base + 2 * j - 1, 1), :]
            if j < 10:
                lower = same + far_ref[pl.ds(base + 2 * j + 1, 1), :]
            upper = pltpu.roll(jnp.broadcast_to(upper, (64, 128)), 0, 1, stride=1, stride_axis=0)
            lower = pltpu.roll(jnp.broadcast_to(lower, (64, 128)), 64, 1, stride=1, stride_axis=0)
            band = jnp.where(mask, jnp.concatenate([upper, lower], axis=0), 0.0).astype(bf16)
            w[128 * j : 128 * j + 128, :] = band

    def dot(w, a):
        part = [cells[n, pl.ds(a, 16), :].astype(bf16) for n in range(17)]
        lhs = jnp.concatenate(
            [jnp.concatenate(part[g : g + 11], axis=1) for g in range(7)], axis=0
        )
        acc[...] += jnp.dot(lhs, w[...], preferred_element_type=f32)

    acc[...] = jnp.zeros((112, 128), f32)
    build(w0, 0)

    def step(t, _):
        a = 2 * t
        build(w1, a + 1)
        dot(w0, a)
        build(w0, a + 2)
        dot(w1, a + 1)
        return 0

    lax.fori_loop(0, 10, step, 0)
    dot(w0, TAPS - 1)

    start = 10 * index_y
    sums = [[None] * 14, [None] * 14]
    for k in range(count):
        high = [recv_ref[k, 176 + 16 * h : 192 + 16 * h, :].astype(f32) for h in range(2)]
        low = [recv_ref[k, 208 + 16 * h : 224 + 16 * h, :].astype(f32) for h in range(2)]
        for h in range(2):
            value = high[h] + low[h]
            rows_y = my_ref[2 * k + h, pl.ds(start, 16), :]
            for y in range(14):
                term = value * rows_y[y : y + 1, :]
                sums[h][y] = term if k == 0 else sums[h][y] + term
    rows = [
        jnp.concatenate([sums[h][2 * n + p] for p in range(2) for h in range(2)], axis=1)
        for n in range(7)
    ]
    top = jnp.dot(
        jnp.concatenate(rows, axis=0), mz_ref[...], precision=HIGHEST, preferred_element_type=f32
    )
    total = acc[...] + top
    r, c = iota2((112, 128))
    cell_x = 10 * index_x - 1 + r % 16
    cell_y = 10 * index_y - 2 + 2 * (r // 16) + c // 64
    inside = (cell_x >= 0) & (cell_x < 320) & (cell_y >= 0) & (cell_y < 80)
    total = jnp.where(inside, total, 0.0)
    r, c = iota2((128, 256))
    up_z = jnp.where(r // 64 == c // 128, weight(c % 128 - 2 * (r % 64)), 0.0)
    wide[...] = jnp.dot(total, up_z, precision=HIGHEST, preferred_element_type=f32)

    def middle_y(y):
        n, par = (y + 2) // 2, y % 2
        return wide[16 * n : 16 * n + 16, 128 * par : 128 * par + 128]

    for y in range(20):
        m = y // 2
        if y % 2 == 0:
            value = middle_y(m)
        else:
            value = 0.5625 * (middle_y(m) + middle_y(m + 1)) - 0.0625 * (
                middle_y(m - 1) + middle_y(m + 2)
            )
        moved[16 * y : 16 * y + 16, :] = value
    planes = [moved[pl.ds(k, 20, stride=16), :] for k in range(13)]
    for x in range(20):
        m = x // 2
        if x % 2 == 0:
            value = planes[m + 1]
        else:
            value = 0.5625 * (planes[m + 1] + planes[m + 2]) - 0.0625 * (planes[m] + planes[m + 3])
        out_ref[x] = value + fine_ref[24 * m : 24 * m + 20, 128 * (x % 2) : 128 * (x % 2) + 128]


def halo(low_edge, high_edge, axis):
    count = lax.axis_size(axis)
    forward = [(i, i + 1) for i in range(count - 1)]
    backward = [(i + 1, i) for i in range(count - 1)]
    return lax.ppermute(high_edge, axis, forward), lax.ppermute(low_edge, axis, backward)


def per_device(charges, kernels):
    count_x = lax.axis_size("gx")
    count_y = lax.axis_size("gy")
    where = jnp.stack([lax.axis_index("gx"), lax.axis_index("gy")]).astype(jnp.int32)
    spread = charges.shape[0] * count_x / 16.0
    shape = jax.ShapeDtypeStruct
    near, far = (
        jnp.dot(kernels.reshape(-1, TAPS), jnp.asarray(m, bf16), preferred_element_type=f32)
        for m in spots_np()
    )
    y_lo, y_hi = halo(charges[:, :10], charges[:, 10:], "gy")
    y_lo, y_hi, near, far = lax.optimization_barrier((y_lo, y_hi, near, far))
    edge_lo, edge_hi = vmem_call(
        rim_kernel,
        [shape((10, 40, 128), bf16)] * 2,
        [pltpu.VMEM((10, 40, 128), f32)],
        "rim",
        (charges, y_lo, y_hi),
    )
    x_lo, x_hi = halo(edge_lo, edge_hi, "gx")
    d, blocks = vmem_call(
        restrict_kernel,
        [shape((2, 20, 48, 128), f32), shape((count_x, 80, 128), bf16)],
        [
            pltpu.VMEM((16, 48, 128), f32),
            pltpu.VMEM((256, 128), f32),
            pltpu.VMEM((9, 24, 128), f32),
            pltpu.VMEM((80, 128), f32),
        ],
        "restrict",
        (where, charges, y_lo, y_hi, x_lo, x_hi),
        smem=1,
    )
    blocks = lax.all_to_all(blocks, "gx", 0, 0)
    fine = fine_sum(0, SPLIT, d, near)
    blocks, fine = lax.optimization_barrier((blocks, fine))
    parts = vmem_call(
        spread_kernel,
        shape((count_y, 240, 128), bf16),
        [pltpu.VMEM((176, 128), f32), pltpu.VMEM((64, 128), f32)],
        "spread",
        (where, blocks, jnp.asarray(matrix_x_np(spread))),
        smem=1,
    )
    parts = lax.all_to_all(parts, "gy", 0, 0)
    fine = fine_sum(SPLIT, TAPS, d, near, fine)
    return vmem_call(
        final_kernel,
        shape((20, 20, 128), f32),
        [
            pltpu.VMEM((17, 40, 128), f32),
            pltpu.VMEM((1408, 128), bf16),
            pltpu.VMEM((1408, 128), bf16),
            pltpu.VMEM((112, 128), f32),
            pltpu.VMEM((320, 128), f32),
            pltpu.VMEM((112, 256), f32),
            pltpu.VMEM((176, 128), f32),
        ],
        "final",
        (
            where,
            parts,
            jnp.asarray(matrix_y_np(spread)),
            jnp.asarray(matrix_z_np(spread)),
            near,
            far,
            fine,
        ),
        smem=1,
    )


def solution(mesh):
    return jax.shard_map(
        per_device,
        mesh=mesh,
        in_specs=(P("gx", "gy", None), P()),
        out_specs=P("gx", "gy", None),
        check_vma=False,
    )
```

```python
import functools
import numpy as np
import jax
import jax.numpy as jnp
from jax import lax
from jax.experimental import pallas as pl
from jax.experimental.pallas import tpu as pltpu
from jax.sharding import PartitionSpec as P

f32 = jnp.float32
bf16 = jnp.bfloat16
spread_norm = 1.2533141
HIGHEST = lax.Precision.HIGHEST
REACH = 10
TAPS = 21


def weight_np(offset):
    d = np.abs(offset)
    return np.where(d == 0, 1.0, np.where(d == 1, 0.5625, np.where(d == 3, -0.0625, 0.0)))


def top_matrix_np(n, spread):
    prolong = weight_np(np.arange(2 * n)[:, None] - 2 * np.arange(n)[None, :])
    offset = (np.arange(n)[:, None] - np.arange(n)[None, :]) / spread
    return prolong @ (np.exp(-offset * offset) / np.sqrt(spread * spread_norm))


def lane_tiles(m):
    return m.reshape(m.shape[0], -1, 128).transpose(1, 0, 2).astype(np.float32)


def matrix_x_np(spread):
    m = top_matrix_np(160, spread).reshape(320, 32, 5)
    out = np.zeros((328, 32, 8))
    out[1:321, :, :5] = m
    return lane_tiles(out.reshape(328, 256))


def matrix_y_np(spread):
    m = top_matrix_np(40, spread).reshape(80, 8, 5)
    out = np.zeros((88, 8, 8))
    out[2:82, :, :5] = m
    return lane_tiles(np.repeat(out.reshape(88, 64), 32, axis=1))


def matrix_z_np(spread):
    m = top_matrix_np(32, spread).T
    out = np.zeros((2, 8, 32, 2, 64))
    for par in range(2):
        out[par, :, :, par, :] = m[None]
    return out.reshape(512, 128).astype(np.float32)


def spots_np():
    taps = np.arange(TAPS)[:, None]
    lanes = np.arange(128)[None, :]
    near = lanes == (REACH - taps) % 128
    far = lanes == (64 + REACH - taps) % 128
    return near, far


def weight(d):
    d = jnp.abs(d)
    return jnp.where(d == 0, 1.0, jnp.where(d == 1, 0.5625, jnp.where(d == 3, -0.0625, 0.0))).astype(f32)


def iota2(shape):
    return (lax.broadcasted_iota(jnp.int32, shape, 0), lax.broadcasted_iota(jnp.int32, shape, 1))


def vmem_call(body, out_shape, scratch, name, args, smem=0, flops=0, hbm_in=(), hbm_out=()):
    def spec(space):
        return pl.BlockSpec(memory_space=space)

    in_specs = [spec(pltpu.SMEM)] * smem + [spec(pltpu.VMEM)] * (len(args) - smem)
    for k in hbm_in:
        in_specs[k] = spec(pl.ANY)
    out_specs = [spec(pltpu.VMEM)] * len(out_shape)
    for k in hbm_out:
        out_specs[k] = spec(pl.ANY)
    return pl.pallas_call(
        body,
        out_shape=out_shape,
        in_specs=in_specs,
        out_specs=out_specs,
        scratch_shapes=scratch,
        compiler_params=pltpu.CompilerParams(vmem_limit_bytes=24 << 20),
        cost_estimate=pl.CostEstimate(flops=flops, bytes_accessed=1 << 16, transcendentals=0),
        name=name,
    )(*args)


def even(index):
    return index % 2 == 0


def rim_kernel(where_ref, blk_ref, near_ref, next_ref, first_ref, second_ref, wide):
    even_x = even(where_ref[0])
    even_y = even(where_ref[1])
    near, other = near_ref[...].astype(f32), next_ref[...].astype(f32)
    wide[0:10] = jnp.where(even_x, other, near)
    wide[10:30] = blk_ref[...].astype(f32)
    wide[30:40] = jnp.where(even_x, near, other)
    low, high = wide[:, 0:10, :], wide[:, 10:20, :]
    first_ref[...] = jnp.where(even_y, high, low).astype(bf16)
    second_ref[...] = jnp.where(even_y, low, high).astype(bf16)


def restrict_kernel(
    where_ref, blk_ref, near_x_ref, next_x_ref, near_y_ref, next_y_ref,
    d_out_ref, first_ref, second_ref, own_ref, out_ref,
    d_ref, planes, cells, mid, pay, sem,
):
    even_x = even(where_ref[0])
    even_y = even(where_ref[1])
    for x in range(40):
        p, i = x % 2, x // 2
        near, other = near_y_ref[x].astype(f32), next_y_ref[x].astype(f32)
        d_ref[p, i, 0:10, :] = jnp.where(even_y, other, near)
        d_ref[p, i, 30:40, :] = jnp.where(even_y, near, other)
        if 10 <= x < 30:
            centre = blk_ref[x - 10].astype(f32)
        else:
            near, other = near_x_ref[x % 30].astype(f32), next_x_ref[x % 30].astype(f32)
            low, high = (other, near) if x < 10 else (near, other)
            centre = jnp.where(even_x, low, high)
        d_ref[p, i, 10:30, :] = centre
        d_ref[p, i, 40:48, :] = jnp.zeros((8, 128), f32)
    save = pltpu.make_async_copy(d_ref, d_out_ref, sem)
    save.start()

    def fine(x):
        return d_ref[x % 2, x // 2]

    for i in range(16):
        c = 2 * i + 4
        planes[i] = (
            fine(c) + 0.5625 * (fine(c - 1) + fine(c + 1)) - 0.0625 * (fine(c - 3) + fine(c + 3))
        )
    for i in range(16):
        def tap(o):
            return planes[i, pl.ds(4 + o, 16, stride=2), :]
        cells[16 * i : 16 * i + 16, :] = (
            tap(0) + 0.5625 * (tap(-1) + tap(1)) - 0.0625 * (tap(-3) + tap(3))
        )
    zero = jnp.zeros((16, 128), f32)
    rows = []
    for n in range(9):
        pair = []
        for y in (2 * n - 4, 2 * n - 3):
            inside = -3 <= y <= 12
            pair.append(cells[pl.ds(y + 3, 16, stride=16), :] if inside else zero)
        rows.append(jnp.concatenate(pair, axis=1))
    r, c = iota2((256, 128))
    down_z = jnp.where(r // 128 == c // 64, weight(r % 128 - 2 * (c % 64)), 0.0)
    value = jnp.dot(
        jnp.concatenate(rows, axis=0), down_z, precision=HIGHEST, preferred_element_type=f32
    )
    r, c = iota2((144, 128))
    cell_x = 10 * where_ref[0] - 3 + r % 16
    cell_y = 10 * where_ref[1] - 4 + 2 * (r // 16) + c // 64
    inside = (cell_x >= 0) & (cell_x < 320) & (cell_y >= 0) & (cell_y < 80)
    value = jnp.where(inside, value, 0.0).astype(bf16).astype(f32)
    for n in range(9):
        mid[n, 0:16, :] = value[16 * n : 16 * n + 16]
        mid[n, 16:24, :] = jnp.zeros((8, 128), f32)
    for n in range(5):
        right, left = mid[n + 2, 1:10, :], mid[n + 2, 6:15, :]
        first_ref[n] = jnp.where(even_x, right, left).astype(bf16)
        second_ref[n] = jnp.where(even_x, left, right).astype(bf16)
        own_ref[n] = mid[n + 2, 0:16, :].astype(bf16)

    lane = lax.broadcasted_iota(jnp.int32, (1, 128), 1)
    odd = lane >= 64
    weight_0 = jnp.where(odd, 0.5625, 1.0)
    weight_1 = jnp.where(odd, 0.5625, 0.0)
    weight_3 = jnp.where(odd, -0.0625, 0.0)
    r, c = iota2((128, 32))
    down_z = weight(r % 64 - 2 * c)
    sums = []
    for y in range(5):
        n = y + 2
        def tap(o):
            def part(k):
                return mid[k, pl.ds(3 + o, 8, stride=2), :]
            return (
                weight_0 * part(n) + weight_1 * part(n - 1) + weight_3 * (part(n - 2) + part(n + 1))
            )
        sums.append(tap(0) + 0.5625 * (tap(-1) + tap(1)) - 0.0625 * (tap(-3) + tap(3)))
    out = jnp.dot(
        jnp.concatenate(sums, axis=0), down_z, precision=HIGHEST, preferred_element_type=f32
    )
    pay[...] = jnp.concatenate([out[8 * y : 8 * y + 8] for y in range(4)], axis=1)
    pay[5:6, :] = jnp.concatenate([out[32 + x : 33 + x] for x in range(4)], axis=1)
    pay[6:8, :] = jnp.zeros((2, 128), f32)
    pay[6:7, 0:32] = out[36:37]
    row = pay[...]
    for k in range(out_ref.shape[0]):
        out_ref[k] = row
    save.wait()


def fine_kernel(lo, hi, d_in_ref, v_ref, out_ref, w0, w1, e0, e1, d_ref, sem):
    load = pltpu.make_async_copy(d_in_ref, d_ref, sem)
    load.start()
    out_ref[...] = jnp.zeros((240, 256), f32)
    r, c = iota2((128, 128))
    mask = jnp.abs(r - c) <= REACH
    zero = jnp.zeros((128, 128), bf16)
    for w in (w0, w1):
        w[0:128, 128:256] = zero
        w[2688:2816, 0:128] = zero

    def build(w, b):
        for a in range(TAPS):
            line = jnp.broadcast_to(v_ref[pl.ds(a * TAPS + b, 1), :], (128, 128))
            line = pltpu.roll(line, 0, 1, stride=1, stride_axis=0)
            band = jnp.where(mask, line, 0.0).astype(bf16)
            w[a * 128 : (a + 1) * 128, 0:128] = band
            w[(a + 1) * 128 : (a + 2) * 128, 128:256] = band

    def dot(w, e, b):
        for p in range(2):
            for q in range(10):
                part = d_ref[p, 2 * q : 2 * q + 2, pl.ds(b, 24), :].reshape(48, 128)
                e[0, 48 * q : 48 * q + 48, p * 128 : (p + 1) * 128] = part.astype(bf16)
            for q in range(9):
                part = d_ref[p, 2 * q + 1 : 2 * q + 3, pl.ds(b, 24), :].reshape(48, 128)
                e[1, 48 * q : 48 * q + 48, p * 128 : (p + 1) * 128] = part.astype(bf16)
        lhs = jnp.concatenate(
            [e[k % 2, 24 * (k - k % 2) : 24 * (k - k % 2) + 240, :] for k in range(11)], axis=1
        )
        out_ref[...] += jnp.dot(lhs, w[...], preferred_element_type=f32)

    build(w0, lo)
    load.wait()

    def step(t, _):
        b = lo + 2 * t
        build(w1, b + 1)
        dot(w0, e0, b)
        build(w0, jnp.minimum(b + 2, TAPS - 1))
        dot(w1, e1, b + 1)
        return 0

    lax.fori_loop(0, (hi - lo) // 2, step, 0)
    if (hi - lo) % 2:
        dot(w0, e0, hi - 1)


def fine_sum(lo, hi, d, v):
    return vmem_call(
        functools.partial(fine_kernel, lo, hi),
        [jax.ShapeDtypeStruct((240, 256), f32)],
        [pltpu.VMEM((2816, 256), bf16)] * 2
        + [pltpu.VMEM((2, 480, 256), bf16)] * 2
        + [pltpu.VMEM((2, 20, 48, 128), f32), pltpu.SemaphoreType.DMA(())],
        "fine_sum",
        (d, v),
        flops=(hi - lo) * 2 * 240 * 2816 * 256,
        hbm_in=(0,),
    )[0]


def spread_kernel(where_ref, recv_ref, mx_ref, own_ref, near_ref, next_ref, out_ref, buf):
    even_x = even(where_ref[0])
    start = 10 * where_ref[0]
    halves = [mx_ref[h, pl.ds(start, 16), :] for h in range(2)]
    lane = lax.broadcasted_iota(jnp.int32, (16, 128), 1) % 8
    rows = [jnp.concatenate(halves, axis=1)]
    for x in range(5):
        at = 5 if x < 4 else 6
        moved = [jnp.where(lane == at, pltpu.roll(h, at - x, 1), 0.0) for h in halves]
        rows.append(jnp.concatenate(moved, axis=1))
    coarse = recv_ref[...].reshape(8 * recv_ref.shape[0], 128)
    value = jnp.dot(
        jnp.concatenate(rows, axis=0), coarse, precision=HIGHEST, preferred_element_type=f32
    )
    last = value[80:96, 0:32]
    for x in range(4):
        last = last + value[16 * x + 16 : 16 * x + 32, 32 * x : 32 * x + 32]
    part = jnp.concatenate([value[0:16], last, jnp.zeros((16, 96), f32)], axis=1)
    for n in range(5):
        near, other = near_ref[n].astype(f32), next_ref[n].astype(f32)
        buf[34 * n : 34 * n + 9, :] = jnp.where(even_x, other, near)
        buf[34 * n + 9 : 34 * n + 25, :] = own_ref[n].astype(f32)
        buf[34 * n + 25 : 34 * n + 34, :] = jnp.where(even_x, near, other)
    buf[170:176, :] = jnp.zeros((6, 128), f32)
    high = part.astype(bf16)
    low = (part - high.astype(f32)).astype(bf16)
    cells = buf[...].astype(bf16)
    for k in range(out_ref.shape[0]):
        out_ref[k, 0:176, :] = cells
        out_ref[k, 176:192, :] = high[:, 0:128]
        out_ref[k, 192:208, :] = high[:, 128:256]
        out_ref[k, 208:224, :] = low[:, 0:128]
        out_ref[k, 224:240, :] = low[:, 128:256]


def final_kernel(
    where_ref, recv_ref, my_ref, mz_ref, near_ref, far_ref, fine_ref, out_ref,
    cells, w0, w1, acc, moved, wide, line,
):
    index_x = where_ref[0]
    index_y = where_ref[1]
    count = recv_ref.shape[0]
    cells[:, 32:40, :] = jnp.zeros((17, 8, 128), f32)
    for step in range(-2, 3):
        source = index_y + step
        inside = (source >= 0) & (source < count)
        got = recv_ref[jnp.clip(source, 0, count - 1), 0:176, :].astype(f32)
        line[...] = jnp.where(inside, got, 0.0)
        for p in range(5):
            n = 5 * step + 6 + p
            if 0 <= n < 17:
                cells[n, 0:34, :] = line[34 * p : 34 * p + 34, :]

    r, c = iota2((128, 128))
    mask = jnp.abs(r % 64 - c % 64) <= REACH

    def band_rows(w, a, at):
        base = TAPS * TAPS + a * TAPS
        for j in range(11):
            same = near_ref[pl.ds(base + 2 * j, 1), :]
            upper = same
            lower = same
            if j > 0:
                upper = same + far_ref[pl.ds(base + 2 * j - 1, 1), :]
            if j < 10:
                lower = same + far_ref[pl.ds(base + 2 * j + 1, 1), :]
            upper = pltpu.roll(jnp.broadcast_to(upper, (64, 128)), 0, 1, stride=1, stride_axis=0)
            lower = pltpu.roll(jnp.broadcast_to(lower, (64, 128)), 64, 1, stride=1, stride_axis=0)
            band = jnp.where(mask, jnp.concatenate([upper, lower], axis=0), 0.0).astype(bf16)
            w[at + 128 * j : at + 128 * j + 128, :] = band

    def build(w, a):
        for k in range(3):
            band_rows(w, a + k, 1408 * k)

    def dot(w, a):
        rows = []
        for k in range(3):
            part = [cells[n, pl.ds(a + k + 1, 16), :].astype(bf16) for n in range(17)]
            rows.append([jnp.concatenate(part[g : g + 11], axis=1) for g in range(7)])
        lhs = jnp.concatenate(
            [jnp.concatenate([rows[k][g] for k in range(3)], axis=1) for g in range(7)], axis=0
        )
        acc[...] += jnp.dot(lhs, w[...], preferred_element_type=f32)

    acc[...] = jnp.zeros((112, 128), f32)
    build(w0, 0)

    def step(t, _):
        a = 6 * t
        build(w1, a + 3)
        dot(w0, a)
        build(w0, a + 6)
        dot(w1, a + 3)
        return 0

    lax.fori_loop(0, 3, step, 0)
    dot(w0, 18)

    start = 10 * index_y
    sums = [[None] * 14, [None] * 14]
    for k in range(count):
        high = [recv_ref[k, 176 + 16 * h : 192 + 16 * h, :].astype(f32) for h in range(2)]
        low = [recv_ref[k, 208 + 16 * h : 224 + 16 * h, :].astype(f32) for h in range(2)]
        for h in range(2):
            value = high[h] + low[h]
            rows_y = my_ref[2 * k + h, pl.ds(start, 16), :]
            for y in range(14):
                term = value * rows_y[y : y + 1, :]
                sums[h][y] = term if k == 0 else sums[h][y] + term
    rows = [
        jnp.concatenate([sums[h][2 * n + p] for p in range(2) for h in range(2)], axis=1)
        for n in range(7)
    ]
    top = jnp.dot(
        jnp.concatenate(rows, axis=0), mz_ref[...], precision=HIGHEST, preferred_element_type=f32
    )
    total = acc[...] + top
    r, c = iota2((112, 128))
    cell_x = 10 * index_x - 1 + r % 16
    cell_y = 10 * index_y - 2 + 2 * (r // 16) + c // 64
    inside = (cell_x >= 0) & (cell_x < 320) & (cell_y >= 0) & (cell_y < 80)
    total = jnp.where(inside, total, 0.0)
    r, c = iota2((128, 256))
    up_z = jnp.where(r // 64 == c // 128, weight(c % 128 - 2 * (r % 64)), 0.0)
    wide[...] = jnp.dot(total, up_z, precision=HIGHEST, preferred_element_type=f32)

    def middle_y(y):
        n, par = (y + 2) // 2, y % 2
        return wide[16 * n : 16 * n + 16, 128 * par : 128 * par + 128]

    for y in range(20):
        m = y // 2
        if y % 2 == 0:
            value = middle_y(m)
        else:
            value = 0.5625 * (middle_y(m) + middle_y(m + 1)) - 0.0625 * (
                middle_y(m - 1) + middle_y(m + 2)
            )
        moved[16 * y : 16 * y + 16, :] = value
    planes = [moved[pl.ds(k, 20, stride=16), :] for k in range(13)]
    for x in range(20):
        m = x // 2
        if x % 2 == 0:
            value = planes[m + 1]
        else:
            value = 0.5625 * (planes[m + 1] + planes[m + 2]) - 0.0625 * (planes[m] + planes[m + 3])
        out_ref[x] = value + fine_ref[24 * m : 24 * m + 20, 128 * (x % 2) : 128 * (x % 2) + 128]


def swap(first, second, axis):
    count = lax.axis_size(axis)
    pairs = [(k, k + 1) for k in range(0, count - 1, 2)]
    others = [(k, k + 1) for k in range(1, count - 1, 2)]

    def both(ends):
        return ends + [(b, a) for a, b in ends]

    return lax.ppermute(first, axis, both(pairs)), lax.ppermute(second, axis, both(others))


def per_device(charges, kernels):
    count_x = lax.axis_size("gx")
    count_y = lax.axis_size("gy")
    where = jnp.stack([lax.axis_index("gx"), lax.axis_index("gy")]).astype(jnp.int32)
    spread = charges.shape[0] * count_x / 16.0
    shape = jax.ShapeDtypeStruct
    near, far = (
        jnp.dot(kernels.reshape(-1, TAPS), jnp.asarray(m, bf16), preferred_element_type=f32)
        for m in spots_np()
    )
    low, high = charges[:10], charges[10:]
    even_x = even(lax.axis_index("gx"))
    near_x, next_x = swap(jnp.where(even_x, high, low), jnp.where(even_x, low, high), "gx")
    first, second = vmem_call(
        rim_kernel,
        [shape((40, 10, 128), bf16)] * 2,
        [pltpu.VMEM((40, 20, 128), f32)],
        "rim",
        (where, charges, near_x, next_x),
        smem=1,
    )
    near_y, next_y = swap(first, second, "gy")
    near_y, next_y, near, far = lax.optimization_barrier((near_y, next_y, near, far))
    d, first, second, own, coarse = vmem_call(
        restrict_kernel,
        [
            shape((2, 20, 48, 128), f32),
            shape((5, 9, 128), bf16),
            shape((5, 9, 128), bf16),
            shape((5, 16, 128), bf16),
            shape((count_x, 8, 128), f32),
        ],
        [
            pltpu.VMEM((2, 20, 48, 128), f32),
            pltpu.VMEM((16, 48, 128), f32),
            pltpu.VMEM((256, 128), f32),
            pltpu.VMEM((9, 24, 128), f32),
            pltpu.VMEM((8, 128), f32),
            pltpu.SemaphoreType.DMA(()),
        ],
        "restrict",
        (where, charges, near_x, next_x, near_y, next_y),
        smem=1,
        hbm_out=(0,),
    )
    near_m, next_m = swap(first, second, "gx")
    coarse = lax.all_to_all(coarse, "gx", 0, 0)
    parts = vmem_call(
        spread_kernel,
        [shape((count_y, 240, 128), bf16)],
        [pltpu.VMEM((176, 128), f32)],
        "spread",
        (where, coarse, jnp.asarray(matrix_x_np(spread)), own, near_m, next_m),
        smem=1,
    )[0]
    parts, near = lax.optimization_barrier((parts, near))
    parts = lax.all_to_all(parts, "gy", 0, 0)
    fine = fine_sum(0, TAPS, d, near)
    return vmem_call(
        final_kernel,
        [shape((20, 20, 128), f32)],
        [
            pltpu.VMEM((17, 40, 128), f32),
            pltpu.VMEM((4224, 128), bf16),
            pltpu.VMEM((4224, 128), bf16),
            pltpu.VMEM((112, 128), f32),
            pltpu.VMEM((320, 128), f32),
            pltpu.VMEM((112, 256), f32),
            pltpu.VMEM((176, 128), f32),
        ],
        "final",
        (
            where,
            parts,
            jnp.asarray(matrix_y_np(spread)),
            jnp.asarray(matrix_z_np(spread)),
            near,
            far,
            fine,
        ),
        smem=1,
    )[0]


def solution(mesh):
    return jax.shard_map(
        per_device,
        mesh=mesh,
        in_specs=(P("gx", "gy", None), P()),
        out_specs=P("gx", "gy", None),
        check_vma=False,
    )
```

```python
import functools
import numpy as np
import jax
import jax.numpy as jnp
from jax import lax
from jax.experimental import pallas as pl
from jax.experimental.pallas import tpu as pltpu
from jax.sharding import PartitionSpec as P

f32 = jnp.float32
bf16 = jnp.bfloat16
spread_norm = 1.2533141
HIGHEST = lax.Precision.HIGHEST
REACH = 10
TAPS = 21
GROUP = 3
SPLIT = 9


def weight_np(offset):
    d = np.abs(offset)
    return np.where(d == 0, 1.0, np.where(d == 1, 0.5625, np.where(d == 3, -0.0625, 0.0)))


def top_matrix_np(n, spread):
    prolong = weight_np(np.arange(2 * n)[:, None] - 2 * np.arange(n)[None, :])
    offset = (np.arange(n)[:, None] - np.arange(n)[None, :]) / spread
    return prolong @ (np.exp(-offset * offset) / np.sqrt(spread * spread_norm))


def lane_tiles(m):
    return m.reshape(m.shape[0], -1, 128).transpose(1, 0, 2).astype(np.float32)


def matrix_x_np(spread):
    m = top_matrix_np(160, spread).reshape(320, 32, 5)
    out = np.zeros((328, 32, 8))
    out[1:321, :, :5] = m
    return lane_tiles(out.reshape(328, 256))


def matrix_y_np(spread):
    m = top_matrix_np(40, spread).reshape(80, 8, 5)
    out = np.zeros((88, 8, 8))
    out[2:82, :, :5] = m
    return lane_tiles(np.repeat(out.reshape(88, 64), 32, axis=1))


def matrix_z_np(spread):
    m = top_matrix_np(32, spread).T
    out = np.zeros((2, 8, 32, 2, 64))
    for par in range(2):
        out[par, :, :, par, :] = m[None]
    return out.reshape(512, 128).astype(np.float32)


def spots_np():
    taps = np.arange(TAPS)[:, None]
    lanes = np.arange(128)[None, :]
    near = lanes == (REACH - taps) % 128
    far = lanes == (64 + REACH - taps) % 128
    return near, far


def weight(d):
    d = jnp.abs(d)
    return jnp.where(d == 0, 1.0, jnp.where(d == 1, 0.5625, jnp.where(d == 3, -0.0625, 0.0))).astype(f32)


def exact_dot(rows, weights):
    count = rows.shape[0]
    high = rows.astype(bf16)
    rest = rows - high.astype(f32)
    middle = rest.astype(bf16)
    low = (rest - middle.astype(f32)).astype(bf16)
    out = jnp.dot(
        jnp.concatenate([high, middle, low], axis=0),
        weights.astype(bf16),
        preferred_element_type=f32,
    )
    return out[0:count] + (out[count : 2 * count] + out[2 * count :])


def iota2(shape):
    return (lax.broadcasted_iota(jnp.int32, shape, 0), lax.broadcasted_iota(jnp.int32, shape, 1))


def vmem_call(body, out_shape, scratch, name, args, smem=0, flops=0, hbm_in=(), hbm_out=()):
    def spec(space):
        return pl.BlockSpec(memory_space=space)

    in_specs = [spec(pltpu.SMEM)] * smem + [spec(pltpu.VMEM)] * (len(args) - smem)
    for k in hbm_in:
        in_specs[k] = spec(pltpu.HBM)
    out_specs = [spec(pltpu.VMEM)] * len(out_shape)
    for k in hbm_out:
        out_specs[k] = spec(pltpu.HBM)
    return pl.pallas_call(
        body,
        out_shape=out_shape,
        in_specs=in_specs,
        out_specs=out_specs,
        scratch_shapes=scratch,
        compiler_params=pltpu.CompilerParams(vmem_limit_bytes=24 << 20),
        cost_estimate=pl.CostEstimate(flops=flops, bytes_accessed=1 << 16, transcendentals=0),
        name=name,
    )(*args)


def even(index):
    return index % 2 == 0


def rim_kernel(where_ref, blk_ref, near_ref, next_ref, first_ref, second_ref, wide):
    even_x = even(where_ref[0])
    even_y = even(where_ref[1])
    near, other = near_ref[...].astype(f32), next_ref[...].astype(f32)
    wide[0:10] = jnp.where(even_x, other, near)
    wide[10:30] = blk_ref[...].astype(f32)
    wide[30:40] = jnp.where(even_x, near, other)
    low, high = wide[:, 0:10, :], wide[:, 10:20, :]
    first_ref[...] = jnp.where(even_y, high, low).astype(bf16)
    second_ref[...] = jnp.where(even_y, low, high).astype(bf16)


def restrict_kernel(
    where_ref, blk_ref, near_x_ref, next_x_ref, near_y_ref, next_y_ref,
    d_out_ref, first_ref, second_ref, own_ref, out_ref,
    d_ref, planes, cells, mid, pay, sem,
):
    even_x = even(where_ref[0])
    even_y = even(where_ref[1])
    for x in range(40):
        p, i = x % 2, x // 2
        near, other = near_y_ref[x].astype(f32), next_y_ref[x].astype(f32)
        d_ref[p, i, 0:10, :] = jnp.where(even_y, other, near)
        d_ref[p, i, 30:40, :] = jnp.where(even_y, near, other)
        if 10 <= x < 30:
            centre = blk_ref[x - 10].astype(f32)
        else:
            near, other = near_x_ref[x % 30].astype(f32), next_x_ref[x % 30].astype(f32)
            low, high = (other, near) if x < 10 else (near, other)
            centre = jnp.where(even_x, low, high)
        d_ref[p, i, 10:30, :] = centre
        d_ref[p, i, 40:48, :] = jnp.zeros((8, 128), f32)
    save = pltpu.make_async_copy(d_ref, d_out_ref, sem)
    save.start()

    def fine(x):
        return d_ref[x % 2, x // 2]

    for i in range(16):
        c = 2 * i + 4
        planes[i] = (
            fine(c) + 0.5625 * (fine(c - 1) + fine(c + 1)) - 0.0625 * (fine(c - 3) + fine(c + 3))
        )
    for i in range(16):
        def tap(o):
            return planes[i, pl.ds(4 + o, 16, stride=2), :]
        cells[16 * i : 16 * i + 16, :] = (
            tap(0) + 0.5625 * (tap(-1) + tap(1)) - 0.0625 * (tap(-3) + tap(3))
        )
    zero = jnp.zeros((16, 128), f32)
    rows = []
    for n in range(9):
        pair = []
        for y in (2 * n - 4, 2 * n - 3):
            inside = -3 <= y <= 12
            pair.append(cells[pl.ds(y + 3, 16, stride=16), :] if inside else zero)
        rows.append(jnp.concatenate(pair, axis=1))
    r, c = iota2((256, 128))
    down_z = jnp.where(r // 128 == c // 64, weight(r % 128 - 2 * (c % 64)), 0.0)
    value = exact_dot(jnp.concatenate(rows, axis=0), down_z)
    r, c = iota2((144, 128))
    cell_x = 10 * where_ref[0] - 3 + r % 16
    cell_y = 10 * where_ref[1] - 4 + 2 * (r // 16) + c // 64
    inside = (cell_x >= 0) & (cell_x < 320) & (cell_y >= 0) & (cell_y < 80)
    value = jnp.where(inside, value, 0.0).astype(bf16).astype(f32)
    for n in range(9):
        mid[n, 0:16, :] = value[16 * n : 16 * n + 16]
        mid[n, 16:24, :] = jnp.zeros((8, 128), f32)
    for n in range(5):
        right, left = mid[n + 2, 1:10, :], mid[n + 2, 6:15, :]
        first_ref[n] = jnp.where(even_x, right, left).astype(bf16)
        second_ref[n] = jnp.where(even_x, left, right).astype(bf16)
        own_ref[n] = mid[n + 2, 0:16, :].astype(bf16)

    lane = lax.broadcasted_iota(jnp.int32, (1, 128), 1)
    odd = lane >= 64
    weight_0 = jnp.where(odd, 0.5625, 1.0)
    weight_1 = jnp.where(odd, 0.5625, 0.0)
    weight_3 = jnp.where(odd, -0.0625, 0.0)
    r, c = iota2((128, 32))
    down_z = weight(r % 64 - 2 * c)
    sums = []
    for y in range(5):
        n = y + 2
        def tap(o):
            def part(k):
                return mid[k, pl.ds(3 + o, 8, stride=2), :]
            return (
                weight_0 * part(n) + weight_1 * part(n - 1) + weight_3 * (part(n - 2) + part(n + 1))
            )
        sums.append(tap(0) + 0.5625 * (tap(-1) + tap(1)) - 0.0625 * (tap(-3) + tap(3)))
    out = exact_dot(jnp.concatenate(sums, axis=0), down_z)
    pay[...] = jnp.concatenate([out[8 * y : 8 * y + 8] for y in range(4)], axis=1)
    pay[5:6, :] = jnp.concatenate([out[32 + x : 33 + x] for x in range(4)], axis=1)
    pay[6:8, :] = jnp.zeros((2, 128), f32)
    pay[6:7, 0:32] = out[36:37]
    row = pay[...]
    for k in range(out_ref.shape[0]):
        out_ref[k] = row
    save.wait()


def fine_kernel(lo, hi, first, d_in_ref, v_ref, *refs):
    if first:
        out_ref, w0, w1, e0, e1, d_ref, sem = refs
    else:
        acc_ref, out_ref, w0, w1, e0, e1, d_ref, sem = refs
    load = pltpu.make_async_copy(d_in_ref, d_ref, sem)
    load.start()
    r, c = iota2((128, 128))
    mask = jnp.abs(r - c) <= REACH
    zero = jnp.zeros((128, 128), bf16)
    for w in (w0, w1):
        for k in range(GROUP):
            w[2816 * k : 2816 * k + 128, 128:256] = zero
            w[2816 * k + 2688 : 2816 * k + 2816, 0:128] = zero

    def build(w, start):
        for k in range(GROUP):
            for a in range(TAPS):
                line = jnp.broadcast_to(v_ref[pl.ds(a * TAPS + start + k, 1), :], (128, 128))
                line = pltpu.roll(line, 0, 1, stride=1, stride_axis=0)
                band = jnp.where(mask, line, 0.0).astype(bf16)
                at = 2816 * k + 128 * a
                w[at : at + 128, 0:128] = band
                w[at + 128 : at + 256, 128:256] = band

    def dot(w, e, start):
        tiles = []
        for k in range(GROUP):
            for p in range(2):
                for q in range(10):
                    part = d_ref[p, 2 * q : 2 * q + 2, pl.ds(start + k, 24), :].reshape(48, 128)
                    e[k, 0, 48 * q : 48 * q + 48, p * 128 : (p + 1) * 128] = part.astype(bf16)
                for q in range(9):
                    part = d_ref[p, 2 * q + 1 : 2 * q + 3, pl.ds(start + k, 24), :].reshape(48, 128)
                    e[k, 1, 48 * q : 48 * q + 48, p * 128 : (p + 1) * 128] = part.astype(bf16)
            tiles += [
                e[k, m % 2, 24 * (m - m % 2) : 24 * (m - m % 2) + 240, :] for m in range(11)
            ]
        lhs = jnp.concatenate(tiles, axis=1)
        out_ref[...] += jnp.dot(lhs, w[...], preferred_element_type=f32)

    build(w0, lo)
    load.wait()
    out_ref[...] = jnp.zeros((240, 256), f32) if first else acc_ref[...]

    def step(t, _):
        b = lo + 2 * GROUP * t
        build(w1, b + GROUP)
        dot(w0, e0, b)
        build(w0, jnp.minimum(b + 2 * GROUP, TAPS - GROUP))
        dot(w1, e1, b + GROUP)
        return 0

    groups = (hi - lo) // GROUP
    lax.fori_loop(0, groups // 2, step, 0)
    if groups % 2:
        dot(w0, e0, hi - GROUP)


def fine_sum(lo, hi, d, v, acc=None):
    return vmem_call(
        functools.partial(fine_kernel, lo, hi, acc is None),
        [jax.ShapeDtypeStruct((240, 256), f32)],
        [pltpu.VMEM((GROUP * 2816, 256), bf16)] * 2
        + [pltpu.VMEM((GROUP, 2, 480, 256), bf16)] * 2
        + [pltpu.VMEM((2, 20, 48, 128), f32), pltpu.SemaphoreType.DMA(())],
        "fine_sum",
        (d, v) if acc is None else (d, v, acc),
        flops=(hi - lo) * 2 * 240 * 2816 * 256,
        hbm_in=(0,),
    )[0]


def spread_kernel(where_ref, recv_ref, mx_ref, own_ref, near_ref, next_ref, out_ref, buf):
    even_x = even(where_ref[0])
    start = 10 * where_ref[0]
    halves = [mx_ref[h, pl.ds(start, 16), :] for h in range(2)]
    lane = lax.broadcasted_iota(jnp.int32, (16, 128), 1) % 8
    rows = [jnp.concatenate(halves, axis=1)]
    for x in range(5):
        at = 5 if x < 4 else 6
        moved = [jnp.where(lane == at, pltpu.roll(h, at - x, 1), 0.0) for h in halves]
        rows.append(jnp.concatenate(moved, axis=1))
    coarse = recv_ref[...].reshape(8 * recv_ref.shape[0], 128)
    value = jnp.dot(
        jnp.concatenate(rows, axis=0), coarse, precision=HIGHEST, preferred_element_type=f32
    )
    last = value[80:96, 0:32]
    for x in range(4):
        last = last + value[16 * x + 16 : 16 * x + 32, 32 * x : 32 * x + 32]
    part = jnp.concatenate([value[0:16], last, jnp.zeros((16, 96), f32)], axis=1)
    for n in range(5):
        near, other = near_ref[n].astype(f32), next_ref[n].astype(f32)
        buf[34 * n : 34 * n + 9, :] = jnp.where(even_x, other, near)
        buf[34 * n + 9 : 34 * n + 25, :] = own_ref[n].astype(f32)
        buf[34 * n + 25 : 34 * n + 34, :] = jnp.where(even_x, near, other)
    buf[170:176, :] = jnp.zeros((6, 128), f32)
    high = part.astype(bf16)
    low = (part - high.astype(f32)).astype(bf16)
    cells = buf[...].astype(bf16)
    for k in range(out_ref.shape[0]):
        out_ref[k, 0:176, :] = cells
        out_ref[k, 176:192, :] = high[:, 0:128]
        out_ref[k, 192:208, :] = high[:, 128:256]
        out_ref[k, 208:224, :] = low[:, 0:128]
        out_ref[k, 224:240, :] = low[:, 128:256]


def final_kernel(
    where_ref, recv_ref, my_ref, mz_ref, near_ref, far_ref, fine_ref, out_ref,
    cells, w0, w1, acc, moved, wide, line,
):
    index_x = where_ref[0]
    index_y = where_ref[1]
    count = recv_ref.shape[0]
    cells[:, 32:40, :] = jnp.zeros((17, 8, 128), f32)
    for step in range(-2, 3):
        source = index_y + step
        inside = (source >= 0) & (source < count)
        got = recv_ref[jnp.clip(source, 0, count - 1), 0:176, :].astype(f32)
        line[...] = jnp.where(inside, got, 0.0)
        for p in range(5):
            n = 5 * step + 6 + p
            if 0 <= n < 17:
                cells[n, 0:34, :] = line[34 * p : 34 * p + 34, :]

    r, c = iota2((128, 128))
    mask = jnp.abs(r % 64 - c % 64) <= REACH

    def band_rows(w, a, at):
        base = TAPS * TAPS + a * TAPS
        for j in range(11):
            same = near_ref[pl.ds(base + 2 * j, 1), :]
            upper = same
            lower = same
            if j > 0:
                upper = same + far_ref[pl.ds(base + 2 * j - 1, 1), :]
            if j < 10:
                lower = same + far_ref[pl.ds(base + 2 * j + 1, 1), :]
            upper = pltpu.roll(jnp.broadcast_to(upper, (64, 128)), 0, 1, stride=1, stride_axis=0)
            lower = pltpu.roll(jnp.broadcast_to(lower, (64, 128)), 64, 1, stride=1, stride_axis=0)
            band = jnp.where(mask, jnp.concatenate([upper, lower], axis=0), 0.0).astype(bf16)
            w[at + 128 * j : at + 128 * j + 128, :] = band

    def build(w, a):
        for k in range(3):
            band_rows(w, a + k, 1408 * k)

    def dot(w, a):
        rows = []
        for k in range(3):
            part = [cells[n, pl.ds(a + k + 1, 16), :].astype(bf16) for n in range(17)]
            rows.append([jnp.concatenate(part[g : g + 11], axis=1) for g in range(7)])
        lhs = jnp.concatenate(
            [jnp.concatenate([rows[k][g] for k in range(3)], axis=1) for g in range(7)], axis=0
        )
        acc[...] += jnp.dot(lhs, w[...], preferred_element_type=f32)

    acc[...] = jnp.zeros((112, 128), f32)
    build(w0, 0)

    def step(t, _):
        a = 6 * t
        build(w1, a + 3)
        dot(w0, a)
        build(w0, a + 6)
        dot(w1, a + 3)
        return 0

    lax.fori_loop(0, 3, step, 0)
    dot(w0, 18)

    start = 10 * index_y
    sums = [[None] * 14, [None] * 14]
    for k in range(count):
        high = [recv_ref[k, 176 + 16 * h : 192 + 16 * h, :].astype(f32) for h in range(2)]
        low = [recv_ref[k, 208 + 16 * h : 224 + 16 * h, :].astype(f32) for h in range(2)]
        for h in range(2):
            value = high[h] + low[h]
            rows_y = my_ref[2 * k + h, pl.ds(start, 16), :]
            for y in range(14):
                term = value * rows_y[y : y + 1, :]
                sums[h][y] = term if k == 0 else sums[h][y] + term
    rows = [
        jnp.concatenate([sums[h][2 * n + p] for p in range(2) for h in range(2)], axis=1)
        for n in range(7)
    ]
    top = jnp.dot(
        jnp.concatenate(rows, axis=0), mz_ref[...], precision=HIGHEST, preferred_element_type=f32
    )
    total = acc[...] + top
    r, c = iota2((112, 128))
    cell_x = 10 * index_x - 1 + r % 16
    cell_y = 10 * index_y - 2 + 2 * (r // 16) + c // 64
    inside = (cell_x >= 0) & (cell_x < 320) & (cell_y >= 0) & (cell_y < 80)
    total = jnp.where(inside, total, 0.0)
    r, c = iota2((128, 256))
    up_z = jnp.where(r // 64 == c // 128, weight(c % 128 - 2 * (r % 64)), 0.0)
    wide[...] = exact_dot(total, up_z)

    def middle_y(y):
        n, par = (y + 2) // 2, y % 2
        return wide[16 * n : 16 * n + 16, 128 * par : 128 * par + 128]

    for y in range(20):
        m = y // 2
        if y % 2 == 0:
            value = middle_y(m)
        else:
            value = 0.5625 * (middle_y(m) + middle_y(m + 1)) - 0.0625 * (
                middle_y(m - 1) + middle_y(m + 2)
            )
        moved[16 * y : 16 * y + 16, :] = value
    planes = [moved[pl.ds(k, 20, stride=16), :] for k in range(13)]
    for x in range(20):
        m = x // 2
        if x % 2 == 0:
            value = planes[m + 1]
        else:
            value = 0.5625 * (planes[m + 1] + planes[m + 2]) - 0.0625 * (planes[m] + planes[m + 3])
        out_ref[x] = value + fine_ref[24 * m : 24 * m + 20, 128 * (x % 2) : 128 * (x % 2) + 128]


def swap(first, second, axis):
    count = lax.axis_size(axis)
    pairs = [(k, k + 1) for k in range(0, count - 1, 2)]
    others = [(k, k + 1) for k in range(1, count - 1, 2)]

    def both(ends):
        return ends + [(b, a) for a, b in ends]

    return lax.ppermute(first, axis, both(pairs)), lax.ppermute(second, axis, both(others))


def per_device(charges, kernels):
    count_x = lax.axis_size("gx")
    count_y = lax.axis_size("gy")
    where = jnp.stack([lax.axis_index("gx"), lax.axis_index("gy")]).astype(jnp.int32)
    spread = charges.shape[0] * count_x / 16.0
    shape = jax.ShapeDtypeStruct
    low, high = charges[:10], charges[10:]
    even_x = even(lax.axis_index("gx"))
    near_x, next_x = swap(jnp.where(even_x, high, low), jnp.where(even_x, low, high), "gx")
    first, second = vmem_call(
        rim_kernel,
        [shape((40, 10, 128), bf16)] * 2,
        [pltpu.VMEM((40, 20, 128), f32)],
        "rim",
        (where, charges, near_x, next_x),
        smem=1,
    )
    first, second, kernels = lax.optimization_barrier((first, second, kernels))
    near, far = (
        jnp.dot(kernels.reshape(-1, TAPS), jnp.asarray(m, bf16), preferred_element_type=f32)
        for m in spots_np()
    )
    near_y, next_y = swap(first, second, "gy")
    near_y, next_y, near, far = lax.optimization_barrier((near_y, next_y, near, far))
    d, first, second, own, coarse = vmem_call(
        restrict_kernel,
        [
            shape((2, 20, 48, 128), f32),
            shape((5, 9, 128), bf16),
            shape((5, 9, 128), bf16),
            shape((5, 16, 128), bf16),
            shape((count_x, 8, 128), f32),
        ],
        [
            pltpu.VMEM((2, 20, 48, 128), f32),
            pltpu.VMEM((16, 48, 128), f32),
            pltpu.VMEM((256, 128), f32),
            pltpu.VMEM((9, 24, 128), f32),
            pltpu.VMEM((8, 128), f32),
            pltpu.SemaphoreType.DMA(()),
        ],
        "restrict",
        (where, charges, near_x, next_x, near_y, next_y),
        smem=1,
        hbm_out=(0,),
    )
    near_m, next_m = swap(first, second, "gx")
    coarse, near_m, next_m = lax.optimization_barrier((coarse, near_m, next_m))
    coarse = lax.all_to_all(coarse, "gx", 0, 0)
    fine = fine_sum(0, SPLIT, d, near)
    coarse, fine = lax.optimization_barrier((coarse, fine))
    parts = vmem_call(
        spread_kernel,
        [shape((count_y, 240, 128), bf16)],
        [pltpu.VMEM((176, 128), f32)],
        "spread",
        (where, coarse, jnp.asarray(matrix_x_np(spread)), own, near_m, next_m),
        smem=1,
    )[0]
    parts, near = lax.optimization_barrier((parts, near))
    parts = lax.all_to_all(parts, "gy", 0, 0)
    fine = fine_sum(SPLIT, TAPS, d, near, fine)
    return vmem_call(
        final_kernel,
        [shape((20, 20, 128), f32)],
        [
            pltpu.VMEM((17, 40, 128), f32),
            pltpu.VMEM((4224, 128), bf16),
            pltpu.VMEM((4224, 128), bf16),
            pltpu.VMEM((112, 128), f32),
            pltpu.VMEM((320, 128), f32),
            pltpu.VMEM((112, 256), f32),
            pltpu.VMEM((176, 128), f32),
        ],
        "final",
        (
            where,
            parts,
            jnp.asarray(matrix_y_np(spread)),
            jnp.asarray(matrix_z_np(spread)),
            near,
            far,
            fine,
        ),
        smem=1,
    )[0]


def solution(mesh):
    return jax.shard_map(
        per_device,
        mesh=mesh,
        in_specs=(P("gx", "gy", None), P()),
        out_specs=P("gx", "gy", None),
        check_vma=False,
    )
```

```python
import functools
import numpy as np
import jax
import jax.numpy as jnp
from jax import lax
from jax.experimental import pallas as pl
from jax.experimental.pallas import tpu as pltpu
from jax.sharding import PartitionSpec as P

f32 = jnp.float32
bf16 = jnp.bfloat16
spread_norm = 1.2533141
HIGHEST = lax.Precision.HIGHEST
REACH = 10
TAPS = 21
GROUP = 3


def weight_np(offset):
    d = np.abs(offset)
    return np.where(d == 0, 1.0, np.where(d == 1, 0.5625, np.where(d == 3, -0.0625, 0.0)))


def top_matrix_np(n, spread):
    prolong = weight_np(np.arange(2 * n)[:, None] - 2 * np.arange(n)[None, :])
    offset = (np.arange(n)[:, None] - np.arange(n)[None, :]) / spread
    return prolong @ (np.exp(-offset * offset) / np.sqrt(spread * spread_norm))


def lane_tiles(m):
    return m.reshape(m.shape[0], -1, 128).transpose(1, 0, 2).astype(np.float32)


def matrix_x_np(spread):
    m = top_matrix_np(160, spread).reshape(320, 32, 5)
    out = np.zeros((328, 32, 8))
    out[1:321, :, :5] = m
    return lane_tiles(out.reshape(328, 256))


def matrix_y_np(spread):
    m = top_matrix_np(40, spread).reshape(80, 8, 5)
    out = np.zeros((88, 8, 8))
    out[2:82, :, :5] = m
    return lane_tiles(np.repeat(out.reshape(88, 64), 32, axis=1))


def matrix_z_np(spread):
    m = top_matrix_np(32, spread).T
    out = np.zeros((2, 8, 32, 2, 64))
    for par in range(2):
        out[par, :, :, par, :] = m[None]
    return out.reshape(512, 128).astype(np.float32)


def spots_np():
    taps = np.arange(TAPS)[:, None]
    lanes = np.arange(128)[None, :]
    near = lanes == (REACH - taps) % 128
    far = lanes == (64 + REACH - taps) % 128
    return near, far


def weight(d):
    d = jnp.abs(d)
    return jnp.where(d == 0, 1.0, jnp.where(d == 1, 0.5625, jnp.where(d == 3, -0.0625, 0.0))).astype(f32)


def exact_dot(rows, weights):
    count = rows.shape[0]
    high = rows.astype(bf16)
    rest = rows - high.astype(f32)
    middle = rest.astype(bf16)
    low = (rest - middle.astype(f32)).astype(bf16)
    out = jnp.dot(
        jnp.concatenate([high, middle, low], axis=0),
        weights.astype(bf16),
        preferred_element_type=f32,
    )
    return out[0:count] + (out[count : 2 * count] + out[2 * count :])


def iota2(shape):
    return (lax.broadcasted_iota(jnp.int32, shape, 0), lax.broadcasted_iota(jnp.int32, shape, 1))


def vmem_call(body, out_shape, scratch, name, args, smem=0, flops=0, limit=8):
    def spec(space):
        return pl.BlockSpec(memory_space=space)

    return pl.pallas_call(
        body,
        out_shape=out_shape,
        in_specs=[spec(pltpu.SMEM)] * smem + [spec(pltpu.VMEM)] * (len(args) - smem),
        out_specs=[spec(pltpu.VMEM)] * len(out_shape),
        scratch_shapes=scratch,
        compiler_params=pltpu.CompilerParams(vmem_limit_bytes=limit << 20),
        cost_estimate=pl.CostEstimate(flops=flops, bytes_accessed=1 << 16, transcendentals=0),
        name=name,
    )(*args)


def even(index):
    return index % 2 == 0


def rim_kernel(where_ref, blk_ref, near_ref, next_ref, first_ref, second_ref, wide, dense):
    even_x = even(where_ref[0])
    even_y = even(where_ref[1])
    near, other = near_ref[...].astype(f32), next_ref[...].astype(f32)
    wide[0:10] = jnp.where(even_x, other, near)
    wide[10:30] = blk_ref[...].astype(f32)
    wide[30:40] = jnp.where(even_x, near, other)
    for x in range(40):
        low, high = wide[x, 0:10, :], wide[x, 10:20, :]
        dense[0, 10 * x : 10 * x + 10, :] = jnp.where(even_y, high, low)
        dense[1, 10 * x : 10 * x + 10, :] = jnp.where(even_y, low, high)
    first_ref[...] = dense[0].astype(bf16)
    second_ref[...] = dense[1].astype(bf16)


def restrict_kernel(
    where_ref, blk_ref, near_x_ref, next_x_ref, near_y_ref, next_y_ref,
    d_out_ref, first_ref, second_ref, own_ref, out_ref,
    d_ref, dense, planes, cells, mid, pay,
):
    even_x = even(where_ref[0])
    even_y = even(where_ref[1])
    near, other = near_y_ref[...].astype(f32), next_y_ref[...].astype(f32)
    dense[0] = jnp.where(even_y, other, near)
    dense[1] = jnp.where(even_y, near, other)
    for x in range(40):
        p, i = x % 2, x // 2
        d_ref[p, i, 0:10, :] = dense[0, 10 * x : 10 * x + 10, :]
        d_ref[p, i, 30:40, :] = dense[1, 10 * x : 10 * x + 10, :]
        if 10 <= x < 30:
            centre = blk_ref[x - 10].astype(f32)
        else:
            near, other = near_x_ref[x % 30].astype(f32), next_x_ref[x % 30].astype(f32)
            low, high = (other, near) if x < 10 else (near, other)
            centre = jnp.where(even_x, low, high)
        d_ref[p, i, 10:30, :] = centre
        d_out_ref[x] = d_ref[p, i, 0:40, :].astype(bf16)

    def fine(x):
        return d_ref[x % 2, x // 2]

    for i in range(16):
        c = 2 * i + 4
        planes[i] = (
            fine(c) + 0.5625 * (fine(c - 1) + fine(c + 1)) - 0.0625 * (fine(c - 3) + fine(c + 3))
        )
    for i in range(16):
        def tap(o):
            return planes[i, pl.ds(4 + o, 16, stride=2), :]
        cells[16 * i : 16 * i + 16, :] = (
            tap(0) + 0.5625 * (tap(-1) + tap(1)) - 0.0625 * (tap(-3) + tap(3))
        )
    zero = jnp.zeros((16, 128), f32)
    rows = []
    for n in range(9):
        pair = []
        for y in (2 * n - 4, 2 * n - 3):
            inside = -3 <= y <= 12
            pair.append(cells[pl.ds(y + 3, 16, stride=16), :] if inside else zero)
        rows.append(jnp.concatenate(pair, axis=1))
    r, c = iota2((256, 128))
    down_z = jnp.where(r // 128 == c // 64, weight(r % 128 - 2 * (c % 64)), 0.0)
    value = exact_dot(jnp.concatenate(rows, axis=0), down_z)
    r, c = iota2((144, 128))
    cell_x = 10 * where_ref[0] - 3 + r % 16
    cell_y = 10 * where_ref[1] - 4 + 2 * (r // 16) + c // 64
    inside = (cell_x >= 0) & (cell_x < 320) & (cell_y >= 0) & (cell_y < 80)
    value = jnp.where(inside, value, 0.0).astype(bf16).astype(f32)
    for n in range(9):
        mid[n, 0:16, :] = value[16 * n : 16 * n + 16]
        mid[n, 16:24, :] = jnp.zeros((8, 128), f32)
    for n in range(5):
        right, left = mid[n + 2, 1:10, :], mid[n + 2, 6:15, :]
        first_ref[n] = jnp.where(even_x, right, left).astype(bf16)
        second_ref[n] = jnp.where(even_x, left, right).astype(bf16)
        own_ref[n] = mid[n + 2, 0:16, :].astype(bf16)

    lane = lax.broadcasted_iota(jnp.int32, (1, 128), 1)
    odd = lane >= 64
    weight_0 = jnp.where(odd, 0.5625, 1.0)
    weight_1 = jnp.where(odd, 0.5625, 0.0)
    weight_3 = jnp.where(odd, -0.0625, 0.0)
    r, c = iota2((128, 32))
    down_z = weight(r % 64 - 2 * c)
    sums = []
    for y in range(5):
        n = y + 2
        def tap(o):
            def part(k):
                return mid[k, pl.ds(3 + o, 8, stride=2), :]
            return (
                weight_0 * part(n) + weight_1 * part(n - 1) + weight_3 * (part(n - 2) + part(n + 1))
            )
        sums.append(tap(0) + 0.5625 * (tap(-1) + tap(1)) - 0.0625 * (tap(-3) + tap(3)))
    out = exact_dot(jnp.concatenate(sums, axis=0), down_z)
    pay[...] = jnp.concatenate([out[8 * y : 8 * y + 8] for y in range(4)], axis=1)
    pay[5:6, :] = jnp.concatenate([out[32 + x : 33 + x] for x in range(4)], axis=1)
    pay[6:8, :] = jnp.zeros((2, 128), f32)
    pay[6:7, 0:32] = out[36:37]
    row = pay[...]
    for k in range(out_ref.shape[0]):
        out_ref[k] = row


def fine_kernel(lo, hi, first, d_in_ref, v_ref, *refs):
    if first:
        out_ref, w0, w1, e0, e1, d_ref = refs
    else:
        acc_ref, out_ref, w0, w1, e0, e1, d_ref = refs
    for x in range(40):
        d_ref[x % 2, x // 2, 0:40, :] = d_in_ref[x].astype(f32)
        d_ref[x % 2, x // 2, 40:48, :] = jnp.zeros((8, 128), f32)
    r, c = iota2((128, 128))
    mask = jnp.abs(r - c) <= REACH
    zero = jnp.zeros((128, 128), bf16)
    for w in (w0, w1):
        for k in range(GROUP):
            w[2816 * k : 2816 * k + 128, 128:256] = zero
            w[2816 * k + 2688 : 2816 * k + 2816, 0:128] = zero

    def build(w, start):
        for k in range(GROUP):
            for a in range(TAPS):
                line = jnp.broadcast_to(v_ref[pl.ds(a * TAPS + start + k, 1), :], (128, 128))
                line = pltpu.roll(line, 0, 1, stride=1, stride_axis=0)
                band = jnp.where(mask, line, 0.0).astype(bf16)
                at = 2816 * k + 128 * a
                w[at : at + 128, 0:128] = band
                w[at + 128 : at + 256, 128:256] = band

    def dot(w, e, start):
        tiles = []
        for k in range(GROUP):
            for p in range(2):
                for q in range(10):
                    part = d_ref[p, 2 * q : 2 * q + 2, pl.ds(start + k, 24), :].reshape(48, 128)
                    e[k, 0, 48 * q : 48 * q + 48, p * 128 : (p + 1) * 128] = part.astype(bf16)
                for q in range(9):
                    part = d_ref[p, 2 * q + 1 : 2 * q + 3, pl.ds(start + k, 24), :].reshape(48, 128)
                    e[k, 1, 48 * q : 48 * q + 48, p * 128 : (p + 1) * 128] = part.astype(bf16)
            tiles += [
                e[k, m % 2, 24 * (m - m % 2) : 24 * (m - m % 2) + 240, :] for m in range(11)
            ]
        lhs = jnp.concatenate(tiles, axis=1)
        out_ref[...] += jnp.dot(lhs, w[...], preferred_element_type=f32)

    build(w0, lo)
    out_ref[...] = jnp.zeros((240, 256), f32) if first else acc_ref[...]

    def step(t, _):
        b = lo + 2 * GROUP * t
        build(w1, b + GROUP)
        dot(w0, e0, b)
        build(w0, jnp.minimum(b + 2 * GROUP, TAPS - GROUP))
        dot(w1, e1, b + GROUP)
        return 0

    groups = (hi - lo) // GROUP
    lax.fori_loop(0, groups // 2, step, 0)
    if groups % 2:
        dot(w0, e0, hi - GROUP)


def fine_sum(lo, hi, d, v, acc=None):
    return vmem_call(
        functools.partial(fine_kernel, lo, hi, acc is None),
        [jax.ShapeDtypeStruct((240, 256), f32)],
        [pltpu.VMEM((GROUP * 2816, 256), bf16)] * 2
        + [pltpu.VMEM((GROUP, 2, 480, 256), bf16)] * 2
        + [pltpu.VMEM((2, 20, 48, 128), f32)],
        "fine_sum",
        (d, v) if acc is None else (d, v, acc),
        flops=(hi - lo) * 2 * 240 * 2816 * 256,
        limit=20,
    )[0]


def spread_kernel(where_ref, recv_ref, mx_ref, own_ref, near_ref, next_ref, out_ref, buf):
    even_x = even(where_ref[0])
    start = 10 * where_ref[0]
    halves = [mx_ref[h, pl.ds(start, 16), :] for h in range(2)]
    lane = lax.broadcasted_iota(jnp.int32, (16, 128), 1) % 8
    rows = [jnp.concatenate(halves, axis=1)]
    for x in range(5):
        at = 5 if x < 4 else 6
        moved = [jnp.where(lane == at, pltpu.roll(h, at - x, 1), 0.0) for h in halves]
        rows.append(jnp.concatenate(moved, axis=1))
    coarse = recv_ref[...].reshape(8 * recv_ref.shape[0], 128)
    value = jnp.dot(
        jnp.concatenate(rows, axis=0), coarse, precision=HIGHEST, preferred_element_type=f32
    )
    last = value[80:96, 0:32]
    for x in range(4):
        last = last + value[16 * x + 16 : 16 * x + 32, 32 * x : 32 * x + 32]
    part = jnp.concatenate([value[0:16], last, jnp.zeros((16, 96), f32)], axis=1)
    for n in range(5):
        near, other = near_ref[n].astype(f32), next_ref[n].astype(f32)
        buf[34 * n : 34 * n + 9, :] = jnp.where(even_x, other, near)
        buf[34 * n + 9 : 34 * n + 25, :] = own_ref[n].astype(f32)
        buf[34 * n + 25 : 34 * n + 34, :] = jnp.where(even_x, near, other)
    buf[170:176, :] = jnp.zeros((6, 128), f32)
    high = part.astype(bf16)
    low = (part - high.astype(f32)).astype(bf16)
    cells = buf[...].astype(bf16)
    for k in range(out_ref.shape[0]):
        out_ref[k, 0:176, :] = cells
        out_ref[k, 176:192, :] = high[:, 0:128]
        out_ref[k, 192:208, :] = high[:, 128:256]
        out_ref[k, 208:224, :] = low[:, 0:128]
        out_ref[k, 224:240, :] = low[:, 128:256]


def final_kernel(
    where_ref, recv_ref, my_ref, mz_ref, near_ref, far_ref, fine_ref, out_ref,
    cells, w0, w1, acc, moved, wide, line,
):
    index_x = where_ref[0]
    index_y = where_ref[1]
    count = recv_ref.shape[0]
    cells[:, 32:40, :] = jnp.zeros((17, 8, 128), f32)
    for step in range(-2, 3):
        source = index_y + step
        inside = (source >= 0) & (source < count)
        got = recv_ref[jnp.clip(source, 0, count - 1), 0:176, :].astype(f32)
        line[...] = jnp.where(inside, got, 0.0)
        for p in range(5):
            n = 5 * step + 6 + p
            if 0 <= n < 17:
                cells[n, 0:34, :] = line[34 * p : 34 * p + 34, :]

    r, c = iota2((128, 128))
    mask = jnp.abs(r % 64 - c % 64) <= REACH

    def band_rows(w, a, at):
        base = TAPS * TAPS + a * TAPS
        for j in range(11):
            same = near_ref[pl.ds(base + 2 * j, 1), :]
            upper = same
            lower = same
            if j > 0:
                upper = same + far_ref[pl.ds(base + 2 * j - 1, 1), :]
            if j < 10:
                lower = same + far_ref[pl.ds(base + 2 * j + 1, 1), :]
            upper = pltpu.roll(jnp.broadcast_to(upper, (64, 128)), 0, 1, stride=1, stride_axis=0)
            lower = pltpu.roll(jnp.broadcast_to(lower, (64, 128)), 64, 1, stride=1, stride_axis=0)
            band = jnp.where(mask, jnp.concatenate([upper, lower], axis=0), 0.0).astype(bf16)
            w[at + 128 * j : at + 128 * j + 128, :] = band

    def build(w, a):
        for k in range(3):
            band_rows(w, a + k, 1408 * k)

    def dot(w, a):
        rows = []
        for k in range(3):
            part = [cells[n, pl.ds(a + k + 1, 16), :].astype(bf16) for n in range(17)]
            rows.append([jnp.concatenate(part[g : g + 11], axis=1) for g in range(7)])
        lhs = jnp.concatenate(
            [jnp.concatenate([rows[k][g] for k in range(3)], axis=1) for g in range(7)], axis=0
        )
        acc[...] += jnp.dot(lhs, w[...], preferred_element_type=f32)

    acc[...] = jnp.zeros((112, 128), f32)
    build(w0, 0)

    def step(t, _):
        a = 6 * t
        build(w1, a + 3)
        dot(w0, a)
        build(w0, a + 6)
        dot(w1, a + 3)
        return 0

    lax.fori_loop(0, 3, step, 0)
    dot(w0, 18)

    start = 10 * index_y
    sums = [[None] * 14, [None] * 14]
    for k in range(count):
        high = [recv_ref[k, 176 + 16 * h : 192 + 16 * h, :].astype(f32) for h in range(2)]
        low = [recv_ref[k, 208 + 16 * h : 224 + 16 * h, :].astype(f32) for h in range(2)]
        for h in range(2):
            value = high[h] + low[h]
            rows_y = my_ref[2 * k + h, pl.ds(start, 16), :]
            for y in range(14):
                term = value * rows_y[y : y + 1, :]
                sums[h][y] = term if k == 0 else sums[h][y] + term
    rows = [
        jnp.concatenate([sums[h][2 * n + p] for p in range(2) for h in range(2)], axis=1)
        for n in range(7)
    ]
    top = jnp.dot(
        jnp.concatenate(rows, axis=0), mz_ref[...], precision=HIGHEST, preferred_element_type=f32
    )
    total = acc[...] + top
    r, c = iota2((112, 128))
    cell_x = 10 * index_x - 1 + r % 16
    cell_y = 10 * index_y - 2 + 2 * (r // 16) + c // 64
    inside = (cell_x >= 0) & (cell_x < 320) & (cell_y >= 0) & (cell_y < 80)
    total = jnp.where(inside, total, 0.0)
    r, c = iota2((128, 256))
    up_z = jnp.where(r // 64 == c // 128, weight(c % 128 - 2 * (r % 64)), 0.0)
    wide[...] = exact_dot(total, up_z)

    def middle_y(y):
        n, par = (y + 2) // 2, y % 2
        return wide[16 * n : 16 * n + 16, 128 * par : 128 * par + 128]

    for y in range(20):
        m = y // 2
        if y % 2 == 0:
            value = middle_y(m)
        else:
            value = 0.5625 * (middle_y(m) + middle_y(m + 1)) - 0.0625 * (
                middle_y(m - 1) + middle_y(m + 2)
            )
        moved[16 * y : 16 * y + 16, :] = value
    planes = [moved[pl.ds(k, 20, stride=16), :] for k in range(13)]
    for x in range(20):
        m = x // 2
        if x % 2 == 0:
            value = planes[m + 1]
        else:
            value = 0.5625 * (planes[m + 1] + planes[m + 2]) - 0.0625 * (planes[m] + planes[m + 3])
        out_ref[x] = value + fine_ref[24 * m : 24 * m + 20, 128 * (x % 2) : 128 * (x % 2) + 128]


def swap(first, second, axis):
    count = lax.axis_size(axis)
    pairs = [(k, k + 1) for k in range(0, count - 1, 2)]
    others = [(k, k + 1) for k in range(1, count - 1, 2)]

    def both(ends):
        return ends + [(b, a) for a, b in ends]

    return lax.ppermute(first, axis, both(pairs)), lax.ppermute(second, axis, both(others))


def per_device(charges, kernels):
    count_x = lax.axis_size("gx")
    count_y = lax.axis_size("gy")
    where = jnp.stack([lax.axis_index("gx"), lax.axis_index("gy")]).astype(jnp.int32)
    spread = charges.shape[0] * count_x / 16.0
    shape = jax.ShapeDtypeStruct
    low, high = charges[:10], charges[10:]
    even_x = even(lax.axis_index("gx"))
    near_x, next_x = swap(jnp.where(even_x, high, low), jnp.where(even_x, low, high), "gx")
    first, second = vmem_call(
        rim_kernel,
        [shape((400, 128), bf16)] * 2,
        [pltpu.VMEM((40, 20, 128), f32), pltpu.VMEM((2, 400, 128), f32)],
        "rim",
        (where, charges, near_x, next_x),
        smem=1,
    )
    first, second, kernels = lax.optimization_barrier((first, second, kernels))
    near, far = (
        jnp.dot(kernels.reshape(-1, TAPS), jnp.asarray(m, bf16), preferred_element_type=f32)
        for m in spots_np()
    )
    near_y, next_y = swap(first, second, "gy")
    near_y, next_y, near, far = lax.optimization_barrier((near_y, next_y, near, far))
    d, first, second, own, coarse = vmem_call(
        restrict_kernel,
        [
            shape((40, 40, 128), bf16),
            shape((5, 9, 128), bf16),
            shape((5, 9, 128), bf16),
            shape((5, 16, 128), bf16),
            shape((count_x, 8, 128), f32),
        ],
        [
            pltpu.VMEM((2, 20, 48, 128), f32),
            pltpu.VMEM((2, 400, 128), f32),
            pltpu.VMEM((16, 48, 128), f32),
            pltpu.VMEM((256, 128), f32),
            pltpu.VMEM((9, 24, 128), f32),
            pltpu.VMEM((8, 128), f32),
        ],
        "restrict",
        (where, charges, near_x, next_x, near_y, next_y),
        smem=1,
    )
    near_m, next_m = swap(first, second, "gx")
    coarse = lax.all_to_all(coarse, "gx", 0, 0)
    parts = vmem_call(
        spread_kernel,
        [shape((count_y, 240, 128), bf16)],
        [pltpu.VMEM((176, 128), f32)],
        "spread",
        (where, coarse, jnp.asarray(matrix_x_np(spread)), own, near_m, next_m),
        smem=1,
    )[0]
    parts, near = lax.optimization_barrier((parts, near))
    parts = lax.all_to_all(parts, "gy", 0, 0)
    fine = fine_sum(0, TAPS, d, near)
    return vmem_call(
        final_kernel,
        [shape((20, 20, 128), f32)],
        [
            pltpu.VMEM((17, 40, 128), f32),
            pltpu.VMEM((4224, 128), bf16),
            pltpu.VMEM((4224, 128), bf16),
            pltpu.VMEM((112, 128), f32),
            pltpu.VMEM((320, 128), f32),
            pltpu.VMEM((112, 256), f32),
            pltpu.VMEM((176, 128), f32),
        ],
        "final",
        (
            where,
            parts,
            jnp.asarray(matrix_y_np(spread)),
            jnp.asarray(matrix_z_np(spread)),
            near,
            far,
            fine,
        ),
        smem=1,
    )[0]


def solution(mesh):
    return jax.shard_map(
        per_device,
        mesh=mesh,
        in_specs=(P("gx", "gy", None), P()),
        out_specs=P("gx", "gy", None),
        check_vma=False,
    )
```

```python
import functools
import numpy as np
import jax
import jax.numpy as jnp
from jax import lax
from jax.experimental import pallas as pl
from jax.experimental.pallas import tpu as pltpu
from jax.sharding import PartitionSpec as P

f32 = jnp.float32
bf16 = jnp.bfloat16
spread_norm = 1.2533141
HIGHEST = lax.Precision.HIGHEST
REACH = 10
TAPS = 21
GROUP = 3
SPLIT = 6


def weight_np(offset):
    d = np.abs(offset)
    return np.where(d == 0, 1.0, np.where(d == 1, 0.5625, np.where(d == 3, -0.0625, 0.0)))


def top_matrix_np(n, spread):
    prolong = weight_np(np.arange(2 * n)[:, None] - 2 * np.arange(n)[None, :])
    offset = (np.arange(n)[:, None] - np.arange(n)[None, :]) / spread
    return prolong @ (np.exp(-offset * offset) / np.sqrt(spread * spread_norm))


def lane_tiles(m):
    return m.reshape(m.shape[0], -1, 128).transpose(1, 0, 2).astype(np.float32)


def matrix_x_np(spread):
    m = top_matrix_np(160, spread).reshape(320, 32, 5)
    out = np.zeros((328, 32, 8))
    out[1:321, :, :5] = m
    return lane_tiles(out.reshape(328, 256))


def matrix_y_np(spread):
    m = top_matrix_np(40, spread).reshape(80, 8, 5)
    out = np.zeros((88, 8, 8))
    out[2:82, :, :5] = m
    return lane_tiles(np.repeat(out.reshape(88, 64), 32, axis=1))


def matrix_z_np(spread):
    m = top_matrix_np(32, spread).T
    out = np.zeros((2, 8, 32, 2, 64))
    for par in range(2):
        out[par, :, :, par, :] = m[None]
    return out.reshape(512, 128).astype(np.float32)


def spots_np():
    taps = np.arange(TAPS)[:, None]
    lanes = np.arange(128)[None, :]
    near = lanes == (REACH - taps) % 128
    far = lanes == (64 + REACH - taps) % 128
    return near, far


def weight(d):
    d = jnp.abs(d)
    return jnp.where(d == 0, 1.0, jnp.where(d == 1, 0.5625, jnp.where(d == 3, -0.0625, 0.0))).astype(f32)


def exact_dot(rows, weights):
    count = rows.shape[0]
    high = rows.astype(bf16)
    rest = rows - high.astype(f32)
    middle = rest.astype(bf16)
    low = (rest - middle.astype(f32)).astype(bf16)
    out = jnp.dot(
        jnp.concatenate([high, middle, low], axis=0),
        weights.astype(bf16),
        preferred_element_type=f32,
    )
    return out[0:count] + (out[count : 2 * count] + out[2 * count :])


def iota2(shape):
    return (lax.broadcasted_iota(jnp.int32, shape, 0), lax.broadcasted_iota(jnp.int32, shape, 1))


def vmem_call(body, out_shape, scratch, name, args, smem=0, flops=0, limit=8):
    def spec(space):
        return pl.BlockSpec(memory_space=space)

    return pl.pallas_call(
        body,
        out_shape=out_shape,
        in_specs=[spec(pltpu.SMEM)] * smem + [spec(pltpu.VMEM)] * (len(args) - smem),
        out_specs=[spec(pltpu.VMEM)] * len(out_shape),
        scratch_shapes=scratch,
        compiler_params=pltpu.CompilerParams(vmem_limit_bytes=limit << 20),
        cost_estimate=pl.CostEstimate(flops=flops, bytes_accessed=1 << 16, transcendentals=0),
        name=name,
    )(*args)


def even(index):
    return index % 2 == 0


def rim_kernel(where_ref, blk_ref, near_ref, next_ref, second_ref, first_ref, wide, dense):
    even_x = even(where_ref[0])
    even_y = even(where_ref[1])
    near, other = near_ref[...].astype(f32), next_ref[...].astype(f32)
    wide[0:10] = jnp.where(even_x, other, near)
    wide[10:30] = blk_ref[...].astype(f32)
    wide[30:40] = jnp.where(even_x, near, other)
    for x in range(40):
        low, high = wide[x, 0:10, :], wide[x, 10:20, :]
        dense[0, 10 * x : 10 * x + 10, :] = jnp.where(even_y, high, low)
        dense[1, 10 * x : 10 * x + 10, :] = jnp.where(even_y, low, high)
    first_ref[...] = dense[0].astype(bf16)
    second_ref[...] = dense[1].astype(bf16)


def restrict_kernel(
    where_ref, blk_ref, near_x_ref, next_x_ref, next_y_ref, near_y_ref,
    d_out_ref, second_ref, first_ref, own_ref, out_ref,
    d_ref, dense, planes, cells, mid, pay,
):
    even_x = even(where_ref[0])
    even_y = even(where_ref[1])
    near, other = near_y_ref[...].astype(f32), next_y_ref[...].astype(f32)
    dense[0] = jnp.where(even_y, other, near)
    dense[1] = jnp.where(even_y, near, other)
    for x in range(40):
        p, i = x % 2, x // 2
        d_ref[p, i, 0:10, :] = dense[0, 10 * x : 10 * x + 10, :]
        d_ref[p, i, 30:40, :] = dense[1, 10 * x : 10 * x + 10, :]
        if 10 <= x < 30:
            centre = blk_ref[x - 10].astype(f32)
        else:
            near, other = near_x_ref[x % 30].astype(f32), next_x_ref[x % 30].astype(f32)
            low, high = (other, near) if x < 10 else (near, other)
            centre = jnp.where(even_x, low, high)
        d_ref[p, i, 10:30, :] = centre
        d_out_ref[x] = d_ref[p, i, 0:40, :].astype(bf16)

    def fine(x):
        return d_ref[x % 2, x // 2]

    for i in range(16):
        c = 2 * i + 4
        planes[i] = (
            fine(c) + 0.5625 * (fine(c - 1) + fine(c + 1)) - 0.0625 * (fine(c - 3) + fine(c + 3))
        )
    for i in range(16):
        def tap(o):
            return planes[i, pl.ds(4 + o, 16, stride=2), :]
        cells[16 * i : 16 * i + 16, :] = (
            tap(0) + 0.5625 * (tap(-1) + tap(1)) - 0.0625 * (tap(-3) + tap(3))
        )
    zero = jnp.zeros((16, 128), f32)
    rows = []
    for n in range(9):
        pair = []
        for y in (2 * n - 4, 2 * n - 3):
            inside = -3 <= y <= 12
            pair.append(cells[pl.ds(y + 3, 16, stride=16), :] if inside else zero)
        rows.append(jnp.concatenate(pair, axis=1))
    r, c = iota2((256, 128))
    down_z = jnp.where(r // 128 == c // 64, weight(r % 128 - 2 * (c % 64)), 0.0)
    value = exact_dot(jnp.concatenate(rows, axis=0), down_z)
    r, c = iota2((144, 128))
    cell_x = 10 * where_ref[0] - 3 + r % 16
    cell_y = 10 * where_ref[1] - 4 + 2 * (r // 16) + c // 64
    inside = (cell_x >= 0) & (cell_x < 320) & (cell_y >= 0) & (cell_y < 80)
    value = jnp.where(inside, value, 0.0).astype(bf16).astype(f32)
    for n in range(9):
        mid[n, 0:16, :] = value[16 * n : 16 * n + 16]
        mid[n, 16:24, :] = jnp.zeros((8, 128), f32)
    for n in range(5):
        right, left = mid[n + 2, 1:10, :], mid[n + 2, 6:15, :]
        first_ref[n] = jnp.where(even_x, right, left).astype(bf16)
        second_ref[n] = jnp.where(even_x, left, right).astype(bf16)
        own_ref[n] = mid[n + 2, 0:16, :].astype(bf16)

    lane = lax.broadcasted_iota(jnp.int32, (1, 128), 1)
    odd = lane >= 64
    weight_0 = jnp.where(odd, 0.5625, 1.0)
    weight_1 = jnp.where(odd, 0.5625, 0.0)
    weight_3 = jnp.where(odd, -0.0625, 0.0)
    r, c = iota2((128, 32))
    down_z = weight(r % 64 - 2 * c)
    sums = []
    for y in range(5):
        n = y + 2
        def tap(o):
            def part(k):
                return mid[k, pl.ds(3 + o, 8, stride=2), :]
            return (
                weight_0 * part(n) + weight_1 * part(n - 1) + weight_3 * (part(n - 2) + part(n + 1))
            )
        sums.append(tap(0) + 0.5625 * (tap(-1) + tap(1)) - 0.0625 * (tap(-3) + tap(3)))
    out = exact_dot(jnp.concatenate(sums, axis=0), down_z)
    pay[...] = jnp.concatenate([out[8 * y : 8 * y + 8] for y in range(4)], axis=1)
    pay[5:6, :] = jnp.concatenate([out[32 + x : 33 + x] for x in range(4)], axis=1)
    pay[6:8, :] = jnp.zeros((2, 128), f32)
    pay[6:7, 0:32] = out[36:37]
    row = pay[...]
    for k in range(out_ref.shape[0]):
        out_ref[k] = row


def fine_kernel(lo, hi, first, d_in_ref, v_ref, *refs):
    if first:
        out_ref, w0, w1, e0, e1, d_ref = refs
    else:
        acc_ref, out_ref, w0, w1, e0, e1, d_ref = refs
    for x in range(40):
        d_ref[x % 2, x // 2, 0:40, :] = d_in_ref[x].astype(f32)
        d_ref[x % 2, x // 2, 40:48, :] = jnp.zeros((8, 128), f32)
    r, c = iota2((128, 128))
    mask = jnp.abs(r - c) <= REACH
    zero = jnp.zeros((128, 128), bf16)
    for w in (w0, w1):
        for k in range(GROUP):
            w[2816 * k : 2816 * k + 128, 128:256] = zero
            w[2816 * k + 2688 : 2816 * k + 2816, 0:128] = zero

    def build(w, start):
        for k in range(GROUP):
            for a in range(TAPS):
                line = jnp.broadcast_to(v_ref[pl.ds(a * TAPS + start + k, 1), :], (128, 128))
                line = pltpu.roll(line, 0, 1, stride=1, stride_axis=0)
                band = jnp.where(mask, line, 0.0).astype(bf16)
                at = 2816 * k + 128 * a
                w[at : at + 128, 0:128] = band
                w[at + 128 : at + 256, 128:256] = band

    def dot(w, e, start):
        tiles = []
        for k in range(GROUP):
            for p in range(2):
                for q in range(10):
                    part = d_ref[p, 2 * q : 2 * q + 2, pl.ds(start + k, 24), :].reshape(48, 128)
                    e[k, 0, 48 * q : 48 * q + 48, p * 128 : (p + 1) * 128] = part.astype(bf16)
                for q in range(9):
                    part = d_ref[p, 2 * q + 1 : 2 * q + 3, pl.ds(start + k, 24), :].reshape(48, 128)
                    e[k, 1, 48 * q : 48 * q + 48, p * 128 : (p + 1) * 128] = part.astype(bf16)
            tiles += [
                e[k, m % 2, 24 * (m - m % 2) : 24 * (m - m % 2) + 240, :] for m in range(11)
            ]
        lhs = jnp.concatenate(tiles, axis=1)
        out_ref[...] += jnp.dot(lhs, w[...], preferred_element_type=f32)

    build(w0, lo)
    out_ref[...] = jnp.zeros((240, 256), f32) if first else acc_ref[...]

    def step(t, _):
        b = lo + 2 * GROUP * t
        build(w1, b + GROUP)
        dot(w0, e0, b)
        build(w0, jnp.minimum(b + 2 * GROUP, TAPS - GROUP))
        dot(w1, e1, b + GROUP)
        return 0

    groups = (hi - lo) // GROUP
    lax.fori_loop(0, groups // 2, step, 0)
    if groups % 2:
        dot(w0, e0, hi - GROUP)


def fine_sum(lo, hi, d, v, acc=None):
    return vmem_call(
        functools.partial(fine_kernel, lo, hi, acc is None),
        [jax.ShapeDtypeStruct((240, 256), f32)],
        [pltpu.VMEM((GROUP * 2816, 256), bf16)] * 2
        + [pltpu.VMEM((GROUP, 2, 480, 256), bf16)] * 2
        + [pltpu.VMEM((2, 20, 48, 128), f32)],
        "fine_sum",
        (d, v) if acc is None else (d, v, acc),
        flops=(hi - lo) * 2 * 240 * 2816 * 256,
        limit=20,
    )[0]


def spread_kernel(where_ref, recv_ref, mx_ref, own_ref, next_ref, near_ref, out_ref, buf):
    even_x = even(where_ref[0])
    start = 10 * where_ref[0]
    halves = [mx_ref[h, pl.ds(start, 16), :] for h in range(2)]
    lane = lax.broadcasted_iota(jnp.int32, (16, 128), 1) % 8
    rows = [jnp.concatenate(halves, axis=1)]
    for x in range(5):
        at = 5 if x < 4 else 6
        moved = [jnp.where(lane == at, pltpu.roll(h, at - x, 1), 0.0) for h in halves]
        rows.append(jnp.concatenate(moved, axis=1))
    coarse = recv_ref[...].reshape(8 * recv_ref.shape[0], 128)
    value = jnp.dot(
        jnp.concatenate(rows, axis=0), coarse, precision=HIGHEST, preferred_element_type=f32
    )
    last = value[80:96, 0:32]
    for x in range(4):
        last = last + value[16 * x + 16 : 16 * x + 32, 32 * x : 32 * x + 32]
    part = jnp.concatenate([value[0:16], last, jnp.zeros((16, 96), f32)], axis=1)
    for n in range(5):
        near, other = near_ref[n].astype(f32), next_ref[n].astype(f32)
        buf[34 * n : 34 * n + 9, :] = jnp.where(even_x, other, near)
        buf[34 * n + 9 : 34 * n + 25, :] = own_ref[n].astype(f32)
        buf[34 * n + 25 : 34 * n + 34, :] = jnp.where(even_x, near, other)
    buf[170:176, :] = jnp.zeros((6, 128), f32)
    high = part.astype(bf16)
    low = (part - high.astype(f32)).astype(bf16)
    cells = buf[...].astype(bf16)
    for k in range(out_ref.shape[0]):
        out_ref[k, 0:176, :] = cells
        out_ref[k, 176:192, :] = high[:, 0:128]
        out_ref[k, 192:208, :] = high[:, 128:256]
        out_ref[k, 208:224, :] = low[:, 0:128]
        out_ref[k, 224:240, :] = low[:, 128:256]


def final_kernel(
    where_ref, recv_ref, my_ref, mz_ref, near_ref, far_ref, fine_ref, out_ref,
    cells, w0, w1, acc, moved, wide, line,
):
    index_x = where_ref[0]
    index_y = where_ref[1]
    count = recv_ref.shape[0]
    cells[:, 32:40, :] = jnp.zeros((17, 8, 128), f32)
    for step in range(-2, 3):
        source = index_y + step
        inside = (source >= 0) & (source < count)
        got = recv_ref[jnp.clip(source, 0, count - 1), 0:176, :].astype(f32)
        line[...] = jnp.where(inside, got, 0.0)
        for p in range(5):
            n = 5 * step + 6 + p
            if 0 <= n < 17:
                cells[n, 0:34, :] = line[34 * p : 34 * p + 34, :]

    r, c = iota2((128, 128))
    mask = jnp.abs(r % 64 - c % 64) <= REACH

    def band_rows(w, a, at):
        base = TAPS * TAPS + a * TAPS
        for j in range(11):
            same = near_ref[pl.ds(base + 2 * j, 1), :]
            upper = same
            lower = same
            if j > 0:
                upper = same + far_ref[pl.ds(base + 2 * j - 1, 1), :]
            if j < 10:
                lower = same + far_ref[pl.ds(base + 2 * j + 1, 1), :]
            upper = pltpu.roll(jnp.broadcast_to(upper, (64, 128)), 0, 1, stride=1, stride_axis=0)
            lower = pltpu.roll(jnp.broadcast_to(lower, (64, 128)), 64, 1, stride=1, stride_axis=0)
            band = jnp.where(mask, jnp.concatenate([upper, lower], axis=0), 0.0).astype(bf16)
            w[at + 128 * j : at + 128 * j + 128, :] = band

    def build(w, a):
        for k in range(3):
            band_rows(w, a + k, 1408 * k)

    def dot(w, a):
        rows = []
        for k in range(3):
            part = [cells[n, pl.ds(a + k + 1, 16), :].astype(bf16) for n in range(17)]
            rows.append([jnp.concatenate(part[g : g + 11], axis=1) for g in range(7)])
        lhs = jnp.concatenate(
            [jnp.concatenate([rows[k][g] for k in range(3)], axis=1) for g in range(7)], axis=0
        )
        acc[...] += jnp.dot(lhs, w[...], preferred_element_type=f32)

    acc[...] = jnp.zeros((112, 128), f32)
    build(w0, 0)

    def step(t, _):
        a = 6 * t
        build(w1, a + 3)
        dot(w0, a)
        build(w0, a + 6)
        dot(w1, a + 3)
        return 0

    lax.fori_loop(0, 3, step, 0)
    dot(w0, 18)

    start = 10 * index_y
    sums = [[None] * 14, [None] * 14]
    for k in range(count):
        high = [recv_ref[k, 176 + 16 * h : 192 + 16 * h, :].astype(f32) for h in range(2)]
        low = [recv_ref[k, 208 + 16 * h : 224 + 16 * h, :].astype(f32) for h in range(2)]
        for h in range(2):
            value = high[h] + low[h]
            rows_y = my_ref[2 * k + h, pl.ds(start, 16), :]
            for y in range(14):
                term = value * rows_y[y : y + 1, :]
                sums[h][y] = term if k == 0 else sums[h][y] + term
    rows = [
        jnp.concatenate([sums[h][2 * n + p] for p in range(2) for h in range(2)], axis=1)
        for n in range(7)
    ]
    top = jnp.dot(
        jnp.concatenate(rows, axis=0), mz_ref[...], precision=HIGHEST, preferred_element_type=f32
    )
    total = acc[...] + top
    r, c = iota2((112, 128))
    cell_x = 10 * index_x - 1 + r % 16
    cell_y = 10 * index_y - 2 + 2 * (r // 16) + c // 64
    inside = (cell_x >= 0) & (cell_x < 320) & (cell_y >= 0) & (cell_y < 80)
    total = jnp.where(inside, total, 0.0)
    r, c = iota2((128, 256))
    up_z = jnp.where(r // 64 == c // 128, weight(c % 128 - 2 * (r % 64)), 0.0)
    wide[...] = exact_dot(total, up_z)

    def middle_y(y):
        n, par = (y + 2) // 2, y % 2
        return wide[16 * n : 16 * n + 16, 128 * par : 128 * par + 128]

    for y in range(20):
        m = y // 2
        if y % 2 == 0:
            value = middle_y(m)
        else:
            value = 0.5625 * (middle_y(m) + middle_y(m + 1)) - 0.0625 * (
                middle_y(m - 1) + middle_y(m + 2)
            )
        moved[16 * y : 16 * y + 16, :] = value
    planes = [moved[pl.ds(k, 20, stride=16), :] for k in range(13)]
    for x in range(20):
        m = x // 2
        if x % 2 == 0:
            value = planes[m + 1]
        else:
            value = 0.5625 * (planes[m + 1] + planes[m + 2]) - 0.0625 * (planes[m] + planes[m + 3])
        out_ref[x] = value + fine_ref[24 * m : 24 * m + 20, 128 * (x % 2) : 128 * (x % 2) + 128]


def swap(first, second, axis):
    count = lax.axis_size(axis)
    pairs = [(k, k + 1) for k in range(0, count - 1, 2)]
    others = [(k, k + 1) for k in range(1, count - 1, 2)]

    def both(ends):
        return ends + [(b, a) for a, b in ends]

    second = lax.ppermute(second, axis, both(others))
    return lax.ppermute(first, axis, both(pairs)), second


def per_device(charges, kernels):
    count_x = lax.axis_size("gx")
    count_y = lax.axis_size("gy")
    where = jnp.stack([lax.axis_index("gx"), lax.axis_index("gy")]).astype(jnp.int32)
    spread = charges.shape[0] * count_x / 16.0
    shape = jax.ShapeDtypeStruct
    low, high = charges[:10], charges[10:]
    even_x = even(lax.axis_index("gx"))
    near_x, next_x = swap(jnp.where(even_x, high, low), jnp.where(even_x, low, high), "gx")
    second, first = vmem_call(
        rim_kernel,
        [shape((400, 128), bf16)] * 2,
        [pltpu.VMEM((40, 20, 128), f32), pltpu.VMEM((2, 400, 128), f32)],
        "rim",
        (where, charges, near_x, next_x),
        smem=1,
    )
    first, second, kernels = lax.optimization_barrier((first, second, kernels))
    near, far = (
        jnp.dot(kernels.reshape(-1, TAPS), jnp.asarray(m, bf16), preferred_element_type=f32)
        for m in spots_np()
    )
    near_y, next_y = swap(first, second, "gy")
    next_y, near_y, near, far = lax.optimization_barrier((next_y, near_y, near, far))
    d, second, first, own, coarse = vmem_call(
        restrict_kernel,
        [
            shape((40, 40, 128), bf16),
            shape((5, 9, 128), bf16),
            shape((5, 9, 128), bf16),
            shape((5, 16, 128), bf16),
            shape((count_x, 8, 128), f32),
        ],
        [
            pltpu.VMEM((2, 20, 48, 128), f32),
            pltpu.VMEM((2, 400, 128), f32),
            pltpu.VMEM((16, 48, 128), f32),
            pltpu.VMEM((256, 128), f32),
            pltpu.VMEM((9, 24, 128), f32),
            pltpu.VMEM((8, 128), f32),
        ],
        "restrict",
        (where, charges, near_x, next_x, next_y, near_y),
        smem=1,
    )
    near_m, next_m = swap(first, second, "gx")
    coarse = lax.all_to_all(coarse, "gx", 0, 0)
    near, near_m = lax.optimization_barrier((near, near_m))
    fine = fine_sum(0, SPLIT, d, near)
    coarse, fine = lax.optimization_barrier((coarse, fine))
    parts = vmem_call(
        spread_kernel,
        [shape((count_y, 240, 128), bf16)],
        [pltpu.VMEM((176, 128), f32)],
        "spread",
        (where, coarse, jnp.asarray(matrix_x_np(spread)), own, next_m, near_m),
        smem=1,
    )[0]
    parts, near = lax.optimization_barrier((parts, near))
    parts = lax.all_to_all(parts, "gy", 0, 0)
    fine = fine_sum(SPLIT, TAPS, d, near, fine)
    return vmem_call(
        final_kernel,
        [shape((20, 20, 128), f32)],
        [
            pltpu.VMEM((17, 40, 128), f32),
            pltpu.VMEM((4224, 128), bf16),
            pltpu.VMEM((4224, 128), bf16),
            pltpu.VMEM((112, 128), f32),
            pltpu.VMEM((320, 128), f32),
            pltpu.VMEM((112, 256), f32),
            pltpu.VMEM((176, 128), f32),
        ],
        "final",
        (
            where,
            parts,
            jnp.asarray(matrix_y_np(spread)),
            jnp.asarray(matrix_z_np(spread)),
            near,
            far,
            fine,
        ),
        smem=1,
    )[0]


def solution(mesh):
    return jax.shard_map(
        per_device,
        mesh=mesh,
        in_specs=(P("gx", "gy", None), P()),
        out_specs=P("gx", "gy", None),
        check_vma=False,
    )
```

```python
import functools
import numpy as np
import jax
import jax.numpy as jnp
from jax import lax
from jax.experimental import pallas as pl
from jax.experimental.pallas import tpu as pltpu
from jax.sharding import PartitionSpec as P

f32 = jnp.float32
bf16 = jnp.bfloat16
spread_norm = 1.2533141
HIGHEST = lax.Precision.HIGHEST
REACH = 10
TAPS = 21
GROUP = 3
SPLIT = 6


def weight_np(offset):
    d = np.abs(offset)
    return np.where(d == 0, 1.0, np.where(d == 1, 0.5625, np.where(d == 3, -0.0625, 0.0)))


def top_matrix_np(n, spread):
    prolong = weight_np(np.arange(2 * n)[:, None] - 2 * np.arange(n)[None, :])
    offset = (np.arange(n)[:, None] - np.arange(n)[None, :]) / spread
    return prolong @ (np.exp(-offset * offset) / np.sqrt(spread * spread_norm))


def lane_tiles(m):
    return m.reshape(m.shape[0], -1, 128).transpose(1, 0, 2).astype(np.float32)


def matrix_x_np(spread):
    m = top_matrix_np(160, spread).reshape(320, 32, 5)
    out = np.zeros((328, 32, 8))
    out[1:321, :, :5] = m
    return lane_tiles(out.reshape(328, 256))


def matrix_y_np(spread):
    m = top_matrix_np(40, spread).reshape(80, 8, 5)
    out = np.zeros((88, 8, 8))
    out[2:82, :, :5] = m
    return lane_tiles(np.repeat(out.reshape(88, 64), 32, axis=1))


def matrix_z_np(spread):
    m = top_matrix_np(32, spread).T
    out = np.zeros((2, 8, 32, 2, 64))
    for par in range(2):
        out[par, :, :, par, :] = m[None]
    return out.reshape(512, 128).astype(np.float32)


def spots_np():
    taps = np.arange(TAPS)[:, None]
    lanes = np.arange(128)[None, :]
    near = lanes == (REACH - taps) % 128
    far = lanes == (64 + REACH - taps) % 128
    return near, far


def weight(d):
    d = jnp.abs(d)
    return jnp.where(d == 0, 1.0, jnp.where(d == 1, 0.5625, jnp.where(d == 3, -0.0625, 0.0))).astype(f32)


def exact_dot(rows, weights):
    count = rows.shape[0]
    high = rows.astype(bf16)
    rest = rows - high.astype(f32)
    middle = rest.astype(bf16)
    low = (rest - middle.astype(f32)).astype(bf16)
    out = jnp.dot(
        jnp.concatenate([high, middle, low], axis=0),
        weights.astype(bf16),
        preferred_element_type=f32,
    )
    return out[0:count] + (out[count : 2 * count] + out[2 * count :])


def iota2(shape):
    return (lax.broadcasted_iota(jnp.int32, shape, 0), lax.broadcasted_iota(jnp.int32, shape, 1))


def vmem_call(body, out_shape, scratch, name, args, smem=0, flops=0, limit=8):
    def spec(space):
        return pl.BlockSpec(memory_space=space)

    return pl.pallas_call(
        body,
        out_shape=out_shape,
        in_specs=[spec(pltpu.SMEM)] * smem + [spec(pltpu.VMEM)] * (len(args) - smem),
        out_specs=[spec(pltpu.VMEM)] * len(out_shape),
        scratch_shapes=scratch,
        compiler_params=pltpu.CompilerParams(vmem_limit_bytes=limit << 20),
        cost_estimate=pl.CostEstimate(flops=flops, bytes_accessed=1 << 16, transcendentals=0),
        name=name,
    )(*args)


def even(index):
    return index % 2 == 0


def rim_kernel(where_ref, blk_ref, near_ref, next_ref, second_ref, first_ref, wide, dense):
    even_x = even(where_ref[0])
    even_y = even(where_ref[1])
    near, other = near_ref[...].astype(f32), next_ref[...].astype(f32)
    wide[0:10] = jnp.where(even_x, other, near)
    wide[10:30] = blk_ref[...].astype(f32)
    wide[30:40] = jnp.where(even_x, near, other)
    for x in range(40):
        low, high = wide[x, 0:10, :], wide[x, 10:20, :]
        dense[0, 10 * x : 10 * x + 10, :] = jnp.where(even_y, high, low)
        dense[1, 10 * x : 10 * x + 10, :] = jnp.where(even_y, low, high)
    first_ref[...] = dense[0].astype(bf16)
    second_ref[...] = dense[1].astype(bf16)


def restrict_kernel(
    where_ref, blk_ref, near_x_ref, next_x_ref, next_y_ref, near_y_ref,
    d_out_ref, second_ref, first_ref, own_ref, out_ref,
    d_ref, dense, planes, cells, mid,
):
    even_x = even(where_ref[0])
    even_y = even(where_ref[1])
    near, other = near_y_ref[...].astype(f32), next_y_ref[...].astype(f32)
    dense[0] = jnp.where(even_y, other, near)
    dense[1] = jnp.where(even_y, near, other)
    for x in range(40):
        p, i = x % 2, x // 2
        d_ref[p, i, 0:10, :] = dense[0, 10 * x : 10 * x + 10, :]
        d_ref[p, i, 30:40, :] = dense[1, 10 * x : 10 * x + 10, :]
        if 10 <= x < 30:
            centre = blk_ref[x - 10].astype(f32)
        else:
            near, other = near_x_ref[x % 30].astype(f32), next_x_ref[x % 30].astype(f32)
            low, high = (other, near) if x < 10 else (near, other)
            centre = jnp.where(even_x, low, high)
        d_ref[p, i, 10:30, :] = centre
        d_out_ref[x] = d_ref[p, i, 0:40, :].astype(bf16)

    def fine(x):
        return d_ref[x % 2, x // 2]

    for i in range(16):
        c = 2 * i + 4
        planes[i] = (
            fine(c) + 0.5625 * (fine(c - 1) + fine(c + 1)) - 0.0625 * (fine(c - 3) + fine(c + 3))
        )
    for i in range(16):
        def tap(o):
            return planes[i, pl.ds(4 + o, 16, stride=2), :]
        cells[16 * i : 16 * i + 16, :] = (
            tap(0) + 0.5625 * (tap(-1) + tap(1)) - 0.0625 * (tap(-3) + tap(3))
        )
    zero = jnp.zeros((16, 128), f32)
    rows = []
    for n in range(9):
        pair = []
        for y in (2 * n - 4, 2 * n - 3):
            inside = -3 <= y <= 12
            pair.append(cells[pl.ds(y + 3, 16, stride=16), :] if inside else zero)
        rows.append(jnp.concatenate(pair, axis=1))
    r, c = iota2((256, 128))
    down_z = jnp.where(r // 128 == c // 64, weight(r % 128 - 2 * (c % 64)), 0.0)
    value = exact_dot(jnp.concatenate(rows, axis=0), down_z)
    r, c = iota2((144, 128))
    cell_x = 10 * where_ref[0] - 3 + r % 16
    cell_y = 10 * where_ref[1] - 4 + 2 * (r // 16) + c // 64
    inside = (cell_x >= 0) & (cell_x < 320) & (cell_y >= 0) & (cell_y < 80)
    value = jnp.where(inside, value, 0.0).astype(bf16).astype(f32)
    for n in range(9):
        mid[n, 0:16, :] = value[16 * n : 16 * n + 16]
        mid[n, 16:24, :] = jnp.zeros((8, 128), f32)
    for n in range(5):
        right, left = mid[n + 2, 1:10, :], mid[n + 2, 6:15, :]
        first_ref[n] = jnp.where(even_x, right, left).astype(bf16)
        second_ref[n] = jnp.where(even_x, left, right).astype(bf16)
        own_ref[n] = mid[n + 2, 0:16, :].astype(bf16)

    lane = lax.broadcasted_iota(jnp.int32, (1, 128), 1)
    odd = lane >= 64
    weight_0 = jnp.where(odd, 0.5625, 1.0)
    weight_1 = jnp.where(odd, 0.5625, 0.0)
    weight_3 = jnp.where(odd, -0.0625, 0.0)
    r, c = iota2((128, 32))
    down_z = weight(r % 64 - 2 * c)
    sums = []
    for y in range(5):
        n = y + 2
        def tap(o):
            def part(k):
                return mid[k, pl.ds(3 + o, 8, stride=2), :]
            return (
                weight_0 * part(n) + weight_1 * part(n - 1) + weight_3 * (part(n - 2) + part(n + 1))
            )
        sums.append(tap(0) + 0.5625 * (tap(-1) + tap(1)) - 0.0625 * (tap(-3) + tap(3)))
    out = exact_dot(jnp.concatenate(sums, axis=0), down_z)
    out_ref[...] = jnp.concatenate([out[8 * y : 8 * y + 8] for y in range(4)], axis=1)
    out_ref[5:6, :] = jnp.concatenate([out[32 + x : 33 + x] for x in range(4)], axis=1)
    out_ref[6:8, :] = jnp.zeros((2, 128), f32)
    out_ref[6:7, 0:32] = out[36:37]


def fine_kernel(lo, hi, first, d_in_ref, v_ref, *refs):
    if first:
        out_ref, w0, w1, e0, e1, d_ref = refs
    else:
        acc_ref, out_ref, w0, w1, e0, e1, d_ref = refs
    for x in range(40):
        d_ref[x % 2, x // 2, 0:40, :] = d_in_ref[x].astype(f32)
        d_ref[x % 2, x // 2, 40:48, :] = jnp.zeros((8, 128), f32)
    r, c = iota2((128, 128))
    mask = jnp.abs(r - c) <= REACH
    zero = jnp.zeros((128, 128), bf16)
    for w in (w0, w1):
        for k in range(GROUP):
            w[2816 * k : 2816 * k + 128, 128:256] = zero
            w[2816 * k + 2688 : 2816 * k + 2816, 0:128] = zero

    def build(w, start):
        for k in range(GROUP):
            for a in range(TAPS):
                line = jnp.broadcast_to(v_ref[pl.ds(a * TAPS + start + k, 1), :], (128, 128))
                line = pltpu.roll(line, 0, 1, stride=1, stride_axis=0)
                band = jnp.where(mask, line, 0.0).astype(bf16)
                at = 2816 * k + 128 * a
                w[at : at + 128, 0:128] = band
                w[at + 128 : at + 256, 128:256] = band

    def dot(w, e, start):
        tiles = []
        for k in range(GROUP):
            for p in range(2):
                for q in range(10):
                    part = d_ref[p, 2 * q : 2 * q + 2, pl.ds(start + k, 24), :].reshape(48, 128)
                    e[k, 0, 48 * q : 48 * q + 48, p * 128 : (p + 1) * 128] = part.astype(bf16)
                for q in range(9):
                    part = d_ref[p, 2 * q + 1 : 2 * q + 3, pl.ds(start + k, 24), :].reshape(48, 128)
                    e[k, 1, 48 * q : 48 * q + 48, p * 128 : (p + 1) * 128] = part.astype(bf16)
            tiles += [
                e[k, m % 2, 24 * (m - m % 2) : 24 * (m - m % 2) + 240, :] for m in range(11)
            ]
        lhs = jnp.concatenate(tiles, axis=1)
        out_ref[...] += jnp.dot(lhs, w[...], preferred_element_type=f32)

    out_ref[...] = jnp.zeros((240, 256), f32) if first else acc_ref[...]

    def step(t, _):
        b = lo + 2 * GROUP * t
        build(w0, b)
        dot(w0, e0, b)
        build(w1, b + GROUP)
        dot(w1, e1, b + GROUP)
        return 0

    groups = (hi - lo) // GROUP
    lax.fori_loop(0, groups // 2, step, 0)
    if groups % 2:
        build(w0, hi - GROUP)
        dot(w0, e0, hi - GROUP)


def fine_sum(lo, hi, d, v, acc=None):
    return vmem_call(
        functools.partial(fine_kernel, lo, hi, acc is None),
        [jax.ShapeDtypeStruct((240, 256), f32)],
        [pltpu.VMEM((GROUP * 2816, 256), bf16)] * 2
        + [pltpu.VMEM((GROUP, 2, 480, 256), bf16)] * 2
        + [pltpu.VMEM((2, 20, 48, 128), f32)],
        "fine_sum",
        (d, v) if acc is None else (d, v, acc),
        flops=(hi - lo) * 2 * 240 * 2816 * 256,
        limit=20,
    )[0]


def spread_kernel(where_ref, recv_ref, mx_ref, own_ref, next_ref, near_ref, out_ref, buf, tail):
    even_x = even(where_ref[0])
    start = 10 * where_ref[0]
    halves = [mx_ref[h, pl.ds(start, 16), :] for h in range(2)]
    lane = lax.broadcasted_iota(jnp.int32, (16, 128), 1) % 8
    rows = [jnp.concatenate(halves, axis=1)]
    for x in range(5):
        at = 5 if x < 4 else 6
        moved = [jnp.where(lane == at, pltpu.roll(h, at - x, 1), 0.0) for h in halves]
        rows.append(jnp.concatenate(moved, axis=1))
    coarse = recv_ref[...].reshape(8 * recv_ref.shape[0], 128)
    value = jnp.dot(
        jnp.concatenate(rows, axis=0), coarse, precision=HIGHEST, preferred_element_type=f32
    )
    last = value[80:96, 0:32]
    for x in range(4):
        last = last + value[16 * x + 16 : 16 * x + 32, 32 * x : 32 * x + 32]
    tail[...] = jnp.concatenate([last, jnp.zeros((16, 96), f32)], axis=1)
    last = tail[pl.ds(0, 4, stride=4), :]
    for k in range(1, 4):
        last = last + pltpu.roll(tail[pl.ds(k, 4, stride=4), :], 32 * k, 1)
    for n in range(5):
        near, other = near_ref[n].astype(f32), next_ref[n].astype(f32)
        buf[33 * n : 33 * n + 8, :] = jnp.where(even_x, other, near)[1:9]
        buf[33 * n + 8 : 33 * n + 24, :] = own_ref[n].astype(f32)
        buf[33 * n + 24 : 33 * n + 33, :] = jnp.where(even_x, near, other)
    for at, part in ((165, last), (176, value[0:16])):
        rows = part.shape[0]
        high = part.astype(bf16).astype(f32)
        buf[at : at + rows, :] = high
        buf[at + rows : at + 2 * rows, :] = part - high
    buf[173:176, :] = jnp.zeros((3, 128), f32)
    out_ref[...] = buf[...].astype(bf16)


def final_kernel(
    where_ref, recv_ref, my_ref, mz_ref, near_ref, far_ref, fine_ref, out_ref, same_ref,
    cells, w0, w1, acc, moved, wide, line, tail,
):
    index_x = where_ref[0]
    index_y = where_ref[1]
    count = recv_ref.shape[0]
    cells[:, 32:40, :] = jnp.zeros((17, 8, 128), f32)
    for step in range(-2, 3):
        source = index_y + step
        inside = (source >= 0) & (source < count)
        got = recv_ref[jnp.clip(source, 0, count - 1), 0:176, :].astype(f32)
        line[...] = jnp.where(inside, got, 0.0)
        for p in range(5):
            n = 5 * step + 6 + p
            if 0 <= n < 17:
                cells[n, 0:33, :] = line[33 * p : 33 * p + 33, :]

    r, c = iota2((128, 128))
    mask = jnp.abs(r % 64 - c % 64) <= REACH

    def band_rows(w, a, at):
        base = TAPS * TAPS + a * TAPS
        for j in range(11):
            same = near_ref[pl.ds(base + 2 * j, 1), :]
            upper = same
            lower = same
            if j > 0:
                upper = same + far_ref[pl.ds(base + 2 * j - 1, 1), :]
            if j < 10:
                lower = same + far_ref[pl.ds(base + 2 * j + 1, 1), :]
            upper = pltpu.roll(jnp.broadcast_to(upper, (64, 128)), 0, 1, stride=1, stride_axis=0)
            lower = pltpu.roll(jnp.broadcast_to(lower, (64, 128)), 64, 1, stride=1, stride_axis=0)
            band = jnp.where(mask, jnp.concatenate([upper, lower], axis=0), 0.0).astype(bf16)
            w[at + 128 * j : at + 128 * j + 128, :] = band

    def build(w, a):
        for k in range(3):
            band_rows(w, a + k, 1408 * k)

    def dot(w, a):
        rows = []
        for k in range(3):
            part = [cells[n, pl.ds(a + k, 16), :].astype(bf16) for n in range(17)]
            rows.append([jnp.concatenate(part[g : g + 11], axis=1) for g in range(7)])
        lhs = jnp.concatenate(
            [jnp.concatenate([rows[k][g] for k in range(3)], axis=1) for g in range(7)], axis=0
        )
        acc[...] += jnp.dot(lhs, w[...], preferred_element_type=f32)

    acc[...] = jnp.zeros((112, 128), f32)
    build(w0, 0)

    def step(t, _):
        a = 6 * t
        build(w1, a + 3)
        dot(w0, a)
        build(w0, a + 6)
        dot(w1, a + 3)
        return 0

    lax.fori_loop(0, 3, step, 0)
    dot(w0, 18)

    start = 10 * index_y
    sums = [[None] * 14, [None] * 14]
    for k in range(count):
        main = recv_ref[k, 176:192, :].astype(f32) + recv_ref[k, 192:208, :].astype(f32)
        last = recv_ref[k, 160:176, :].astype(f32)
        last = last[5:9] + last[9:13]
        tail[k, pl.ds(0, 4, stride=4), :] = last
        for r in range(1, 4):
            tail[k, pl.ds(r, 4, stride=4), :] = pltpu.roll(last, 128 - 32 * r, 1)
        for h, value in ((0, main), (1, tail[k])):
            rows_y = my_ref[2 * k + h, pl.ds(start, 16), :]
            for y in range(14):
                term = value * rows_y[y : y + 1, :]
                sums[h][y] = term if k == 0 else sums[h][y] + term
    rows = [
        jnp.concatenate([sums[h][2 * n + p] for p in range(2) for h in range(2)], axis=1)
        for n in range(7)
    ]
    top = jnp.dot(
        jnp.concatenate(rows, axis=0), mz_ref[...], precision=HIGHEST, preferred_element_type=f32
    )
    total = acc[...] + top
    r, c = iota2((112, 128))
    cell_x = 10 * index_x - 1 + r % 16
    cell_y = 10 * index_y - 2 + 2 * (r // 16) + c // 64
    inside = (cell_x >= 0) & (cell_x < 320) & (cell_y >= 0) & (cell_y < 80)
    total = jnp.where(inside, total, 0.0)
    r, c = iota2((128, 256))
    up_z = jnp.where(r // 64 == c // 128, weight(c % 128 - 2 * (r % 64)), 0.0)
    wide[...] = exact_dot(total, up_z)

    def middle_y(y):
        n, par = (y + 2) // 2, y % 2
        return wide[16 * n : 16 * n + 16, 128 * par : 128 * par + 128]

    for y in range(20):
        m = y // 2
        if y % 2 == 0:
            value = middle_y(m)
        else:
            value = 0.5625 * (middle_y(m) + middle_y(m + 1)) - 0.0625 * (
                middle_y(m - 1) + middle_y(m + 2)
            )
        moved[16 * y : 16 * y + 16, :] = value
    planes = [moved[pl.ds(k, 20, stride=16), :] for k in range(13)]
    for x in range(20):
        m = x // 2
        if x % 2 == 0:
            value = planes[m + 1]
        else:
            value = 0.5625 * (planes[m + 1] + planes[m + 2]) - 0.0625 * (planes[m] + planes[m + 3])
        out_ref[x] = value
        same_ref[x] = fine_ref[24 * m : 24 * m + 20, 128 * (x % 2) : 128 * (x % 2) + 128]


def swap(first, second, axis):
    count = lax.axis_size(axis)
    pairs = [(k, k + 1) for k in range(0, count - 1, 2)]
    others = [(k, k + 1) for k in range(1, count - 1, 2)]

    def both(ends):
        return ends + [(b, a) for a, b in ends]

    second = lax.ppermute(second, axis, both(others))
    return lax.ppermute(first, axis, both(pairs)), second


def per_device(charges, kernels):
    count_x = lax.axis_size("gx")
    count_y = lax.axis_size("gy")
    where = jnp.stack([lax.axis_index("gx"), lax.axis_index("gy")]).astype(jnp.int32)
    spread = charges.shape[0] * count_x / 16.0
    shape = jax.ShapeDtypeStruct
    low, high = charges[:10], charges[10:]
    even_x = even(lax.axis_index("gx"))
    near_x, next_x = swap(jnp.where(even_x, high, low), jnp.where(even_x, low, high), "gx")
    second, first = vmem_call(
        rim_kernel,
        [shape((400, 128), bf16)] * 2,
        [pltpu.VMEM((40, 20, 128), f32), pltpu.VMEM((2, 400, 128), f32)],
        "rim",
        (where, charges, near_x, next_x),
        smem=1,
    )
    first, second, kernels = lax.optimization_barrier((first, second, kernels))
    near, far = (
        jnp.dot(kernels.reshape(-1, TAPS), jnp.asarray(m, bf16), preferred_element_type=f32)
        for m in spots_np()
    )
    near_y, next_y = swap(first, second, "gy")
    next_y, near_y, near, far = lax.optimization_barrier((next_y, near_y, near, far))
    d, second, first, own, coarse = vmem_call(
        restrict_kernel,
        [
            shape((40, 40, 128), bf16),
            shape((5, 9, 128), bf16),
            shape((5, 9, 128), bf16),
            shape((5, 16, 128), bf16),
            shape((8, 128), f32),
        ],
        [
            pltpu.VMEM((2, 20, 48, 128), f32),
            pltpu.VMEM((2, 400, 128), f32),
            pltpu.VMEM((16, 48, 128), f32),
            pltpu.VMEM((256, 128), f32),
            pltpu.VMEM((9, 24, 128), f32),
        ],
        "restrict",
        (where, charges, near_x, next_x, next_y, near_y),
        smem=1,
    )
    near_m, next_m = swap(first, second, "gx")
    coarse = lax.all_to_all(jnp.broadcast_to(coarse, (count_x, 8, 128)), "gx", 0, 0)
    near, near_m = lax.optimization_barrier((near, near_m))
    fine = fine_sum(0, SPLIT, d, near)
    coarse, fine = lax.optimization_barrier((coarse, fine))
    parts = vmem_call(
        spread_kernel,
        [shape((208, 128), bf16)],
        [pltpu.VMEM((208, 128), f32), pltpu.VMEM((16, 128), f32)],
        "spread",
        (where, coarse, jnp.asarray(matrix_x_np(spread)), own, next_m, near_m),
        smem=1,
    )[0]
    parts, near = lax.optimization_barrier((parts, near))
    parts = lax.all_to_all(jnp.broadcast_to(parts, (count_y, 208, 128)), "gy", 0, 0)
    fine = fine_sum(SPLIT, TAPS, d, near, fine)
    total, fine = vmem_call(
        final_kernel,
        [shape((20, 20, 128), f32)] * 2,
        [
            pltpu.VMEM((17, 40, 128), f32),
            pltpu.VMEM((4224, 128), bf16),
            pltpu.VMEM((4224, 128), bf16),
            pltpu.VMEM((112, 128), f32),
            pltpu.VMEM((320, 128), f32),
            pltpu.VMEM((112, 256), f32),
            pltpu.VMEM((176, 128), f32),
            pltpu.VMEM((count_y, 16, 128), f32),
        ],
        "final",
        (
            where,
            parts,
            jnp.asarray(matrix_y_np(spread)),
            jnp.asarray(matrix_z_np(spread)),
            near,
            far,
            fine,
        ),
        smem=1,
    )
    return total + fine


def solution(mesh):
    return jax.shard_map(
        per_device,
        mesh=mesh,
        in_specs=(P("gx", "gy", None), P()),
        out_specs=P("gx", "gy", None),
        check_vma=False,
    )
```

```python
import functools
import numpy as np
import jax
import jax.numpy as jnp
from jax import lax
from jax.experimental import pallas as pl
from jax.experimental.pallas import tpu as pltpu
from jax.sharding import PartitionSpec as P

f32 = jnp.float32
bf16 = jnp.bfloat16
spread_norm = 1.2533141
HIGHEST = lax.Precision.HIGHEST
REACH = 10
TAPS = 21
GROUP = 3
SPLIT = 9


def weight_np(offset):
    d = np.abs(offset)
    return np.where(d == 0, 1.0, np.where(d == 1, 0.5625, np.where(d == 3, -0.0625, 0.0)))


def top_matrix_np(n, spread):
    prolong = weight_np(np.arange(2 * n)[:, None] - 2 * np.arange(n)[None, :])
    offset = (np.arange(n)[:, None] - np.arange(n)[None, :]) / spread
    return prolong @ (np.exp(-offset * offset) / np.sqrt(spread * spread_norm))


def lane_tiles(m):
    return m.reshape(m.shape[0], -1, 128).transpose(1, 0, 2).astype(np.float32)


def matrix_x_np(spread):
    m = top_matrix_np(160, spread).reshape(320, 32, 5)
    out = np.zeros((328, 32, 8))
    out[1:321, :, :5] = m
    return out.reshape(328, 16, 2, 8).transpose(2, 0, 1, 3).reshape(2, 328, 128).astype(np.float32)


def matrix_y_np(spread):
    m = top_matrix_np(40, spread).reshape(80, 8, 5)
    out = np.zeros((88, 8, 8))
    out[2:82, :, :5] = m
    return lane_tiles(np.repeat(out.reshape(88, 64), 32, axis=1))


def matrix_z_np(spread):
    m = top_matrix_np(32, spread).T
    out = np.zeros((2, 8, 32, 2, 64))
    for par in range(2):
        out[par, :, :, par, :] = m[None]
    return out.reshape(512, 128).astype(np.float32)


def spots_np():
    taps = np.arange(TAPS)[:, None]
    lanes = np.arange(128)[None, :]
    near = lanes == (REACH - taps) % 128
    far = lanes == (64 + REACH - taps) % 128
    return near, far


def weight(d):
    d = jnp.abs(d)
    return jnp.where(d == 0, 1.0, jnp.where(d == 1, 0.5625, jnp.where(d == 3, -0.0625, 0.0))).astype(f32)


def exact_dot(rows, weights):
    count = rows.shape[0]
    high = rows.astype(bf16)
    rest = rows - high.astype(f32)
    middle = rest.astype(bf16)
    low = (rest - middle.astype(f32)).astype(bf16)
    out = jnp.dot(
        jnp.concatenate([high, middle, low], axis=0),
        weights.astype(bf16),
        preferred_element_type=f32,
    )
    return out[0:count] + (out[count : 2 * count] + out[2 * count :])


def iota2(shape):
    return (lax.broadcasted_iota(jnp.int32, shape, 0), lax.broadcasted_iota(jnp.int32, shape, 1))


def vmem_call(body, out_shape, scratch, name, args, smem=0, flops=0, limit=8):
    def spec(space):
        return pl.BlockSpec(memory_space=space)

    return pl.pallas_call(
        body,
        out_shape=out_shape,
        in_specs=[spec(pltpu.SMEM)] * smem + [spec(pltpu.VMEM)] * (len(args) - smem),
        out_specs=[spec(pltpu.VMEM)] * len(out_shape),
        scratch_shapes=scratch,
        compiler_params=pltpu.CompilerParams(vmem_limit_bytes=limit << 20),
        cost_estimate=pl.CostEstimate(flops=flops, bytes_accessed=1 << 16, transcendentals=0),
        name=name,
    )(*args)


def even(index):
    return index % 2 == 0


def rim_kernel(where_ref, blk_ref, near_ref, next_ref, second_ref, first_ref, wide, dense):
    even_x = even(where_ref[0])
    even_y = even(where_ref[1])
    near = jnp.where(even_x, near_ref[0:10].astype(f32), near_ref[10:20].astype(f32))
    other = next_ref[...].astype(f32)
    wide[0:10] = jnp.where(even_x, other, near)
    wide[10:30] = blk_ref[...].astype(f32)
    wide[30:40] = jnp.where(even_x, near, other)
    for x in range(40):
        low, high = wide[x, 0:10, :], wide[x, 10:20, :]
        dense[0, 10 * x : 10 * x + 10, :] = jnp.where(even_y, high, low)
        dense[1, 10 * x : 10 * x + 10, :] = jnp.where(even_y, low, high)
    first_ref[...] = dense[0].astype(bf16)
    second_ref[...] = dense[1].astype(bf16)


def restrict_kernel(
    where_ref, blk_ref, near_x_ref, next_x_ref, next_y_ref, near_y_ref,
    d_out_ref, second_ref, first_ref, own_ref, out_ref,
    d_ref, dense, planes, cells, mid,
):
    even_x = even(where_ref[0])
    even_y = even(where_ref[1])
    near, other = near_y_ref[...].astype(f32), next_y_ref[...].astype(f32)
    dense[0] = jnp.where(even_y, other, near)
    dense[1] = jnp.where(even_y, near, other)
    for x in range(40):
        p, i = x % 2, x // 2
        d_ref[p, i, 0:10, :] = dense[0, 10 * x : 10 * x + 10, :]
        d_ref[p, i, 30:40, :] = dense[1, 10 * x : 10 * x + 10, :]
        if 10 <= x < 30:
            centre = blk_ref[x - 10].astype(f32)
        else:
            other = next_x_ref[x % 30].astype(f32)
            if x < 10:
                centre = jnp.where(even_x, other, near_x_ref[x + 10].astype(f32))
            else:
                centre = jnp.where(even_x, near_x_ref[x - 30].astype(f32), other)
        d_ref[p, i, 10:30, :] = centre
        d_out_ref[x] = d_ref[p, i, 0:40, :].astype(bf16)

    def fine(x):
        return d_ref[x % 2, x // 2]

    for i in range(16):
        c = 2 * i + 4
        planes[i] = (
            fine(c) + 0.5625 * (fine(c - 1) + fine(c + 1)) - 0.0625 * (fine(c - 3) + fine(c + 3))
        )
    for i in range(16):
        def tap(o):
            return planes[i, pl.ds(4 + o, 16, stride=2), :]
        cells[16 * i : 16 * i + 16, :] = (
            tap(0) + 0.5625 * (tap(-1) + tap(1)) - 0.0625 * (tap(-3) + tap(3))
        )
    zero = jnp.zeros((16, 128), f32)
    rows = []
    for n in range(9):
        pair = []
        for y in (2 * n - 4, 2 * n - 3):
            inside = -3 <= y <= 12
            pair.append(cells[pl.ds(y + 3, 16, stride=16), :] if inside else zero)
        rows.append(jnp.concatenate(pair, axis=1))
    r, c = iota2((256, 128))
    down_z = jnp.where(r // 128 == c // 64, weight(r % 128 - 2 * (c % 64)), 0.0)
    value = exact_dot(jnp.concatenate(rows, axis=0), down_z)
    r, c = iota2((144, 128))
    cell_x = 10 * where_ref[0] - 3 + r % 16
    cell_y = 10 * where_ref[1] - 4 + 2 * (r // 16) + c // 64
    inside = (cell_x >= 0) & (cell_x < 320) & (cell_y >= 0) & (cell_y < 80)
    value = jnp.where(inside, value, 0.0).astype(bf16).astype(f32)
    for n in range(9):
        mid[n, 0:16, :] = value[16 * n : 16 * n + 16]
        mid[n, 16:24, :] = jnp.zeros((8, 128), f32)
    for n in range(5):
        right, left = mid[n + 2, 1:10, :], mid[n + 2, 6:15, :]
        first_ref[n] = jnp.where(even_x, right, left).astype(bf16)
        second_ref[n] = jnp.where(even_x, left, right).astype(bf16)
        own_ref[n] = mid[n + 2, 0:16, :].astype(bf16)

    lane = lax.broadcasted_iota(jnp.int32, (1, 128), 1)
    odd = lane >= 64
    weight_0 = jnp.where(odd, 0.5625, 1.0)
    weight_1 = jnp.where(odd, 0.5625, 0.0)
    weight_3 = jnp.where(odd, -0.0625, 0.0)
    r, c = iota2((128, 32))
    down_z = weight(r % 64 - 2 * c)
    sums = []
    for y in range(5):
        n = y + 2
        def tap(o):
            def part(k):
                return mid[k, pl.ds(3 + o, 8, stride=2), :]
            return (
                weight_0 * part(n) + weight_1 * part(n - 1) + weight_3 * (part(n - 2) + part(n + 1))
            )
        sums.append(tap(0) + 0.5625 * (tap(-1) + tap(1)) - 0.0625 * (tap(-3) + tap(3)))
    out = exact_dot(jnp.concatenate(sums, axis=0), down_z)
    out_ref[...] = jnp.concatenate([out[8 * y : 8 * y + 8] for y in range(4)], axis=1)
    out_ref[5:6, :] = jnp.concatenate([out[32 + x : 33 + x] for x in range(4)], axis=1)
    out_ref[6:8, :] = jnp.zeros((2, 128), f32)
    out_ref[6:7, 0:32] = out[36:37]


def fine_kernel(lo, hi, first, d_in_ref, v_ref, *refs):
    if first:
        out_ref, w0, w1, e0, e1, d_ref = refs
    else:
        acc_ref, out_ref, w0, w1, e0, e1, d_ref = refs
    for x in range(40):
        d_ref[x % 2, x // 2, 0:40, :] = d_in_ref[x].astype(f32)
        d_ref[x % 2, x // 2, 40:48, :] = jnp.zeros((8, 128), f32)
    r, c = iota2((128, 128))
    mask = jnp.abs(r - c) <= REACH
    zero = jnp.zeros((128, 128), bf16)
    for w in (w0, w1):
        for k in range(GROUP):
            w[2816 * k : 2816 * k + 128, 128:256] = zero
            w[2816 * k + 2688 : 2816 * k + 2816, 0:128] = zero

    def build(w, start):
        for k in range(GROUP):
            for a in range(TAPS):
                line = jnp.broadcast_to(v_ref[pl.ds(a * TAPS + start + k, 1), :], (128, 128))
                line = pltpu.roll(line, 0, 1, stride=1, stride_axis=0)
                band = jnp.where(mask, line, 0.0).astype(bf16)
                at = 2816 * k + 128 * a
                w[at : at + 128, 0:128] = band
                w[at + 128 : at + 256, 128:256] = band

    def dot(w, e, start):
        tiles = []
        for k in range(GROUP):
            for p in range(2):
                for q in range(10):
                    part = d_ref[p, 2 * q : 2 * q + 2, pl.ds(start + k, 24), :].reshape(48, 128)
                    e[k, 0, 48 * q : 48 * q + 48, p * 128 : (p + 1) * 128] = part.astype(bf16)
                for q in range(9):
                    part = d_ref[p, 2 * q + 1 : 2 * q + 3, pl.ds(start + k, 24), :].reshape(48, 128)
                    e[k, 1, 48 * q : 48 * q + 48, p * 128 : (p + 1) * 128] = part.astype(bf16)
            tiles += [
                e[k, m % 2, 24 * (m - m % 2) : 24 * (m - m % 2) + 240, :] for m in range(11)
            ]
        lhs = jnp.concatenate(tiles, axis=1)
        out_ref[...] += jnp.dot(lhs, w[...], preferred_element_type=f32)

    out_ref[...] = jnp.zeros((240, 256), f32) if first else acc_ref[...]

    def step(t, _):
        b = lo + 2 * GROUP * t
        build(w0, b)
        dot(w0, e0, b)
        build(w1, b + GROUP)
        dot(w1, e1, b + GROUP)
        return 0

    groups = (hi - lo) // GROUP
    lax.fori_loop(0, groups // 2, step, 0)
    if groups % 2:
        build(w0, hi - GROUP)
        dot(w0, e0, hi - GROUP)


def fine_sum(lo, hi, d, v, acc=None):
    return vmem_call(
        functools.partial(fine_kernel, lo, hi, acc is None),
        [jax.ShapeDtypeStruct((240, 256), f32)],
        [pltpu.VMEM((GROUP * 2816, 256), bf16)] * 2
        + [pltpu.VMEM((GROUP, 2, 480, 256), bf16)] * 2
        + [pltpu.VMEM((2, 20, 48, 128), f32)],
        "fine_sum",
        (d, v) if acc is None else (d, v, acc),
        flops=(hi - lo) * 2 * 240 * 2816 * 256,
        limit=20,
    )[0]


def spread_kernel(
    where_ref, recv_ref, other_ref, mx_ref, own_ref, next_ref, near_ref, out_ref, buf, tail
):
    even_x = even(where_ref[0])
    start = 10 * where_ref[0]
    core = where_ref[0] % 2
    halves = [mx_ref[h, pl.ds(start, 16), :] for h in (core, 1 - core)]
    lane = lax.broadcasted_iota(jnp.int32, (16, 128), 1) % 8
    rows = [jnp.concatenate(halves, axis=1)]
    for x in range(5):
        at = 5 if x < 4 else 6
        moved = [jnp.where(lane == at, pltpu.roll(h, at - x, 1), 0.0) for h in halves]
        rows.append(jnp.concatenate(moved, axis=1))
    coarse = jnp.concatenate([recv_ref[...], other_ref[...]], axis=0).reshape(256, 128)
    value = jnp.dot(
        jnp.concatenate(rows, axis=0), coarse, precision=HIGHEST, preferred_element_type=f32
    )
    last = value[80:96, 0:32]
    for x in range(4):
        last = last + value[16 * x + 16 : 16 * x + 32, 32 * x : 32 * x + 32]
    tail[...] = jnp.concatenate([last, jnp.zeros((16, 96), f32)], axis=1)
    last = tail[pl.ds(0, 4, stride=4), :]
    for k in range(1, 4):
        last = last + pltpu.roll(tail[pl.ds(k, 4, stride=4), :], 32 * k, 1)
    for n in range(5):
        near, other = near_ref[n].astype(f32), next_ref[n].astype(f32)
        buf[33 * n : 33 * n + 8, :] = jnp.where(even_x, other, near)[1:9]
        buf[33 * n + 8 : 33 * n + 24, :] = own_ref[n].astype(f32)
        buf[33 * n + 24 : 33 * n + 33, :] = jnp.where(even_x, near, other)
    for at, part in ((165, last), (176, value[0:16])):
        rows = part.shape[0]
        high = part.astype(bf16).astype(f32)
        buf[at : at + rows, :] = high
        buf[at + rows : at + 2 * rows, :] = part - high
    buf[173:176, :] = jnp.zeros((3, 128), f32)
    out_ref[...] = buf[...].astype(bf16)


def final_kernel(
    where_ref, recv_ref, my_ref, mz_ref, near_ref, far_ref, fine_ref, out_ref, same_ref,
    cells, w0, w1, acc, moved, wide, line, tail,
):
    index_x = where_ref[0]
    index_y = where_ref[1]
    count = recv_ref.shape[0]
    cells[:, 32:40, :] = jnp.zeros((17, 8, 128), f32)
    for step in range(-2, 3):
        source = index_y + step
        inside = (source >= 0) & (source < count)
        got = recv_ref[jnp.clip(source, 0, count - 1), 0:176, :].astype(f32)
        line[...] = jnp.where(inside, got, 0.0)
        for p in range(5):
            n = 5 * step + 6 + p
            if 0 <= n < 17:
                cells[n, 0:33, :] = line[33 * p : 33 * p + 33, :]

    r, c = iota2((128, 128))
    mask = jnp.abs(r % 64 - c % 64) <= REACH

    def band_rows(w, a, at):
        base = TAPS * TAPS + a * TAPS
        for j in range(11):
            same = near_ref[pl.ds(base + 2 * j, 1), :]
            upper = same
            lower = same
            if j > 0:
                upper = same + far_ref[pl.ds(base + 2 * j - 1, 1), :]
            if j < 10:
                lower = same + far_ref[pl.ds(base + 2 * j + 1, 1), :]
            upper = pltpu.roll(jnp.broadcast_to(upper, (64, 128)), 0, 1, stride=1, stride_axis=0)
            lower = pltpu.roll(jnp.broadcast_to(lower, (64, 128)), 64, 1, stride=1, stride_axis=0)
            band = jnp.where(mask, jnp.concatenate([upper, lower], axis=0), 0.0).astype(bf16)
            w[at + 128 * j : at + 128 * j + 128, :] = band

    def build(w, a):
        for k in range(3):
            band_rows(w, a + k, 1408 * k)

    def dot(w, a):
        rows = []
        for k in range(3):
            part = [cells[n, pl.ds(a + k, 16), :].astype(bf16) for n in range(17)]
            rows.append([jnp.concatenate(part[g : g + 11], axis=1) for g in range(7)])
        lhs = jnp.concatenate(
            [jnp.concatenate([rows[k][g] for k in range(3)], axis=1) for g in range(7)], axis=0
        )
        acc[...] += jnp.dot(lhs, w[...], preferred_element_type=f32)

    acc[...] = jnp.zeros((112, 128), f32)
    build(w0, 0)

    def step(t, _):
        a = 6 * t
        build(w1, a + 3)
        dot(w0, a)
        build(w0, a + 6)
        dot(w1, a + 3)
        return 0

    lax.fori_loop(0, 3, step, 0)
    dot(w0, 18)

    start = 10 * index_y
    sums = [[None] * 14, [None] * 14]
    for k in range(count):
        main = recv_ref[k, 176:192, :].astype(f32) + recv_ref[k, 192:208, :].astype(f32)
        last = recv_ref[k, 160:176, :].astype(f32)
        last = last[5:9] + last[9:13]
        tail[k, pl.ds(0, 4, stride=4), :] = last
        for r in range(1, 4):
            tail[k, pl.ds(r, 4, stride=4), :] = pltpu.roll(last, 128 - 32 * r, 1)
        for h, value in ((0, main), (1, tail[k])):
            rows_y = my_ref[2 * k + h, pl.ds(start, 16), :]
            for y in range(14):
                term = value * rows_y[y : y + 1, :]
                sums[h][y] = term if k == 0 else sums[h][y] + term
    rows = [
        jnp.concatenate([sums[h][2 * n + p] for p in range(2) for h in range(2)], axis=1)
        for n in range(7)
    ]
    top = jnp.dot(
        jnp.concatenate(rows, axis=0), mz_ref[...], precision=HIGHEST, preferred_element_type=f32
    )
    total = acc[...] + top
    r, c = iota2((112, 128))
    cell_x = 10 * index_x - 1 + r % 16
    cell_y = 10 * index_y - 2 + 2 * (r // 16) + c // 64
    inside = (cell_x >= 0) & (cell_x < 320) & (cell_y >= 0) & (cell_y < 80)
    total = jnp.where(inside, total, 0.0)
    r, c = iota2((128, 256))
    up_z = jnp.where(r // 64 == c // 128, weight(c % 128 - 2 * (r % 64)), 0.0)
    wide[...] = exact_dot(total, up_z)

    def middle_y(y):
        n, par = (y + 2) // 2, y % 2
        return wide[16 * n : 16 * n + 16, 128 * par : 128 * par + 128]

    for y in range(20):
        m = y // 2
        if y % 2 == 0:
            value = middle_y(m)
        else:
            value = 0.5625 * (middle_y(m) + middle_y(m + 1)) - 0.0625 * (
                middle_y(m - 1) + middle_y(m + 2)
            )
        moved[16 * y : 16 * y + 16, :] = value
    planes = [moved[pl.ds(k, 20, stride=16), :] for k in range(13)]
    for x in range(20):
        m = x // 2
        if x % 2 == 0:
            value = planes[m + 1]
        else:
            value = 0.5625 * (planes[m + 1] + planes[m + 2]) - 0.0625 * (planes[m] + planes[m + 3])
        out_ref[x] = value
        same_ref[x] = fine_ref[24 * m : 24 * m + 20, 128 * (x % 2) : 128 * (x % 2) + 128]


def partners(count, first):
    return [(k, k + 1) for k in range(first, count - 1, 2)]


def both_ways(pairs):
    return pairs + [(b, a) for a, b in pairs]


def swap(first, second, axis):
    count = lax.axis_size(axis)
    second = lax.ppermute(second, axis, both_ways(partners(count, 1)))
    return lax.ppermute(first, axis, both_ways(partners(count, 0))), second


def per_device(charges, kernels):
    count_x = lax.axis_size("gx")
    count_y = lax.axis_size("gy")
    where = jnp.stack([lax.axis_index("gx"), lax.axis_index("gy")]).astype(jnp.int32)
    spread = charges.shape[0] * count_x / 16.0
    shape = jax.ShapeDtypeStruct
    low, high = charges[:10], charges[10:]
    even_x = even(lax.axis_index("gx"))
    edge, block = lax.optimization_barrier((jnp.where(even_x, low, high), charges))
    near_x, next_x = swap(block, edge, "gx")
    second, first = vmem_call(
        rim_kernel,
        [shape((400, 128), bf16)] * 2,
        [pltpu.VMEM((40, 20, 128), f32), pltpu.VMEM((2, 400, 128), f32)],
        "rim",
        (where, charges, near_x, next_x),
        smem=1,
    )
    first, second, kernels = lax.optimization_barrier((first, second, kernels))
    near, far = (
        jnp.dot(kernels.reshape(-1, TAPS), jnp.asarray(m, bf16), preferred_element_type=f32)
        for m in spots_np()
    )
    near_y, next_y = swap(first, second, "gy")
    next_y, near_y, near, far = lax.optimization_barrier((next_y, near_y, near, far))
    d, second, first, own, coarse = vmem_call(
        restrict_kernel,
        [
            shape((40, 40, 128), bf16),
            shape((5, 9, 128), bf16),
            shape((5, 9, 128), bf16),
            shape((5, 16, 128), bf16),
            shape((8, 128), f32),
        ],
        [
            pltpu.VMEM((2, 20, 48, 128), f32),
            pltpu.VMEM((2, 400, 128), f32),
            pltpu.VMEM((16, 48, 128), f32),
            pltpu.VMEM((256, 128), f32),
            pltpu.VMEM((9, 24, 128), f32),
        ],
        "restrict",
        (where, charges, near_x, next_x, next_y, near_y),
        smem=1,
    )
    near_m, next_m = swap(first, second, "gx")
    chips = count_x // 2
    groups = [[2 * q + core for q in range(chips)] for core in range(2)]
    coarse = lax.all_to_all(
        jnp.broadcast_to(coarse, (chips, 8, 128)), "gx", 0, 0, axis_index_groups=groups
    )
    near, near_m = lax.optimization_barrier((near, near_m))
    fine = fine_sum(0, SPLIT, d, near)
    coarse, fine, next_m = lax.optimization_barrier((coarse, fine, next_m))
    other = lax.ppermute(coarse, "gx", both_ways(partners(count_x, 0)))
    parts = vmem_call(
        spread_kernel,
        [shape((208, 128), bf16)],
        [pltpu.VMEM((208, 128), f32), pltpu.VMEM((16, 128), f32)],
        "spread",
        (where, coarse, other, jnp.asarray(matrix_x_np(spread)), own, next_m, near_m),
        smem=1,
    )[0]
    parts, near = lax.optimization_barrier((parts, near))
    parts = lax.all_to_all(jnp.broadcast_to(parts, (count_y, 208, 128)), "gy", 0, 0)
    fine = fine_sum(SPLIT, TAPS, d, near, fine)
    total, fine = vmem_call(
        final_kernel,
        [shape((20, 20, 128), f32)] * 2,
        [
            pltpu.VMEM((17, 40, 128), f32),
            pltpu.VMEM((4224, 128), bf16),
            pltpu.VMEM((4224, 128), bf16),
            pltpu.VMEM((112, 128), f32),
            pltpu.VMEM((320, 128), f32),
            pltpu.VMEM((112, 256), f32),
            pltpu.VMEM((176, 128), f32),
            pltpu.VMEM((count_y, 16, 128), f32),
        ],
        "final",
        (
            where,
            parts,
            jnp.asarray(matrix_y_np(spread)),
            jnp.asarray(matrix_z_np(spread)),
            near,
            far,
            fine,
        ),
        smem=1,
    )
    return total + fine


def solution(mesh):
    return jax.shard_map(
        per_device,
        mesh=mesh,
        in_specs=(P("gx", "gy", None), P()),
        out_specs=P("gx", "gy", None),
        check_vma=False,
    )
```

```python
import functools
import numpy as np
import jax
import jax.numpy as jnp
from jax import lax
from jax.experimental import pallas as pl
from jax.experimental.pallas import tpu as pltpu
from jax.sharding import PartitionSpec as P

f32 = jnp.float32
bf16 = jnp.bfloat16
spread_norm = 1.2533141
REACH = 10
TAPS = 21
GROUP = 3
SPLIT = 6


def weight_np(offset):
    d = np.abs(offset)
    return np.where(d == 0, 1.0, np.where(d == 1, 0.5625, np.where(d == 3, -0.0625, 0.0)))


def top_matrix_np(n, spread):
    prolong = weight_np(np.arange(2 * n)[:, None] - 2 * np.arange(n)[None, :])
    offset = (np.arange(n)[:, None] - np.arange(n)[None, :]) / spread
    return prolong @ (np.exp(-offset * offset) / np.sqrt(spread * spread_norm))


def lane_tiles(m):
    return m.reshape(m.shape[0], -1, 128).transpose(1, 0, 2).astype(np.float32)


def matrix_x_np(spread):
    m = top_matrix_np(160, spread).reshape(320, 32, 5)
    out = np.zeros((328, 32, 8))
    out[1:321, :, :5] = m
    return lane_tiles(out.reshape(328, 256))


def matrix_y_np(spread):
    m = top_matrix_np(40, spread).reshape(80, 8, 5)
    out = np.zeros((88, 8, 8))
    out[2:82, :, :5] = m
    return lane_tiles(np.repeat(out.reshape(88, 64), 32, axis=1))


def matrix_z_np(spread):
    m = top_matrix_np(32, spread).T
    out = np.zeros((2, 8, 32, 2, 64))
    for par in range(2):
        out[par, :, :, par, :] = m[None]
    return out.reshape(512, 128).astype(np.float32)


def spots_np():
    taps = np.arange(TAPS)[:, None]
    lanes = np.arange(128)[None, :]
    near = lanes == (REACH - taps) % 128
    far = lanes == (64 + REACH - taps) % 128
    return near, far


def weight(d):
    d = jnp.abs(d)
    return jnp.where(d == 0, 1.0, jnp.where(d == 1, 0.5625, jnp.where(d == 3, -0.0625, 0.0))).astype(f32)


def exact_dot(rows, weights):
    count = rows.shape[0]
    high = rows.astype(bf16)
    rest = rows - high.astype(f32)
    middle = rest.astype(bf16)
    low = (rest - middle.astype(f32)).astype(bf16)
    out = jnp.dot(
        jnp.concatenate([high, middle, low], axis=0),
        weights.astype(bf16),
        preferred_element_type=f32,
    )
    return out[0:count] + (out[count : 2 * count] + out[2 * count :])


def parts_of(value):
    high = value.astype(bf16)
    return high, (value - high.astype(f32)).astype(bf16)


def two_part_dot(rows, weights):
    high, low = parts_of(rows)
    w_high, w_low = parts_of(weights)
    return jnp.dot(
        jnp.concatenate([high, high, low], axis=1),
        jnp.concatenate([w_high, w_low, w_high], axis=0),
        preferred_element_type=f32,
    )


def iota2(shape):
    return (lax.broadcasted_iota(jnp.int32, shape, 0), lax.broadcasted_iota(jnp.int32, shape, 1))


def vmem_call(body, out_shape, scratch, name, args, smem=0, flops=0, limit=8):
    def spec(space):
        return pl.BlockSpec(memory_space=space)

    return pl.pallas_call(
        body,
        out_shape=out_shape,
        in_specs=[spec(pltpu.SMEM)] * smem + [spec(pltpu.VMEM)] * (len(args) - smem),
        out_specs=[spec(pltpu.VMEM)] * len(out_shape),
        scratch_shapes=scratch,
        compiler_params=pltpu.CompilerParams(vmem_limit_bytes=limit << 20),
        cost_estimate=pl.CostEstimate(flops=flops, bytes_accessed=1 << 16, transcendentals=0),
        name=name,
    )(*args)


def even(index):
    return index % 2 == 0


def rim_kernel(where_ref, blk_ref, near_ref, next_ref, second_ref, first_ref, wide, dense):
    even_x = even(where_ref[0])
    wide[pl.ds(jnp.where(even_x, 30, 0), 10), 0:20, :] = near_ref[...].astype(f32)
    wide[pl.ds(jnp.where(even_x, 0, 30), 10), 0:20, :] = next_ref[...].astype(f32)
    wide[10:30, 0:20, :] = blk_ref[...].astype(f32)
    start = jnp.where(even(where_ref[1]), 10, 0)
    for x in range(40):
        dense[0, 10 * x : 10 * x + 10, :] = wide[x, pl.ds(start, 10), :]
        dense[1, 10 * x : 10 * x + 10, :] = wide[x, pl.ds(10 - start, 10), :]
    first_ref[...] = dense[0].astype(bf16)
    second_ref[...] = dense[1].astype(bf16)


def restrict_kernel(
    where_ref, blk_ref, near_x_ref, next_x_ref, next_y_ref, near_y_ref,
    d_out_ref, second_ref, first_ref, own_ref, out_ref,
    d_ref, dense, sides, planes, cells, mid,
):
    even_x = even(where_ref[0])
    even_y = even(where_ref[1])
    upper = jnp.where(even_y, 1, 0)
    dense[upper] = near_y_ref[...].astype(f32)
    dense[1 - upper] = next_y_ref[...].astype(f32)
    upper = jnp.where(even_x, 1, 0)
    sides[upper, :, 0:20, :] = near_x_ref[...].astype(f32)
    sides[1 - upper, :, 0:20, :] = next_x_ref[...].astype(f32)
    for x in range(40):
        p, i = x % 2, x // 2
        d_ref[p, i, 0:10, :] = dense[0, 10 * x : 10 * x + 10, :]
        d_ref[p, i, 30:40, :] = dense[1, 10 * x : 10 * x + 10, :]
        if 10 <= x < 30:
            centre = blk_ref[x - 10].astype(f32)
        else:
            centre = sides[x // 30, x % 30, 0:20, :]
        d_ref[p, i, 10:30, :] = centre
        d_out_ref[x] = d_ref[p, i, 0:40, :].astype(bf16)

    def fine(x):
        return d_ref[x % 2, x // 2]

    for i in range(16):
        c = 2 * i + 4
        planes[i] = (
            fine(c) + 0.5625 * (fine(c - 1) + fine(c + 1)) - 0.0625 * (fine(c - 3) + fine(c + 3))
        )
    for i in range(16):
        def tap(o):
            return planes[i, pl.ds(4 + o, 16, stride=2), :]
        cells[16 * i : 16 * i + 16, :] = (
            tap(0) + 0.5625 * (tap(-1) + tap(1)) - 0.0625 * (tap(-3) + tap(3))
        )
    zero = jnp.zeros((16, 128), f32)
    rows = []
    for n in range(9):
        pair = []
        for y in (2 * n - 4, 2 * n - 3):
            inside = -3 <= y <= 12
            pair.append(cells[pl.ds(y + 3, 16, stride=16), :] if inside else zero)
        rows.append(jnp.concatenate(pair, axis=1))
    r, c = iota2((256, 128))
    down_z = jnp.where(r // 128 == c // 64, weight(r % 128 - 2 * (c % 64)), 0.0)
    value = exact_dot(jnp.concatenate(rows, axis=0), down_z)
    r, c = iota2((144, 128))
    cell_x = 10 * where_ref[0] - 3 + r % 16
    cell_y = 10 * where_ref[1] - 4 + 2 * (r // 16) + c // 64
    inside = (cell_x >= 0) & (cell_x < 320) & (cell_y >= 0) & (cell_y < 80)
    value = jnp.where(inside, value, 0.0).astype(bf16).astype(f32)
    for n in range(9):
        mid[n, 0:16, :] = value[16 * n : 16 * n + 16]
        mid[n, 16:24, :] = jnp.zeros((8, 128), f32)
    for n in range(5):
        right, left = mid[n + 2, 1:10, :], mid[n + 2, 6:15, :]
        first_ref[n] = jnp.where(even_x, right, left).astype(bf16)
        second_ref[n] = jnp.where(even_x, left, right).astype(bf16)
        own_ref[n] = mid[n + 2, 0:16, :].astype(bf16)

    lane = lax.broadcasted_iota(jnp.int32, (1, 128), 1)
    odd = lane >= 64
    weight_0 = jnp.where(odd, 0.5625, 1.0)
    weight_1 = jnp.where(odd, 0.5625, 0.0)
    weight_3 = jnp.where(odd, -0.0625, 0.0)
    r, c = iota2((128, 32))
    down_z = weight(r % 64 - 2 * c)
    sums = []
    for y in range(5):
        n = y + 2
        def tap(o):
            def part(k):
                return mid[k, pl.ds(3 + o, 8, stride=2), :]
            return (
                weight_0 * part(n) + weight_1 * part(n - 1) + weight_3 * (part(n - 2) + part(n + 1))
            )
        sums.append(tap(0) + 0.5625 * (tap(-1) + tap(1)) - 0.0625 * (tap(-3) + tap(3)))
    out = exact_dot(jnp.concatenate(sums, axis=0), down_z)
    main = jnp.concatenate([out[8 * y : 8 * y + 8] for y in range(4)], axis=1)[0:5]
    last = jnp.concatenate([out[32 + x : 33 + x] for x in range(4)], axis=1)
    rest = jnp.concatenate([out[36:37], jnp.zeros((1, 96), f32)], axis=1)
    row = jnp.concatenate([main, last, rest, jnp.zeros((1, 128), f32)], axis=0)
    for k in range(out_ref.shape[0]):
        out_ref[k] = row


def fine_kernel(lo, hi, first, d_in_ref, v_ref, *refs):
    if first:
        out_ref, w0, w1, e0, e1, d_ref = refs
    else:
        acc_ref, out_ref, w0, w1, e0, e1, d_ref = refs
    for x in range(40):
        d_ref[x % 2, x // 2, 0:40, :] = d_in_ref[x].astype(f32)
        d_ref[x % 2, x // 2, 40:48, :] = jnp.zeros((8, 128), f32)
    r, c = iota2((128, 128))
    mask = jnp.abs(r - c) <= REACH
    zero = jnp.zeros((128, 128), bf16)
    for w in (w0, w1):
        for k in range(GROUP):
            w[2816 * k : 2816 * k + 128, 128:256] = zero
            w[2816 * k + 2688 : 2816 * k + 2816, 0:128] = zero

    def build(w, start):
        for k in range(GROUP):
            for a in range(TAPS):
                line = jnp.broadcast_to(v_ref[pl.ds(a * TAPS + start + k, 1), :], (128, 128))
                line = pltpu.roll(line, 0, 1, stride=1, stride_axis=0)
                band = jnp.where(mask, line, 0.0).astype(bf16)
                at = 2816 * k + 128 * a
                w[at : at + 128, 0:128] = band
                w[at + 128 : at + 256, 128:256] = band

    def dot(w, e, start):
        tiles = []
        for k in range(GROUP):
            for p in range(2):
                for q in range(10):
                    part = d_ref[p, 2 * q : 2 * q + 2, pl.ds(start + k, 24), :].reshape(48, 128)
                    e[k, 0, 48 * q : 48 * q + 48, p * 128 : (p + 1) * 128] = part.astype(bf16)
                for q in range(9):
                    part = d_ref[p, 2 * q + 1 : 2 * q + 3, pl.ds(start + k, 24), :].reshape(48, 128)
                    e[k, 1, 48 * q : 48 * q + 48, p * 128 : (p + 1) * 128] = part.astype(bf16)
            tiles += [
                e[k, m % 2, 24 * (m - m % 2) : 24 * (m - m % 2) + 240, :] for m in range(11)
            ]
        lhs = jnp.concatenate(tiles, axis=1)
        out_ref[...] += jnp.dot(lhs, w[...], preferred_element_type=f32)

    out_ref[...] = jnp.zeros((240, 256), f32) if first else acc_ref[...]

    def step(t, _):
        b = lo + 2 * GROUP * t
        build(w0, b)
        dot(w0, e0, b)
        build(w1, b + GROUP)
        dot(w1, e1, b + GROUP)
        return 0

    groups = (hi - lo) // GROUP
    lax.fori_loop(0, groups // 2, step, 0)
    if groups % 2:
        build(w0, hi - GROUP)
        dot(w0, e0, hi - GROUP)


def fine_sum(lo, hi, d, v, acc=None):
    return vmem_call(
        functools.partial(fine_kernel, lo, hi, acc is None),
        [jax.ShapeDtypeStruct((240, 256), f32)],
        [pltpu.VMEM((GROUP * 2816, 256), bf16)] * 2
        + [pltpu.VMEM((GROUP, 2, 480, 256), bf16)] * 2
        + [pltpu.VMEM((2, 20, 48, 128), f32)],
        "fine_sum",
        (d, v) if acc is None else (d, v, acc),
        flops=(hi - lo) * 2 * 240 * 2816 * 256,
        limit=20,
    )[0]


def spread_kernel(where_ref, recv_ref, mx_ref, own_ref, next_ref, near_ref, out_ref, buf, tail):
    even_x = even(where_ref[0])
    start = 10 * where_ref[0]
    halves = [mx_ref[h, pl.ds(start, 16), :] for h in range(2)]
    lane = lax.broadcasted_iota(jnp.int32, (16, 128), 1) % 8
    rows = [jnp.concatenate(halves, axis=1)]
    for x in range(5):
        at = 5 if x < 4 else 6
        moved = [jnp.where(lane == at, pltpu.roll(h, at - x, 1), 0.0) for h in halves]
        rows.append(jnp.concatenate(moved, axis=1))
    coarse = recv_ref[...].reshape(8 * recv_ref.shape[0], 128)
    value = two_part_dot(jnp.concatenate(rows, axis=0), coarse)
    last = value[80:96, 0:32]
    for x in range(4):
        last = last + value[16 * x + 16 : 16 * x + 32, 32 * x : 32 * x + 32]
    tail[...] = jnp.concatenate([last, jnp.zeros((16, 96), f32)], axis=1)
    last = tail[pl.ds(0, 4, stride=4), :]
    for k in range(1, 4):
        last = last + pltpu.roll(tail[pl.ds(k, 4, stride=4), :], 32 * k, 1)
    for n in range(5):
        near, other = near_ref[n].astype(f32), next_ref[n].astype(f32)
        buf[33 * n : 33 * n + 8, :] = jnp.where(even_x, other, near)[1:9]
        buf[33 * n + 8 : 33 * n + 24, :] = own_ref[n].astype(f32)
        buf[33 * n + 24 : 33 * n + 33, :] = jnp.where(even_x, near, other)
    for at, part in ((165, last), (176, value[0:16])):
        rows = part.shape[0]
        high = part.astype(bf16).astype(f32)
        buf[at : at + rows, :] = high
        buf[at + rows : at + 2 * rows, :] = part - high
    buf[173:176, :] = jnp.zeros((3, 128), f32)
    packed = buf[...].astype(bf16)
    for k in range(out_ref.shape[0]):
        out_ref[k] = packed


def final_kernel(
    where_ref, recv_ref, my_ref, mz_ref, near_ref, far_ref, fine_ref, out_ref,
    cells, w0, w1, acc, moved, wide, line, tail,
):
    index_x = where_ref[0]
    index_y = where_ref[1]
    count = recv_ref.shape[0]
    cells[:, 32:40, :] = jnp.zeros((17, 8, 128), f32)
    for step in range(-2, 3):
        source = index_y + step
        inside = (source >= 0) & (source < count)
        got = recv_ref[jnp.clip(source, 0, count - 1), 0:176, :].astype(f32)
        line[...] = jnp.where(inside, got, 0.0)
        for p in range(5):
            n = 5 * step + 6 + p
            if 0 <= n < 17:
                cells[n, 0:33, :] = line[33 * p : 33 * p + 33, :]

    r, c = iota2((128, 128))
    mask = jnp.abs(r % 64 - c % 64) <= REACH

    def band_rows(w, a, at):
        base = TAPS * TAPS + a * TAPS
        for j in range(11):
            same = near_ref[pl.ds(base + 2 * j, 1), :]
            upper = same
            lower = same
            if j > 0:
                upper = same + far_ref[pl.ds(base + 2 * j - 1, 1), :]
            if j < 10:
                lower = same + far_ref[pl.ds(base + 2 * j + 1, 1), :]
            upper = pltpu.roll(jnp.broadcast_to(upper, (64, 128)), 0, 1, stride=1, stride_axis=0)
            lower = pltpu.roll(jnp.broadcast_to(lower, (64, 128)), 64, 1, stride=1, stride_axis=0)
            band = jnp.where(mask, jnp.concatenate([upper, lower], axis=0), 0.0).astype(bf16)
            w[at + 128 * j : at + 128 * j + 128, :] = band

    def build(w, a):
        for k in range(3):
            band_rows(w, a + k, 1408 * k)

    def dot(w, a):
        rows = []
        for k in range(3):
            part = [cells[n, pl.ds(a + k, 16), :].astype(bf16) for n in range(17)]
            rows.append([jnp.concatenate(part[g : g + 11], axis=1) for g in range(7)])
        lhs = jnp.concatenate(
            [jnp.concatenate([rows[k][g] for k in range(3)], axis=1) for g in range(7)], axis=0
        )
        acc[...] += jnp.dot(lhs, w[...], preferred_element_type=f32)

    acc[...] = jnp.zeros((112, 128), f32)
    build(w0, 0)

    def step(t, _):
        a = 6 * t
        build(w1, a + 3)
        dot(w0, a)
        build(w0, a + 6)
        dot(w1, a + 3)
        return 0

    lax.fori_loop(0, 3, step, 0)
    dot(w0, 18)

    start = 10 * index_y
    sums = [[None] * 14, [None] * 14]
    for k in range(count):
        main = recv_ref[k, 176:192, :].astype(f32) + recv_ref[k, 192:208, :].astype(f32)
        last = recv_ref[k, 160:176, :].astype(f32)
        last = last[5:9] + last[9:13]
        tail[k, pl.ds(0, 4, stride=4), :] = last
        for r in range(1, 4):
            tail[k, pl.ds(r, 4, stride=4), :] = pltpu.roll(last, 128 - 32 * r, 1)
        for h, value in ((0, main), (1, tail[k])):
            rows_y = my_ref[2 * k + h, pl.ds(start, 16), :]
            for y in range(14):
                term = value * rows_y[y : y + 1, :]
                sums[h][y] = term if k == 0 else sums[h][y] + term
    rows = [
        jnp.concatenate([sums[h][2 * n + p] for p in range(2) for h in range(2)], axis=1)
        for n in range(7)
    ]
    top = two_part_dot(jnp.concatenate(rows, axis=0), mz_ref[...])
    total = acc[...] + top
    r, c = iota2((112, 128))
    cell_x = 10 * index_x - 1 + r % 16
    cell_y = 10 * index_y - 2 + 2 * (r // 16) + c // 64
    inside = (cell_x >= 0) & (cell_x < 320) & (cell_y >= 0) & (cell_y < 80)
    total = jnp.where(inside, total, 0.0)
    r, c = iota2((128, 256))
    up_z = jnp.where(r // 64 == c // 128, weight(c % 128 - 2 * (r % 64)), 0.0)
    wide[...] = exact_dot(total, up_z)

    def middle_y(y):
        n, par = (y + 2) // 2, y % 2
        return wide[16 * n : 16 * n + 16, 128 * par : 128 * par + 128]

    for y in range(20):
        m = y // 2
        if y % 2 == 0:
            value = middle_y(m)
        else:
            value = 0.5625 * (middle_y(m) + middle_y(m + 1)) - 0.0625 * (
                middle_y(m - 1) + middle_y(m + 2)
            )
        moved[16 * y : 16 * y + 16, :] = value
    planes = [moved[pl.ds(k, 20, stride=16), :] for k in range(13)]
    for x in range(20):
        m = x // 2
        if x % 2 == 0:
            value = planes[m + 1]
        else:
            value = 0.5625 * (planes[m + 1] + planes[m + 2]) - 0.0625 * (planes[m] + planes[m + 3])
        out_ref[x] = value + fine_ref[24 * m : 24 * m + 20, 128 * (x % 2) : 128 * (x % 2) + 128]


def swap(first, second, axis):
    count = lax.axis_size(axis)
    pairs = [(k, k + 1) for k in range(0, count - 1, 2)]
    others = [(k, k + 1) for k in range(1, count - 1, 2)]

    def both(ends):
        return ends + [(b, a) for a, b in ends]

    second = lax.ppermute(second, axis, both(others))
    return lax.ppermute(first, axis, both(pairs)), second


def per_device(charges, kernels):
    count_x = lax.axis_size("gx")
    count_y = lax.axis_size("gy")
    where = jnp.stack([lax.axis_index("gx"), lax.axis_index("gy")]).astype(jnp.int32)
    spread = charges.shape[0] * count_x / 16.0
    shape = jax.ShapeDtypeStruct
    low, high = charges[:10], charges[10:]
    even_x = even(lax.axis_index("gx"))
    near_x, next_x = swap(jnp.where(even_x, high, low), jnp.where(even_x, low, high), "gx")
    second, first = vmem_call(
        rim_kernel,
        [shape((400, 128), bf16)] * 2,
        [pltpu.VMEM((40, 24, 128), f32), pltpu.VMEM((2, 400, 128), f32)],
        "rim",
        (where, charges, near_x, next_x),
        smem=1,
    )
    first, second, kernels = lax.optimization_barrier((first, second, kernels))
    near, far = (
        jnp.dot(kernels.reshape(-1, TAPS), jnp.asarray(m, bf16), preferred_element_type=f32)
        for m in spots_np()
    )
    near_y, next_y = swap(first, second, "gy")
    next_y, near_y, near, far = lax.optimization_barrier((next_y, near_y, near, far))
    d, second, first, own, coarse = vmem_call(
        restrict_kernel,
        [
            shape((40, 40, 128), bf16),
            shape((5, 9, 128), bf16),
            shape((5, 9, 128), bf16),
            shape((5, 16, 128), bf16),
            shape((count_x, 8, 128), f32),
        ],
        [
            pltpu.VMEM((2, 20, 48, 128), f32),
            pltpu.VMEM((2, 400, 128), f32),
            pltpu.VMEM((2, 10, 24, 128), f32),
            pltpu.VMEM((16, 48, 128), f32),
            pltpu.VMEM((256, 128), f32),
            pltpu.VMEM((9, 24, 128), f32),
        ],
        "restrict",
        (where, charges, near_x, next_x, next_y, near_y),
        smem=1,
    )
    near_m, next_m = swap(first, second, "gx")
    coarse = lax.all_to_all(coarse, "gx", 0, 0)
    near, near_m = lax.optimization_barrier((near, near_m))
    fine = fine_sum(0, SPLIT, d, near)
    coarse, fine = lax.optimization_barrier((coarse, fine))
    parts = vmem_call(
        spread_kernel,
        [shape((count_y, 208, 128), bf16)],
        [pltpu.VMEM((208, 128), f32), pltpu.VMEM((16, 128), f32)],
        "spread",
        (where, coarse, jnp.asarray(matrix_x_np(spread)), own, next_m, near_m),
        smem=1,
    )[0]
    parts, near = lax.optimization_barrier((parts, near))
    parts = lax.all_to_all(parts, "gy", 0, 0)
    fine = fine_sum(SPLIT, TAPS, d, near, fine)
    return vmem_call(
        final_kernel,
        [shape((20, 20, 128), f32)],
        [
            pltpu.VMEM((17, 40, 128), f32),
            pltpu.VMEM((4224, 128), bf16),
            pltpu.VMEM((4224, 128), bf16),
            pltpu.VMEM((112, 128), f32),
            pltpu.VMEM((320, 128), f32),
            pltpu.VMEM((112, 256), f32),
            pltpu.VMEM((176, 128), f32),
            pltpu.VMEM((count_y, 16, 128), f32),
        ],
        "final",
        (
            where,
            parts,
            jnp.asarray(matrix_y_np(spread)),
            jnp.asarray(matrix_z_np(spread)),
            near,
            far,
            fine,
        ),
        smem=1,
    )[0]


def solution(mesh):
    return jax.shard_map(
        per_device,
        mesh=mesh,
        in_specs=(P("gx", "gy", None), P()),
        out_specs=P("gx", "gy", None),
        check_vma=False,
    )
```

```python
import functools
import numpy as np
import jax
import jax.numpy as jnp
from jax import lax
from jax.experimental import pallas as pl
from jax.experimental.pallas import tpu as pltpu
from jax.sharding import PartitionSpec as P

f32 = jnp.float32
bf16 = jnp.bfloat16
spread_norm = 1.2533141
REACH = 10
TAPS = 21
GROUP = 3
SPLIT = 6


def weight_np(offset):
    d = np.abs(offset)
    return np.where(d == 0, 1.0, np.where(d == 1, 0.5625, np.where(d == 3, -0.0625, 0.0)))


def top_matrix_np(n, spread):
    prolong = weight_np(np.arange(2 * n)[:, None] - 2 * np.arange(n)[None, :])
    offset = (np.arange(n)[:, None] - np.arange(n)[None, :]) / spread
    return prolong @ (np.exp(-offset * offset) / np.sqrt(spread * spread_norm))


def lane_tiles(m):
    return m.reshape(m.shape[0], -1, 128).transpose(1, 0, 2).astype(np.float32)


def matrix_x_np(spread):
    m = top_matrix_np(160, spread).reshape(320, 32, 5)
    out = np.zeros((328, 32, 8))
    out[1:321, :, :5] = m
    return lane_tiles(out.reshape(328, 256))


def matrix_y_np(spread):
    m = top_matrix_np(40, spread).reshape(80, 8, 5)
    out = np.zeros((88, 8, 8))
    out[2:82, :, :5] = m
    return lane_tiles(np.repeat(out.reshape(88, 64), 32, axis=1))


def matrix_z_np(spread):
    m = top_matrix_np(32, spread).T
    out = np.zeros((2, 8, 32, 2, 64))
    for par in range(2):
        out[par, :, :, par, :] = m[None]
    return out.reshape(512, 128).astype(np.float32)


def spots_np():
    taps = np.arange(TAPS)[:, None]
    lanes = np.arange(128)[None, :]
    near = lanes == (REACH - taps) % 128
    far = lanes == (64 + REACH - taps) % 128
    return near, far


def weight(d):
    d = jnp.abs(d)
    return jnp.where(d == 0, 1.0, jnp.where(d == 1, 0.5625, jnp.where(d == 3, -0.0625, 0.0))).astype(f32)


def exact_dot(rows, weights):
    count = rows.shape[0]
    high = rows.astype(bf16)
    rest = rows - high.astype(f32)
    middle = rest.astype(bf16)
    low = (rest - middle.astype(f32)).astype(bf16)
    out = jnp.dot(
        jnp.concatenate([high, middle, low], axis=0),
        weights.astype(bf16),
        preferred_element_type=f32,
    )
    return out[0:count] + (out[count : 2 * count] + out[2 * count :])


def parts_of(value):
    high = value.astype(bf16)
    return high, (value - high.astype(f32)).astype(bf16)


def two_part_dot(rows, weights):
    high, low = parts_of(rows)
    w_high, w_low = parts_of(weights)
    return jnp.dot(
        jnp.concatenate([high, high, low], axis=1),
        jnp.concatenate([w_high, w_low, w_high], axis=0),
        preferred_element_type=f32,
    )


def iota2(shape):
    return (lax.broadcasted_iota(jnp.int32, shape, 0), lax.broadcasted_iota(jnp.int32, shape, 1))


def vmem_call(body, out_shape, scratch, name, args, smem=0, flops=0, limit=8):
    def spec(space):
        return pl.BlockSpec(memory_space=space)

    return pl.pallas_call(
        body,
        out_shape=out_shape,
        in_specs=[spec(pltpu.SMEM)] * smem + [spec(pltpu.VMEM)] * (len(args) - smem),
        out_specs=[spec(pltpu.VMEM)] * len(out_shape),
        scratch_shapes=scratch,
        compiler_params=pltpu.CompilerParams(vmem_limit_bytes=limit << 20),
        cost_estimate=pl.CostEstimate(flops=flops, bytes_accessed=1 << 16, transcendentals=0),
        name=name,
    )(*args)


def even(index):
    return index % 2 == 0


def rim_rows(where_ref, wide, dense, count):
    start = jnp.where(even(where_ref[1]), 10, 0)
    for x in range(count):
        dense[0, 10 * x : 10 * x + 10, :] = wide[x, pl.ds(start, 10), :]
        dense[1, 10 * x : 10 * x + 10, :] = wide[x, pl.ds(10 - start, 10), :]


def rim_own_kernel(where_ref, blk_ref, out_ref, wide, dense):
    wide[:, 0:20, :] = blk_ref[...].astype(f32)
    rim_rows(where_ref, wide, dense, 20)
    out_ref[...] = dense[...]


def rim_kernel(where_ref, own_ref, near_ref, next_ref, first_ref, second_ref, wide, dense):
    even_x = even(where_ref[0])
    wide[pl.ds(jnp.where(even_x, 10, 0), 10), 0:20, :] = near_ref[...].astype(f32)
    wide[pl.ds(jnp.where(even_x, 0, 10), 10), 0:20, :] = next_ref[...].astype(f32)
    rim_rows(where_ref, wide, dense, 20)
    for k, out_ref in enumerate((first_ref, second_ref)):
        out_ref[...] = jnp.concatenate([own_ref[k], dense[k]], axis=0).astype(bf16)


def restrict_kernel(
    where_ref, blk_ref, near_x_ref, next_x_ref, next_y_ref, near_y_ref,
    d_out_ref, second_ref, first_ref, own_ref, out_ref,
    d_ref, dense, sides, planes, cells, mid,
):
    even_x = even(where_ref[0])
    even_y = even(where_ref[1])
    upper = jnp.where(even_y, 1, 0)
    dense[upper] = near_y_ref[...].astype(f32)
    dense[1 - upper] = next_y_ref[...].astype(f32)
    upper = jnp.where(even_x, 1, 0)
    sides[upper, :, 0:20, :] = near_x_ref[...].astype(f32)
    sides[1 - upper, :, 0:20, :] = next_x_ref[...].astype(f32)
    for x in range(40):
        p, i = x % 2, x // 2
        at = 10 * (x - 10 if 10 <= x < 30 else x + 20 if x < 10 else x)
        d_ref[p, i, 0:10, :] = dense[0, at : at + 10, :]
        d_ref[p, i, 30:40, :] = dense[1, at : at + 10, :]
        if 10 <= x < 30:
            centre = blk_ref[x - 10].astype(f32)
        else:
            centre = sides[x // 30, x % 30, 0:20, :]
        d_ref[p, i, 10:30, :] = centre
        d_out_ref[x] = d_ref[p, i, 0:40, :].astype(bf16)

    def fine(x):
        return d_ref[x % 2, x // 2]

    for i in range(16):
        c = 2 * i + 4
        planes[i] = (
            fine(c) + 0.5625 * (fine(c - 1) + fine(c + 1)) - 0.0625 * (fine(c - 3) + fine(c + 3))
        )
    for i in range(16):
        def tap(o):
            return planes[i, pl.ds(4 + o, 16, stride=2), :]
        cells[16 * i : 16 * i + 16, :] = (
            tap(0) + 0.5625 * (tap(-1) + tap(1)) - 0.0625 * (tap(-3) + tap(3))
        )
    zero = jnp.zeros((16, 128), f32)
    rows = []
    for n in range(9):
        pair = []
        for y in (2 * n - 4, 2 * n - 3):
            inside = -3 <= y <= 12
            pair.append(cells[pl.ds(y + 3, 16, stride=16), :] if inside else zero)
        rows.append(jnp.concatenate(pair, axis=1))
    r, c = iota2((256, 128))
    down_z = jnp.where(r // 128 == c // 64, weight(r % 128 - 2 * (c % 64)), 0.0)
    value = exact_dot(jnp.concatenate(rows, axis=0), down_z)
    r, c = iota2((144, 128))
    cell_x = 10 * where_ref[0] - 3 + r % 16
    cell_y = 10 * where_ref[1] - 4 + 2 * (r // 16) + c // 64
    inside = (cell_x >= 0) & (cell_x < 320) & (cell_y >= 0) & (cell_y < 80)
    value = jnp.where(inside, value, 0.0).astype(bf16).astype(f32)
    for n in range(9):
        mid[n, 0:16, :] = value[16 * n : 16 * n + 16]
        mid[n, 16:24, :] = jnp.zeros((8, 128), f32)
    for n in range(5):
        right, left = mid[n + 2, 1:10, :], mid[n + 2, 6:15, :]
        first_ref[n] = jnp.where(even_x, right, left).astype(bf16)
        second_ref[n] = jnp.where(even_x, left, right).astype(bf16)
        own_ref[n] = mid[n + 2, 0:16, :].astype(bf16)

    lane = lax.broadcasted_iota(jnp.int32, (1, 128), 1)
    odd = lane >= 64
    weight_0 = jnp.where(odd, 0.5625, 1.0)
    weight_1 = jnp.where(odd, 0.5625, 0.0)
    weight_3 = jnp.where(odd, -0.0625, 0.0)
    r, c = iota2((128, 32))
    down_z = weight(r % 64 - 2 * c)
    sums = []
    for y in range(5):
        n = y + 2
        def tap(o):
            def part(k):
                return mid[k, pl.ds(3 + o, 8, stride=2), :]
            return (
                weight_0 * part(n) + weight_1 * part(n - 1) + weight_3 * (part(n - 2) + part(n + 1))
            )
        sums.append(tap(0) + 0.5625 * (tap(-1) + tap(1)) - 0.0625 * (tap(-3) + tap(3)))
    out = exact_dot(jnp.concatenate(sums, axis=0), down_z)
    main = jnp.concatenate([out[8 * y : 8 * y + 8] for y in range(4)], axis=1)[0:5]
    last = jnp.concatenate([out[32 + x : 33 + x] for x in range(4)], axis=1)
    rest = jnp.concatenate([out[36:37], jnp.zeros((1, 96), f32)], axis=1)
    row = jnp.concatenate([main, last, rest, jnp.zeros((1, 128), f32)], axis=0)
    for k in range(out_ref.shape[0]):
        out_ref[k] = row


def fine_kernel(lo, hi, first, d_in_ref, v_ref, *refs):
    if first:
        out_ref, w0, w1, e0, e1, d_ref = refs
    else:
        acc_ref, out_ref, w0, w1, e0, e1, d_ref = refs
    for x in range(40):
        d_ref[x % 2, x // 2, 0:40, :] = d_in_ref[x].astype(f32)
        d_ref[x % 2, x // 2, 40:48, :] = jnp.zeros((8, 128), f32)
    r, c = iota2((128, 128))
    mask = jnp.abs(r - c) <= REACH
    zero = jnp.zeros((128, 128), bf16)
    for w in (w0, w1):
        for k in range(GROUP):
            w[2816 * k : 2816 * k + 128, 128:256] = zero
            w[2816 * k + 2688 : 2816 * k + 2816, 0:128] = zero

    def build(w, start):
        for k in range(GROUP):
            for a in range(TAPS):
                line = jnp.broadcast_to(v_ref[pl.ds(a * TAPS + start + k, 1), :], (128, 128))
                line = pltpu.roll(line, 0, 1, stride=1, stride_axis=0)
                band = jnp.where(mask, line, 0.0).astype(bf16)
                at = 2816 * k + 128 * a
                w[at : at + 128, 0:128] = band
                w[at + 128 : at + 256, 128:256] = band

    def dot(w, e, start):
        tiles = []
        for k in range(GROUP):
            for p in range(2):
                for q in range(10):
                    part = d_ref[p, 2 * q : 2 * q + 2, pl.ds(start + k, 24), :].reshape(48, 128)
                    e[k, 0, 48 * q : 48 * q + 48, p * 128 : (p + 1) * 128] = part.astype(bf16)
                for q in range(9):
                    part = d_ref[p, 2 * q + 1 : 2 * q + 3, pl.ds(start + k, 24), :].reshape(48, 128)
                    e[k, 1, 48 * q : 48 * q + 48, p * 128 : (p + 1) * 128] = part.astype(bf16)
            tiles += [
                e[k, m % 2, 24 * (m - m % 2) : 24 * (m - m % 2) + 240, :] for m in range(11)
            ]
        lhs = jnp.concatenate(tiles, axis=1)
        out_ref[...] += jnp.dot(lhs, w[...], preferred_element_type=f32)

    out_ref[...] = jnp.zeros((240, 256), f32) if first else acc_ref[...]

    def step(t, _):
        b = lo + 2 * GROUP * t
        build(w0, b)
        dot(w0, e0, b)
        build(w1, b + GROUP)
        dot(w1, e1, b + GROUP)
        return 0

    groups = (hi - lo) // GROUP
    lax.fori_loop(0, groups // 2, step, 0)
    if groups % 2:
        build(w0, hi - GROUP)
        dot(w0, e0, hi - GROUP)


def fine_sum(lo, hi, d, v, acc=None):
    return vmem_call(
        functools.partial(fine_kernel, lo, hi, acc is None),
        [jax.ShapeDtypeStruct((240, 256), f32)],
        [pltpu.VMEM((GROUP * 2816, 256), bf16)] * 2
        + [pltpu.VMEM((GROUP, 2, 480, 256), bf16)] * 2
        + [pltpu.VMEM((2, 20, 48, 128), f32)],
        "fine_sum",
        (d, v) if acc is None else (d, v, acc),
        flops=(hi - lo) * 2 * 240 * 2816 * 256,
        limit=20,
    )[0]


def spread_kernel(where_ref, recv_ref, mx_ref, own_ref, next_ref, near_ref, out_ref, buf, tail):
    even_x = even(where_ref[0])
    start = 10 * where_ref[0]
    halves = [mx_ref[h, pl.ds(start, 16), :] for h in range(2)]
    lane = lax.broadcasted_iota(jnp.int32, (16, 128), 1) % 8
    rows = [jnp.concatenate(halves, axis=1)]
    for x in range(5):
        at = 5 if x < 4 else 6
        moved = [jnp.where(lane == at, pltpu.roll(h, at - x, 1), 0.0) for h in halves]
        rows.append(jnp.concatenate(moved, axis=1))
    coarse = recv_ref[...].reshape(8 * recv_ref.shape[0], 128)
    value = two_part_dot(jnp.concatenate(rows, axis=0), coarse)
    last = value[80:96, 0:32]
    for x in range(4):
        last = last + value[16 * x + 16 : 16 * x + 32, 32 * x : 32 * x + 32]
    tail[...] = jnp.concatenate([last, jnp.zeros((16, 96), f32)], axis=1)
    last = tail[pl.ds(0, 4, stride=4), :]
    for k in range(1, 4):
        last = last + pltpu.roll(tail[pl.ds(k, 4, stride=4), :], 32 * k, 1)
    for n in range(5):
        near, other = near_ref[n].astype(f32), next_ref[n].astype(f32)
        buf[33 * n : 33 * n + 8, :] = jnp.where(even_x, other, near)[1:9]
        buf[33 * n + 8 : 33 * n + 24, :] = own_ref[n].astype(f32)
        buf[33 * n + 24 : 33 * n + 33, :] = jnp.where(even_x, near, other)
    for at, part in ((165, last), (176, value[0:16])):
        rows = part.shape[0]
        high = part.astype(bf16).astype(f32)
        buf[at : at + rows, :] = high
        buf[at + rows : at + 2 * rows, :] = part - high
    buf[173:176, :] = jnp.zeros((3, 128), f32)
    packed = buf[...].astype(bf16)
    for k in range(out_ref.shape[0]):
        out_ref[k] = packed


def final_kernel(
    where_ref, recv_ref, my_ref, mz_ref, near_ref, far_ref, fine_ref, out_ref,
    cells, w0, w1, acc, moved, wide, line, tail,
):
    index_x = where_ref[0]
    index_y = where_ref[1]
    count = recv_ref.shape[0]
    cells[:, 32:40, :] = jnp.zeros((17, 8, 128), f32)
    for step in range(-2, 3):
        source = index_y + step
        inside = (source >= 0) & (source < count)
        got = recv_ref[jnp.clip(source, 0, count - 1), 0:176, :].astype(f32)
        line[...] = jnp.where(inside, got, 0.0)
        for p in range(5):
            n = 5 * step + 6 + p
            if 0 <= n < 17:
                cells[n, 0:33, :] = line[33 * p : 33 * p + 33, :]

    r, c = iota2((128, 128))
    mask = jnp.abs(r % 64 - c % 64) <= REACH

    def band_rows(w, a, at):
        base = TAPS * TAPS + a * TAPS
        for j in range(11):
            same = near_ref[pl.ds(base + 2 * j, 1), :]
            upper = same
            lower = same
            if j > 0:
                upper = same + far_ref[pl.ds(base + 2 * j - 1, 1), :]
            if j < 10:
                lower = same + far_ref[pl.ds(base + 2 * j + 1, 1), :]
            upper = pltpu.roll(jnp.broadcast_to(upper, (64, 128)), 0, 1, stride=1, stride_axis=0)
            lower = pltpu.roll(jnp.broadcast_to(lower, (64, 128)), 64, 1, stride=1, stride_axis=0)
            band = jnp.where(mask, jnp.concatenate([upper, lower], axis=0), 0.0).astype(bf16)
            w[at + 128 * j : at + 128 * j + 128, :] = band

    def build(w, a):
        for k in range(3):
            band_rows(w, a + k, 1408 * k)

    def dot(w, a):
        rows = []
        for k in range(3):
            part = [cells[n, pl.ds(a + k, 16), :].astype(bf16) for n in range(17)]
            rows.append([jnp.concatenate(part[g : g + 11], axis=1) for g in range(7)])
        lhs = jnp.concatenate(
            [jnp.concatenate([rows[k][g] for k in range(3)], axis=1) for g in range(7)], axis=0
        )
        acc[...] += jnp.dot(lhs, w[...], preferred_element_type=f32)

    acc[...] = jnp.zeros((112, 128), f32)
    build(w0, 0)

    def step(t, _):
        a = 6 * t
        build(w1, a + 3)
        dot(w0, a)
        build(w0, a + 6)
        dot(w1, a + 3)
        return 0

    lax.fori_loop(0, 3, step, 0)
    dot(w0, 18)

    start = 10 * index_y
    sums = [[None] * 14, [None] * 14]
    for k in range(count):
        main = recv_ref[k, 176:192, :].astype(f32) + recv_ref[k, 192:208, :].astype(f32)
        last = recv_ref[k, 160:176, :].astype(f32)
        last = last[5:9] + last[9:13]
        tail[k, pl.ds(0, 4, stride=4), :] = last
        for r in range(1, 4):
            tail[k, pl.ds(r, 4, stride=4), :] = pltpu.roll(last, 128 - 32 * r, 1)
        for h, value in ((0, main), (1, tail[k])):
            rows_y = my_ref[2 * k + h, pl.ds(start, 16), :]
            for y in range(14):
                term = value * rows_y[y : y + 1, :]
                sums[h][y] = term if k == 0 else sums[h][y] + term
    rows = [
        jnp.concatenate([sums[h][2 * n + p] for p in range(2) for h in range(2)], axis=1)
        for n in range(7)
    ]
    top = two_part_dot(jnp.concatenate(rows, axis=0), mz_ref[...])
    total = acc[...] + top
    r, c = iota2((112, 128))
    cell_x = 10 * index_x - 1 + r % 16
    cell_y = 10 * index_y - 2 + 2 * (r // 16) + c // 64
    inside = (cell_x >= 0) & (cell_x < 320) & (cell_y >= 0) & (cell_y < 80)
    total = jnp.where(inside, total, 0.0)
    r, c = iota2((128, 256))
    up_z = jnp.where(r // 64 == c // 128, weight(c % 128 - 2 * (r % 64)), 0.0)
    wide[...] = exact_dot(total, up_z)

    def middle_y(y):
        n, par = (y + 2) // 2, y % 2
        return wide[16 * n : 16 * n + 16, 128 * par : 128 * par + 128]

    for y in range(20):
        m = y // 2
        if y % 2 == 0:
            value = middle_y(m)
        else:
            value = 0.5625 * (middle_y(m) + middle_y(m + 1)) - 0.0625 * (
                middle_y(m - 1) + middle_y(m + 2)
            )
        moved[16 * y : 16 * y + 16, :] = value
    planes = [moved[pl.ds(k, 20, stride=16), :] for k in range(13)]
    for x in range(20):
        m = x // 2
        if x % 2 == 0:
            value = planes[m + 1]
        else:
            value = 0.5625 * (planes[m + 1] + planes[m + 2]) - 0.0625 * (planes[m] + planes[m + 3])
        out_ref[x] = value + fine_ref[24 * m : 24 * m + 20, 128 * (x % 2) : 128 * (x % 2) + 128]


def swap(first, second, axis):
    count = lax.axis_size(axis)
    pairs = [(k, k + 1) for k in range(0, count - 1, 2)]
    others = [(k, k + 1) for k in range(1, count - 1, 2)]

    def both(ends):
        return ends + [(b, a) for a, b in ends]

    second = lax.ppermute(second, axis, both(others))
    return lax.ppermute(first, axis, both(pairs)), second


def per_device(charges, kernels):
    count_x = lax.axis_size("gx")
    count_y = lax.axis_size("gy")
    where = jnp.stack([lax.axis_index("gx"), lax.axis_index("gy")]).astype(jnp.int32)
    spread = charges.shape[0] * count_x / 16.0
    shape = jax.ShapeDtypeStruct
    low, high = charges[:10], charges[10:]
    even_x = even(lax.axis_index("gx"))
    near_x, next_x = swap(jnp.where(even_x, high, low), jnp.where(even_x, low, high), "gx")
    scratch = [pltpu.VMEM((20, 24, 128), f32), pltpu.VMEM((2, 200, 128), f32)]
    own = vmem_call(
        rim_own_kernel,
        [shape((2, 200, 128), f32)],
        scratch,
        "rim_own",
        (where, charges),
        smem=1,
        flops=1 << 20,
    )[0]
    first, second = vmem_call(
        rim_kernel,
        [shape((400, 128), bf16)] * 2,
        scratch,
        "rim",
        (where, own, near_x, next_x),
        smem=1,
    )
    first, second, kernels = lax.optimization_barrier((first, second, kernels))
    near, far = (
        jnp.dot(kernels.reshape(-1, TAPS), jnp.asarray(m, bf16), preferred_element_type=f32)
        for m in spots_np()
    )
    near_y, next_y = swap(first, second, "gy")
    next_y, near_y, near, far = lax.optimization_barrier((next_y, near_y, near, far))
    d, second, first, own, coarse = vmem_call(
        restrict_kernel,
        [
            shape((40, 40, 128), bf16),
            shape((5, 9, 128), bf16),
            shape((5, 9, 128), bf16),
            shape((5, 16, 128), bf16),
            shape((count_x, 8, 128), f32),
        ],
        [
            pltpu.VMEM((2, 20, 48, 128), f32),
            pltpu.VMEM((2, 400, 128), f32),
            pltpu.VMEM((2, 10, 24, 128), f32),
            pltpu.VMEM((16, 48, 128), f32),
            pltpu.VMEM((256, 128), f32),
            pltpu.VMEM((9, 24, 128), f32),
        ],
        "restrict",
        (where, charges, near_x, next_x, next_y, near_y),
        smem=1,
    )
    near_m, next_m = swap(first, second, "gx")
    coarse = lax.all_to_all(coarse, "gx", 0, 0)
    near, near_m = lax.optimization_barrier((near, near_m))
    fine = fine_sum(0, SPLIT, d, near)
    coarse, fine = lax.optimization_barrier((coarse, fine))
    parts = vmem_call(
        spread_kernel,
        [shape((count_y, 208, 128), bf16)],
        [pltpu.VMEM((208, 128), f32), pltpu.VMEM((16, 128), f32)],
        "spread",
        (where, coarse, jnp.asarray(matrix_x_np(spread)), own, next_m, near_m),
        smem=1,
    )[0]
    parts, near = lax.optimization_barrier((parts, near))
    parts = lax.all_to_all(parts, "gy", 0, 0)
    fine = fine_sum(SPLIT, TAPS, d, near, fine)
    return vmem_call(
        final_kernel,
        [shape((20, 20, 128), f32)],
        [
            pltpu.VMEM((17, 40, 128), f32),
            pltpu.VMEM((4224, 128), bf16),
            pltpu.VMEM((4224, 128), bf16),
            pltpu.VMEM((112, 128), f32),
            pltpu.VMEM((320, 128), f32),
            pltpu.VMEM((112, 256), f32),
            pltpu.VMEM((176, 128), f32),
            pltpu.VMEM((count_y, 16, 128), f32),
        ],
        "final",
        (
            where,
            parts,
            jnp.asarray(matrix_y_np(spread)),
            jnp.asarray(matrix_z_np(spread)),
            near,
            far,
            fine,
        ),
        smem=1,
    )[0]


def solution(mesh):
    return jax.shard_map(
        per_device,
        mesh=mesh,
        in_specs=(P("gx", "gy", None), P()),
        out_specs=P("gx", "gy", None),
        check_vma=False,
    )
```

```python
import functools
import numpy as np
import jax
import jax.numpy as jnp
from jax import lax
from jax.experimental import pallas as pl
from jax.experimental.pallas import tpu as pltpu
from jax.sharding import PartitionSpec as P

f32 = jnp.float32
bf16 = jnp.bfloat16
spread_norm = 1.2533141
REACH = 10
TAPS = 21
GROUP = 3
SPLIT = 6


def weight_np(offset):
    d = np.abs(offset)
    return np.where(d == 0, 1.0, np.where(d == 1, 0.5625, np.where(d == 3, -0.0625, 0.0)))


def top_matrix_np(n, spread):
    prolong = weight_np(np.arange(2 * n)[:, None] - 2 * np.arange(n)[None, :])
    offset = (np.arange(n)[:, None] - np.arange(n)[None, :]) / spread
    return prolong @ (np.exp(-offset * offset) / np.sqrt(spread * spread_norm))


def lane_tiles(m):
    return m.reshape(m.shape[0], -1, 128).transpose(1, 0, 2).astype(np.float32)


def matrix_x_np(spread):
    m = top_matrix_np(160, spread).reshape(320, 32, 5)
    out = np.zeros((328, 32, 8))
    out[1:321, :, :5] = m
    return lane_tiles(out.reshape(328, 256))


def matrix_y_np(spread):
    m = top_matrix_np(40, spread).reshape(80, 8, 5)
    out = np.zeros((88, 8, 8))
    out[2:82, :, :5] = m
    return lane_tiles(np.repeat(out.reshape(88, 64), 32, axis=1))


def matrix_z_np(spread):
    m = top_matrix_np(32, spread).T
    out = np.zeros((2, 8, 32, 2, 64))
    for par in range(2):
        out[par, :, :, par, :] = m[None]
    return out.reshape(512, 128).astype(np.float32)


def spots_np():
    taps = np.arange(TAPS)[:, None]
    lanes = np.arange(128)[None, :]
    near = lanes == (REACH - taps) % 128
    far = lanes == (64 + REACH - taps) % 128
    return near, far


def weight(d):
    d = jnp.abs(d)
    return jnp.where(d == 0, 1.0, jnp.where(d == 1, 0.5625, jnp.where(d == 3, -0.0625, 0.0))).astype(f32)


def exact_dot(rows, weights):
    count = rows.shape[0]
    high = rows.astype(bf16)
    rest = rows - high.astype(f32)
    middle = rest.astype(bf16)
    low = (rest - middle.astype(f32)).astype(bf16)
    out = jnp.dot(
        jnp.concatenate([high, middle, low], axis=0),
        weights.astype(bf16),
        preferred_element_type=f32,
    )
    return out[0:count] + (out[count : 2 * count] + out[2 * count :])


def parts_of(value):
    high = value.astype(bf16)
    return high, (value - high.astype(f32)).astype(bf16)


def two_part_dot(rows, weights):
    high, low = parts_of(rows)
    w_high, w_low = parts_of(weights)
    return jnp.dot(
        jnp.concatenate([high, high, low], axis=1),
        jnp.concatenate([w_high, w_low, w_high], axis=0),
        preferred_element_type=f32,
    )


def iota2(shape):
    return (lax.broadcasted_iota(jnp.int32, shape, 0), lax.broadcasted_iota(jnp.int32, shape, 1))


def vmem_call(body, out_shape, scratch, name, args, flops=0, limit=8):
    def spec(space):
        return pl.BlockSpec(memory_space=space)

    return pl.pallas_call(
        body,
        out_shape=out_shape,
        in_specs=[spec(pltpu.VMEM)] * len(args),
        out_specs=[spec(pltpu.VMEM)] * len(out_shape),
        scratch_shapes=scratch,
        compiler_params=pltpu.CompilerParams(vmem_limit_bytes=limit << 20),
        cost_estimate=pl.CostEstimate(flops=flops, bytes_accessed=1 << 16, transcendentals=0),
        name=name,
    )(*args)


def even(index):
    return index % 2 == 0


def rim_rows(wide, dense, count):
    start = jnp.where(even(lax.axis_index("gy")), 10, 0)
    for x in range(count):
        dense[0, 10 * x : 10 * x + 10, :] = wide[x, pl.ds(start, 10), :]
        dense[1, 10 * x : 10 * x + 10, :] = wide[x, pl.ds(10 - start, 10), :]


def rim_own_kernel(blk_ref, out_ref, wide, dense):
    wide[:, 0:20, :] = blk_ref[...].astype(f32)
    rim_rows(wide, dense, 20)
    out_ref[...] = dense[...]


def rim_kernel(own_ref, near_ref, next_ref, first_ref, second_ref, wide, dense):
    even_x = even(lax.axis_index("gx"))
    wide[pl.ds(jnp.where(even_x, 10, 0), 10), 0:20, :] = near_ref[...].astype(f32)
    wide[pl.ds(jnp.where(even_x, 0, 10), 10), 0:20, :] = next_ref[...].astype(f32)
    rim_rows(wide, dense, 20)
    for k, out_ref in enumerate((first_ref, second_ref)):
        out_ref[...] = jnp.concatenate([own_ref[k], dense[k]], axis=0).astype(bf16)


def restrict_kernel(
    blk_ref, near_x_ref, next_x_ref, next_y_ref, near_y_ref,
    d_out_ref, second_ref, first_ref, own_ref, out_ref,
    d_ref, dense, sides, planes, cells, mid,
):
    even_x = even(lax.axis_index("gx"))
    even_y = even(lax.axis_index("gy"))
    upper = jnp.where(even_y, 1, 0)
    dense[upper] = near_y_ref[...].astype(f32)
    dense[1 - upper] = next_y_ref[...].astype(f32)
    upper = jnp.where(even_x, 1, 0)
    sides[upper, :, 0:20, :] = near_x_ref[...].astype(f32)
    sides[1 - upper, :, 0:20, :] = next_x_ref[...].astype(f32)
    for x in range(40):
        p, i = x % 2, x // 2
        at = 10 * (x - 10 if 10 <= x < 30 else x + 20 if x < 10 else x)
        d_ref[p, i, 0:10, :] = dense[0, at : at + 10, :]
        d_ref[p, i, 30:40, :] = dense[1, at : at + 10, :]
        if 10 <= x < 30:
            centre = blk_ref[x - 10].astype(f32)
        else:
            centre = sides[x // 30, x % 30, 0:20, :]
        d_ref[p, i, 10:30, :] = centre
        d_out_ref[x] = d_ref[p, i, 0:40, :].astype(bf16)

    def fine(x):
        return d_ref[x % 2, x // 2]

    for i in range(16):
        c = 2 * i + 4
        planes[i] = (
            fine(c) + 0.5625 * (fine(c - 1) + fine(c + 1)) - 0.0625 * (fine(c - 3) + fine(c + 3))
        )
    for i in range(16):
        def tap(o):
            return planes[i, pl.ds(4 + o, 16, stride=2), :]
        cells[16 * i : 16 * i + 16, :] = (
            tap(0) + 0.5625 * (tap(-1) + tap(1)) - 0.0625 * (tap(-3) + tap(3))
        )
    zero = jnp.zeros((16, 128), f32)
    rows = []
    for n in range(9):
        pair = []
        for y in (2 * n - 4, 2 * n - 3):
            inside = -3 <= y <= 12
            pair.append(cells[pl.ds(y + 3, 16, stride=16), :] if inside else zero)
        rows.append(jnp.concatenate(pair, axis=1))
    r, c = iota2((256, 128))
    down_z = jnp.where(r // 128 == c // 64, weight(r % 128 - 2 * (c % 64)), 0.0)
    value = exact_dot(jnp.concatenate(rows, axis=0), down_z)
    r, c = iota2((144, 128))
    cell_x = 10 * lax.axis_index("gx") - 3 + r % 16
    cell_y = 10 * lax.axis_index("gy") - 4 + 2 * (r // 16) + c // 64
    inside = (cell_x >= 0) & (cell_x < 320) & (cell_y >= 0) & (cell_y < 80)
    value = jnp.where(inside, value, 0.0).astype(bf16).astype(f32)
    for n in range(9):
        mid[n, 0:16, :] = value[16 * n : 16 * n + 16]
        mid[n, 16:24, :] = jnp.zeros((8, 128), f32)
    for n in range(5):
        right, left = mid[n + 2, 1:10, :], mid[n + 2, 6:15, :]
        first_ref[n] = jnp.where(even_x, right, left).astype(bf16)
        second_ref[n] = jnp.where(even_x, left, right).astype(bf16)
        own_ref[n] = mid[n + 2, 0:16, :].astype(bf16)

    lane = lax.broadcasted_iota(jnp.int32, (1, 128), 1)
    odd = lane >= 64
    weight_0 = jnp.where(odd, 0.5625, 1.0)
    weight_1 = jnp.where(odd, 0.5625, 0.0)
    weight_3 = jnp.where(odd, -0.0625, 0.0)
    r, c = iota2((128, 32))
    down_z = weight(r % 64 - 2 * c)
    sums = []
    for y in range(5):
        n = y + 2
        def tap(o):
            def part(k):
                return mid[k, pl.ds(3 + o, 8, stride=2), :]
            return (
                weight_0 * part(n) + weight_1 * part(n - 1) + weight_3 * (part(n - 2) + part(n + 1))
            )
        sums.append(tap(0) + 0.5625 * (tap(-1) + tap(1)) - 0.0625 * (tap(-3) + tap(3)))
    out = exact_dot(jnp.concatenate(sums, axis=0), down_z)
    main = jnp.concatenate([out[8 * y : 8 * y + 8] for y in range(4)], axis=1)[0:5]
    last = jnp.concatenate([out[32 + x : 33 + x] for x in range(4)], axis=1)
    rest = jnp.concatenate([out[36:37], jnp.zeros((1, 96), f32)], axis=1)
    row = jnp.concatenate([main, last, rest, jnp.zeros((1, 128), f32)], axis=0)
    for k in range(out_ref.shape[0]):
        out_ref[k] = row


def fine_kernel(lo, hi, first, d_in_ref, v_ref, *refs):
    if first:
        out_ref, w0, w1, e0, e1, d_ref = refs
    else:
        acc_ref, out_ref, w0, w1, e0, e1, d_ref = refs
    for x in range(40):
        d_ref[x % 2, x // 2, 0:40, :] = d_in_ref[x].astype(f32)
        d_ref[x % 2, x // 2, 40:48, :] = jnp.zeros((8, 128), f32)
    r, c = iota2((128, 128))
    mask = jnp.abs(r - c) <= REACH
    zero = jnp.zeros((128, 128), bf16)
    for w in (w0, w1):
        for k in range(GROUP):
            w[2816 * k : 2816 * k + 128, 128:256] = zero
            w[2816 * k + 2688 : 2816 * k + 2816, 0:128] = zero

    def build(w, start):
        for k in range(GROUP):
            for a in range(TAPS):
                line = jnp.broadcast_to(v_ref[pl.ds(a * TAPS + start + k, 1), :], (128, 128))
                line = pltpu.roll(line, 0, 1, stride=1, stride_axis=0)
                band = jnp.where(mask, line, 0.0).astype(bf16)
                at = 2816 * k + 128 * a
                w[at : at + 128, 0:128] = band
                w[at + 128 : at + 256, 128:256] = band

    def dot(w, e, start):
        tiles = []
        for k in range(GROUP):
            for p in range(2):
                for q in range(10):
                    part = d_ref[p, 2 * q : 2 * q + 2, pl.ds(start + k, 24), :].reshape(48, 128)
                    e[k, 0, 48 * q : 48 * q + 48, p * 128 : (p + 1) * 128] = part.astype(bf16)
                for q in range(9):
                    part = d_ref[p, 2 * q + 1 : 2 * q + 3, pl.ds(start + k, 24), :].reshape(48, 128)
                    e[k, 1, 48 * q : 48 * q + 48, p * 128 : (p + 1) * 128] = part.astype(bf16)
            tiles += [
                e[k, m % 2, 24 * (m - m % 2) : 24 * (m - m % 2) + 240, :] for m in range(11)
            ]
        lhs = jnp.concatenate(tiles, axis=1)
        out_ref[...] += jnp.dot(lhs, w[...], preferred_element_type=f32)

    out_ref[...] = jnp.zeros((240, 256), f32) if first else acc_ref[...]

    def step(t, _):
        b = lo + 2 * GROUP * t
        build(w0, b)
        dot(w0, e0, b)
        build(w1, b + GROUP)
        dot(w1, e1, b + GROUP)
        return 0

    groups = (hi - lo) // GROUP
    lax.fori_loop(0, groups // 2, step, 0)
    if groups % 2:
        build(w0, hi - GROUP)
        dot(w0, e0, hi - GROUP)


def fine_sum(lo, hi, d, v, acc=None):
    return vmem_call(
        functools.partial(fine_kernel, lo, hi, acc is None),
        [jax.ShapeDtypeStruct((240, 256), f32)],
        [pltpu.VMEM((GROUP * 2816, 256), bf16)] * 2
        + [pltpu.VMEM((GROUP, 2, 480, 256), bf16)] * 2
        + [pltpu.VMEM((2, 20, 48, 128), f32)],
        "fine_sum",
        (d, v) if acc is None else (d, v, acc),
        flops=(hi - lo) * 2 * 240 * 2816 * 256,
        limit=20,
    )[0]


def spread_kernel(recv_ref, mx_ref, own_ref, next_ref, near_ref, out_ref, buf, tail):
    even_x = even(lax.axis_index("gx"))
    start = 10 * lax.axis_index("gx")
    halves = [mx_ref[h, pl.ds(start, 16), :] for h in range(2)]
    lane = lax.broadcasted_iota(jnp.int32, (16, 128), 1) % 8
    rows = [jnp.concatenate(halves, axis=1)]
    for x in range(5):
        at = 5 if x < 4 else 6
        moved = [jnp.where(lane == at, pltpu.roll(h, at - x, 1), 0.0) for h in halves]
        rows.append(jnp.concatenate(moved, axis=1))
    coarse = recv_ref[...].reshape(8 * recv_ref.shape[0], 128)
    value = two_part_dot(jnp.concatenate(rows, axis=0), coarse)
    last = value[80:96, 0:32]
    for x in range(4):
        last = last + value[16 * x + 16 : 16 * x + 32, 32 * x : 32 * x + 32]
    tail[...] = jnp.concatenate([last, jnp.zeros((16, 96), f32)], axis=1)
    last = tail[pl.ds(0, 4, stride=4), :]
    for k in range(1, 4):
        last = last + pltpu.roll(tail[pl.ds(k, 4, stride=4), :], 32 * k, 1)
    for n in range(5):
        near, other = near_ref[n].astype(f32), next_ref[n].astype(f32)
        buf[33 * n : 33 * n + 8, :] = jnp.where(even_x, other, near)[1:9]
        buf[33 * n + 8 : 33 * n + 24, :] = own_ref[n].astype(f32)
        buf[33 * n + 24 : 33 * n + 33, :] = jnp.where(even_x, near, other)
    for at, part in ((165, last), (176, value[0:16])):
        rows = part.shape[0]
        high = part.astype(bf16).astype(f32)
        buf[at : at + rows, :] = high
        buf[at + rows : at + 2 * rows, :] = part - high
    buf[173:176, :] = jnp.zeros((3, 128), f32)
    packed = buf[...].astype(bf16)
    for k in range(out_ref.shape[0]):
        out_ref[k] = packed


def final_kernel(
    recv_ref, my_ref, mz_ref, near_ref, far_ref, fine_ref, out_ref,
    cells, w0, w1, acc, moved, wide, line, tail,
):
    index_x = lax.axis_index("gx")
    index_y = lax.axis_index("gy")
    count = recv_ref.shape[0]
    cells[:, 32:40, :] = jnp.zeros((17, 8, 128), f32)
    for step in range(-2, 3):
        source = index_y + step
        inside = (source >= 0) & (source < count)
        got = recv_ref[jnp.clip(source, 0, count - 1), 0:176, :].astype(f32)
        line[...] = jnp.where(inside, got, 0.0)
        for p in range(5):
            n = 5 * step + 6 + p
            if 0 <= n < 17:
                cells[n, 0:33, :] = line[33 * p : 33 * p + 33, :]

    r, c = iota2((128, 128))
    mask = jnp.abs(r % 64 - c % 64) <= REACH

    def band_rows(w, a, at):
        base = TAPS * TAPS + a * TAPS
        for j in range(11):
            same = near_ref[pl.ds(base + 2 * j, 1), :]
            upper = same
            lower = same
            if j > 0:
                upper = same + far_ref[pl.ds(base + 2 * j - 1, 1), :]
            if j < 10:
                lower = same + far_ref[pl.ds(base + 2 * j + 1, 1), :]
            upper = pltpu.roll(jnp.broadcast_to(upper, (64, 128)), 0, 1, stride=1, stride_axis=0)
            lower = pltpu.roll(jnp.broadcast_to(lower, (64, 128)), 64, 1, stride=1, stride_axis=0)
            band = jnp.where(mask, jnp.concatenate([upper, lower], axis=0), 0.0).astype(bf16)
            w[at + 128 * j : at + 128 * j + 128, :] = band

    def build(w, a):
        for k in range(3):
            band_rows(w, a + k, 1408 * k)

    def dot(w, a):
        rows = []
        for k in range(3):
            part = [cells[n, pl.ds(a + k, 16), :].astype(bf16) for n in range(17)]
            rows.append([jnp.concatenate(part[g : g + 11], axis=1) for g in range(7)])
        lhs = jnp.concatenate(
            [jnp.concatenate([rows[k][g] for k in range(3)], axis=1) for g in range(7)], axis=0
        )
        acc[...] += jnp.dot(lhs, w[...], preferred_element_type=f32)

    acc[...] = jnp.zeros((112, 128), f32)
    build(w0, 0)

    def step(t, _):
        a = 6 * t
        build(w1, a + 3)
        dot(w0, a)
        build(w0, a + 6)
        dot(w1, a + 3)
        return 0

    lax.fori_loop(0, 3, step, 0)
    dot(w0, 18)

    start = 10 * index_y
    sums = [[None] * 14, [None] * 14]
    for k in range(count):
        main = recv_ref[k, 176:192, :].astype(f32) + recv_ref[k, 192:208, :].astype(f32)
        last = recv_ref[k, 160:176, :].astype(f32)
        last = last[5:9] + last[9:13]
        tail[k, pl.ds(0, 4, stride=4), :] = last
        for r in range(1, 4):
            tail[k, pl.ds(r, 4, stride=4), :] = pltpu.roll(last, 128 - 32 * r, 1)
        for h, value in ((0, main), (1, tail[k])):
            rows_y = my_ref[2 * k + h, pl.ds(start, 16), :]
            for y in range(14):
                term = value * rows_y[y : y + 1, :]
                sums[h][y] = term if k == 0 else sums[h][y] + term
    rows = [
        jnp.concatenate([sums[h][2 * n + p] for p in range(2) for h in range(2)], axis=1)
        for n in range(7)
    ]
    top = two_part_dot(jnp.concatenate(rows, axis=0), mz_ref[...])
    total = acc[...] + top
    r, c = iota2((112, 128))
    cell_x = 10 * index_x - 1 + r % 16
    cell_y = 10 * index_y - 2 + 2 * (r // 16) + c // 64
    inside = (cell_x >= 0) & (cell_x < 320) & (cell_y >= 0) & (cell_y < 80)
    total = jnp.where(inside, total, 0.0)
    r, c = iota2((128, 256))
    up_z = jnp.where(r // 64 == c // 128, weight(c % 128 - 2 * (r % 64)), 0.0)
    wide[...] = exact_dot(total, up_z)

    def middle_y(y):
        n, par = (y + 2) // 2, y % 2
        return wide[16 * n : 16 * n + 16, 128 * par : 128 * par + 128]

    for y in range(20):
        m = y // 2
        if y % 2 == 0:
            value = middle_y(m)
        else:
            value = 0.5625 * (middle_y(m) + middle_y(m + 1)) - 0.0625 * (
                middle_y(m - 1) + middle_y(m + 2)
            )
        moved[16 * y : 16 * y + 16, :] = value
    planes = [moved[pl.ds(k, 20, stride=16), :] for k in range(13)]
    for x in range(20):
        m = x // 2
        if x % 2 == 0:
            value = planes[m + 1]
        else:
            value = 0.5625 * (planes[m + 1] + planes[m + 2]) - 0.0625 * (planes[m] + planes[m + 3])
        out_ref[x] = value + fine_ref[24 * m : 24 * m + 20, 128 * (x % 2) : 128 * (x % 2) + 128]


def swap(first, second, axis):
    count = lax.axis_size(axis)
    pairs = [(k, k + 1) for k in range(0, count - 1, 2)]
    others = [(k, k + 1) for k in range(1, count - 1, 2)]

    def both(ends):
        return ends + [(b, a) for a, b in ends]

    second = lax.ppermute(second, axis, both(others))
    return lax.ppermute(first, axis, both(pairs)), second


def per_device(charges, kernels):
    count_x = lax.axis_size("gx")
    count_y = lax.axis_size("gy")
    spread = charges.shape[0] * count_x / 16.0
    shape = jax.ShapeDtypeStruct
    low, high = charges[:10], charges[10:]
    even_x = even(lax.axis_index("gx"))
    near_x, next_x = swap(jnp.where(even_x, high, low), jnp.where(even_x, low, high), "gx")
    scratch = [pltpu.VMEM((20, 24, 128), f32), pltpu.VMEM((2, 200, 128), f32)]
    own = vmem_call(
        rim_own_kernel,
        [shape((2, 200, 128), f32)],
        scratch,
        "rim_own",
        (charges,),
        flops=1 << 20,
    )[0]
    first, second = vmem_call(
        rim_kernel,
        [shape((400, 128), bf16)] * 2,
        scratch,
        "rim",
        (own, near_x, next_x),
    )
    first, second, kernels = lax.optimization_barrier((first, second, kernels))
    near, far = (
        jnp.dot(kernels.reshape(-1, TAPS), jnp.asarray(m, bf16), preferred_element_type=f32)
        for m in spots_np()
    )
    near_y, next_y = swap(first, second, "gy")
    next_y, near_y, near, far = lax.optimization_barrier((next_y, near_y, near, far))
    d, second, first, own, coarse = vmem_call(
        restrict_kernel,
        [
            shape((40, 40, 128), bf16),
            shape((5, 9, 128), bf16),
            shape((5, 9, 128), bf16),
            shape((5, 16, 128), bf16),
            shape((count_x, 8, 128), f32),
        ],
        [
            pltpu.VMEM((2, 20, 48, 128), f32),
            pltpu.VMEM((2, 400, 128), f32),
            pltpu.VMEM((2, 10, 24, 128), f32),
            pltpu.VMEM((16, 48, 128), f32),
            pltpu.VMEM((256, 128), f32),
            pltpu.VMEM((9, 24, 128), f32),
        ],
        "restrict",
        (charges, near_x, next_x, next_y, near_y),
    )
    near_m, next_m = swap(first, second, "gx")
    coarse = lax.all_to_all(coarse, "gx", 0, 0)
    near, near_m = lax.optimization_barrier((near, near_m))
    fine = fine_sum(0, SPLIT, d, near)
    coarse, fine = lax.optimization_barrier((coarse, fine))
    parts = vmem_call(
        spread_kernel,
        [shape((count_y, 208, 128), bf16)],
        [pltpu.VMEM((208, 128), f32), pltpu.VMEM((16, 128), f32)],
        "spread",
        (coarse, jnp.asarray(matrix_x_np(spread)), own, next_m, near_m),
    )[0]
    parts, near = lax.optimization_barrier((parts, near))
    parts = lax.all_to_all(parts, "gy", 0, 0)
    fine = fine_sum(SPLIT, TAPS, d, near, fine)
    return vmem_call(
        final_kernel,
        [shape((20, 20, 128), f32)],
        [
            pltpu.VMEM((17, 40, 128), f32),
            pltpu.VMEM((4224, 128), bf16),
            pltpu.VMEM((4224, 128), bf16),
            pltpu.VMEM((112, 128), f32),
            pltpu.VMEM((320, 128), f32),
            pltpu.VMEM((112, 256), f32),
            pltpu.VMEM((176, 128), f32),
            pltpu.VMEM((count_y, 16, 128), f32),
        ],
        "final",
        (
            parts,
            jnp.asarray(matrix_y_np(spread)),
            jnp.asarray(matrix_z_np(spread)),
            near,
            far,
            fine,
        ),
    )[0]


def solution(mesh):
    return jax.shard_map(
        per_device,
        mesh=mesh,
        in_specs=(P("gx", "gy", None), P()),
        out_specs=P("gx", "gy", None),
        check_vma=False,
    )
```

```python
import functools
import numpy as np
import jax
import jax.numpy as jnp
from jax import lax
from jax.experimental import pallas as pl
from jax.experimental.pallas import tpu as pltpu
from jax.sharding import PartitionSpec as P

f32 = jnp.float32
bf16 = jnp.bfloat16
spread_norm = 1.2533141
REACH = 10
TAPS = 21
GROUP = 3
SPLIT = 6


def weight_np(offset):
    d = np.abs(offset)
    return np.where(d == 0, 1.0, np.where(d == 1, 0.5625, np.where(d == 3, -0.0625, 0.0)))


def top_matrix_np(n, spread):
    prolong = weight_np(np.arange(2 * n)[:, None] - 2 * np.arange(n)[None, :])
    offset = (np.arange(n)[:, None] - np.arange(n)[None, :]) / spread
    return prolong @ (np.exp(-offset * offset) / np.sqrt(spread * spread_norm))


def lane_tiles(m):
    return m.reshape(m.shape[0], -1, 128).transpose(1, 0, 2).astype(np.float32)


def matrix_x_np(spread):
    m = top_matrix_np(160, spread).reshape(320, 32, 5)
    out = np.zeros((328, 32, 8))
    out[1:321, :, :5] = m
    return lane_tiles(out.reshape(328, 256))


def matrix_y_np(spread):
    m = top_matrix_np(40, spread).reshape(80, 8, 5)
    out = np.zeros((88, 8, 8))
    out[2:82, :, :5] = m
    return lane_tiles(np.repeat(out.reshape(88, 64), 32, axis=1))


def matrix_z_np(spread):
    m = top_matrix_np(32, spread).T
    out = np.zeros((2, 8, 32, 2, 64))
    for par in range(2):
        out[par, :, :, par, :] = m[None]
    return out.reshape(512, 128).astype(np.float32)


def spots_np():
    taps = np.arange(TAPS)[:, None]
    lanes = np.arange(128)[None, :]
    near = lanes == (REACH - taps) % 128
    far = lanes == (64 + REACH - taps) % 128
    return near, far


def weight(d):
    d = jnp.abs(d)
    return jnp.where(d == 0, 1.0, jnp.where(d == 1, 0.5625, jnp.where(d == 3, -0.0625, 0.0))).astype(f32)


def exact_dot(rows, weights):
    count = rows.shape[0]
    high = rows.astype(bf16)
    rest = rows - high.astype(f32)
    middle = rest.astype(bf16)
    low = (rest - middle.astype(f32)).astype(bf16)
    out = jnp.dot(
        jnp.concatenate([high, middle, low], axis=0),
        weights.astype(bf16),
        preferred_element_type=f32,
    )
    return out[0:count] + (out[count : 2 * count] + out[2 * count :])


def parts_of(value):
    high = value.astype(bf16)
    return high, (value - high.astype(f32)).astype(bf16)


def two_part_dot(rows, weights):
    high, low = parts_of(rows)
    w_high, w_low = parts_of(weights)
    return jnp.dot(
        jnp.concatenate([high, high, low], axis=1),
        jnp.concatenate([w_high, w_low, w_high], axis=0),
        preferred_element_type=f32,
    )


def iota2(shape):
    return (lax.broadcasted_iota(jnp.int32, shape, 0), lax.broadcasted_iota(jnp.int32, shape, 1))


def vmem_call(body, out_shape, scratch, name, args, flops=0, limit=8):
    def spec(space):
        return pl.BlockSpec(memory_space=space)

    return pl.pallas_call(
        body,
        out_shape=out_shape,
        in_specs=[spec(pltpu.VMEM)] * len(args),
        out_specs=[spec(pltpu.VMEM)] * len(out_shape),
        scratch_shapes=scratch,
        compiler_params=pltpu.CompilerParams(vmem_limit_bytes=limit << 20),
        cost_estimate=pl.CostEstimate(flops=flops, bytes_accessed=1 << 16, transcendentals=0),
        name=name,
    )(*args)


def even(index):
    return index % 2 == 0


def edges_kernel(blk_ref, first_ref, second_ref, wide, dense):
    wide[:, 0:20, :] = blk_ref[...].astype(f32)
    start = jnp.where(even(lax.axis_index("gx")), 10, 0)
    for x in range(10):
        dense[0, 20 * x : 20 * x + 20, :] = wide[start + x, 0:20, :]
        dense[1, 20 * x : 20 * x + 20, :] = wide[10 - start + x, 0:20, :]
    first_ref[...] = dense[0].astype(bf16)
    second_ref[...] = dense[1].astype(bf16)


def rim_rows(wide, dense, count):
    start = jnp.where(even(lax.axis_index("gy")), 10, 0)
    for x in range(count):
        dense[0, 10 * x : 10 * x + 10, :] = wide[x, pl.ds(start, 10), :]
        dense[1, 10 * x : 10 * x + 10, :] = wide[x, pl.ds(10 - start, 10), :]


def rim_own_kernel(blk_ref, out_ref, wide, dense):
    wide[:, 0:20, :] = blk_ref[...].astype(f32)
    rim_rows(wide, dense, 20)
    out_ref[...] = dense[...]


def rim_kernel(own_ref, next_ref, near_ref, first_ref, second_ref, wide, dense):
    even_x = even(lax.axis_index("gx"))
    start = jnp.where(even_x, 10, 0)
    dense[0] = near_ref[...].astype(f32)
    dense[1] = next_ref[...].astype(f32)
    for x in range(10):
        wide[start + x, 0:20, :] = dense[0, 20 * x : 20 * x + 20, :]
        wide[10 - start + x, 0:20, :] = dense[1, 20 * x : 20 * x + 20, :]
    rim_rows(wide, dense, 20)
    for k, out_ref in enumerate((first_ref, second_ref)):
        out_ref[...] = jnp.concatenate([own_ref[k], dense[k]], axis=0).astype(bf16)


def restrict_kernel(
    blk_ref, near_x_ref, next_x_ref, next_y_ref, near_y_ref,
    d_out_ref, second_ref, first_ref, own_ref, out_ref,
    d_ref, dense, sides, planes, cells, mid,
):
    even_x = even(lax.axis_index("gx"))
    even_y = even(lax.axis_index("gy"))
    upper = jnp.where(even_y, 1, 0)
    dense[upper] = near_y_ref[...].astype(f32)
    dense[1 - upper] = next_y_ref[...].astype(f32)
    upper = jnp.where(even_x, 1, 0)
    sides[upper] = near_x_ref[...].astype(f32)
    sides[1 - upper] = next_x_ref[...].astype(f32)
    for x in range(40):
        p, i = x % 2, x // 2
        at = 10 * (x - 10 if 10 <= x < 30 else x + 20 if x < 10 else x)
        d_ref[p, i, 0:10, :] = dense[0, at : at + 10, :]
        d_ref[p, i, 30:40, :] = dense[1, at : at + 10, :]
        if 10 <= x < 30:
            centre = blk_ref[x - 10].astype(f32)
        else:
            at = 20 * (x % 30)
            centre = sides[x // 30, at : at + 20, :]
        d_ref[p, i, 10:30, :] = centre
        d_out_ref[x] = d_ref[p, i, 0:40, :].astype(bf16)

    def fine(x):
        return d_ref[x % 2, x // 2]

    for i in range(16):
        c = 2 * i + 4
        planes[i] = (
            fine(c) + 0.5625 * (fine(c - 1) + fine(c + 1)) - 0.0625 * (fine(c - 3) + fine(c + 3))
        )
    for i in range(16):
        def tap(o):
            return planes[i, pl.ds(4 + o, 16, stride=2), :]
        cells[16 * i : 16 * i + 16, :] = (
            tap(0) + 0.5625 * (tap(-1) + tap(1)) - 0.0625 * (tap(-3) + tap(3))
        )
    zero = jnp.zeros((16, 128), f32)
    rows = []
    for n in range(9):
        pair = []
        for y in (2 * n - 4, 2 * n - 3):
            inside = -3 <= y <= 12
            pair.append(cells[pl.ds(y + 3, 16, stride=16), :] if inside else zero)
        rows.append(jnp.concatenate(pair, axis=1))
    r, c = iota2((256, 128))
    down_z = jnp.where(r // 128 == c // 64, weight(r % 128 - 2 * (c % 64)), 0.0)
    value = exact_dot(jnp.concatenate(rows, axis=0), down_z)
    r, c = iota2((144, 128))
    cell_x = 10 * lax.axis_index("gx") - 3 + r % 16
    cell_y = 10 * lax.axis_index("gy") - 4 + 2 * (r // 16) + c // 64
    inside = (cell_x >= 0) & (cell_x < 320) & (cell_y >= 0) & (cell_y < 80)
    value = jnp.where(inside, value, 0.0).astype(bf16).astype(f32)
    for n in range(9):
        mid[n, 0:16, :] = value[16 * n : 16 * n + 16]
        mid[n, 16:24, :] = jnp.zeros((8, 128), f32)
    for n in range(5):
        right, left = mid[n + 2, 1:10, :], mid[n + 2, 6:15, :]
        first_ref[n] = jnp.where(even_x, right, left).astype(bf16)
        second_ref[n] = jnp.where(even_x, left, right).astype(bf16)
        own_ref[n] = mid[n + 2, 0:16, :].astype(bf16)

    lane = lax.broadcasted_iota(jnp.int32, (1, 128), 1)
    odd = lane >= 64
    weight_0 = jnp.where(odd, 0.5625, 1.0)
    weight_1 = jnp.where(odd, 0.5625, 0.0)
    weight_3 = jnp.where(odd, -0.0625, 0.0)
    r, c = iota2((128, 32))
    down_z = weight(r % 64 - 2 * c)
    sums = []
    for y in range(5):
        n = y + 2
        def tap(o):
            def part(k):
                return mid[k, pl.ds(3 + o, 8, stride=2), :]
            return (
                weight_0 * part(n) + weight_1 * part(n - 1) + weight_3 * (part(n - 2) + part(n + 1))
            )
        sums.append(tap(0) + 0.5625 * (tap(-1) + tap(1)) - 0.0625 * (tap(-3) + tap(3)))
    out = exact_dot(jnp.concatenate(sums, axis=0), down_z)
    main = jnp.concatenate([out[8 * y : 8 * y + 8] for y in range(4)], axis=1)[0:5]
    last = jnp.concatenate([out[32 + x : 33 + x] for x in range(4)], axis=1)
    rest = jnp.concatenate([out[36:37], jnp.zeros((1, 96), f32)], axis=1)
    row = jnp.concatenate([main, last, rest, jnp.zeros((1, 128), f32)], axis=0)
    for k in range(out_ref.shape[0]):
        out_ref[k] = row


def fine_kernel(lo, hi, first, d_in_ref, v_ref, *refs):
    if first:
        out_ref, w0, w1, e0, e1, d_ref = refs
    else:
        acc_ref, out_ref, w0, w1, e0, e1, d_ref = refs
    for x in range(40):
        d_ref[x % 2, x // 2, 0:40, :] = d_in_ref[x].astype(f32)
        d_ref[x % 2, x // 2, 40:48, :] = jnp.zeros((8, 128), f32)
    r, c = iota2((128, 128))
    mask = jnp.abs(r - c) <= REACH
    zero = jnp.zeros((128, 128), bf16)
    for w in (w0, w1):
        for k in range(GROUP):
            w[2816 * k : 2816 * k + 128, 128:256] = zero
            w[2816 * k + 2688 : 2816 * k + 2816, 0:128] = zero

    def build(w, start):
        for k in range(GROUP):
            for a in range(TAPS):
                line = jnp.broadcast_to(v_ref[pl.ds(a * TAPS + start + k, 1), :], (128, 128))
                line = pltpu.roll(line, 0, 1, stride=1, stride_axis=0)
                band = jnp.where(mask, line, 0.0).astype(bf16)
                at = 2816 * k + 128 * a
                w[at : at + 128, 0:128] = band
                w[at + 128 : at + 256, 128:256] = band

    def dot(w, e, start):
        tiles = []
        for k in range(GROUP):
            for p in range(2):
                for q in range(10):
                    part = d_ref[p, 2 * q : 2 * q + 2, pl.ds(start + k, 24), :].reshape(48, 128)
                    e[k, 0, 48 * q : 48 * q + 48, p * 128 : (p + 1) * 128] = part.astype(bf16)
                for q in range(9):
                    part = d_ref[p, 2 * q + 1 : 2 * q + 3, pl.ds(start + k, 24), :].reshape(48, 128)
                    e[k, 1, 48 * q : 48 * q + 48, p * 128 : (p + 1) * 128] = part.astype(bf16)
            tiles += [
                e[k, m % 2, 24 * (m - m % 2) : 24 * (m - m % 2) + 240, :] for m in range(11)
            ]
        lhs = jnp.concatenate(tiles, axis=1)
        out_ref[...] += jnp.dot(lhs, w[...], preferred_element_type=f32)

    out_ref[...] = jnp.zeros((240, 256), f32) if first else acc_ref[...]

    def step(t, _):
        b = lo + 2 * GROUP * t
        build(w0, b)
        dot(w0, e0, b)
        build(w1, b + GROUP)
        dot(w1, e1, b + GROUP)
        return 0

    groups = (hi - lo) // GROUP
    lax.fori_loop(0, groups // 2, step, 0)
    if groups % 2:
        build(w0, hi - GROUP)
        dot(w0, e0, hi - GROUP)


def fine_sum(lo, hi, d, v, acc=None):
    return vmem_call(
        functools.partial(fine_kernel, lo, hi, acc is None),
        [jax.ShapeDtypeStruct((240, 256), f32)],
        [pltpu.VMEM((GROUP * 2816, 256), bf16)] * 2
        + [pltpu.VMEM((GROUP, 2, 480, 256), bf16)] * 2
        + [pltpu.VMEM((2, 20, 48, 128), f32)],
        "fine_sum",
        (d, v) if acc is None else (d, v, acc),
        flops=(hi - lo) * 2 * 240 * 2816 * 256,
        limit=20,
    )[0]


def spread_kernel(recv_ref, mx_ref, own_ref, next_ref, near_ref, out_ref, buf, tail):
    even_x = even(lax.axis_index("gx"))
    start = 10 * lax.axis_index("gx")
    halves = [mx_ref[h, pl.ds(start, 16), :] for h in range(2)]
    lane = lax.broadcasted_iota(jnp.int32, (16, 128), 1) % 8
    rows = [jnp.concatenate(halves, axis=1)]
    for x in range(5):
        at = 5 if x < 4 else 6
        moved = [jnp.where(lane == at, pltpu.roll(h, at - x, 1), 0.0) for h in halves]
        rows.append(jnp.concatenate(moved, axis=1))
    coarse = recv_ref[...].reshape(8 * recv_ref.shape[0], 128)
    value = two_part_dot(jnp.concatenate(rows, axis=0), coarse)
    last = value[80:96, 0:32]
    for x in range(4):
        last = last + value[16 * x + 16 : 16 * x + 32, 32 * x : 32 * x + 32]
    tail[...] = jnp.concatenate([last, jnp.zeros((16, 96), f32)], axis=1)
    last = tail[pl.ds(0, 4, stride=4), :]
    for k in range(1, 4):
        last = last + pltpu.roll(tail[pl.ds(k, 4, stride=4), :], 32 * k, 1)
    for n in range(5):
        near, other = near_ref[n].astype(f32), next_ref[n].astype(f32)
        buf[33 * n : 33 * n + 8, :] = jnp.where(even_x, other, near)[1:9]
        buf[33 * n + 8 : 33 * n + 24, :] = own_ref[n].astype(f32)
        buf[33 * n + 24 : 33 * n + 33, :] = jnp.where(even_x, near, other)
    for at, part in ((165, last), (176, value[0:16])):
        rows = part.shape[0]
        high = part.astype(bf16).astype(f32)
        buf[at : at + rows, :] = high
        buf[at + rows : at + 2 * rows, :] = part - high
    buf[173:176, :] = jnp.zeros((3, 128), f32)
    packed = buf[...].astype(bf16)
    for k in range(out_ref.shape[0]):
        out_ref[k] = packed


def final_kernel(
    recv_ref, my_ref, mz_ref, near_ref, far_ref, fine_ref, out_ref,
    cells, w0, w1, acc, moved, wide, line, tail,
):
    index_x = lax.axis_index("gx")
    index_y = lax.axis_index("gy")
    count = recv_ref.shape[0]
    cells[:, 32:40, :] = jnp.zeros((17, 8, 128), f32)
    for step in range(-2, 3):
        source = index_y + step
        inside = (source >= 0) & (source < count)
        got = recv_ref[jnp.clip(source, 0, count - 1), 0:176, :].astype(f32)
        line[...] = jnp.where(inside, got, 0.0)
        for p in range(5):
            n = 5 * step + 6 + p
            if 0 <= n < 17:
                cells[n, 0:33, :] = line[33 * p : 33 * p + 33, :]

    r, c = iota2((128, 128))
    mask = jnp.abs(r % 64 - c % 64) <= REACH

    def band_rows(w, a, at):
        base = TAPS * TAPS + a * TAPS
        for j in range(11):
            same = near_ref[pl.ds(base + 2 * j, 1), :]
            upper = same
            lower = same
            if j > 0:
                upper = same + far_ref[pl.ds(base + 2 * j - 1, 1), :]
            if j < 10:
                lower = same + far_ref[pl.ds(base + 2 * j + 1, 1), :]
            upper = pltpu.roll(jnp.broadcast_to(upper, (64, 128)), 0, 1, stride=1, stride_axis=0)
            lower = pltpu.roll(jnp.broadcast_to(lower, (64, 128)), 64, 1, stride=1, stride_axis=0)
            band = jnp.where(mask, jnp.concatenate([upper, lower], axis=0), 0.0).astype(bf16)
            w[at + 128 * j : at + 128 * j + 128, :] = band

    def build(w, a):
        for k in range(3):
            band_rows(w, a + k, 1408 * k)

    def dot(w, a):
        rows = []
        for k in range(3):
            part = [cells[n, pl.ds(a + k, 16), :].astype(bf16) for n in range(17)]
            rows.append([jnp.concatenate(part[g : g + 11], axis=1) for g in range(7)])
        lhs = jnp.concatenate(
            [jnp.concatenate([rows[k][g] for k in range(3)], axis=1) for g in range(7)], axis=0
        )
        acc[...] += jnp.dot(lhs, w[...], preferred_element_type=f32)

    acc[...] = jnp.zeros((112, 128), f32)
    build(w0, 0)

    def step(t, _):
        a = 6 * t
        build(w1, a + 3)
        dot(w0, a)
        build(w0, a + 6)
        dot(w1, a + 3)
        return 0

    lax.fori_loop(0, 3, step, 0)
    dot(w0, 18)

    start = 10 * index_y
    sums = [[None] * 14, [None] * 14]
    for k in range(count):
        main = recv_ref[k, 176:192, :].astype(f32) + recv_ref[k, 192:208, :].astype(f32)
        last = recv_ref[k, 160:176, :].astype(f32)
        last = last[5:9] + last[9:13]
        tail[k, pl.ds(0, 4, stride=4), :] = last
        for r in range(1, 4):
            tail[k, pl.ds(r, 4, stride=4), :] = pltpu.roll(last, 128 - 32 * r, 1)
        for h, value in ((0, main), (1, tail[k])):
            rows_y = my_ref[2 * k + h, pl.ds(start, 16), :]
            for y in range(14):
                term = value * rows_y[y : y + 1, :]
                sums[h][y] = term if k == 0 else sums[h][y] + term
    rows = [
        jnp.concatenate([sums[h][2 * n + p] for p in range(2) for h in range(2)], axis=1)
        for n in range(7)
    ]
    top = two_part_dot(jnp.concatenate(rows, axis=0), mz_ref[...])
    total = acc[...] + top
    r, c = iota2((112, 128))
    cell_x = 10 * index_x - 1 + r % 16
    cell_y = 10 * index_y - 2 + 2 * (r // 16) + c // 64
    inside = (cell_x >= 0) & (cell_x < 320) & (cell_y >= 0) & (cell_y < 80)
    total = jnp.where(inside, total, 0.0)
    r, c = iota2((128, 256))
    up_z = jnp.where(r // 64 == c // 128, weight(c % 128 - 2 * (r % 64)), 0.0)
    wide[...] = exact_dot(total, up_z)

    def middle_y(y):
        n, par = (y + 2) // 2, y % 2
        return wide[16 * n : 16 * n + 16, 128 * par : 128 * par + 128]

    for y in range(20):
        m = y // 2
        if y % 2 == 0:
            value = middle_y(m)
        else:
            value = 0.5625 * (middle_y(m) + middle_y(m + 1)) - 0.0625 * (
                middle_y(m - 1) + middle_y(m + 2)
            )
        moved[16 * y : 16 * y + 16, :] = value
    planes = [moved[pl.ds(k, 20, stride=16), :] for k in range(13)]
    for x in range(20):
        m = x // 2
        if x % 2 == 0:
            value = planes[m + 1]
        else:
            value = 0.5625 * (planes[m + 1] + planes[m + 2]) - 0.0625 * (planes[m] + planes[m + 3])
        out_ref[x] = value + fine_ref[24 * m : 24 * m + 20, 128 * (x % 2) : 128 * (x % 2) + 128]


def swap(first, second, axis):
    count = lax.axis_size(axis)
    pairs = [(k, k + 1) for k in range(0, count - 1, 2)]
    others = [(k, k + 1) for k in range(1, count - 1, 2)]

    def both(ends):
        return ends + [(b, a) for a, b in ends]

    second = lax.ppermute(second, axis, both(others))
    return lax.ppermute(first, axis, both(pairs)), second


def per_device(charges, kernels):
    count_x = lax.axis_size("gx")
    count_y = lax.axis_size("gy")
    spread = charges.shape[0] * count_x / 16.0
    shape = jax.ShapeDtypeStruct
    scratch = [pltpu.VMEM((20, 24, 128), f32), pltpu.VMEM((2, 200, 128), f32)]
    first, second = vmem_call(
        edges_kernel, [shape((200, 128), bf16)] * 2, scratch, "edges", (charges,)
    )
    near_x, next_x = swap(first, second, "gx")
    own = vmem_call(
        rim_own_kernel,
        [shape((2, 200, 128), f32)],
        scratch,
        "rim_own",
        (charges,),
        flops=1 << 20,
    )[0]
    first, second = vmem_call(
        rim_kernel,
        [shape((400, 128), bf16)] * 2,
        scratch,
        "rim",
        (own, next_x, near_x),
    )
    first, second, kernels = lax.optimization_barrier((first, second, kernels))
    near, far = (
        jnp.dot(kernels.reshape(-1, TAPS), jnp.asarray(m, bf16), preferred_element_type=f32)
        for m in spots_np()
    )
    near_y, next_y = swap(first, second, "gy")
    next_y, near_y, near, far = lax.optimization_barrier((next_y, near_y, near, far))
    d, second, first, own, coarse = vmem_call(
        restrict_kernel,
        [
            shape((40, 40, 128), bf16),
            shape((5, 9, 128), bf16),
            shape((5, 9, 128), bf16),
            shape((5, 16, 128), bf16),
            shape((count_x, 8, 128), f32),
        ],
        [
            pltpu.VMEM((2, 20, 48, 128), f32),
            pltpu.VMEM((2, 400, 128), f32),
            pltpu.VMEM((2, 200, 128), f32),
            pltpu.VMEM((16, 48, 128), f32),
            pltpu.VMEM((256, 128), f32),
            pltpu.VMEM((9, 24, 128), f32),
        ],
        "restrict",
        (charges, near_x, next_x, next_y, near_y),
    )
    near_m, next_m = swap(first, second, "gx")
    coarse = lax.all_to_all(coarse, "gx", 0, 0)
    near, near_m = lax.optimization_barrier((near, near_m))
    fine = fine_sum(0, SPLIT, d, near)
    coarse, fine = lax.optimization_barrier((coarse, fine))
    parts = vmem_call(
        spread_kernel,
        [shape((count_y, 208, 128), bf16)],
        [pltpu.VMEM((208, 128), f32), pltpu.VMEM((16, 128), f32)],
        "spread",
        (coarse, jnp.asarray(matrix_x_np(spread)), own, next_m, near_m),
    )[0]
    parts, near = lax.optimization_barrier((parts, near))
    parts = lax.all_to_all(parts, "gy", 0, 0)
    fine = fine_sum(SPLIT, TAPS, d, near, fine)
    return vmem_call(
        final_kernel,
        [shape((20, 20, 128), f32)],
        [
            pltpu.VMEM((17, 40, 128), f32),
            pltpu.VMEM((4224, 128), bf16),
            pltpu.VMEM((4224, 128), bf16),
            pltpu.VMEM((112, 128), f32),
            pltpu.VMEM((320, 128), f32),
            pltpu.VMEM((112, 256), f32),
            pltpu.VMEM((176, 128), f32),
            pltpu.VMEM((count_y, 16, 128), f32),
        ],
        "final",
        (
            parts,
            jnp.asarray(matrix_y_np(spread)),
            jnp.asarray(matrix_z_np(spread)),
            near,
            far,
            fine,
        ),
    )[0]


def solution(mesh):
    return jax.shard_map(
        per_device,
        mesh=mesh,
        in_specs=(P("gx", "gy", None), P()),
        out_specs=P("gx", "gy", None),
        check_vma=False,
    )
```

```python
import functools
import numpy as np
import jax
import jax.numpy as jnp
from jax import lax
from jax.experimental import pallas as pl
from jax.experimental.pallas import tpu as pltpu
from jax.sharding import PartitionSpec as P

f32 = jnp.float32
bf16 = jnp.bfloat16
spread_norm = 1.2533141
REACH = 10
TAPS = 21
GROUP = 3
SPLIT = 6


def weight_np(offset):
    d = np.abs(offset)
    return np.where(d == 0, 1.0, np.where(d == 1, 0.5625, np.where(d == 3, -0.0625, 0.0)))


def top_matrix_np(n, spread):
    prolong = weight_np(np.arange(2 * n)[:, None] - 2 * np.arange(n)[None, :])
    offset = (np.arange(n)[:, None] - np.arange(n)[None, :]) / spread
    return prolong @ (np.exp(-offset * offset) / np.sqrt(spread * spread_norm))


def lane_tiles(m):
    return m.reshape(m.shape[0], -1, 128).transpose(1, 0, 2).astype(np.float32)


def matrix_x_np(spread):
    m = top_matrix_np(160, spread).reshape(320, 32, 5)
    out = np.zeros((328, 32, 8))
    out[1:321, :, :5] = m
    return lane_tiles(out.reshape(328, 256))


def matrix_y_np(spread):
    m = top_matrix_np(40, spread).reshape(80, 8, 5)
    out = np.zeros((88, 8, 8))
    out[2:82, :, :5] = m
    return lane_tiles(np.repeat(out.reshape(88, 64), 32, axis=1))


def matrix_z_np(spread):
    m = top_matrix_np(32, spread).T
    out = np.zeros((2, 8, 32, 2, 64))
    for par in range(2):
        out[par, :, :, par, :] = m[None]
    return out.reshape(512, 128).astype(np.float32)


def spots_np():
    taps = np.arange(TAPS)[:, None]
    lanes = np.arange(128)[None, :]
    near = lanes == (REACH - taps) % 128
    far = lanes == (64 + REACH - taps) % 128
    return near, far


def weight(d):
    d = jnp.abs(d)
    return jnp.where(d == 0, 1.0, jnp.where(d == 1, 0.5625, jnp.where(d == 3, -0.0625, 0.0))).astype(f32)


def exact_dot(rows, weights):
    count = rows.shape[0]
    high = rows.astype(bf16)
    rest = rows - high.astype(f32)
    middle = rest.astype(bf16)
    low = (rest - middle.astype(f32)).astype(bf16)
    out = jnp.dot(
        jnp.concatenate([high, middle, low], axis=0),
        weights.astype(bf16),
        preferred_element_type=f32,
    )
    return out[0:count] + (out[count : 2 * count] + out[2 * count :])


def parts_of(value):
    high = value.astype(bf16)
    return high, (value - high.astype(f32)).astype(bf16)


def two_part_dot(rows, weights):
    high, low = parts_of(rows)
    w_high, w_low = parts_of(weights)
    return jnp.dot(
        jnp.concatenate([high, high, low], axis=1),
        jnp.concatenate([w_high, w_low, w_high], axis=0),
        preferred_element_type=f32,
    )


def iota2(shape):
    return (lax.broadcasted_iota(jnp.int32, shape, 0), lax.broadcasted_iota(jnp.int32, shape, 1))


def vmem_call(body, out_shape, scratch, name, args, flops=0, limit=8):
    def spec(space):
        return pl.BlockSpec(memory_space=space)

    return pl.pallas_call(
        body,
        out_shape=out_shape,
        in_specs=[spec(pltpu.VMEM)] * len(args),
        out_specs=[spec(pltpu.VMEM)] * len(out_shape),
        scratch_shapes=scratch,
        compiler_params=pltpu.CompilerParams(vmem_limit_bytes=limit << 20),
        cost_estimate=pl.CostEstimate(flops=flops, bytes_accessed=1 << 16, transcendentals=0),
        name=name,
    )(*args)


def even(index):
    return index % 2 == 0


def edges_kernel(blk_ref, first_ref, second_ref, wide, dense):
    wide[:, 0:20, :] = blk_ref[...].astype(f32)
    start = jnp.where(even(lax.axis_index("gx")), 10, 0)
    for x in range(10):
        dense[0, 20 * x : 20 * x + 20, :] = wide[start + x, 0:20, :]
        dense[1, 20 * x : 20 * x + 20, :] = wide[10 - start + x, 0:20, :]
    first_ref[...] = dense[0].astype(bf16)
    second_ref[...] = dense[1].astype(bf16)


def rim_rows(wide, dense, count):
    start = jnp.where(even(lax.axis_index("gy")), 10, 0)
    for x in range(count):
        dense[0, 10 * x : 10 * x + 10, :] = wide[x, pl.ds(start, 10), :]
        dense[1, 10 * x : 10 * x + 10, :] = wide[x, pl.ds(10 - start, 10), :]


def rim_own_kernel(blk_ref, out_ref, wide, dense):
    wide[:, 0:20, :] = blk_ref[...].astype(f32)
    rim_rows(wide, dense, 20)
    out_ref[...] = dense[...]


def rim_kernel(own_ref, next_ref, near_ref, first_ref, second_ref, wide, dense):
    even_x = even(lax.axis_index("gx"))
    start = jnp.where(even_x, 10, 0)
    dense[0] = near_ref[...].astype(f32)
    dense[1] = next_ref[...].astype(f32)
    for x in range(10):
        wide[start + x, 0:20, :] = dense[0, 20 * x : 20 * x + 20, :]
        wide[10 - start + x, 0:20, :] = dense[1, 20 * x : 20 * x + 20, :]
    rim_rows(wide, dense, 20)
    for k, out_ref in enumerate((first_ref, second_ref)):
        out_ref[...] = jnp.concatenate([own_ref[k], dense[k]], axis=0).astype(bf16)


def restrict_kernel(
    blk_ref, next_x_ref, near_x_ref, next_y_ref, near_y_ref,
    d_out_ref, second_ref, first_ref, own_ref, out_ref,
    d_ref, dense, sides, planes, cells, mid,
):
    even_x = even(lax.axis_index("gx"))
    even_y = even(lax.axis_index("gy"))
    upper = jnp.where(even_y, 1, 0)
    dense[upper] = near_y_ref[...].astype(f32)
    dense[1 - upper] = next_y_ref[...].astype(f32)
    upper = jnp.where(even_x, 1, 0)
    sides[upper] = near_x_ref[...].astype(f32)
    sides[1 - upper] = next_x_ref[...].astype(f32)
    for x in range(40):
        p, i = x % 2, x // 2
        at = 10 * (x - 10 if 10 <= x < 30 else x + 20 if x < 10 else x)
        d_ref[p, i, 0:10, :] = dense[0, at : at + 10, :]
        d_ref[p, i, 30:40, :] = dense[1, at : at + 10, :]
        if 10 <= x < 30:
            centre = blk_ref[x - 10].astype(f32)
        else:
            at = 20 * (x % 30)
            centre = sides[x // 30, at : at + 20, :]
        d_ref[p, i, 10:30, :] = centre
        d_out_ref[x] = d_ref[p, i, 0:40, :].astype(bf16)

    def fine(x):
        return d_ref[x % 2, x // 2]

    for i in range(16):
        c = 2 * i + 4
        planes[i] = (
            fine(c) + 0.5625 * (fine(c - 1) + fine(c + 1)) - 0.0625 * (fine(c - 3) + fine(c + 3))
        )
    for i in range(16):
        def tap(o):
            return planes[i, pl.ds(4 + o, 16, stride=2), :]
        cells[16 * i : 16 * i + 16, :] = (
            tap(0) + 0.5625 * (tap(-1) + tap(1)) - 0.0625 * (tap(-3) + tap(3))
        )
    zero = jnp.zeros((16, 128), f32)
    rows = []
    for n in range(9):
        pair = []
        for y in (2 * n - 4, 2 * n - 3):
            inside = -3 <= y <= 12
            pair.append(cells[pl.ds(y + 3, 16, stride=16), :] if inside else zero)
        rows.append(jnp.concatenate(pair, axis=1))
    r, c = iota2((256, 128))
    down_z = jnp.where(r // 128 == c // 64, weight(r % 128 - 2 * (c % 64)), 0.0)
    value = exact_dot(jnp.concatenate(rows, axis=0), down_z)
    r, c = iota2((144, 128))
    cell_x = 10 * lax.axis_index("gx") - 3 + r % 16
    cell_y = 10 * lax.axis_index("gy") - 4 + 2 * (r // 16) + c // 64
    inside = (cell_x >= 0) & (cell_x < 320) & (cell_y >= 0) & (cell_y < 80)
    value = jnp.where(inside, value, 0.0).astype(bf16).astype(f32)
    for n in range(9):
        mid[n, 0:16, :] = value[16 * n : 16 * n + 16]
        mid[n, 16:24, :] = jnp.zeros((8, 128), f32)
    for n in range(5):
        right, left = mid[n + 2, 1:10, :], mid[n + 2, 6:15, :]
        first_ref[n] = jnp.where(even_x, right, left).astype(bf16)
        second_ref[n] = jnp.where(even_x, left, right).astype(bf16)
        own_ref[n] = mid[n + 2, 0:16, :].astype(bf16)

    lane = lax.broadcasted_iota(jnp.int32, (1, 128), 1)
    odd = lane >= 64
    weight_0 = jnp.where(odd, 0.5625, 1.0)
    weight_1 = jnp.where(odd, 0.5625, 0.0)
    weight_3 = jnp.where(odd, -0.0625, 0.0)
    r, c = iota2((128, 32))
    down_z = weight(r % 64 - 2 * c)
    sums = []
    for y in range(5):
        n = y + 2
        def tap(o):
            def part(k):
                return mid[k, pl.ds(3 + o, 8, stride=2), :]
            return (
                weight_0 * part(n) + weight_1 * part(n - 1) + weight_3 * (part(n - 2) + part(n + 1))
            )
        sums.append(tap(0) + 0.5625 * (tap(-1) + tap(1)) - 0.0625 * (tap(-3) + tap(3)))
    out = exact_dot(jnp.concatenate(sums, axis=0), down_z)
    main = jnp.concatenate([out[8 * y : 8 * y + 8] for y in range(4)], axis=1)[0:5]
    last = jnp.concatenate([out[32 + x : 33 + x] for x in range(4)], axis=1)
    rest = jnp.concatenate([out[36:37], jnp.zeros((1, 96), f32)], axis=1)
    row = jnp.concatenate([main, last, rest, jnp.zeros((1, 128), f32)], axis=0)
    for k in range(out_ref.shape[0]):
        out_ref[k] = row


def fine_kernel(lo, hi, first, d_in_ref, v_ref, *refs):
    if first:
        out_ref, w0, w1, e0, e1, d_ref = refs
    else:
        acc_ref, out_ref, w0, w1, e0, e1, d_ref = refs
    for x in range(40):
        d_ref[x % 2, x // 2, 0:40, :] = d_in_ref[x].astype(f32)
        d_ref[x % 2, x // 2, 40:48, :] = jnp.zeros((8, 128), f32)
    r, c = iota2((128, 128))
    mask = jnp.abs(r - c) <= REACH
    zero = jnp.zeros((128, 128), bf16)
    for w in (w0, w1):
        for k in range(GROUP):
            w[2816 * k : 2816 * k + 128, 128:256] = zero
            w[2816 * k + 2688 : 2816 * k + 2816, 0:128] = zero

    def build(w, start):
        for k in range(GROUP):
            for a in range(TAPS):
                line = jnp.broadcast_to(v_ref[pl.ds(a * TAPS + start + k, 1), :], (128, 128))
                line = pltpu.roll(line, 0, 1, stride=1, stride_axis=0)
                band = jnp.where(mask, line, 0.0).astype(bf16)
                at = 2816 * k + 128 * a
                w[at : at + 128, 0:128] = band
                w[at + 128 : at + 256, 128:256] = band

    def dot(w, e, start):
        tiles = []
        for k in range(GROUP):
            for p in range(2):
                for q in range(10):
                    part = d_ref[p, 2 * q : 2 * q + 2, pl.ds(start + k, 24), :].reshape(48, 128)
                    e[k, 0, 48 * q : 48 * q + 48, p * 128 : (p + 1) * 128] = part.astype(bf16)
                for q in range(9):
                    part = d_ref[p, 2 * q + 1 : 2 * q + 3, pl.ds(start + k, 24), :].reshape(48, 128)
                    e[k, 1, 48 * q : 48 * q + 48, p * 128 : (p + 1) * 128] = part.astype(bf16)
            tiles += [
                e[k, m % 2, 24 * (m - m % 2) : 24 * (m - m % 2) + 240, :] for m in range(11)
            ]
        lhs = jnp.concatenate(tiles, axis=1)
        out_ref[...] += jnp.dot(lhs, w[...], preferred_element_type=f32)

    out_ref[...] = jnp.zeros((240, 256), f32) if first else acc_ref[...]

    def step(t, _):
        b = lo + 2 * GROUP * t
        build(w0, b)
        dot(w0, e0, b)
        build(w1, b + GROUP)
        dot(w1, e1, b + GROUP)
        return 0

    groups = (hi - lo) // GROUP
    lax.fori_loop(0, groups // 2, step, 0)
    if groups % 2:
        build(w0, hi - GROUP)
        dot(w0, e0, hi - GROUP)


def fine_sum(lo, hi, d, v, acc=None):
    return vmem_call(
        functools.partial(fine_kernel, lo, hi, acc is None),
        [jax.ShapeDtypeStruct((240, 256), f32)],
        [pltpu.VMEM((GROUP * 2816, 256), bf16)] * 2
        + [pltpu.VMEM((GROUP, 2, 480, 256), bf16)] * 2
        + [pltpu.VMEM((2, 20, 48, 128), f32)],
        "fine_sum",
        (d, v) if acc is None else (d, v, acc),
        flops=(hi - lo) * 2 * 240 * 2816 * 256,
        limit=20,
    )[0]


def spread_kernel(recv_ref, mx_ref, own_ref, next_ref, near_ref, out_ref, buf, tail):
    even_x = even(lax.axis_index("gx"))
    start = 10 * lax.axis_index("gx")
    halves = [mx_ref[h, pl.ds(start, 16), :] for h in range(2)]
    lane = lax.broadcasted_iota(jnp.int32, (16, 128), 1) % 8
    rows = [jnp.concatenate(halves, axis=1)]
    for x in range(5):
        at = 5 if x < 4 else 6
        moved = [jnp.where(lane == at, pltpu.roll(h, at - x, 1), 0.0) for h in halves]
        rows.append(jnp.concatenate(moved, axis=1))
    coarse = recv_ref[...].reshape(8 * recv_ref.shape[0], 128)
    value = two_part_dot(jnp.concatenate(rows, axis=0), coarse)
    last = value[80:96, 0:32]
    for x in range(4):
        last = last + value[16 * x + 16 : 16 * x + 32, 32 * x : 32 * x + 32]
    tail[...] = jnp.concatenate([last, jnp.zeros((16, 96), f32)], axis=1)
    last = tail[pl.ds(0, 4, stride=4), :]
    for k in range(1, 4):
        last = last + pltpu.roll(tail[pl.ds(k, 4, stride=4), :], 32 * k, 1)
    for n in range(5):
        near, other = near_ref[n].astype(f32), next_ref[n].astype(f32)
        buf[33 * n : 33 * n + 8, :] = jnp.where(even_x, other, near)[1:9]
        buf[33 * n + 8 : 33 * n + 24, :] = own_ref[n].astype(f32)
        buf[33 * n + 24 : 33 * n + 33, :] = jnp.where(even_x, near, other)
    for at, part in ((165, last), (176, value[0:16])):
        rows = part.shape[0]
        high = part.astype(bf16).astype(f32)
        buf[at : at + rows, :] = high
        buf[at + rows : at + 2 * rows, :] = part - high
    buf[173:176, :] = jnp.zeros((3, 128), f32)
    packed = buf[...].astype(bf16)
    for k in range(out_ref.shape[0]):
        out_ref[k] = packed


def final_kernel(
    recv_ref, my_ref, mz_ref, near_ref, far_ref, fine_ref, out_ref,
    cells, w0, w1, acc, moved, wide, line, tail,
):
    index_x = lax.axis_index("gx")
    index_y = lax.axis_index("gy")
    count = recv_ref.shape[0]
    cells[:, 32:40, :] = jnp.zeros((17, 8, 128), f32)
    for step in range(-2, 3):
        source = index_y + step
        inside = (source >= 0) & (source < count)
        got = recv_ref[jnp.clip(source, 0, count - 1), 0:176, :].astype(f32)
        line[...] = jnp.where(inside, got, 0.0)
        for p in range(5):
            n = 5 * step + 6 + p
            if 0 <= n < 17:
                cells[n, 0:33, :] = line[33 * p : 33 * p + 33, :]

    r, c = iota2((128, 128))
    mask = jnp.abs(r % 64 - c % 64) <= REACH

    def band_rows(w, a, at):
        base = TAPS * TAPS + a * TAPS
        for j in range(11):
            same = near_ref[pl.ds(base + 2 * j, 1), :]
            upper = same
            lower = same
            if j > 0:
                upper = same + far_ref[pl.ds(base + 2 * j - 1, 1), :]
            if j < 10:
                lower = same + far_ref[pl.ds(base + 2 * j + 1, 1), :]
            upper = pltpu.roll(jnp.broadcast_to(upper, (64, 128)), 0, 1, stride=1, stride_axis=0)
            lower = pltpu.roll(jnp.broadcast_to(lower, (64, 128)), 64, 1, stride=1, stride_axis=0)
            band = jnp.where(mask, jnp.concatenate([upper, lower], axis=0), 0.0).astype(bf16)
            w[at + 128 * j : at + 128 * j + 128, :] = band

    def build(w, a):
        for k in range(3):
            band_rows(w, a + k, 1408 * k)

    def dot(w, a):
        rows = []
        for k in range(3):
            part = [cells[n, pl.ds(a + k, 16), :].astype(bf16) for n in range(17)]
            rows.append([jnp.concatenate(part[g : g + 11], axis=1) for g in range(7)])
        lhs = jnp.concatenate(
            [jnp.concatenate([rows[k][g] for k in range(3)], axis=1) for g in range(7)], axis=0
        )
        acc[...] += jnp.dot(lhs, w[...], preferred_element_type=f32)

    acc[...] = jnp.zeros((112, 128), f32)
    build(w0, 0)

    def step(t, _):
        a = 6 * t
        build(w1, a + 3)
        dot(w0, a)
        build(w0, a + 6)
        dot(w1, a + 3)
        return 0

    lax.fori_loop(0, 3, step, 0)
    dot(w0, 18)

    start = 10 * index_y
    sums = [[None] * 14, [None] * 14]
    for k in range(count):
        main = recv_ref[k, 176:192, :].astype(f32) + recv_ref[k, 192:208, :].astype(f32)
        last = recv_ref[k, 160:176, :].astype(f32)
        last = last[5:9] + last[9:13]
        tail[k, pl.ds(0, 4, stride=4), :] = last
        for r in range(1, 4):
            tail[k, pl.ds(r, 4, stride=4), :] = pltpu.roll(last, 128 - 32 * r, 1)
        for h, value in ((0, main), (1, tail[k])):
            rows_y = my_ref[2 * k + h, pl.ds(start, 16), :]
            for y in range(14):
                term = value * rows_y[y : y + 1, :]
                sums[h][y] = term if k == 0 else sums[h][y] + term
    rows = [
        jnp.concatenate([sums[h][2 * n + p] for p in range(2) for h in range(2)], axis=1)
        for n in range(7)
    ]
    top = two_part_dot(jnp.concatenate(rows, axis=0), mz_ref[...])
    total = acc[...] + top
    r, c = iota2((112, 128))
    cell_x = 10 * index_x - 1 + r % 16
    cell_y = 10 * index_y - 2 + 2 * (r // 16) + c // 64
    inside = (cell_x >= 0) & (cell_x < 320) & (cell_y >= 0) & (cell_y < 80)
    total = jnp.where(inside, total, 0.0)
    r, c = iota2((128, 256))
    up_z = jnp.where(r // 64 == c // 128, weight(c % 128 - 2 * (r % 64)), 0.0)
    wide[...] = exact_dot(total, up_z)

    def middle_y(y):
        n, par = (y + 2) // 2, y % 2
        return wide[16 * n : 16 * n + 16, 128 * par : 128 * par + 128]

    for y in range(20):
        m = y // 2
        if y % 2 == 0:
            value = middle_y(m)
        else:
            value = 0.5625 * (middle_y(m) + middle_y(m + 1)) - 0.0625 * (
                middle_y(m - 1) + middle_y(m + 2)
            )
        moved[16 * y : 16 * y + 16, :] = value
    planes = [moved[pl.ds(k, 20, stride=16), :] for k in range(13)]
    for x in range(20):
        m = x // 2
        if x % 2 == 0:
            value = planes[m + 1]
        else:
            value = 0.5625 * (planes[m + 1] + planes[m + 2]) - 0.0625 * (planes[m] + planes[m + 3])
        out_ref[x] = value + fine_ref[24 * m : 24 * m + 20, 128 * (x % 2) : 128 * (x % 2) + 128]


def swap(first, second, axis):
    count = lax.axis_size(axis)
    pairs = [(k, k + 1) for k in range(0, count - 1, 2)]
    others = [(k, k + 1) for k in range(1, count - 1, 2)]

    def both(ends):
        return ends + [(b, a) for a, b in ends]

    second = lax.ppermute(second, axis, both(others))
    return lax.ppermute(first, axis, both(pairs)), second


def per_device(charges, kernels):
    count_x = lax.axis_size("gx")
    count_y = lax.axis_size("gy")
    spread = charges.shape[0] * count_x / 16.0
    shape = jax.ShapeDtypeStruct
    scratch = [pltpu.VMEM((20, 24, 128), f32), pltpu.VMEM((2, 200, 128), f32)]
    first, second = vmem_call(
        edges_kernel, [shape((200, 128), bf16)] * 2, scratch, "edges", (charges,)
    )
    near_x, next_x = swap(first, second, "gx")
    own = vmem_call(
        rim_own_kernel,
        [shape((2, 200, 128), f32)],
        scratch,
        "rim_own",
        (charges,),
        flops=1 << 20,
    )[0]
    first, second = vmem_call(
        rim_kernel,
        [shape((400, 128), bf16)] * 2,
        scratch,
        "rim",
        (own, next_x, near_x),
    )
    first, second, kernels = lax.optimization_barrier((first, second, kernels))
    near, far = (
        jnp.dot(kernels.reshape(-1, TAPS), jnp.asarray(m, bf16), preferred_element_type=f32)
        for m in spots_np()
    )
    near_y, next_y = swap(first, second, "gy")
    next_y, near_y, near, far = lax.optimization_barrier((next_y, near_y, near, far))
    d, second, first, own, coarse = vmem_call(
        restrict_kernel,
        [
            shape((40, 40, 128), bf16),
            shape((5, 9, 128), bf16),
            shape((5, 9, 128), bf16),
            shape((5, 16, 128), bf16),
            shape((count_x, 8, 128), f32),
        ],
        [
            pltpu.VMEM((2, 20, 48, 128), f32),
            pltpu.VMEM((2, 400, 128), f32),
            pltpu.VMEM((2, 200, 128), f32),
            pltpu.VMEM((16, 48, 128), f32),
            pltpu.VMEM((256, 128), f32),
            pltpu.VMEM((9, 24, 128), f32),
        ],
        "restrict",
        (charges, next_x, near_x, next_y, near_y),
    )
    near_m, next_m = swap(first, second, "gx")
    coarse = lax.all_to_all(coarse, "gx", 0, 0)
    fine = fine_sum(0, SPLIT, d, near)
    coarse, fine = lax.optimization_barrier((coarse, fine))
    parts = vmem_call(
        spread_kernel,
        [shape((count_y, 208, 128), bf16)],
        [pltpu.VMEM((208, 128), f32), pltpu.VMEM((16, 128), f32)],
        "spread",
        (coarse, jnp.asarray(matrix_x_np(spread)), own, next_m, near_m),
    )[0]
    parts, near = lax.optimization_barrier((parts, near))
    parts = lax.all_to_all(parts, "gy", 0, 0)
    fine = fine_sum(SPLIT, TAPS, d, near, fine)
    return vmem_call(
        final_kernel,
        [shape((20, 20, 128), f32)],
        [
            pltpu.VMEM((17, 40, 128), f32),
            pltpu.VMEM((4224, 128), bf16),
            pltpu.VMEM((4224, 128), bf16),
            pltpu.VMEM((112, 128), f32),
            pltpu.VMEM((320, 128), f32),
            pltpu.VMEM((112, 256), f32),
            pltpu.VMEM((176, 128), f32),
            pltpu.VMEM((count_y, 16, 128), f32),
        ],
        "final",
        (
            parts,
            jnp.asarray(matrix_y_np(spread)),
            jnp.asarray(matrix_z_np(spread)),
            near,
            far,
            fine,
        ),
    )[0]


def solution(mesh):
    return jax.shard_map(
        per_device,
        mesh=mesh,
        in_specs=(P("gx", "gy", None), P()),
        out_specs=P("gx", "gy", None),
        check_vma=False,
    )
```

```python
import functools
import numpy as np
import jax
import jax.numpy as jnp
from jax import lax
from jax.experimental import pallas as pl
from jax.experimental.pallas import tpu as pltpu
from jax.sharding import PartitionSpec as P

f32 = jnp.float32
bf16 = jnp.bfloat16
spread_norm = 1.2533141
REACH = 10
TAPS = 21
GROUP = 3
SPLIT = 9


def weight_np(offset):
    d = np.abs(offset)
    return np.where(d == 0, 1.0, np.where(d == 1, 0.5625, np.where(d == 3, -0.0625, 0.0)))


def top_matrix_np(n, spread):
    prolong = weight_np(np.arange(2 * n)[:, None] - 2 * np.arange(n)[None, :])
    offset = (np.arange(n)[:, None] - np.arange(n)[None, :]) / spread
    return prolong @ (np.exp(-offset * offset) / np.sqrt(spread * spread_norm))


def lane_tiles(m):
    return m.reshape(m.shape[0], -1, 128).transpose(1, 0, 2).astype(np.float32)


def matrix_x_np(spread):
    m = top_matrix_np(160, spread).reshape(320, 32, 5)
    out = np.zeros((328, 32, 8))
    out[1:321, :, :5] = m
    return lane_tiles(out.reshape(328, 256))


def matrix_y_np(spread):
    m = top_matrix_np(40, spread).reshape(80, 8, 5)
    out = np.zeros((88, 8, 8))
    out[2:82, :, :5] = m
    return lane_tiles(np.repeat(out.reshape(88, 64), 32, axis=1))


def matrix_z_np(spread):
    m = top_matrix_np(32, spread).T
    out = np.zeros((2, 8, 32, 2, 64))
    for par in range(2):
        out[par, :, :, par, :] = m[None]
    return out.reshape(512, 128).astype(np.float32)


def spots_np():
    taps = np.arange(TAPS)[:, None]
    lanes = np.arange(128)[None, :]
    near = lanes == (REACH - taps) % 128
    far = lanes == (64 + REACH - taps) % 128
    return near, far


def weight(d):
    d = jnp.abs(d)
    return jnp.where(d == 0, 1.0, jnp.where(d == 1, 0.5625, jnp.where(d == 3, -0.0625, 0.0))).astype(f32)


def exact_dot(rows, weights):
    count = rows.shape[0]
    high = rows.astype(bf16)
    rest = rows - high.astype(f32)
    middle = rest.astype(bf16)
    low = (rest - middle.astype(f32)).astype(bf16)
    out = jnp.dot(
        jnp.concatenate([high, middle, low], axis=0),
        weights.astype(bf16),
        preferred_element_type=f32,
    )
    return out[0:count] + (out[count : 2 * count] + out[2 * count :])


def parts_of(value):
    high = value.astype(bf16)
    return high, (value - high.astype(f32)).astype(bf16)


def two_part_dot(rows, weights):
    high, low = parts_of(rows)
    w_high, w_low = parts_of(weights)
    return jnp.dot(
        jnp.concatenate([high, high, low], axis=1),
        jnp.concatenate([w_high, w_low, w_high], axis=0),
        preferred_element_type=f32,
    )


def iota2(shape):
    return (lax.broadcasted_iota(jnp.int32, shape, 0), lax.broadcasted_iota(jnp.int32, shape, 1))


def vmem_call(body, out_shape, scratch, name, args, flops=0, limit=8):
    def spec(space):
        return pl.BlockSpec(memory_space=space)

    return pl.pallas_call(
        body,
        out_shape=out_shape,
        in_specs=[spec(pltpu.VMEM)] * len(args),
        out_specs=[spec(pltpu.VMEM)] * len(out_shape),
        scratch_shapes=scratch,
        compiler_params=pltpu.CompilerParams(vmem_limit_bytes=limit << 20),
        cost_estimate=pl.CostEstimate(flops=flops, bytes_accessed=1 << 16, transcendentals=0),
        name=name,
    )(*args)


def even(index):
    return index % 2 == 0


def edges_kernel(blk_ref, first_ref, second_ref, wide, dense):
    wide[:, 0:20, :] = blk_ref[...].astype(f32)
    start = jnp.where(even(lax.axis_index("gx")), 10, 0)
    for x in range(10):
        dense[0, 20 * x : 20 * x + 20, :] = wide[start + x, 0:20, :]
        dense[1, 20 * x : 20 * x + 20, :] = wide[10 - start + x, 0:20, :]
    first_ref[...] = dense[0].astype(bf16)
    second_ref[...] = dense[1].astype(bf16)


def rim_rows(wide, dense, count):
    start = jnp.where(even(lax.axis_index("gy")), 10, 0)
    for x in range(count):
        dense[0, 10 * x : 10 * x + 10, :] = wide[x, pl.ds(start, 10), :]
        dense[1, 10 * x : 10 * x + 10, :] = wide[x, pl.ds(10 - start, 10), :]


def rim_own_kernel(blk_ref, out_ref, wide, dense):
    wide[:, 0:20, :] = blk_ref[...].astype(f32)
    rim_rows(wide, dense, 20)
    out_ref[...] = dense[...]


def rim_kernel(own_ref, next_ref, near_ref, first_ref, second_ref, wide, dense):
    even_x = even(lax.axis_index("gx"))
    start = jnp.where(even_x, 10, 0)
    dense[0] = near_ref[...].astype(f32)
    dense[1] = next_ref[...].astype(f32)
    for x in range(10):
        wide[start + x, 0:20, :] = dense[0, 20 * x : 20 * x + 20, :]
        wide[10 - start + x, 0:20, :] = dense[1, 20 * x : 20 * x + 20, :]
    rim_rows(wide, dense, 20)
    for k, out_ref in enumerate((first_ref, second_ref)):
        out_ref[...] = jnp.concatenate([own_ref[k], dense[k]], axis=0).astype(bf16)


def restrict_kernel(
    blk_ref, next_x_ref, near_x_ref, next_y_ref, near_y_ref,
    d_out_ref, second_ref, first_ref, own_ref, out_ref,
    d_ref, dense, sides, planes, cells, mid,
):
    even_x = even(lax.axis_index("gx"))
    even_y = even(lax.axis_index("gy"))
    upper = jnp.where(even_y, 1, 0)
    dense[upper] = near_y_ref[...].astype(f32)
    dense[1 - upper] = next_y_ref[...].astype(f32)
    upper = jnp.where(even_x, 1, 0)
    sides[upper] = near_x_ref[...].astype(f32)
    sides[1 - upper] = next_x_ref[...].astype(f32)
    for x in range(40):
        p, i = x % 2, x // 2
        at = 10 * (x - 10 if 10 <= x < 30 else x + 20 if x < 10 else x)
        d_ref[p, i, 0:10, :] = dense[0, at : at + 10, :]
        d_ref[p, i, 30:40, :] = dense[1, at : at + 10, :]
        if 10 <= x < 30:
            centre = blk_ref[x - 10].astype(f32)
        else:
            at = 20 * (x % 30)
            centre = sides[x // 30, at : at + 20, :]
        d_ref[p, i, 10:30, :] = centre
        d_out_ref[x] = d_ref[p, i, 0:40, :].astype(bf16)

    def fine(x):
        return d_ref[x % 2, x // 2]

    for i in range(16):
        c = 2 * i + 4
        planes[i] = (
            fine(c) + 0.5625 * (fine(c - 1) + fine(c + 1)) - 0.0625 * (fine(c - 3) + fine(c + 3))
        )
    for i in range(16):
        def tap(o):
            return planes[i, pl.ds(4 + o, 16, stride=2), :]
        cells[16 * i : 16 * i + 16, :] = (
            tap(0) + 0.5625 * (tap(-1) + tap(1)) - 0.0625 * (tap(-3) + tap(3))
        )
    zero = jnp.zeros((16, 128), f32)
    rows = []
    for n in range(9):
        pair = []
        for y in (2 * n - 4, 2 * n - 3):
            inside = -3 <= y <= 12
            pair.append(cells[pl.ds(y + 3, 16, stride=16), :] if inside else zero)
        rows.append(jnp.concatenate(pair, axis=1))
    r, c = iota2((256, 128))
    down_z = jnp.where(r // 128 == c // 64, weight(r % 128 - 2 * (c % 64)), 0.0)
    value = exact_dot(jnp.concatenate(rows, axis=0), down_z)
    r, c = iota2((144, 128))
    cell_x = 10 * lax.axis_index("gx") - 3 + r % 16
    cell_y = 10 * lax.axis_index("gy") - 4 + 2 * (r // 16) + c // 64
    inside = (cell_x >= 0) & (cell_x < 320) & (cell_y >= 0) & (cell_y < 80)
    value = jnp.where(inside, value, 0.0).astype(bf16).astype(f32)
    for n in range(9):
        mid[n, 0:16, :] = value[16 * n : 16 * n + 16]
        mid[n, 16:24, :] = jnp.zeros((8, 128), f32)
    for n in range(5):
        right, left = mid[n + 2, 1:10, :], mid[n + 2, 6:15, :]
        first_ref[n] = jnp.where(even_x, right, left).astype(bf16)
        second_ref[n] = jnp.where(even_x, left, right).astype(bf16)
        own_ref[n] = mid[n + 2, 0:16, :].astype(bf16)

    lane = lax.broadcasted_iota(jnp.int32, (1, 128), 1)
    odd = lane >= 64
    weight_0 = jnp.where(odd, 0.5625, 1.0)
    weight_1 = jnp.where(odd, 0.5625, 0.0)
    weight_3 = jnp.where(odd, -0.0625, 0.0)
    r, c = iota2((128, 32))
    down_z = weight(r % 64 - 2 * c)
    sums = []
    for y in range(5):
        n = y + 2
        def tap(o):
            def part(k):
                return mid[k, pl.ds(3 + o, 8, stride=2), :]
            return (
                weight_0 * part(n) + weight_1 * part(n - 1) + weight_3 * (part(n - 2) + part(n + 1))
            )
        sums.append(tap(0) + 0.5625 * (tap(-1) + tap(1)) - 0.0625 * (tap(-3) + tap(3)))
    out = exact_dot(jnp.concatenate(sums, axis=0), down_z)
    main = jnp.concatenate([out[8 * y : 8 * y + 8] for y in range(4)], axis=1)[0:5]
    last = jnp.concatenate([out[32 + x : 33 + x] for x in range(4)], axis=1)
    rest = jnp.concatenate([out[36:37], jnp.zeros((1, 96), f32)], axis=1)
    row = jnp.concatenate([main, last, rest, jnp.zeros((1, 128), f32)], axis=0)
    for k in range(out_ref.shape[0]):
        out_ref[k] = row


def fine_kernel(lo, hi, first, d_in_ref, v_ref, *refs):
    if first:
        out_ref, w0, w1, e0, e1, d_ref = refs
    else:
        acc_ref, out_ref, w0, w1, e0, e1, d_ref = refs
    for x in range(40):
        d_ref[x % 2, x // 2, 0:40, :] = d_in_ref[x].astype(f32)
        d_ref[x % 2, x // 2, 40:48, :] = jnp.zeros((8, 128), f32)
    r, c = iota2((128, 128))
    mask = jnp.abs(r - c) <= REACH
    zero = jnp.zeros((128, 128), bf16)
    for w in (w0, w1):
        for k in range(GROUP):
            w[2816 * k : 2816 * k + 128, 128:256] = zero
            w[2816 * k + 2688 : 2816 * k + 2816, 0:128] = zero

    def build(w, start):
        for k in range(GROUP):
            for a in range(TAPS):
                line = jnp.broadcast_to(v_ref[pl.ds(a * TAPS + start + k, 1), :], (128, 128))
                line = pltpu.roll(line, 0, 1, stride=1, stride_axis=0)
                band = jnp.where(mask, line, 0.0).astype(bf16)
                at = 2816 * k + 128 * a
                w[at : at + 128, 0:128] = band
                w[at + 128 : at + 256, 128:256] = band

    def dot(w, e, start):
        tiles = []
        for k in range(GROUP):
            for p in range(2):
                for q in range(10):
                    part = d_ref[p, 2 * q : 2 * q + 2, pl.ds(start + k, 24), :].reshape(48, 128)
                    e[k, 0, 48 * q : 48 * q + 48, p * 128 : (p + 1) * 128] = part.astype(bf16)
                for q in range(9):
                    part = d_ref[p, 2 * q + 1 : 2 * q + 3, pl.ds(start + k, 24), :].reshape(48, 128)
                    e[k, 1, 48 * q : 48 * q + 48, p * 128 : (p + 1) * 128] = part.astype(bf16)
            tiles += [
                e[k, m % 2, 24 * (m - m % 2) : 24 * (m - m % 2) + 240, :] for m in range(11)
            ]
        lhs = jnp.concatenate(tiles, axis=1)
        out_ref[...] += jnp.dot(lhs, w[...], preferred_element_type=f32)

    out_ref[...] = jnp.zeros((240, 256), f32) if first else acc_ref[...]

    def step(t, _):
        b = lo + 2 * GROUP * t
        build(w0, b)
        dot(w0, e0, b)
        build(w1, b + GROUP)
        dot(w1, e1, b + GROUP)
        return 0

    groups = (hi - lo) // GROUP
    lax.fori_loop(0, groups // 2, step, 0)
    if groups % 2:
        build(w0, hi - GROUP)
        dot(w0, e0, hi - GROUP)


def fine_sum(lo, hi, d, v, acc=None):
    return vmem_call(
        functools.partial(fine_kernel, lo, hi, acc is None),
        [jax.ShapeDtypeStruct((240, 256), f32)],
        [pltpu.VMEM((GROUP * 2816, 256), bf16)] * 2
        + [pltpu.VMEM((GROUP, 2, 480, 256), bf16)] * 2
        + [pltpu.VMEM((2, 20, 48, 128), f32)],
        "fine_sum",
        (d, v) if acc is None else (d, v, acc),
        flops=(hi - lo) * 2 * 240 * 2816 * 256,
        limit=20,
    )[0]


def spread_kernel(recv_ref, mx_ref, own_ref, next_ref, near_ref, out_ref, buf, tail):
    even_x = even(lax.axis_index("gx"))
    start = 10 * lax.axis_index("gx")
    halves = [mx_ref[h, pl.ds(start, 16), :] for h in range(2)]
    lane = lax.broadcasted_iota(jnp.int32, (16, 128), 1) % 8
    rows = [jnp.concatenate(halves, axis=1)]
    for x in range(5):
        at = 5 if x < 4 else 6
        moved = [jnp.where(lane == at, pltpu.roll(h, at - x, 1), 0.0) for h in halves]
        rows.append(jnp.concatenate(moved, axis=1))
    coarse = recv_ref[...].reshape(8 * recv_ref.shape[0], 128)
    value = two_part_dot(jnp.concatenate(rows, axis=0), coarse)
    last = value[80:96, 0:32]
    for x in range(4):
        last = last + value[16 * x + 16 : 16 * x + 32, 32 * x : 32 * x + 32]
    tail[...] = jnp.concatenate([last, jnp.zeros((16, 96), f32)], axis=1)
    last = tail[pl.ds(0, 4, stride=4), :]
    for k in range(1, 4):
        last = last + pltpu.roll(tail[pl.ds(k, 4, stride=4), :], 32 * k, 1)
    for n in range(5):
        near, other = near_ref[n].astype(f32), next_ref[n].astype(f32)
        buf[33 * n : 33 * n + 8, :] = jnp.where(even_x, other, near)[1:9]
        buf[33 * n + 8 : 33 * n + 24, :] = own_ref[n].astype(f32)
        buf[33 * n + 24 : 33 * n + 33, :] = jnp.where(even_x, near, other)
    for at, part in ((165, last), (176, value[0:16])):
        rows = part.shape[0]
        high = part.astype(bf16).astype(f32)
        buf[at : at + rows, :] = high
        buf[at + rows : at + 2 * rows, :] = part - high
    buf[173:176, :] = jnp.zeros((3, 128), f32)
    packed = buf[...].astype(bf16)
    for k in range(out_ref.shape[0]):
        out_ref[k] = packed


def final_kernel(
    recv_ref, my_ref, mz_ref, near_ref, far_ref, fine_ref, out_ref,
    cells, w0, w1, acc, moved, wide, line, tail,
):
    index_x = lax.axis_index("gx")
    index_y = lax.axis_index("gy")
    count = recv_ref.shape[0]
    cells[:, 32:40, :] = jnp.zeros((17, 8, 128), f32)
    for step in range(-2, 3):
        source = index_y + step
        inside = (source >= 0) & (source < count)
        got = recv_ref[jnp.clip(source, 0, count - 1), 0:176, :].astype(f32)
        line[...] = jnp.where(inside, got, 0.0)
        for p in range(5):
            n = 5 * step + 6 + p
            if 0 <= n < 17:
                cells[n, 0:33, :] = line[33 * p : 33 * p + 33, :]

    r, c = iota2((128, 128))
    mask = jnp.abs(r % 64 - c % 64) <= REACH

    def band_rows(w, a, at):
        base = TAPS * TAPS + a * TAPS
        for j in range(11):
            same = near_ref[pl.ds(base + 2 * j, 1), :]
            upper = same
            lower = same
            if j > 0:
                upper = same + far_ref[pl.ds(base + 2 * j - 1, 1), :]
            if j < 10:
                lower = same + far_ref[pl.ds(base + 2 * j + 1, 1), :]
            upper = pltpu.roll(jnp.broadcast_to(upper, (64, 128)), 0, 1, stride=1, stride_axis=0)
            lower = pltpu.roll(jnp.broadcast_to(lower, (64, 128)), 64, 1, stride=1, stride_axis=0)
            band = jnp.where(mask, jnp.concatenate([upper, lower], axis=0), 0.0).astype(bf16)
            w[at + 128 * j : at + 128 * j + 128, :] = band

    def build(w, a):
        for k in range(3):
            band_rows(w, a + k, 1408 * k)

    def dot(w, a):
        rows = []
        for k in range(3):
            part = [cells[n, pl.ds(a + k, 16), :].astype(bf16) for n in range(17)]
            rows.append([jnp.concatenate(part[g : g + 11], axis=1) for g in range(7)])
        lhs = jnp.concatenate(
            [jnp.concatenate([rows[k][g] for k in range(3)], axis=1) for g in range(7)], axis=0
        )
        acc[...] += jnp.dot(lhs, w[...], preferred_element_type=f32)

    acc[...] = jnp.zeros((112, 128), f32)
    build(w0, 0)

    def step(t, _):
        a = 6 * t
        build(w1, a + 3)
        dot(w0, a)
        build(w0, a + 6)
        dot(w1, a + 3)
        return 0

    lax.fori_loop(0, 3, step, 0)
    dot(w0, 18)

    start = 10 * index_y
    sums = [[None] * 14, [None] * 14]
    for k in range(count):
        main = recv_ref[k, 176:192, :].astype(f32) + recv_ref[k, 192:208, :].astype(f32)
        last = recv_ref[k, 160:176, :].astype(f32)
        last = last[5:9] + last[9:13]
        tail[k, pl.ds(0, 4, stride=4), :] = last
        for r in range(1, 4):
            tail[k, pl.ds(r, 4, stride=4), :] = pltpu.roll(last, 128 - 32 * r, 1)
        for h, value in ((0, main), (1, tail[k])):
            rows_y = my_ref[2 * k + h, pl.ds(start, 16), :]
            for y in range(14):
                term = value * rows_y[y : y + 1, :]
                sums[h][y] = term if k == 0 else sums[h][y] + term
    rows = [
        jnp.concatenate([sums[h][2 * n + p] for p in range(2) for h in range(2)], axis=1)
        for n in range(7)
    ]
    top = two_part_dot(jnp.concatenate(rows, axis=0), mz_ref[...])
    total = acc[...] + top
    r, c = iota2((112, 128))
    cell_x = 10 * index_x - 1 + r % 16
    cell_y = 10 * index_y - 2 + 2 * (r // 16) + c // 64
    inside = (cell_x >= 0) & (cell_x < 320) & (cell_y >= 0) & (cell_y < 80)
    total = jnp.where(inside, total, 0.0)
    r, c = iota2((128, 256))
    up_z = jnp.where(r // 64 == c // 128, weight(c % 128 - 2 * (r % 64)), 0.0)
    wide[...] = exact_dot(total, up_z)

    def middle_y(y):
        n, par = (y + 2) // 2, y % 2
        return wide[16 * n : 16 * n + 16, 128 * par : 128 * par + 128]

    for y in range(20):
        m = y // 2
        if y % 2 == 0:
            value = middle_y(m)
        else:
            value = 0.5625 * (middle_y(m) + middle_y(m + 1)) - 0.0625 * (
                middle_y(m - 1) + middle_y(m + 2)
            )
        moved[16 * y : 16 * y + 16, :] = value
    planes = [moved[pl.ds(k, 20, stride=16), :] for k in range(13)]
    for x in range(20):
        m = x // 2
        if x % 2 == 0:
            value = planes[m + 1]
        else:
            value = 0.5625 * (planes[m + 1] + planes[m + 2]) - 0.0625 * (planes[m] + planes[m + 3])
        out_ref[x] = value + fine_ref[24 * m : 24 * m + 20, 128 * (x % 2) : 128 * (x % 2) + 128]


def swap(first, second, axis):
    count = lax.axis_size(axis)
    pairs = [(k, k + 1) for k in range(0, count - 1, 2)]
    others = [(k, k + 1) for k in range(1, count - 1, 2)]

    def both(ends):
        return ends + [(b, a) for a, b in ends]

    second = lax.ppermute(second, axis, both(others))
    return lax.ppermute(first, axis, both(pairs)), second


def per_device(charges, kernels):
    count_x = lax.axis_size("gx")
    count_y = lax.axis_size("gy")
    spread = charges.shape[0] * count_x / 16.0
    shape = jax.ShapeDtypeStruct
    scratch = [pltpu.VMEM((20, 24, 128), f32), pltpu.VMEM((2, 200, 128), f32)]
    first, second = vmem_call(
        edges_kernel, [shape((200, 128), bf16)] * 2, scratch, "edges", (charges,)
    )
    near_x, next_x = swap(first, second, "gx")
    own = vmem_call(
        rim_own_kernel,
        [shape((2, 200, 128), f32)],
        scratch,
        "rim_own",
        (charges,),
        flops=1 << 20,
    )[0]
    first, second = vmem_call(
        rim_kernel,
        [shape((400, 128), bf16)] * 2,
        scratch,
        "rim",
        (own, next_x, near_x),
    )
    first, second, kernels = lax.optimization_barrier((first, second, kernels))
    near, far = (
        jnp.dot(kernels.reshape(-1, TAPS), jnp.asarray(m, bf16), preferred_element_type=f32)
        for m in spots_np()
    )
    near_y, next_y = swap(first, second, "gy")
    next_y, near_y, near, far = lax.optimization_barrier((next_y, near_y, near, far))
    d, second, first, own, coarse = vmem_call(
        restrict_kernel,
        [
            shape((40, 40, 128), bf16),
            shape((5, 9, 128), bf16),
            shape((5, 9, 128), bf16),
            shape((5, 16, 128), bf16),
            shape((count_x, 8, 128), f32),
        ],
        [
            pltpu.VMEM((2, 20, 48, 128), f32),
            pltpu.VMEM((2, 400, 128), f32),
            pltpu.VMEM((2, 200, 128), f32),
            pltpu.VMEM((16, 48, 128), f32),
            pltpu.VMEM((256, 128), f32),
            pltpu.VMEM((9, 24, 128), f32),
        ],
        "restrict",
        (charges, next_x, near_x, next_y, near_y),
    )
    near_m, next_m = swap(first, second, "gx")
    coarse = lax.all_to_all(coarse, "gx", 0, 0)
    fine = fine_sum(0, SPLIT, d, near)
    coarse, fine = lax.optimization_barrier((coarse, fine))
    parts = vmem_call(
        spread_kernel,
        [shape((count_y, 208, 128), bf16)],
        [pltpu.VMEM((208, 128), f32), pltpu.VMEM((16, 128), f32)],
        "spread",
        (coarse, jnp.asarray(matrix_x_np(spread)), own, next_m, near_m),
    )[0]
    parts, near = lax.optimization_barrier((parts, near))
    parts = lax.all_to_all(parts, "gy", 0, 0)
    fine = fine_sum(SPLIT, TAPS, d, near, fine)
    return vmem_call(
        final_kernel,
        [shape((20, 20, 128), f32)],
        [
            pltpu.VMEM((17, 40, 128), f32),
            pltpu.VMEM((4224, 128), bf16),
            pltpu.VMEM((4224, 128), bf16),
            pltpu.VMEM((112, 128), f32),
            pltpu.VMEM((320, 128), f32),
            pltpu.VMEM((112, 256), f32),
            pltpu.VMEM((176, 128), f32),
            pltpu.VMEM((count_y, 16, 128), f32),
        ],
        "final",
        (
            parts,
            jnp.asarray(matrix_y_np(spread)),
            jnp.asarray(matrix_z_np(spread)),
            near,
            far,
            fine,
        ),
    )[0]


def solution(mesh):
    return jax.shard_map(
        per_device,
        mesh=mesh,
        in_specs=(P("gx", "gy", None), P()),
        out_specs=P("gx", "gy", None),
        check_vma=False,
    )
```

```python
import functools
import numpy as np
import jax
import jax.numpy as jnp
from jax import lax
from jax.experimental import pallas as pl
from jax.experimental.pallas import tpu as pltpu
from jax.sharding import PartitionSpec as P

f32 = jnp.float32
bf16 = jnp.bfloat16
spread_norm = 1.2533141
REACH = 10
TAPS = 21
GROUP = 3
SPLIT = 6


def weight_np(offset):
    d = np.abs(offset)
    return np.where(d == 0, 1.0, np.where(d == 1, 0.5625, np.where(d == 3, -0.0625, 0.0)))


def top_matrix_np(n, spread):
    prolong = weight_np(np.arange(2 * n)[:, None] - 2 * np.arange(n)[None, :])
    offset = (np.arange(n)[:, None] - np.arange(n)[None, :]) / spread
    return prolong @ (np.exp(-offset * offset) / np.sqrt(spread * spread_norm))


def lane_tiles(m):
    return m.reshape(m.shape[0], -1, 128).transpose(1, 0, 2).astype(np.float32)


def matrix_x_np(spread):
    m = top_matrix_np(160, spread).reshape(320, 32, 5)
    out = np.zeros((328, 32, 8))
    out[1:321, :, :5] = m
    return lane_tiles(out.reshape(328, 256))


def matrix_y_np(spread):
    m = top_matrix_np(40, spread).reshape(80, 8, 5)
    out = np.zeros((88, 8, 8))
    out[2:82, :, :5] = m
    return lane_tiles(np.repeat(out.reshape(88, 64), 32, axis=1))


def matrix_z_np(spread):
    m = top_matrix_np(32, spread).T
    out = np.zeros((2, 8, 32, 2, 64))
    for par in range(2):
        out[par, :, :, par, :] = m[None]
    return out.reshape(512, 128).astype(np.float32)


def spots_np():
    taps = np.arange(TAPS)[:, None]
    lanes = np.arange(128)[None, :]
    near = lanes == (REACH - taps) % 128
    far = lanes == (64 + REACH - taps) % 128
    return near, far


def weight(d):
    d = jnp.abs(d)
    return jnp.where(d == 0, 1.0, jnp.where(d == 1, 0.5625, jnp.where(d == 3, -0.0625, 0.0))).astype(f32)


def exact_dot(rows, weights):
    count = rows.shape[0]
    high = rows.astype(bf16)
    rest = rows - high.astype(f32)
    middle = rest.astype(bf16)
    low = (rest - middle.astype(f32)).astype(bf16)
    out = jnp.dot(
        jnp.concatenate([high, middle, low], axis=0),
        weights.astype(bf16),
        preferred_element_type=f32,
    )
    return out[0:count] + (out[count : 2 * count] + out[2 * count :])


def parts_of(value):
    high = value.astype(bf16)
    return high, (value - high.astype(f32)).astype(bf16)


def two_part_dot(rows, weights):
    high, low = parts_of(rows)
    w_high, w_low = parts_of(weights)
    return jnp.dot(
        jnp.concatenate([high, high, low], axis=1),
        jnp.concatenate([w_high, w_low, w_high], axis=0),
        preferred_element_type=f32,
    )


def iota2(shape):
    return (lax.broadcasted_iota(jnp.int32, shape, 0), lax.broadcasted_iota(jnp.int32, shape, 1))


def vmem_call(body, out_shape, scratch, name, args, flops=0, limit=8):
    def spec(space):
        return pl.BlockSpec(memory_space=space)

    return pl.pallas_call(
        body,
        out_shape=out_shape,
        in_specs=[spec(pltpu.VMEM)] * len(args),
        out_specs=[spec(pltpu.VMEM)] * len(out_shape),
        scratch_shapes=scratch,
        compiler_params=pltpu.CompilerParams(vmem_limit_bytes=limit << 20),
        cost_estimate=pl.CostEstimate(flops=flops, bytes_accessed=1 << 16, transcendentals=0),
        name=name,
    )(*args)


def even(index):
    return index % 2 == 0


def edges_kernel(blk_ref, first_ref, second_ref, wide, dense):
    wide[:, 0:20, :] = blk_ref[...].astype(f32)
    start = jnp.where(even(lax.axis_index("gx")), 10, 0)
    for x in range(10):
        dense[0, 20 * x : 20 * x + 20, :] = wide[start + x, 0:20, :]
        dense[1, 20 * x : 20 * x + 20, :] = wide[10 - start + x, 0:20, :]
    first_ref[...] = dense[0].astype(bf16)
    second_ref[...] = dense[1].astype(bf16)


def rim_rows(wide, dense, count):
    start = jnp.where(even(lax.axis_index("gy")), 10, 0)
    for x in range(count):
        dense[0, 10 * x : 10 * x + 10, :] = wide[x, pl.ds(start, 10), :]
        dense[1, 10 * x : 10 * x + 10, :] = wide[x, pl.ds(10 - start, 10), :]


def rim_own_kernel(blk_ref, out_ref, wide, dense):
    wide[:, 0:20, :] = blk_ref[...].astype(f32)
    rim_rows(wide, dense, 20)
    out_ref[...] = dense[...]


def rim_kernel(own_ref, next_ref, near_ref, first_ref, second_ref, wide, dense):
    even_x = even(lax.axis_index("gx"))
    start = jnp.where(even_x, 10, 0)
    dense[0] = near_ref[...].astype(f32)
    dense[1] = next_ref[...].astype(f32)
    for x in range(10):
        wide[start + x, 0:20, :] = dense[0, 20 * x : 20 * x + 20, :]
        wide[10 - start + x, 0:20, :] = dense[1, 20 * x : 20 * x + 20, :]
    rim_rows(wide, dense, 20)
    for k, out_ref in enumerate((first_ref, second_ref)):
        out_ref[...] = jnp.concatenate([own_ref[k], dense[k]], axis=0).astype(bf16)


def assemble(blk_ref, next_x_ref, near_x_ref, next_y_ref, near_y_ref, d_ref, dense, sides):
    even_x = even(lax.axis_index("gx"))
    even_y = even(lax.axis_index("gy"))
    upper = jnp.where(even_y, 1, 0)
    dense[upper] = near_y_ref[...].astype(f32)
    dense[1 - upper] = next_y_ref[...].astype(f32)
    upper = jnp.where(even_x, 1, 0)
    sides[upper] = near_x_ref[...].astype(f32)
    sides[1 - upper] = next_x_ref[...].astype(f32)
    for x in range(40):
        p, i = x % 2, x // 2
        at = 10 * (x - 10 if 10 <= x < 30 else x + 20 if x < 10 else x)
        d_ref[p, i, 0:10, :] = dense[0, at : at + 10, :]
        d_ref[p, i, 30:40, :] = dense[1, at : at + 10, :]
        if 10 <= x < 30:
            centre = blk_ref[x - 10].astype(f32)
        else:
            at = 20 * (x % 30)
            centre = sides[x // 30, at : at + 20, :]
        d_ref[p, i, 10:30, :] = centre


def pack_kernel(
    blk_ref, next_x_ref, near_x_ref, next_y_ref, near_y_ref, mid_ref,
    d_out_ref, second_ref, first_ref,
    d_ref, dense, sides, mid,
):
    even_x = even(lax.axis_index("gx"))
    for n in range(5):
        mid[n] = mid_ref[n + 2].astype(f32)
        right, left = mid[n, 1:10, :], mid[n, 6:15, :]
        first_ref[n] = jnp.where(even_x, right, left).astype(bf16)
        second_ref[n] = jnp.where(even_x, left, right).astype(bf16)
    assemble(blk_ref, next_x_ref, near_x_ref, next_y_ref, near_y_ref, d_ref, dense, sides)
    for x in range(40):
        d_out_ref[x] = d_ref[x % 2, x // 2, 0:40, :].astype(bf16)


def restrict_kernel(
    blk_ref, next_x_ref, near_x_ref, next_y_ref, near_y_ref,
    own_ref, out_ref,
    d_ref, dense, sides, planes, cells, mid,
):
    assemble(blk_ref, next_x_ref, near_x_ref, next_y_ref, near_y_ref, d_ref, dense, sides)

    def fine(x):
        return d_ref[x % 2, x // 2]

    for i in range(16):
        c = 2 * i + 4
        planes[i] = (
            fine(c) + 0.5625 * (fine(c - 1) + fine(c + 1)) - 0.0625 * (fine(c - 3) + fine(c + 3))
        )
    for i in range(16):
        def tap(o):
            return planes[i, pl.ds(4 + o, 16, stride=2), :]
        cells[16 * i : 16 * i + 16, :] = (
            tap(0) + 0.5625 * (tap(-1) + tap(1)) - 0.0625 * (tap(-3) + tap(3))
        )
    zero = jnp.zeros((16, 128), f32)
    rows = []
    for n in range(9):
        pair = []
        for y in (2 * n - 4, 2 * n - 3):
            inside = -3 <= y <= 12
            pair.append(cells[pl.ds(y + 3, 16, stride=16), :] if inside else zero)
        rows.append(jnp.concatenate(pair, axis=1))
    r, c = iota2((256, 128))
    down_z = jnp.where(r // 128 == c // 64, weight(r % 128 - 2 * (c % 64)), 0.0)
    value = exact_dot(jnp.concatenate(rows, axis=0), down_z)
    r, c = iota2((144, 128))
    cell_x = 10 * lax.axis_index("gx") - 3 + r % 16
    cell_y = 10 * lax.axis_index("gy") - 4 + 2 * (r // 16) + c // 64
    inside = (cell_x >= 0) & (cell_x < 320) & (cell_y >= 0) & (cell_y < 80)
    value = jnp.where(inside, value, 0.0).astype(bf16).astype(f32)
    for n in range(9):
        mid[n, 0:16, :] = value[16 * n : 16 * n + 16]
        mid[n, 16:24, :] = jnp.zeros((8, 128), f32)
    for n in range(9):
        own_ref[n] = value[16 * n : 16 * n + 16].astype(bf16)

    lane = lax.broadcasted_iota(jnp.int32, (1, 128), 1)
    odd = lane >= 64
    weight_0 = jnp.where(odd, 0.5625, 1.0)
    weight_1 = jnp.where(odd, 0.5625, 0.0)
    weight_3 = jnp.where(odd, -0.0625, 0.0)
    r, c = iota2((128, 32))
    down_z = weight(r % 64 - 2 * c)
    sums = []
    for y in range(5):
        n = y + 2
        def tap(o):
            def part(k):
                return mid[k, pl.ds(3 + o, 8, stride=2), :]
            return (
                weight_0 * part(n) + weight_1 * part(n - 1) + weight_3 * (part(n - 2) + part(n + 1))
            )
        sums.append(tap(0) + 0.5625 * (tap(-1) + tap(1)) - 0.0625 * (tap(-3) + tap(3)))
    out = exact_dot(jnp.concatenate(sums, axis=0), down_z)
    main = jnp.concatenate([out[8 * y : 8 * y + 8] for y in range(4)], axis=1)[0:5]
    last = jnp.concatenate([out[32 + x : 33 + x] for x in range(4)], axis=1)
    rest = jnp.concatenate([out[36:37], jnp.zeros((1, 96), f32)], axis=1)
    row = jnp.concatenate([main, last, rest, jnp.zeros((1, 128), f32)], axis=0)
    for k in range(out_ref.shape[0]):
        out_ref[k] = row


def fine_kernel(lo, hi, first, d_in_ref, v_ref, *refs):
    if first:
        out_ref, w0, w1, e0, e1, d_ref = refs
    else:
        acc_ref, out_ref, w0, w1, e0, e1, d_ref = refs
    for x in range(40):
        d_ref[x % 2, x // 2, 0:40, :] = d_in_ref[x].astype(f32)
        d_ref[x % 2, x // 2, 40:48, :] = jnp.zeros((8, 128), f32)
    r, c = iota2((128, 128))
    mask = jnp.abs(r - c) <= REACH
    zero = jnp.zeros((128, 128), bf16)
    for w in (w0, w1):
        for k in range(GROUP):
            w[2816 * k : 2816 * k + 128, 128:256] = zero
            w[2816 * k + 2688 : 2816 * k + 2816, 0:128] = zero

    def build(w, start):
        for k in range(GROUP):
            for a in range(TAPS):
                line = jnp.broadcast_to(v_ref[pl.ds(a * TAPS + start + k, 1), :], (128, 128))
                line = pltpu.roll(line, 0, 1, stride=1, stride_axis=0)
                band = jnp.where(mask, line, 0.0).astype(bf16)
                at = 2816 * k + 128 * a
                w[at : at + 128, 0:128] = band
                w[at + 128 : at + 256, 128:256] = band

    def dot(w, e, start):
        tiles = []
        for k in range(GROUP):
            for p in range(2):
                for q in range(10):
                    part = d_ref[p, 2 * q : 2 * q + 2, pl.ds(start + k, 24), :].reshape(48, 128)
                    e[k, 0, 48 * q : 48 * q + 48, p * 128 : (p + 1) * 128] = part.astype(bf16)
                for q in range(9):
                    part = d_ref[p, 2 * q + 1 : 2 * q + 3, pl.ds(start + k, 24), :].reshape(48, 128)
                    e[k, 1, 48 * q : 48 * q + 48, p * 128 : (p + 1) * 128] = part.astype(bf16)
            tiles += [
                e[k, m % 2, 24 * (m - m % 2) : 24 * (m - m % 2) + 240, :] for m in range(11)
            ]
        lhs = jnp.concatenate(tiles, axis=1)
        out_ref[...] += jnp.dot(lhs, w[...], preferred_element_type=f32)

    out_ref[...] = jnp.zeros((240, 256), f32) if first else acc_ref[...]

    def step(t, _):
        b = lo + 2 * GROUP * t
        build(w0, b)
        dot(w0, e0, b)
        build(w1, b + GROUP)
        dot(w1, e1, b + GROUP)
        return 0

    groups = (hi - lo) // GROUP
    lax.fori_loop(0, groups // 2, step, 0)
    if groups % 2:
        build(w0, hi - GROUP)
        dot(w0, e0, hi - GROUP)


def fine_sum(lo, hi, d, v, acc=None):
    return vmem_call(
        functools.partial(fine_kernel, lo, hi, acc is None),
        [jax.ShapeDtypeStruct((240, 256), f32)],
        [pltpu.VMEM((GROUP * 2816, 256), bf16)] * 2
        + [pltpu.VMEM((GROUP, 2, 480, 256), bf16)] * 2
        + [pltpu.VMEM((2, 20, 48, 128), f32)],
        "fine_sum",
        (d, v) if acc is None else (d, v, acc),
        flops=(hi - lo) * 2 * 240 * 2816 * 256,
        limit=20,
    )[0]


def spread_kernel(recv_ref, mx_ref, own_ref, next_ref, near_ref, out_ref, buf, tail):
    even_x = even(lax.axis_index("gx"))
    start = 10 * lax.axis_index("gx")
    halves = [mx_ref[h, pl.ds(start, 16), :] for h in range(2)]
    lane = lax.broadcasted_iota(jnp.int32, (16, 128), 1) % 8
    rows = [jnp.concatenate(halves, axis=1)]
    for x in range(5):
        at = 5 if x < 4 else 6
        moved = [jnp.where(lane == at, pltpu.roll(h, at - x, 1), 0.0) for h in halves]
        rows.append(jnp.concatenate(moved, axis=1))
    coarse = recv_ref[...].reshape(8 * recv_ref.shape[0], 128)
    value = two_part_dot(jnp.concatenate(rows, axis=0), coarse)
    last = value[80:96, 0:32]
    for x in range(4):
        last = last + value[16 * x + 16 : 16 * x + 32, 32 * x : 32 * x + 32]
    tail[...] = jnp.concatenate([last, jnp.zeros((16, 96), f32)], axis=1)
    last = tail[pl.ds(0, 4, stride=4), :]
    for k in range(1, 4):
        last = last + pltpu.roll(tail[pl.ds(k, 4, stride=4), :], 32 * k, 1)
    for n in range(5):
        near, other = near_ref[n].astype(f32), next_ref[n].astype(f32)
        buf[33 * n : 33 * n + 8, :] = jnp.where(even_x, other, near)[1:9]
        buf[33 * n + 8 : 33 * n + 24, :] = own_ref[n + 2].astype(f32)
        buf[33 * n + 24 : 33 * n + 33, :] = jnp.where(even_x, near, other)
    for at, part in ((165, last), (176, value[0:16])):
        rows = part.shape[0]
        high = part.astype(bf16).astype(f32)
        buf[at : at + rows, :] = high
        buf[at + rows : at + 2 * rows, :] = part - high
    buf[173:176, :] = jnp.zeros((3, 128), f32)
    packed = buf[...].astype(bf16)
    for k in range(out_ref.shape[0]):
        out_ref[k] = packed


def final_kernel(
    recv_ref, my_ref, mz_ref, near_ref, far_ref, fine_ref, out_ref,
    cells, w0, w1, acc, moved, wide, line, tail,
):
    index_x = lax.axis_index("gx")
    index_y = lax.axis_index("gy")
    count = recv_ref.shape[0]
    cells[:, 32:40, :] = jnp.zeros((17, 8, 128), f32)
    for step in range(-2, 3):
        source = index_y + step
        inside = (source >= 0) & (source < count)
        got = recv_ref[jnp.clip(source, 0, count - 1), 0:176, :].astype(f32)
        line[...] = jnp.where(inside, got, 0.0)
        for p in range(5):
            n = 5 * step + 6 + p
            if 0 <= n < 17:
                cells[n, 0:33, :] = line[33 * p : 33 * p + 33, :]

    r, c = iota2((128, 128))
    mask = jnp.abs(r % 64 - c % 64) <= REACH

    def band_rows(w, a, at):
        base = TAPS * TAPS + a * TAPS
        for j in range(11):
            same = near_ref[pl.ds(base + 2 * j, 1), :]
            upper = same
            lower = same
            if j > 0:
                upper = same + far_ref[pl.ds(base + 2 * j - 1, 1), :]
            if j < 10:
                lower = same + far_ref[pl.ds(base + 2 * j + 1, 1), :]
            upper = pltpu.roll(jnp.broadcast_to(upper, (64, 128)), 0, 1, stride=1, stride_axis=0)
            lower = pltpu.roll(jnp.broadcast_to(lower, (64, 128)), 64, 1, stride=1, stride_axis=0)
            band = jnp.where(mask, jnp.concatenate([upper, lower], axis=0), 0.0).astype(bf16)
            w[at + 128 * j : at + 128 * j + 128, :] = band

    def build(w, a):
        for k in range(3):
            band_rows(w, a + k, 1408 * k)

    def dot(w, a):
        rows = []
        for k in range(3):
            part = [cells[n, pl.ds(a + k, 16), :].astype(bf16) for n in range(17)]
            rows.append([jnp.concatenate(part[g : g + 11], axis=1) for g in range(7)])
        lhs = jnp.concatenate(
            [jnp.concatenate([rows[k][g] for k in range(3)], axis=1) for g in range(7)], axis=0
        )
        acc[...] += jnp.dot(lhs, w[...], preferred_element_type=f32)

    acc[...] = jnp.zeros((112, 128), f32)
    build(w0, 0)

    def step(t, _):
        a = 6 * t
        build(w1, a + 3)
        dot(w0, a)
        build(w0, a + 6)
        dot(w1, a + 3)
        return 0

    lax.fori_loop(0, 3, step, 0)
    dot(w0, 18)

    start = 10 * index_y
    sums = [[None] * 14, [None] * 14]
    for k in range(count):
        main = recv_ref[k, 176:192, :].astype(f32) + recv_ref[k, 192:208, :].astype(f32)
        last = recv_ref[k, 160:176, :].astype(f32)
        last = last[5:9] + last[9:13]
        tail[k, pl.ds(0, 4, stride=4), :] = last
        for r in range(1, 4):
            tail[k, pl.ds(r, 4, stride=4), :] = pltpu.roll(last, 128 - 32 * r, 1)
        for h, value in ((0, main), (1, tail[k])):
            rows_y = my_ref[2 * k + h, pl.ds(start, 16), :]
            for y in range(14):
                term = value * rows_y[y : y + 1, :]
                sums[h][y] = term if k == 0 else sums[h][y] + term
    rows = [
        jnp.concatenate([sums[h][2 * n + p] for p in range(2) for h in range(2)], axis=1)
        for n in range(7)
    ]
    top = two_part_dot(jnp.concatenate(rows, axis=0), mz_ref[...])
    total = acc[...] + top
    r, c = iota2((112, 128))
    cell_x = 10 * index_x - 1 + r % 16
    cell_y = 10 * index_y - 2 + 2 * (r // 16) + c // 64
    inside = (cell_x >= 0) & (cell_x < 320) & (cell_y >= 0) & (cell_y < 80)
    total = jnp.where(inside, total, 0.0)
    r, c = iota2((128, 256))
    up_z = jnp.where(r // 64 == c // 128, weight(c % 128 - 2 * (r % 64)), 0.0)
    wide[...] = exact_dot(total, up_z)

    def middle_y(y):
        n, par = (y + 2) // 2, y % 2
        return wide[16 * n : 16 * n + 16, 128 * par : 128 * par + 128]

    for y in range(20):
        m = y // 2
        if y % 2 == 0:
            value = middle_y(m)
        else:
            value = 0.5625 * (middle_y(m) + middle_y(m + 1)) - 0.0625 * (
                middle_y(m - 1) + middle_y(m + 2)
            )
        moved[16 * y : 16 * y + 16, :] = value
    planes = [moved[pl.ds(k, 20, stride=16), :] for k in range(13)]
    for x in range(20):
        m = x // 2
        if x % 2 == 0:
            value = planes[m + 1]
        else:
            value = 0.5625 * (planes[m + 1] + planes[m + 2]) - 0.0625 * (planes[m] + planes[m + 3])
        out_ref[x] = value + fine_ref[24 * m : 24 * m + 20, 128 * (x % 2) : 128 * (x % 2) + 128]


def swap(first, second, axis):
    count = lax.axis_size(axis)
    pairs = [(k, k + 1) for k in range(0, count - 1, 2)]
    others = [(k, k + 1) for k in range(1, count - 1, 2)]

    def both(ends):
        return ends + [(b, a) for a, b in ends]

    second = lax.ppermute(second, axis, both(others))
    return lax.ppermute(first, axis, both(pairs)), second


def per_device(charges, kernels):
    count_x = lax.axis_size("gx")
    count_y = lax.axis_size("gy")
    spread = charges.shape[0] * count_x / 16.0
    shape = jax.ShapeDtypeStruct
    scratch = [pltpu.VMEM((20, 24, 128), f32), pltpu.VMEM((2, 200, 128), f32)]
    first, second = vmem_call(
        edges_kernel, [shape((200, 128), bf16)] * 2, scratch, "edges", (charges,)
    )
    near_x, next_x = swap(first, second, "gx")
    own = vmem_call(
        rim_own_kernel,
        [shape((2, 200, 128), f32)],
        scratch,
        "rim_own",
        (charges,),
        flops=1 << 20,
    )[0]
    first, second = vmem_call(
        rim_kernel,
        [shape((400, 128), bf16)] * 2,
        scratch,
        "rim",
        (own, next_x, near_x),
    )
    first, second, kernels = lax.optimization_barrier((first, second, kernels))
    near, far = (
        jnp.dot(kernels.reshape(-1, TAPS), jnp.asarray(m, bf16), preferred_element_type=f32)
        for m in spots_np()
    )
    near_y, next_y = swap(first, second, "gy")
    next_y, near_y, near, far = lax.optimization_barrier((next_y, near_y, near, far))
    pieces = (charges, next_x, near_x, next_y, near_y)
    scratch = [
        pltpu.VMEM((2, 20, 48, 128), f32),
        pltpu.VMEM((2, 400, 128), f32),
        pltpu.VMEM((2, 200, 128), f32),
    ]
    own, coarse = vmem_call(
        restrict_kernel,
        [shape((9, 16, 128), bf16), shape((count_x, 8, 128), f32)],
        scratch
        + [
            pltpu.VMEM((16, 48, 128), f32),
            pltpu.VMEM((256, 128), f32),
            pltpu.VMEM((9, 24, 128), f32),
        ],
        "restrict",
        pieces,
    )
    d, second, first = vmem_call(
        pack_kernel,
        [
            shape((40, 40, 128), bf16),
            shape((5, 9, 128), bf16),
            shape((5, 9, 128), bf16),
        ],
        scratch + [pltpu.VMEM((5, 16, 128), f32)],
        "pack",
        pieces + (own,),
    )
    near_m, next_m = swap(first, second, "gx")
    coarse = lax.all_to_all(coarse, "gx", 0, 0)
    fine = fine_sum(0, SPLIT, d, near)
    coarse, fine = lax.optimization_barrier((coarse, fine))
    parts = vmem_call(
        spread_kernel,
        [shape((count_y, 208, 128), bf16)],
        [pltpu.VMEM((208, 128), f32), pltpu.VMEM((16, 128), f32)],
        "spread",
        (coarse, jnp.asarray(matrix_x_np(spread)), own, next_m, near_m),
    )[0]
    parts, near = lax.optimization_barrier((parts, near))
    parts = lax.all_to_all(parts, "gy", 0, 0)
    fine = fine_sum(SPLIT, TAPS, d, near, fine)
    return vmem_call(
        final_kernel,
        [shape((20, 20, 128), f32)],
        [
            pltpu.VMEM((17, 40, 128), f32),
            pltpu.VMEM((4224, 128), bf16),
            pltpu.VMEM((4224, 128), bf16),
            pltpu.VMEM((112, 128), f32),
            pltpu.VMEM((320, 128), f32),
            pltpu.VMEM((112, 256), f32),
            pltpu.VMEM((176, 128), f32),
            pltpu.VMEM((count_y, 16, 128), f32),
        ],
        "final",
        (
            parts,
            jnp.asarray(matrix_y_np(spread)),
            jnp.asarray(matrix_z_np(spread)),
            near,
            far,
            fine,
        ),
    )[0]


def solution(mesh):
    return jax.shard_map(
        per_device,
        mesh=mesh,
        in_specs=(P("gx", "gy", None), P()),
        out_specs=P("gx", "gy", None),
        check_vma=False,
    )
```

```python
import functools
import numpy as np
import jax
import jax.numpy as jnp
from jax import lax
from jax.experimental import pallas as pl
from jax.experimental.pallas import tpu as pltpu
from jax.sharding import PartitionSpec as P

f32 = jnp.float32
bf16 = jnp.bfloat16
spread_norm = 1.2533141
REACH = 10
TAPS = 21
GROUP = 3
SPLIT = 6


def weight_np(offset):
    d = np.abs(offset)
    return np.where(d == 0, 1.0, np.where(d == 1, 0.5625, np.where(d == 3, -0.0625, 0.0)))


def top_matrix_np(n, spread):
    prolong = weight_np(np.arange(2 * n)[:, None] - 2 * np.arange(n)[None, :])
    offset = (np.arange(n)[:, None] - np.arange(n)[None, :]) / spread
    return prolong @ (np.exp(-offset * offset) / np.sqrt(spread * spread_norm))


def lane_tiles(m):
    return m.reshape(m.shape[0], -1, 128).transpose(1, 0, 2).astype(np.float32)


def matrix_x_np(spread):
    m = top_matrix_np(160, spread).reshape(320, 32, 5)
    out = np.zeros((328, 32, 8))
    out[1:321, :, :5] = m
    return lane_tiles(out.reshape(328, 256))


def matrix_y_np(spread):
    m = top_matrix_np(40, spread).reshape(80, 8, 5)
    out = np.zeros((88, 8, 8))
    out[2:82, :, :5] = m
    return lane_tiles(np.repeat(out.reshape(88, 64), 32, axis=1))


def matrix_z_np(spread):
    m = top_matrix_np(32, spread).T
    out = np.zeros((2, 8, 32, 2, 64))
    for par in range(2):
        out[par, :, :, par, :] = m[None]
    return out.reshape(512, 128).astype(np.float32)


def spots_np():
    taps = np.arange(TAPS)[:, None]
    lanes = np.arange(128)[None, :]
    near = lanes == (REACH - taps) % 128
    far = lanes == (64 + REACH - taps) % 128
    return near, far


def weight(d):
    d = jnp.abs(d)
    return jnp.where(d == 0, 1.0, jnp.where(d == 1, 0.5625, jnp.where(d == 3, -0.0625, 0.0))).astype(f32)


def exact_dot(rows, weights):
    count = rows.shape[0]
    high = rows.astype(bf16)
    rest = rows - high.astype(f32)
    middle = rest.astype(bf16)
    low = (rest - middle.astype(f32)).astype(bf16)
    out = jnp.dot(
        jnp.concatenate([high, middle, low], axis=0),
        weights.astype(bf16),
        preferred_element_type=f32,
    )
    return out[0:count] + (out[count : 2 * count] + out[2 * count :])


def parts_of(value):
    high = value.astype(bf16)
    return high, (value - high.astype(f32)).astype(bf16)


def two_part_dot(rows, weights):
    high, low = parts_of(rows)
    w_high, w_low = parts_of(weights)
    return jnp.dot(
        jnp.concatenate([high, high, low], axis=1),
        jnp.concatenate([w_high, w_low, w_high], axis=0),
        preferred_element_type=f32,
    )


def iota2(shape):
    return (lax.broadcasted_iota(jnp.int32, shape, 0), lax.broadcasted_iota(jnp.int32, shape, 1))


def vmem_call(body, out_shape, scratch, name, args, flops=0, limit=8):
    def spec(space):
        return pl.BlockSpec(memory_space=space)

    return pl.pallas_call(
        body,
        out_shape=out_shape,
        in_specs=[spec(pltpu.VMEM)] * len(args),
        out_specs=[spec(pltpu.VMEM)] * len(out_shape),
        scratch_shapes=scratch,
        compiler_params=pltpu.CompilerParams(vmem_limit_bytes=limit << 20),
        cost_estimate=pl.CostEstimate(flops=flops, bytes_accessed=1 << 16, transcendentals=0),
        name=name,
    )(*args)


def even(index):
    return index % 2 == 0


def edges_kernel(blk_ref, first_ref, second_ref, wide, dense):
    wide[:, 0:20, :] = blk_ref[...].astype(f32)
    start = jnp.where(even(lax.axis_index("gx")), 10, 0)
    for x in range(10):
        dense[0, 20 * x : 20 * x + 20, :] = wide[start + x, 0:20, :]
        dense[1, 20 * x : 20 * x + 20, :] = wide[10 - start + x, 0:20, :]
    first_ref[...] = dense[0].astype(bf16)
    second_ref[...] = dense[1].astype(bf16)


def rim_rows(wide, dense, count):
    start = jnp.where(even(lax.axis_index("gy")), 10, 0)
    for x in range(count):
        dense[0, 10 * x : 10 * x + 10, :] = wide[x, pl.ds(start, 10), :]
        dense[1, 10 * x : 10 * x + 10, :] = wide[x, pl.ds(10 - start, 10), :]


def rim_own_kernel(blk_ref, out_ref, wide, dense):
    wide[:, 0:20, :] = blk_ref[...].astype(f32)
    rim_rows(wide, dense, 20)
    out_ref[...] = dense[...]


def rim_kernel(own_ref, next_ref, near_ref, first_ref, second_ref, wide, dense):
    even_x = even(lax.axis_index("gx"))
    start = jnp.where(even_x, 10, 0)
    dense[0] = near_ref[...].astype(f32)
    dense[1] = next_ref[...].astype(f32)
    for x in range(10):
        wide[start + x, 0:20, :] = dense[0, 20 * x : 20 * x + 20, :]
        wide[10 - start + x, 0:20, :] = dense[1, 20 * x : 20 * x + 20, :]
    rim_rows(wide, dense, 20)
    for k, out_ref in enumerate((first_ref, second_ref)):
        out_ref[...] = jnp.concatenate([own_ref[k], dense[k]], axis=0).astype(bf16)


def assemble(blk_ref, next_x_ref, near_x_ref, next_y_ref, near_y_ref, d_ref, dense, sides):
    even_x = even(lax.axis_index("gx"))
    even_y = even(lax.axis_index("gy"))
    upper = jnp.where(even_y, 1, 0)
    dense[upper] = near_y_ref[...].astype(f32)
    dense[1 - upper] = next_y_ref[...].astype(f32)
    upper = jnp.where(even_x, 1, 0)
    sides[upper] = near_x_ref[...].astype(f32)
    sides[1 - upper] = next_x_ref[...].astype(f32)
    for x in range(40):
        p, i = x % 2, x // 2
        at = 10 * (x - 10 if 10 <= x < 30 else x + 20 if x < 10 else x)
        d_ref[p, i, 0:10, :] = dense[0, at : at + 10, :]
        d_ref[p, i, 30:40, :] = dense[1, at : at + 10, :]
        if 10 <= x < 30:
            centre = blk_ref[x - 10].astype(f32)
        else:
            at = 20 * (x % 30)
            centre = sides[x // 30, at : at + 20, :]
        d_ref[p, i, 10:30, :] = centre


def pack_kernel(
    blk_ref, next_x_ref, near_x_ref, next_y_ref, near_y_ref, mid_ref,
    d_out_ref, second_ref, first_ref,
    d_ref, dense, sides, mid,
):
    even_x = even(lax.axis_index("gx"))
    for n in range(5):
        mid[n] = mid_ref[n + 2].astype(f32)
        right, left = mid[n, 1:10, :], mid[n, 6:15, :]
        first_ref[n] = jnp.where(even_x, right, left).astype(bf16)
        second_ref[n] = jnp.where(even_x, left, right).astype(bf16)
    assemble(blk_ref, next_x_ref, near_x_ref, next_y_ref, near_y_ref, d_ref, dense, sides)
    for x in range(40):
        d_out_ref[x] = d_ref[x % 2, x // 2, 0:40, :].astype(bf16)


def restrict_kernel(
    blk_ref, next_x_ref, near_x_ref, next_y_ref, near_y_ref,
    own_ref, out_ref,
    d_ref, dense, sides, planes, cells, mid,
):
    assemble(blk_ref, next_x_ref, near_x_ref, next_y_ref, near_y_ref, d_ref, dense, sides)

    def fine(x):
        return d_ref[x % 2, x // 2]

    for i in range(16):
        c = 2 * i + 4
        planes[i] = (
            fine(c) + 0.5625 * (fine(c - 1) + fine(c + 1)) - 0.0625 * (fine(c - 3) + fine(c + 3))
        )
    for i in range(16):
        def tap(o):
            return planes[i, pl.ds(4 + o, 16, stride=2), :]
        cells[16 * i : 16 * i + 16, :] = (
            tap(0) + 0.5625 * (tap(-1) + tap(1)) - 0.0625 * (tap(-3) + tap(3))
        )
    zero = jnp.zeros((16, 128), f32)
    rows = []
    for n in range(9):
        pair = []
        for y in (2 * n - 4, 2 * n - 3):
            inside = -3 <= y <= 12
            pair.append(cells[pl.ds(y + 3, 16, stride=16), :] if inside else zero)
        rows.append(jnp.concatenate(pair, axis=1))
    r, c = iota2((256, 128))
    down_z = jnp.where(r // 128 == c // 64, weight(r % 128 - 2 * (c % 64)), 0.0)
    value = exact_dot(jnp.concatenate(rows, axis=0), down_z)
    r, c = iota2((144, 128))
    cell_x = 10 * lax.axis_index("gx") - 3 + r % 16
    cell_y = 10 * lax.axis_index("gy") - 4 + 2 * (r // 16) + c // 64
    inside = (cell_x >= 0) & (cell_x < 320) & (cell_y >= 0) & (cell_y < 80)
    value = jnp.where(inside, value, 0.0).astype(bf16).astype(f32)
    for n in range(9):
        mid[n, 0:16, :] = value[16 * n : 16 * n + 16]
        mid[n, 16:24, :] = jnp.zeros((8, 128), f32)
    for n in range(9):
        own_ref[n] = value[16 * n : 16 * n + 16].astype(bf16)

    lane = lax.broadcasted_iota(jnp.int32, (1, 128), 1)
    odd = lane >= 64
    weight_0 = jnp.where(odd, 0.5625, 1.0)
    weight_1 = jnp.where(odd, 0.5625, 0.0)
    weight_3 = jnp.where(odd, -0.0625, 0.0)
    r, c = iota2((128, 32))
    down_z = weight(r % 64 - 2 * c)
    sums = []
    for y in range(5):
        n = y + 2
        def tap(o):
            def part(k):
                return mid[k, pl.ds(3 + o, 8, stride=2), :]
            return (
                weight_0 * part(n) + weight_1 * part(n - 1) + weight_3 * (part(n - 2) + part(n + 1))
            )
        sums.append(tap(0) + 0.5625 * (tap(-1) + tap(1)) - 0.0625 * (tap(-3) + tap(3)))
    out = exact_dot(jnp.concatenate(sums, axis=0), down_z)
    main = jnp.concatenate([out[8 * y : 8 * y + 8] for y in range(4)], axis=1)[0:5]
    last = jnp.concatenate([out[32 + x : 33 + x] for x in range(4)], axis=1)
    rest = jnp.concatenate([out[36:37], jnp.zeros((1, 96), f32)], axis=1)
    row = jnp.concatenate([main, last, rest, jnp.zeros((1, 128), f32)], axis=0)
    for k in range(out_ref.shape[0]):
        out_ref[k] = row


def fine_kernel(lo, hi, first, d_in_ref, v_ref, *refs):
    if first:
        out_ref, w0, w1, e0, e1, d_ref = refs
    else:
        acc_ref, out_ref, w0, w1, e0, e1, d_ref = refs
    for x in range(40):
        d_ref[x % 2, x // 2, 0:40, :] = d_in_ref[x].astype(f32)
        d_ref[x % 2, x // 2, 40:48, :] = jnp.zeros((8, 128), f32)
    r, c = iota2((128, 128))
    mask = jnp.abs(r - c) <= REACH
    zero = jnp.zeros((128, 128), bf16)
    for w in (w0, w1):
        for k in range(GROUP):
            w[2816 * k : 2816 * k + 128, 128:256] = zero
            w[2816 * k + 2688 : 2816 * k + 2816, 0:128] = zero

    def build(w, start):
        for k in range(GROUP):
            for a in range(TAPS):
                line = jnp.broadcast_to(v_ref[pl.ds(a * TAPS + start + k, 1), :], (128, 128))
                line = pltpu.roll(line, 0, 1, stride=1, stride_axis=0)
                band = jnp.where(mask, line, 0.0).astype(bf16)
                at = 2816 * k + 128 * a
                w[at : at + 128, 0:128] = band
                w[at + 128 : at + 256, 128:256] = band

    def dot(w, e, start):
        tiles = []
        for k in range(GROUP):
            for p in range(2):
                for q in range(10):
                    part = d_ref[p, 2 * q : 2 * q + 2, pl.ds(start + k, 24), :].reshape(48, 128)
                    e[k, 0, 48 * q : 48 * q + 48, p * 128 : (p + 1) * 128] = part.astype(bf16)
                for q in range(9):
                    part = d_ref[p, 2 * q + 1 : 2 * q + 3, pl.ds(start + k, 24), :].reshape(48, 128)
                    e[k, 1, 48 * q : 48 * q + 48, p * 128 : (p + 1) * 128] = part.astype(bf16)
            tiles += [
                e[k, m % 2, 24 * (m - m % 2) : 24 * (m - m % 2) + 240, :] for m in range(11)
            ]
        lhs = jnp.concatenate(tiles, axis=1)
        out_ref[...] += jnp.dot(lhs, w[...], preferred_element_type=f32)

    out_ref[...] = jnp.zeros((240, 256), f32) if first else acc_ref[...]

    def step(t, _):
        b = lo + 2 * GROUP * t
        build(w0, b)
        dot(w0, e0, b)
        build(w1, b + GROUP)
        dot(w1, e1, b + GROUP)
        return 0

    groups = (hi - lo) // GROUP
    lax.fori_loop(0, groups // 2, step, 0)
    if groups % 2:
        build(w0, hi - GROUP)
        dot(w0, e0, hi - GROUP)


def fine_sum(lo, hi, d, v, acc=None):
    return vmem_call(
        functools.partial(fine_kernel, lo, hi, acc is None),
        [jax.ShapeDtypeStruct((240, 256), f32)],
        [pltpu.VMEM((GROUP * 2816, 256), bf16)] * 2
        + [pltpu.VMEM((GROUP, 2, 480, 256), bf16)] * 2
        + [pltpu.VMEM((2, 20, 48, 128), f32)],
        "fine_sum",
        (d, v) if acc is None else (d, v, acc),
        flops=(hi - lo) * 2 * 240 * 2816 * 256,
        limit=20,
    )[0]


def spread_kernel(recv_ref, mx_ref, own_ref, next_ref, near_ref, out_ref, buf, tail):
    even_x = even(lax.axis_index("gx"))
    start = 10 * lax.axis_index("gx")
    halves = [mx_ref[h, pl.ds(start, 16), :] for h in range(2)]
    lane = lax.broadcasted_iota(jnp.int32, (16, 128), 1) % 8
    rows = [jnp.concatenate(halves, axis=1)]
    for x in range(5):
        at = 5 if x < 4 else 6
        moved = [jnp.where(lane == at, pltpu.roll(h, at - x, 1), 0.0) for h in halves]
        rows.append(jnp.concatenate(moved, axis=1))
    coarse = recv_ref[...].reshape(8 * recv_ref.shape[0], 128)
    value = two_part_dot(jnp.concatenate(rows, axis=0), coarse)
    last = value[80:96, 0:32]
    for x in range(4):
        last = last + value[16 * x + 16 : 16 * x + 32, 32 * x : 32 * x + 32]
    tail[...] = jnp.concatenate([last, jnp.zeros((16, 96), f32)], axis=1)
    last = tail[pl.ds(0, 4, stride=4), :]
    for k in range(1, 4):
        last = last + pltpu.roll(tail[pl.ds(k, 4, stride=4), :], 32 * k, 1)
    for n in range(5):
        near, other = near_ref[n].astype(f32), next_ref[n].astype(f32)
        buf[33 * n : 33 * n + 8, :] = jnp.where(even_x, other, near)[1:9]
        buf[33 * n + 8 : 33 * n + 24, :] = own_ref[n + 2].astype(f32)
        buf[33 * n + 24 : 33 * n + 33, :] = jnp.where(even_x, near, other)
    for at, part in ((165, last), (173, value[0:13])):
        rows = part.shape[0]
        high = part.astype(bf16).astype(f32)
        buf[at : at + rows, :] = high
        buf[at + rows : at + 2 * rows, :] = part - high
    buf[199:200, :] = jnp.zeros((1, 128), f32)
    packed = buf[...].astype(bf16)
    for k in range(out_ref.shape[0]):
        out_ref[k] = packed


def final_kernel(
    recv_ref, my_ref, mz_ref, near_ref, far_ref, fine_ref, out_ref,
    cells, w0, w1, acc, moved, wide, line, tail,
):
    index_x = lax.axis_index("gx")
    index_y = lax.axis_index("gy")
    count = recv_ref.shape[0]
    cells[:, 32:40, :] = jnp.zeros((17, 8, 128), f32)
    for step in range(-2, 3):
        source = index_y + step
        inside = (source >= 0) & (source < count)
        got = recv_ref[jnp.clip(source, 0, count - 1), 0:176, :].astype(f32)
        line[...] = jnp.where(inside, got, 0.0)
        for p in range(5):
            n = 5 * step + 6 + p
            if 0 <= n < 17:
                cells[n, 0:33, :] = line[33 * p : 33 * p + 33, :]

    r, c = iota2((128, 128))
    mask = jnp.abs(r % 64 - c % 64) <= REACH

    def band_rows(w, a, at):
        base = TAPS * TAPS + a * TAPS
        for j in range(11):
            same = near_ref[pl.ds(base + 2 * j, 1), :]
            upper = same
            lower = same
            if j > 0:
                upper = same + far_ref[pl.ds(base + 2 * j - 1, 1), :]
            if j < 10:
                lower = same + far_ref[pl.ds(base + 2 * j + 1, 1), :]
            upper = pltpu.roll(jnp.broadcast_to(upper, (64, 128)), 0, 1, stride=1, stride_axis=0)
            lower = pltpu.roll(jnp.broadcast_to(lower, (64, 128)), 64, 1, stride=1, stride_axis=0)
            band = jnp.where(mask, jnp.concatenate([upper, lower], axis=0), 0.0).astype(bf16)
            w[at + 128 * j : at + 128 * j + 128, :] = band

    def build(w, a):
        for k in range(3):
            band_rows(w, a + k, 1408 * k)

    def dot(w, a):
        rows = []
        for k in range(3):
            part = [cells[n, pl.ds(a + k, 16), :].astype(bf16) for n in range(17)]
            rows.append([jnp.concatenate(part[g : g + 11], axis=1) for g in range(7)])
        lhs = jnp.concatenate(
            [jnp.concatenate([rows[k][g] for k in range(3)], axis=1) for g in range(7)], axis=0
        )
        acc[...] += jnp.dot(lhs, w[...], preferred_element_type=f32)

    acc[...] = jnp.zeros((112, 128), f32)
    build(w0, 0)

    def step(t, _):
        a = 6 * t
        build(w1, a + 3)
        dot(w0, a)
        build(w0, a + 6)
        dot(w1, a + 3)
        return 0

    lax.fori_loop(0, 3, step, 0)
    dot(w0, 18)

    start = 10 * index_y
    sums = [[None] * 14, [None] * 14]
    for k in range(count):
        got = recv_ref[k].astype(f32)
        main = jnp.concatenate([got[173:186] + got[186:199], jnp.zeros((3, 128), f32)], axis=0)
        last = got[165:169] + got[169:173]
        tail[k, pl.ds(0, 4, stride=4), :] = last
        for r in range(1, 4):
            tail[k, pl.ds(r, 4, stride=4), :] = pltpu.roll(last, 128 - 32 * r, 1)
        for h, value in ((0, main), (1, tail[k])):
            rows_y = my_ref[2 * k + h, pl.ds(start, 16), :]
            for y in range(14):
                term = value * rows_y[y : y + 1, :]
                sums[h][y] = term if k == 0 else sums[h][y] + term
    rows = [
        jnp.concatenate([sums[h][2 * n + p] for p in range(2) for h in range(2)], axis=1)
        for n in range(7)
    ]
    top = two_part_dot(jnp.concatenate(rows, axis=0), mz_ref[...])
    total = acc[...] + top
    r, c = iota2((112, 128))
    cell_x = 10 * index_x - 1 + r % 16
    cell_y = 10 * index_y - 2 + 2 * (r // 16) + c // 64
    inside = (cell_x >= 0) & (cell_x < 320) & (cell_y >= 0) & (cell_y < 80)
    total = jnp.where(inside, total, 0.0)
    r, c = iota2((128, 256))
    up_z = jnp.where(r // 64 == c // 128, weight(c % 128 - 2 * (r % 64)), 0.0)
    wide[...] = exact_dot(total, up_z)

    def middle_y(y):
        n, par = (y + 2) // 2, y % 2
        return wide[16 * n : 16 * n + 16, 128 * par : 128 * par + 128]

    for y in range(20):
        m = y // 2
        if y % 2 == 0:
            value = middle_y(m)
        else:
            value = 0.5625 * (middle_y(m) + middle_y(m + 1)) - 0.0625 * (
                middle_y(m - 1) + middle_y(m + 2)
            )
        moved[16 * y : 16 * y + 16, :] = value
    planes = [moved[pl.ds(k, 20, stride=16), :] for k in range(13)]
    for x in range(20):
        m = x // 2
        if x % 2 == 0:
            value = planes[m + 1]
        else:
            value = 0.5625 * (planes[m + 1] + planes[m + 2]) - 0.0625 * (planes[m] + planes[m + 3])
        out_ref[x] = value + fine_ref[24 * m : 24 * m + 20, 128 * (x % 2) : 128 * (x % 2) + 128]


def swap(first, second, axis):
    count = lax.axis_size(axis)
    pairs = [(k, k + 1) for k in range(0, count - 1, 2)]
    others = [(k, k + 1) for k in range(1, count - 1, 2)]

    def both(ends):
        return ends + [(b, a) for a, b in ends]

    second = lax.ppermute(second, axis, both(others))
    return lax.ppermute(first, axis, both(pairs)), second


def per_device(charges, kernels):
    count_x = lax.axis_size("gx")
    count_y = lax.axis_size("gy")
    spread = charges.shape[0] * count_x / 16.0
    shape = jax.ShapeDtypeStruct
    scratch = [pltpu.VMEM((20, 24, 128), f32), pltpu.VMEM((2, 200, 128), f32)]
    first, second = vmem_call(
        edges_kernel, [shape((200, 128), bf16)] * 2, scratch, "edges", (charges,)
    )
    near_x, next_x = swap(first, second, "gx")
    own = vmem_call(
        rim_own_kernel,
        [shape((2, 200, 128), f32)],
        scratch,
        "rim_own",
        (charges,),
        flops=1 << 20,
    )[0]
    first, second = vmem_call(
        rim_kernel,
        [shape((400, 128), bf16)] * 2,
        scratch,
        "rim",
        (own, next_x, near_x),
    )
    first, second, kernels = lax.optimization_barrier((first, second, kernels))
    near, far = (
        jnp.dot(kernels.reshape(-1, TAPS), jnp.asarray(m, bf16), preferred_element_type=f32)
        for m in spots_np()
    )
    near_y, next_y = swap(first, second, "gy")
    next_y, near_y, near, far = lax.optimization_barrier((next_y, near_y, near, far))
    pieces = (charges, next_x, near_x, next_y, near_y)
    scratch = [
        pltpu.VMEM((2, 20, 48, 128), f32),
        pltpu.VMEM((2, 400, 128), f32),
        pltpu.VMEM((2, 200, 128), f32),
    ]
    own, coarse = vmem_call(
        restrict_kernel,
        [shape((9, 16, 128), bf16), shape((count_x, 8, 128), f32)],
        scratch
        + [
            pltpu.VMEM((16, 48, 128), f32),
            pltpu.VMEM((256, 128), f32),
            pltpu.VMEM((9, 24, 128), f32),
        ],
        "restrict",
        pieces,
    )
    d, second, first = vmem_call(
        pack_kernel,
        [
            shape((40, 40, 128), bf16),
            shape((5, 9, 128), bf16),
            shape((5, 9, 128), bf16),
        ],
        scratch + [pltpu.VMEM((5, 16, 128), f32)],
        "pack",
        pieces + (own,),
    )
    near_m, next_m = swap(first, second, "gx")
    coarse = lax.all_to_all(coarse, "gx", 0, 0)
    fine = fine_sum(0, SPLIT, d, near)
    coarse, fine = lax.optimization_barrier((coarse, fine))
    parts = vmem_call(
        spread_kernel,
        [shape((count_y, 200, 128), bf16)],
        [pltpu.VMEM((200, 128), f32), pltpu.VMEM((16, 128), f32)],
        "spread",
        (coarse, jnp.asarray(matrix_x_np(spread)), own, next_m, near_m),
    )[0]
    parts, near = lax.optimization_barrier((parts, near))
    parts = lax.all_to_all(parts, "gy", 0, 0)
    fine = fine_sum(SPLIT, TAPS, d, near, fine)
    return vmem_call(
        final_kernel,
        [shape((20, 20, 128), f32)],
        [
            pltpu.VMEM((17, 40, 128), f32),
            pltpu.VMEM((4224, 128), bf16),
            pltpu.VMEM((4224, 128), bf16),
            pltpu.VMEM((112, 128), f32),
            pltpu.VMEM((320, 128), f32),
            pltpu.VMEM((112, 256), f32),
            pltpu.VMEM((176, 128), f32),
            pltpu.VMEM((count_y, 16, 128), f32),
        ],
        "final",
        (
            parts,
            jnp.asarray(matrix_y_np(spread)),
            jnp.asarray(matrix_z_np(spread)),
            near,
            far,
            fine,
        ),
    )[0]


def solution(mesh):
    return jax.shard_map(
        per_device,
        mesh=mesh,
        in_specs=(P("gx", "gy", None), P()),
        out_specs=P("gx", "gy", None),
        check_vma=False,
    )
```

```python
import functools
import numpy as np
import jax
import jax.numpy as jnp
from jax import lax
from jax.experimental import pallas as pl
from jax.experimental.pallas import tpu as pltpu
from jax.sharding import PartitionSpec as P

f32 = jnp.float32
bf16 = jnp.bfloat16
spread_norm = 1.2533141
REACH = 10
TAPS = 21
GROUP = 3
SPLIT = 9


def weight_np(offset):
    d = np.abs(offset)
    return np.where(d == 0, 1.0, np.where(d == 1, 0.5625, np.where(d == 3, -0.0625, 0.0)))


def top_matrix_np(n, spread):
    prolong = weight_np(np.arange(2 * n)[:, None] - 2 * np.arange(n)[None, :])
    offset = (np.arange(n)[:, None] - np.arange(n)[None, :]) / spread
    return prolong @ (np.exp(-offset * offset) / np.sqrt(spread * spread_norm))


def lane_tiles(m):
    return m.reshape(m.shape[0], -1, 128).transpose(1, 0, 2).astype(np.float32)


def matrix_x_np(spread):
    m = top_matrix_np(160, spread).reshape(320, 32, 5)
    out = np.zeros((328, 32, 8))
    out[1:321, :, :5] = m
    return lane_tiles(out.reshape(328, 256))


def matrix_y_np(spread):
    m = top_matrix_np(40, spread).reshape(80, 8, 5)
    out = np.zeros((88, 8, 8))
    out[2:82, :, :5] = m
    return lane_tiles(np.repeat(out.reshape(88, 64), 32, axis=1))


def matrix_z_np(spread):
    m = top_matrix_np(32, spread).T
    out = np.zeros((2, 8, 32, 2, 64))
    for par in range(2):
        out[par, :, :, par, :] = m[None]
    return out.reshape(512, 128).astype(np.float32)


def spots_np():
    taps = np.arange(TAPS)[:, None]
    lanes = np.arange(128)[None, :]
    near = lanes == (REACH - taps) % 128
    far = lanes == (64 + REACH - taps) % 128
    return near, far


def weight(d):
    d = jnp.abs(d)
    return jnp.where(d == 0, 1.0, jnp.where(d == 1, 0.5625, jnp.where(d == 3, -0.0625, 0.0))).astype(f32)


def exact_dot(rows, weights):
    count = rows.shape[0]
    high = rows.astype(bf16)
    rest = rows - high.astype(f32)
    middle = rest.astype(bf16)
    low = (rest - middle.astype(f32)).astype(bf16)
    out = jnp.dot(
        jnp.concatenate([high, middle, low], axis=0),
        weights.astype(bf16),
        preferred_element_type=f32,
    )
    return out[0:count] + (out[count : 2 * count] + out[2 * count :])


def parts_of(value):
    high = value.astype(bf16)
    return high, (value - high.astype(f32)).astype(bf16)


def two_part_dot(rows, weights):
    high, low = parts_of(rows)
    w_high, w_low = parts_of(weights)
    return jnp.dot(
        jnp.concatenate([high, high, low], axis=1),
        jnp.concatenate([w_high, w_low, w_high], axis=0),
        preferred_element_type=f32,
    )


def iota2(shape):
    return (lax.broadcasted_iota(jnp.int32, shape, 0), lax.broadcasted_iota(jnp.int32, shape, 1))


def vmem_call(body, out_shape, scratch, name, args, flops=0, limit=8):
    def spec(space):
        return pl.BlockSpec(memory_space=space)

    return pl.pallas_call(
        body,
        out_shape=out_shape,
        in_specs=[spec(pltpu.VMEM)] * len(args),
        out_specs=[spec(pltpu.VMEM)] * len(out_shape),
        scratch_shapes=scratch,
        compiler_params=pltpu.CompilerParams(vmem_limit_bytes=limit << 20),
        cost_estimate=pl.CostEstimate(flops=flops, bytes_accessed=1 << 16, transcendentals=0),
        name=name,
    )(*args)


def even(index):
    return index % 2 == 0


def edges_kernel(blk_ref, first_ref, second_ref, wide, dense):
    wide[:, 0:20, :] = blk_ref[...].astype(f32)
    start = jnp.where(even(lax.axis_index("gx")), 10, 0)
    for x in range(10):
        dense[0, 20 * x : 20 * x + 20, :] = wide[start + x, 0:20, :]
        dense[1, 20 * x : 20 * x + 20, :] = wide[10 - start + x, 0:20, :]
    first_ref[...] = dense[0].astype(bf16)
    second_ref[...] = dense[1].astype(bf16)


def rim_rows(wide, dense, count):
    start = jnp.where(even(lax.axis_index("gy")), 10, 0)
    for x in range(count):
        dense[0, 10 * x : 10 * x + 10, :] = wide[x, pl.ds(start, 10), :]
        dense[1, 10 * x : 10 * x + 10, :] = wide[x, pl.ds(10 - start, 10), :]


def rim_own_kernel(blk_ref, out_ref, wide, dense):
    wide[:, 0:20, :] = blk_ref[...].astype(f32)
    rim_rows(wide, dense, 20)
    out_ref[...] = dense[...]


def rim_kernel(own_ref, next_ref, near_ref, first_ref, second_ref, wide, dense):
    even_x = even(lax.axis_index("gx"))
    start = jnp.where(even_x, 10, 0)
    dense[0] = near_ref[...].astype(f32)
    dense[1] = next_ref[...].astype(f32)
    for x in range(10):
        wide[start + x, 0:20, :] = dense[0, 20 * x : 20 * x + 20, :]
        wide[10 - start + x, 0:20, :] = dense[1, 20 * x : 20 * x + 20, :]
    rim_rows(wide, dense, 20)
    for k, out_ref in enumerate((first_ref, second_ref)):
        out_ref[...] = jnp.concatenate([own_ref[k], dense[k]], axis=0).astype(bf16)


def assemble(blk_ref, next_x_ref, near_x_ref, next_y_ref, near_y_ref, d_ref, dense, sides):
    even_x = even(lax.axis_index("gx"))
    even_y = even(lax.axis_index("gy"))
    upper = jnp.where(even_y, 1, 0)
    dense[upper] = near_y_ref[...].astype(f32)
    dense[1 - upper] = next_y_ref[...].astype(f32)
    upper = jnp.where(even_x, 1, 0)
    sides[upper] = near_x_ref[...].astype(f32)
    sides[1 - upper] = next_x_ref[...].astype(f32)
    for x in range(40):
        p, i = x % 2, x // 2
        at = 10 * (x - 10 if 10 <= x < 30 else x + 20 if x < 10 else x)
        d_ref[p, i, 0:10, :] = dense[0, at : at + 10, :]
        d_ref[p, i, 30:40, :] = dense[1, at : at + 10, :]
        if 10 <= x < 30:
            centre = blk_ref[x - 10].astype(f32)
        else:
            at = 20 * (x % 30)
            centre = sides[x // 30, at : at + 20, :]
        d_ref[p, i, 10:30, :] = centre


def pack_kernel(
    blk_ref, next_x_ref, near_x_ref, next_y_ref, near_y_ref, mid_ref,
    d_out_ref, second_ref, first_ref,
    d_ref, dense, sides, mid,
):
    even_x = even(lax.axis_index("gx"))
    for n in range(5):
        mid[n] = mid_ref[n + 2].astype(f32)
        right, left = mid[n, 1:10, :], mid[n, 6:15, :]
        first_ref[n] = jnp.where(even_x, right, left).astype(bf16)
        second_ref[n] = jnp.where(even_x, left, right).astype(bf16)
    assemble(blk_ref, next_x_ref, near_x_ref, next_y_ref, near_y_ref, d_ref, dense, sides)
    for x in range(40):
        d_out_ref[x] = d_ref[x % 2, x // 2, 0:40, :].astype(bf16)


def restrict_kernel(
    blk_ref, next_x_ref, near_x_ref, next_y_ref, near_y_ref,
    own_ref, out_ref,
    d_ref, dense, sides, planes, cells, mid,
):
    assemble(blk_ref, next_x_ref, near_x_ref, next_y_ref, near_y_ref, d_ref, dense, sides)

    def fine(x):
        return d_ref[x % 2, x // 2]

    for i in range(16):
        c = 2 * i + 4
        planes[i] = (
            fine(c) + 0.5625 * (fine(c - 1) + fine(c + 1)) - 0.0625 * (fine(c - 3) + fine(c + 3))
        )
    for i in range(16):
        def tap(o):
            return planes[i, pl.ds(4 + o, 16, stride=2), :]
        cells[16 * i : 16 * i + 16, :] = (
            tap(0) + 0.5625 * (tap(-1) + tap(1)) - 0.0625 * (tap(-3) + tap(3))
        )
    zero = jnp.zeros((16, 128), f32)
    rows = []
    for n in range(9):
        pair = []
        for y in (2 * n - 4, 2 * n - 3):
            inside = -3 <= y <= 12
            pair.append(cells[pl.ds(y + 3, 16, stride=16), :] if inside else zero)
        rows.append(jnp.concatenate(pair, axis=1))
    r, c = iota2((256, 128))
    down_z = jnp.where(r // 128 == c // 64, weight(r % 128 - 2 * (c % 64)), 0.0)
    value = exact_dot(jnp.concatenate(rows, axis=0), down_z)
    r, c = iota2((144, 128))
    cell_x = 10 * lax.axis_index("gx") - 3 + r % 16
    cell_y = 10 * lax.axis_index("gy") - 4 + 2 * (r // 16) + c // 64
    inside = (cell_x >= 0) & (cell_x < 320) & (cell_y >= 0) & (cell_y < 80)
    value = jnp.where(inside, value, 0.0).astype(bf16).astype(f32)
    for n in range(9):
        mid[n, 0:16, :] = value[16 * n : 16 * n + 16]
        mid[n, 16:24, :] = jnp.zeros((8, 128), f32)
    for n in range(9):
        own_ref[n] = value[16 * n : 16 * n + 16].astype(bf16)

    lane = lax.broadcasted_iota(jnp.int32, (1, 128), 1)
    odd = lane >= 64
    weight_0 = jnp.where(odd, 0.5625, 1.0)
    weight_1 = jnp.where(odd, 0.5625, 0.0)
    weight_3 = jnp.where(odd, -0.0625, 0.0)
    r, c = iota2((128, 32))
    down_z = weight(r % 64 - 2 * c)
    sums = []
    for y in range(5):
        n = y + 2
        def tap(o):
            def part(k):
                return mid[k, pl.ds(3 + o, 8, stride=2), :]
            return (
                weight_0 * part(n) + weight_1 * part(n - 1) + weight_3 * (part(n - 2) + part(n + 1))
            )
        sums.append(tap(0) + 0.5625 * (tap(-1) + tap(1)) - 0.0625 * (tap(-3) + tap(3)))
    out = exact_dot(jnp.concatenate(sums, axis=0), down_z)
    main = jnp.concatenate([out[8 * y : 8 * y + 8] for y in range(4)], axis=1)[0:5]
    last = jnp.concatenate([out[32 + x : 33 + x] for x in range(4)], axis=1)
    rest = jnp.concatenate([out[36:37], jnp.zeros((1, 96), f32)], axis=1)
    row = jnp.concatenate([main, last, rest, jnp.zeros((1, 128), f32)], axis=0)
    for k in range(out_ref.shape[0]):
        out_ref[k] = row


def fine_kernel(lo, hi, first, d_in_ref, v_ref, *refs):
    if first:
        out_ref, w0, w1, e0, e1, d_ref = refs
    else:
        acc_ref, out_ref, w0, w1, e0, e1, d_ref = refs
    for x in range(40):
        d_ref[x % 2, x // 2, 0:40, :] = d_in_ref[x].astype(f32)
        d_ref[x % 2, x // 2, 40:48, :] = jnp.zeros((8, 128), f32)
    r, c = iota2((128, 128))
    mask = jnp.abs(r - c) <= REACH
    zero = jnp.zeros((128, 128), bf16)
    for w in (w0, w1):
        for k in range(GROUP):
            w[2816 * k : 2816 * k + 128, 128:256] = zero
            w[2816 * k + 2688 : 2816 * k + 2816, 0:128] = zero

    def build(w, start):
        for k in range(GROUP):
            for a in range(TAPS):
                line = jnp.broadcast_to(v_ref[pl.ds(a * TAPS + start + k, 1), :], (128, 128))
                line = pltpu.roll(line, 0, 1, stride=1, stride_axis=0)
                band = jnp.where(mask, line, 0.0).astype(bf16)
                at = 2816 * k + 128 * a
                w[at : at + 128, 0:128] = band
                w[at + 128 : at + 256, 128:256] = band

    def dot(w, e, start):
        tiles = []
        for k in range(GROUP):
            for p in range(2):
                for q in range(10):
                    part = d_ref[p, 2 * q : 2 * q + 2, pl.ds(start + k, 24), :].reshape(48, 128)
                    e[k, 0, 48 * q : 48 * q + 48, p * 128 : (p + 1) * 128] = part.astype(bf16)
                for q in range(9):
                    part = d_ref[p, 2 * q + 1 : 2 * q + 3, pl.ds(start + k, 24), :].reshape(48, 128)
                    e[k, 1, 48 * q : 48 * q + 48, p * 128 : (p + 1) * 128] = part.astype(bf16)
            tiles += [
                e[k, m % 2, 24 * (m - m % 2) : 24 * (m - m % 2) + 240, :] for m in range(11)
            ]
        lhs = jnp.concatenate(tiles, axis=1)
        out_ref[...] += jnp.dot(lhs, w[...], preferred_element_type=f32)

    out_ref[...] = jnp.zeros((240, 256), f32) if first else acc_ref[...]

    def step(t, _):
        b = lo + 2 * GROUP * t
        build(w0, b)
        dot(w0, e0, b)
        build(w1, b + GROUP)
        dot(w1, e1, b + GROUP)
        return 0

    groups = (hi - lo) // GROUP
    lax.fori_loop(0, groups // 2, step, 0)
    if groups % 2:
        build(w0, hi - GROUP)
        dot(w0, e0, hi - GROUP)


def fine_sum(lo, hi, d, v, acc=None):
    return vmem_call(
        functools.partial(fine_kernel, lo, hi, acc is None),
        [jax.ShapeDtypeStruct((240, 256), f32)],
        [pltpu.VMEM((GROUP * 2816, 256), bf16)] * 2
        + [pltpu.VMEM((GROUP, 2, 480, 256), bf16)] * 2
        + [pltpu.VMEM((2, 20, 48, 128), f32)],
        "fine_sum",
        (d, v) if acc is None else (d, v, acc),
        flops=(hi - lo) * 2 * 240 * 2816 * 256,
        limit=20,
    )[0]


def spread_kernel(recv_ref, mx_ref, own_ref, next_ref, near_ref, out_ref, buf, tail):
    even_x = even(lax.axis_index("gx"))
    start = 10 * lax.axis_index("gx")
    halves = [mx_ref[h, pl.ds(start, 16), :] for h in range(2)]
    lane = lax.broadcasted_iota(jnp.int32, (16, 128), 1) % 8
    rows = [jnp.concatenate(halves, axis=1)]
    for x in range(5):
        at = 5 if x < 4 else 6
        moved = [jnp.where(lane == at, pltpu.roll(h, at - x, 1), 0.0) for h in halves]
        rows.append(jnp.concatenate(moved, axis=1))
    coarse = recv_ref[...].reshape(8 * recv_ref.shape[0], 128)
    value = two_part_dot(jnp.concatenate(rows, axis=0), coarse)
    last = value[80:96, 0:32]
    for x in range(4):
        last = last + value[16 * x + 16 : 16 * x + 32, 32 * x : 32 * x + 32]
    tail[...] = jnp.concatenate([last, jnp.zeros((16, 96), f32)], axis=1)
    last = tail[pl.ds(0, 4, stride=4), :]
    for k in range(1, 4):
        last = last + pltpu.roll(tail[pl.ds(k, 4, stride=4), :], 32 * k, 1)
    for n in range(5):
        near, other = near_ref[n].astype(f32), next_ref[n].astype(f32)
        buf[33 * n : 33 * n + 8, :] = jnp.where(even_x, other, near)[1:9]
        buf[33 * n + 8 : 33 * n + 24, :] = own_ref[n + 2].astype(f32)
        buf[33 * n + 24 : 33 * n + 33, :] = jnp.where(even_x, near, other)
    for at, part in ((165, last), (176, value[0:16])):
        rows = part.shape[0]
        high = part.astype(bf16).astype(f32)
        buf[at : at + rows, :] = high
        buf[at + rows : at + 2 * rows, :] = part - high
    buf[173:176, :] = jnp.zeros((3, 128), f32)
    packed = buf[...].astype(bf16)
    for k in range(out_ref.shape[0]):
        out_ref[k] = packed


def final_kernel(
    recv_ref, my_ref, mz_ref, near_ref, far_ref, fine_ref, out_ref,
    cells, w0, w1, acc, moved, wide, line, tail,
):
    index_x = lax.axis_index("gx")
    index_y = lax.axis_index("gy")
    count = recv_ref.shape[0]
    cells[:, 32:40, :] = jnp.zeros((17, 8, 128), f32)
    for step in range(-2, 3):
        source = index_y + step
        inside = (source >= 0) & (source < count)
        got = recv_ref[jnp.clip(source, 0, count - 1), 0:176, :].astype(f32)
        line[...] = jnp.where(inside, got, 0.0)
        for p in range(5):
            n = 5 * step + 6 + p
            if 0 <= n < 17:
                cells[n, 0:33, :] = line[33 * p : 33 * p + 33, :]

    r, c = iota2((128, 128))
    mask = jnp.abs(r % 64 - c % 64) <= REACH

    def band_rows(w, a, at):
        base = TAPS * TAPS + a * TAPS
        for j in range(11):
            same = near_ref[pl.ds(base + 2 * j, 1), :]
            upper = same
            lower = same
            if j > 0:
                upper = same + far_ref[pl.ds(base + 2 * j - 1, 1), :]
            if j < 10:
                lower = same + far_ref[pl.ds(base + 2 * j + 1, 1), :]
            upper = pltpu.roll(jnp.broadcast_to(upper, (64, 128)), 0, 1, stride=1, stride_axis=0)
            lower = pltpu.roll(jnp.broadcast_to(lower, (64, 128)), 64, 1, stride=1, stride_axis=0)
            band = jnp.where(mask, jnp.concatenate([upper, lower], axis=0), 0.0).astype(bf16)
            w[at + 128 * j : at + 128 * j + 128, :] = band

    def build(w, a):
        for k in range(3):
            band_rows(w, a + k, 1408 * k)

    def dot(w, a):
        rows = []
        for k in range(3):
            part = [cells[n, pl.ds(a + k, 16), :].astype(bf16) for n in range(17)]
            rows.append([jnp.concatenate(part[g : g + 11], axis=1) for g in range(7)])
        lhs = jnp.concatenate(
            [jnp.concatenate([rows[k][g] for k in range(3)], axis=1) for g in range(7)], axis=0
        )
        acc[...] += jnp.dot(lhs, w[...], preferred_element_type=f32)

    acc[...] = jnp.zeros((112, 128), f32)
    build(w0, 0)

    def step(t, _):
        a = 6 * t
        build(w1, a + 3)
        dot(w0, a)
        build(w0, a + 6)
        dot(w1, a + 3)
        return 0

    lax.fori_loop(0, 3, step, 0)
    dot(w0, 18)

    start = 10 * index_y
    sums = [[None] * 14, [None] * 14]
    for k in range(count):
        main = recv_ref[k, 176:192, :].astype(f32) + recv_ref[k, 192:208, :].astype(f32)
        last = recv_ref[k, 160:176, :].astype(f32)
        last = last[5:9] + last[9:13]
        tail[k, pl.ds(0, 4, stride=4), :] = last
        for r in range(1, 4):
            tail[k, pl.ds(r, 4, stride=4), :] = pltpu.roll(last, 128 - 32 * r, 1)
        for h, value in ((0, main), (1, tail[k])):
            rows_y = my_ref[2 * k + h, pl.ds(start, 16), :]
            for y in range(14):
                term = value * rows_y[y : y + 1, :]
                sums[h][y] = term if k == 0 else sums[h][y] + term
    rows = [
        jnp.concatenate([sums[h][2 * n + p] for p in range(2) for h in range(2)], axis=1)
        for n in range(7)
    ]
    top = two_part_dot(jnp.concatenate(rows, axis=0), mz_ref[...])
    total = acc[...] + top
    r, c = iota2((112, 128))
    cell_x = 10 * index_x - 1 + r % 16
    cell_y = 10 * index_y - 2 + 2 * (r // 16) + c // 64
    inside = (cell_x >= 0) & (cell_x < 320) & (cell_y >= 0) & (cell_y < 80)
    total = jnp.where(inside, total, 0.0)
    r, c = iota2((128, 256))
    up_z = jnp.where(r // 64 == c // 128, weight(c % 128 - 2 * (r % 64)), 0.0)
    wide[...] = exact_dot(total, up_z)

    def middle_y(y):
        n, par = (y + 2) // 2, y % 2
        return wide[16 * n : 16 * n + 16, 128 * par : 128 * par + 128]

    for y in range(20):
        m = y // 2
        if y % 2 == 0:
            value = middle_y(m)
        else:
            value = 0.5625 * (middle_y(m) + middle_y(m + 1)) - 0.0625 * (
                middle_y(m - 1) + middle_y(m + 2)
            )
        moved[16 * y : 16 * y + 16, :] = value
    planes = [moved[pl.ds(k, 20, stride=16), :] for k in range(13)]
    for x in range(20):
        m = x // 2
        if x % 2 == 0:
            value = planes[m + 1]
        else:
            value = 0.5625 * (planes[m + 1] + planes[m + 2]) - 0.0625 * (planes[m] + planes[m + 3])
        out_ref[x] = value + fine_ref[24 * m : 24 * m + 20, 128 * (x % 2) : 128 * (x % 2) + 128]


def swap(first, second, axis):
    count = lax.axis_size(axis)
    pairs = [(k, k + 1) for k in range(0, count - 1, 2)]
    others = [(k, k + 1) for k in range(1, count - 1, 2)]

    def both(ends):
        return ends + [(b, a) for a, b in ends]

    second = lax.ppermute(second, axis, both(others))
    return lax.ppermute(first, axis, both(pairs)), second


def per_device(charges, kernels):
    count_x = lax.axis_size("gx")
    count_y = lax.axis_size("gy")
    spread = charges.shape[0] * count_x / 16.0
    shape = jax.ShapeDtypeStruct
    scratch = [pltpu.VMEM((20, 24, 128), f32), pltpu.VMEM((2, 200, 128), f32)]
    first, second = vmem_call(
        edges_kernel, [shape((200, 128), bf16)] * 2, scratch, "edges", (charges,)
    )
    near_x, next_x = swap(first, second, "gx")
    own = vmem_call(
        rim_own_kernel,
        [shape((2, 200, 128), f32)],
        scratch,
        "rim_own",
        (charges,),
        flops=1 << 20,
    )[0]
    first, second = vmem_call(
        rim_kernel,
        [shape((400, 128), bf16)] * 2,
        scratch,
        "rim",
        (own, next_x, near_x),
    )
    first, second, kernels = lax.optimization_barrier((first, second, kernels))
    near, far = (
        jnp.dot(kernels.reshape(-1, TAPS), jnp.asarray(m, bf16), preferred_element_type=f32)
        for m in spots_np()
    )
    near_y, next_y = swap(first, second, "gy")
    next_y, near_y, near, far = lax.optimization_barrier((next_y, near_y, near, far))
    pieces = (charges, next_x, near_x, next_y, near_y)
    scratch = [
        pltpu.VMEM((2, 20, 48, 128), f32),
        pltpu.VMEM((2, 400, 128), f32),
        pltpu.VMEM((2, 200, 128), f32),
    ]
    own, coarse = vmem_call(
        restrict_kernel,
        [shape((9, 16, 128), bf16), shape((count_x, 8, 128), f32)],
        scratch
        + [
            pltpu.VMEM((16, 48, 128), f32),
            pltpu.VMEM((256, 128), f32),
            pltpu.VMEM((9, 24, 128), f32),
        ],
        "restrict",
        pieces,
    )
    d, second, first = vmem_call(
        pack_kernel,
        [
            shape((40, 40, 128), bf16),
            shape((5, 9, 128), bf16),
            shape((5, 9, 128), bf16),
        ],
        scratch + [pltpu.VMEM((5, 16, 128), f32)],
        "pack",
        pieces + (own,),
    )
    near_m, next_m = swap(first, second, "gx")
    coarse = lax.all_to_all(coarse, "gx", 0, 0)
    fine = fine_sum(0, SPLIT, d, near)
    coarse, fine = lax.optimization_barrier((coarse, fine))
    parts = vmem_call(
        spread_kernel,
        [shape((count_y, 208, 128), bf16)],
        [pltpu.VMEM((208, 128), f32), pltpu.VMEM((16, 128), f32)],
        "spread",
        (coarse, jnp.asarray(matrix_x_np(spread)), own, next_m, near_m),
    )[0]
    parts, near = lax.optimization_barrier((parts, near))
    parts = lax.all_to_all(parts, "gy", 0, 0)
    fine = fine_sum(SPLIT, TAPS, d, near, fine)
    return vmem_call(
        final_kernel,
        [shape((20, 20, 128), f32)],
        [
            pltpu.VMEM((17, 40, 128), f32),
            pltpu.VMEM((4224, 128), bf16),
            pltpu.VMEM((4224, 128), bf16),
            pltpu.VMEM((112, 128), f32),
            pltpu.VMEM((320, 128), f32),
            pltpu.VMEM((112, 256), f32),
            pltpu.VMEM((176, 128), f32),
            pltpu.VMEM((count_y, 16, 128), f32),
        ],
        "final",
        (
            parts,
            jnp.asarray(matrix_y_np(spread)),
            jnp.asarray(matrix_z_np(spread)),
            near,
            far,
            fine,
        ),
    )[0]


def solution(mesh):
    return jax.shard_map(
        per_device,
        mesh=mesh,
        in_specs=(P("gx", "gy", None), P()),
        out_specs=P("gx", "gy", None),
        check_vma=False,
    )
```
